32 devices in a mesh: dp: 16 (over z, y, x), tensor: 2 (over core).
Axes of the slice: x: 2, y: 2, z: 4, core: 2. Of those that a mesh axis runs over, the one named last changes fastest.
Arguments:
- tokens: bfloat16 [16, 2048, 768], P('dp', 'tensor'), may hold values from -6 to 6
- segment_ids: int32 [16, 2048], P('dp', 'tensor'), may hold values from 0 to 7, never falling along the last dimension, each value on 1 to 1536 neighbouring positions
- routes: int32 [16, 2048, 2], P('dp', 'tensor'), may hold values from 0 to 11, all different within a row
- prev_logits: float32 [16, 2048, 12], P('dp', 'tensor'), may hold values from -6 to 6
- cotangent: bfloat16 [16, 2048, 768], P('dp', 'tensor'), may hold values from -6 to 6
- proj_weight: bfloat16 [3, 768, 768], P(None, 'dp', 'tensor'), may hold values from -0.21875 to 0.21875
- out_weight: bfloat16 [768, 768], P('dp', 'tensor'), may hold values from -0.875 to 0.875
- norm_gain: bfloat16 [2, 768], P(None, 'dp'), may hold values from 0.5 to 1.5
- expert_weight: bfloat16 [8, 3, 768, 2048], P(None, None, 'dp', 'tensor'), may hold values from -0.21875 to 0.21875
- router: bfloat16 [768, 16], P('dp'), may hold values from -0.109375 to 0.109375
- constant_vectors: bfloat16 [2, 768], P(None, 'dp'), may hold values from -6 to 6
- gate_mixing: float32 [12, 12], replicated, may hold values from -1.25 to 1.25
Outputs:
- mixed: bfloat16 [16, 2048, 768], P('dp', 'tensor')
- tokens_grad: float32 [16, 2048, 768], P('dp', 'tensor')
- prev_grad: float32 [16, 2048, 12], P('dp', 'tensor')
- proj_grad: float32 [3, 768, 768], P(None, 'dp', 'tensor')
- out_proj_grad: float32 [768, 768], P('dp', 'tensor')
- gain_grad: float32 [2, 768], P(None, 'dp')
- expert_grad: float32 [8, 3, 768, 2048], P(None, None, 'dp', 'tensor')
- router_grad: float32 [768, 16], P('dp')
- constant_grad: float32 [2, 768], P(None, 'dp')
- mixing_grad: float32 [12, 12], replicated
The draws below stay inside these ranges and needn't reach their ends.
Inputs may be any that keep to these rules, and one draw needn't show every extreme that they name: `segment_ids`: within a sequence the ids never fall; each document holds at most 1536 tokens, and one holds exactly 1536. `routes`: the two experts of a token differ.
All inputs are finite; a program needn't handle non-finite values.
Results may differ from the reference program's by a relative error of at most 0.017.
Values may be sent and summed in bfloat16 or wider, within the bound.
A program may use at most 384 MiB of HBM per device.

```python
import math
import jax
import jax.numpy as jnp
import numpy as np
from jax import lax

D = 768
HEADS = 12
HEAD_DIM = 64
FF = 2048
EXPERTS_FF = 8
EXPERTS = 12
TOP = 2
DOCS = 8
SEQ = 2048
HHD = 768
SEQS = 16
CAPACITY = 341
DOC_MOST = 1536


def shard_levels(rng, extent, pieces, low, top_value):
    gain = 1.0
    for dim, shards_of in pieces:
        steps = jax.random.uniform(jax.random.fold_in(jax.random.fold_in(rng, 6), dim), (shards_of,), jnp.float32, low / len(pieces), top_value / len(pieces))
        gain = gain * jnp.repeat(jnp.exp(steps), extent[dim] // shards_of).reshape((-1,) + (1,) * (len(extent) - 1 - dim))
    return gain


def choose_distinct(stream_key, rows, amount, top, lift):
    sequence = jax.random.permutation(jax.random.fold_in(stream_key, 1), amount)
    favour = sequence
    for power in range(3):
        favour = favour * favour // amount
    favour = favour * lift // amount
    chance = jax.random.randint(jax.random.fold_in(stream_key, 2), (rows, amount), 0, 4096) + favour
    holders = jax.random.permutation(jax.random.fold_in(stream_key, 3), rows)[jnp.arange(amount) % rows]
    chance = jnp.where(jnp.arange(rows)[:, None] == holders[None, :], 1 << 14, chance)
    score = chance * amount + jnp.arange(amount)
    return lax.top_k(score.astype(jnp.int32), top)[1].astype(jnp.int32)


def split_up(count, total, limit, lean):
    weights = [(1 << 20) // math.isqrt(rank ** lean) + 1 for rank in range(2, count + 1)]
    surplus, given = total - limit - (count - 1), [1] * (count - 1)
    while surplus > 0:
        candidates = [i for i in range(count - 1) if given[i] < limit]
        whole, left = sum([weights[i] for i in candidates]), surplus
        for i in candidates:
            extra = min(limit - given[i], max(1, left * weights[i] // whole), surplus)
            given[i] = given[i] + extra
            surplus = surplus - extra
    return np.array([limit] + given)


def uneven_parts(rng, amount, total, limit, slope):
    if amount == 2:
        one = jax.random.randint(rng, (), max(1, total - limit), min(limit, total - 1) + 1)
        return jnp.stack([one, total - one])
    lengths = jnp.asarray(split_up(amount, total, limit, slope), jnp.int32)
    twos = (amount - 1) // 2
    giver, sink = lengths[1:1 + 2 * twos:2], lengths[2:2 + 2 * twos:2]
    margin = jnp.minimum(giver - 1, limit - sink)
    passed = jax.random.randint(jax.random.fold_in(rng, 1), (twos,), 0, 1 << 20) % (margin + 1)
    lengths = lengths.at[1:1 + 2 * twos:2].set(giver - passed).at[2:2 + 2 * twos:2].set(sink + passed)
    return lengths[jax.random.permutation(jax.random.fold_in(rng, 2), amount)]


def centred(stream_key, dims, scale, limit, split=(), held_as=jnp.bfloat16):
    values = jax.random.normal(stream_key, dims, jnp.float32) * scale
    if len(split) > 0:
        values = shard_levels(stream_key, dims, split, -0.22, 0.18) * values
    return jnp.clip(values, min=-limit, max=limit).astype(held_as)


def setup_inputs(seed: int = 0) -> dict:
    splits = jax.random.split(jax.random.key(seed), 13)
    return {
        "tokens": centred(splits[0], (SEQS, SEQ, D), 1.0, 6.0, ((0, 16), (1, 2))),
        "segment_ids": jax.vmap(lambda own: jnp.searchsorted(jnp.cumsum(uneven_parts(own, DOCS, SEQ, DOC_MOST, 2)), jnp.arange(SEQ), side="right"))(jax.random.split(splits[1], SEQS)).reshape((SEQS, SEQ)).astype(jnp.int32),
        "routes": choose_distinct(splits[2], SEQS * SEQ, EXPERTS, TOP, 1365).reshape((SEQS, SEQ, TOP)),
        "prev_logits": centred(splits[3], (SEQS, SEQ, EXPERTS), 1.0, 6.0, ((0, 16), (1, 2)), jnp.float32),
        "cotangent": centred(splits[4], (SEQS, SEQ, D), 1.0, 6.0, ((0, 16), (1, 2))),
        "proj_weight": centred(splits[5], (3, D, HHD), D ** -0.5, 0.21875, ((1, 16), (2, 2))),
        "out_weight": centred(splits[6], (D, HHD), (HHD // 16) ** -0.5, 0.875, ((0, 16), (1, 2))),
        "norm_gain": jnp.clip(1.0 + 0.1 * jax.random.normal(splits[7], (2, D), jnp.float32), 0.5, 1.5).astype(jnp.bfloat16),
        "expert_weight": centred(splits[8], (EXPERTS_FF, 3, D, FF), D ** -0.5, 0.21875, ((2, 16), (3, 2))),
        "router": centred(splits[9], (D, EXPERTS + 4), (4 * D) ** -0.5, 0.109375, ((0, 16),)),
        "constant_vectors": centred(splits[10], (2, D), 1.0, 6.0, ((1, 16),)),
        "gate_mixing": centred(splits[11], (EXPERTS, EXPERTS), 24 ** -0.5, 1.25, (), jnp.float32),
    }


EPS = 1e-05
HIGH = lax.Precision.HIGHEST
NEG = -1e+30

@jax.custom_vjp
def low(v):
    return lax.optimization_barrier(v.astype(jnp.bfloat16)).astype(jnp.float32)

@jax.custom_vjp
def low_back(v):
    return v

def low_keep(v):
    return (low(v), None)

def low_pass(kept, grad):
    return (grad,)

def back_keep(v):
    return (v, None)

def back_low(kept, grad):
    return (low(grad),)
low.defvjp(low_keep, low_pass)
low_back.defvjp(back_keep, back_low)

def rms_scale(rows):
    return lax.rsqrt(lax.optimization_barrier(jnp.mean(rows * rows, axis=-1, keepdims=True)) + EPS)

def softmax_last(values):
    peak = lax.optimization_barrier(jnp.max(values, axis=-1, keepdims=True))
    expo = jnp.exp(values - peak)
    return expo / lax.optimization_barrier(jnp.sum(expo, axis=-1, keepdims=True))

def slot_table(flat_routes):
    onehot = (flat_routes[:, None] == jnp.arange(EXPERTS_FF, dtype=jnp.int32)[None, :]).astype(jnp.int32)
    position = lax.optimization_barrier(jnp.sum((jnp.cumsum(onehot, axis=0) - onehot) * onehot, axis=1)).astype(jnp.int32)
    keep = (flat_routes < EXPERTS_FF) & (position < CAPACITY)
    target = jnp.where(keep, flat_routes, EXPERTS_FF).astype(jnp.int32)
    pairs = jnp.arange(flat_routes.shape[0], dtype=jnp.int32)
    empty = jnp.full((EXPERTS_FF, CAPACITY), flat_routes.shape[0], jnp.int32)
    return empty.at[target, position].set(pairs, mode='drop')

def layer(rows_in, prev, proj, outw, gains, experts, router, constants, mixing, segs, rts, table):
    seq = rows_in.shape[0]
    width = rows_in.shape[1]
    normed_one = low(rows_in * rms_scale(rows_in) * gains[0])

    def project(index):
        return low_back(low(jnp.dot(normed_one, proj[index], precision=HIGH))).reshape(seq, HEADS, HEAD_DIM)
    queries = project(0)
    keys = project(1)
    values = project(2)
    block = min(512, seq)
    scale = HEAD_DIM ** (-0.5)
    cols = jnp.arange(seq, dtype=jnp.int32)

    def one_block(start):
        q_blk = lax.dynamic_slice_in_dim(queries, start, block, 0)
        seg_rows = lax.dynamic_slice_in_dim(segs, start, block, 0)
        rows = start + jnp.arange(block, dtype=jnp.int32)
        allowed = (cols[None, :] <= rows[:, None]) & (segs[None, :] == seg_rows[:, None])
        scores = low_back(jnp.einsum('qhd,khd->hqk', q_blk, keys, precision=HIGH) * scale)
        masked = jnp.where(allowed[None], scores, NEG)
        probs = softmax_last(masked)
        return jnp.einsum('hqk,khd->qhd', low(probs), values, precision=HIGH)
    starts = (jnp.arange(seq // block, dtype=jnp.int32) * block).astype(jnp.int32)
    heads_out = lax.map(jax.checkpoint(one_block), starts)
    mixed_heads = low_back(low(heads_out.reshape(seq, HEADS * HEAD_DIM)))
    attn_out = low_back(jnp.dot(mixed_heads, outw.T, precision=HIGH))
    resid = rows_in + attn_out
    normed_two = low(resid * rms_scale(resid) * gains[1])
    router_rows = jnp.dot(normed_two, router, precision=HIGH)
    logits = router_rows[:, :EXPERTS] + jnp.dot(prev, mixing, precision=HIGH)
    picks = (rts[:, :, None] == jnp.arange(EXPERTS, dtype=jnp.int32)[None, None, :]).astype(jnp.float32)
    gates = softmax_last(lax.optimization_barrier(jnp.sum(picks * logits[:, None, :], axis=-1)))
    gates_low = low(gates)
    slot_tok = table // 2
    pad_two = jnp.concatenate([normed_two, jnp.zeros((1, width), jnp.float32)], 0)
    slot_rows = pad_two[slot_tok]
    slot_gate = jnp.concatenate([gates_low.reshape(-1), jnp.zeros((1,), jnp.float32)], 0)[table]
    pre_gate = low_back(jnp.einsum('ecd,edf->ecf', slot_rows, experts[:, 0], precision=HIGH))
    pre_up = low_back(jnp.einsum('ecd,edf->ecf', slot_rows, experts[:, 1], precision=HIGH))
    hidden = low(pre_gate * jax.nn.sigmoid(pre_gate) * pre_up)
    expert_out = low_back(jnp.einsum('ecf,edf->ecd', hidden, experts[:, 2], precision=HIGH))
    ffn_out = jnp.zeros((seq + 1, width), jnp.float32).at[slot_tok].add(expert_out * slot_gate[:, :, None])[:seq]
    alphas = softmax_last(router_rows[:, EXPERTS:].reshape(seq, 2, 2))
    copy_weight = lax.optimization_barrier(jnp.sum(gates * picks[:, :, EXPERTS_FF + 1], axis=1))
    const_weight = lax.optimization_barrier(jnp.sum(gates[:, :, None] * picks[:, :, EXPERTS_FF + 2:], axis=1))
    own_weight = copy_weight + lax.optimization_barrier(jnp.sum(const_weight * alphas[:, :, 0], axis=1))
    other_out = own_weight[:, None] * normed_two + jnp.dot(const_weight * alphas[:, :, 1], constants, precision=HIGH)
    return resid + ffn_out + other_out

def reference(tokens, segment_ids, routes, prev_logits, cotangent, proj_weight, out_weight, norm_gain, expert_weight, router, constant_vectors, gate_mixing):
    proj = proj_weight.astype(jnp.float32)
    outw = out_weight.astype(jnp.float32)
    gains = norm_gain.astype(jnp.float32)
    experts = expert_weight.astype(jnp.float32)
    router_f = router.astype(jnp.float32)
    constants = constant_vectors.astype(jnp.float32)

    def step(totals, items):
        rows, prev, grad_rows, segs, rts = items
        table = slot_table(rts.reshape(-1))

        def forward(rows_in, prev_in, proj_in, outw_in, gains_in, experts_in, router_in, constants_in, mixing_in):
            return layer(rows_in, prev_in, proj_in, outw_in, gains_in, experts_in, router_in, constants_in, mixing_in, segs, rts, table)
        result, pull = jax.vjp(forward, rows.astype(jnp.float32), prev, proj, outw, gains, experts, router_f, constants, gate_mixing)
        grads = pull(grad_rows.astype(jnp.float32))
        totals = tuple((total + grad for total, grad in zip(totals, grads[2:])))
        return (totals, (result.astype(jnp.bfloat16), grads[0], grads[1]))
    init = (jnp.zeros_like(proj), jnp.zeros_like(outw), jnp.zeros_like(gains), jnp.zeros_like(experts), jnp.zeros_like(router_f), jnp.zeros_like(constants), jnp.zeros_like(gate_mixing))
    totals, outputs = lax.scan(step, init, (tokens, prev_logits, cotangent, segment_ids, routes))
    return (outputs[0], outputs[1], outputs[2], totals[0], totals[1], totals[2], totals[3], totals[4], totals[5], totals[6])
```

```python
import jax
import jax.numpy as jnp
from jax import lax
from jax.sharding import PartitionSpec as P

HEAD_DIM = 64
EXPERTS_FF = 8
EXPERTS = 12
CAPACITY = 341


EPS = 1e-05
HIGH = lax.Precision.HIGHEST
NEG = -1e30
LANES = 128
single = jnp.float32
half = jnp.bfloat16


def rms_scale(rows):
    return lax.rsqrt(jnp.mean(rows * rows, axis=-1, keepdims=True) + EPS)


def softmax_last(values):
    peak = jnp.max(values, axis=-1, keepdims=True)
    expo = jnp.exp(values - peak)
    return expo / jnp.sum(expo, axis=-1, keepdims=True)


def mm(a, b):
    return jnp.dot(a, b, preferred_element_type=single)


def mm_nt(a, b):
    return lax.dot_general(a, b, (((1,), (1,)), ((), ())), preferred_element_type=single)


def mm_tn(a, b):
    return lax.dot_general(a, b, (((0,), (0,)), ((), ())), preferred_element_type=single)


def swap(x):
    return lax.ppermute(x, "tensor", [(0, 1), (1, 0)])


def in_order(own, other):
    first = lax.axis_index("tensor") == 0
    return jnp.concatenate([jnp.where(first, own, other), jnp.where(first, other, own)], 0)


def half_of(full, which):
    count = full.shape[0] // 2
    return lax.dynamic_slice_in_dim(full, which * count, count, 0)


def pair_sum(full):
    core = lax.axis_index("tensor")
    other = swap(half_of(full, 1 - core).astype(half))
    return half_of(full, core) + other.astype(single)


def slot_onehot(routes_all, core, per_core, padded):
    seq = routes_all.shape[0]
    experts = jnp.arange(EXPERTS_FF, dtype=jnp.int32)
    member = (routes_all[:, 0:1] == experts) | (routes_all[:, 1:2] == experts)
    chunk = min(128, seq)
    blocks = member.astype(half).reshape(seq // chunk, chunk, EXPERTS_FF)
    order = jnp.arange(chunk)
    strict = (order[None, :] < order[:, None]).astype(half)
    within = jnp.einsum("ij,bje->bie", strict, blocks, preferred_element_type=single)
    totals = jnp.sum(blocks.astype(single), axis=1)
    number = jnp.arange(seq // chunk)
    before = jnp.dot((number[None, :] < number[:, None]).astype(single), totals, precision=HIGH)
    position = (within + before[:, None, :]).reshape(seq, EXPERTS_FF).astype(jnp.int32)
    place = position - core * per_core
    kept = member & (position < CAPACITY) & (place >= 0) & (place < per_core)
    place = jnp.where(kept, place, -1).T
    slots = jnp.arange(padded, dtype=jnp.int32)
    return (place[:, None, :] == slots[None, :, None]).astype(half)


def block_scores(q_blk, key_rows, seg_rows, seg_keys, first):
    count = q_blk.shape[0]
    rows = first + jnp.arange(count, dtype=jnp.int32)
    cols = jnp.arange(key_rows.shape[0], dtype=jnp.int32)
    allowed = (cols[None, :] <= rows[:, None]) & (seg_keys[None, :] == seg_rows[:, None])
    scores = jnp.einsum(
        "qhd,khd->hqk", q_blk, key_rows, preferred_element_type=jnp.float32
    ) * HEAD_DIM ** (-0.5)
    return jnp.where(allowed[None], scores, NEG)


def attention_forward(queries, keys_all, values_all, seg_keys):
    seq, heads_local = queries.shape[:2]
    block = min(512, seq)
    outputs = []
    log_totals = []
    for first in range(0, seq, block):
        last = first + block
        scores = block_scores(
            queries[first:last], keys_all[:last], seg_keys[first:last], seg_keys[:last], first
        )
        peak = jnp.max(scores, axis=-1, keepdims=True)
        expo = jnp.exp(scores - peak)
        total = jnp.sum(expo, axis=-1, keepdims=True)
        probs_low = (expo / total).astype(half)
        outputs.append(
            jnp.einsum(
                "hqk,khd->qhd", probs_low, values_all[:last], preferred_element_type=single
            ).astype(half)
        )
        log_totals.append(peak + jnp.log(total))
    return jnp.concatenate(outputs, 0).reshape(seq, heads_local * HEAD_DIM), log_totals


def attention_backward(queries, keys_all, values_all, seg_keys, log_totals, heads_grad):
    seq, heads_local = queries.shape[:2]
    block = min(512, seq)
    query_grads = []
    key_grad = jnp.zeros((seq, heads_local, HEAD_DIM), single)
    value_grad = jnp.zeros((seq, heads_local, HEAD_DIM), single)
    for index, first in enumerate(range(0, seq, block)):
        last = first + block
        q_blk = queries[first:last]
        scores = block_scores(q_blk, keys_all[:last], seg_keys[first:last], seg_keys[:last], first)
        probs = jnp.exp(scores - log_totals[index])
        prob_grad = jnp.einsum(
            "qhd,khd->hqk", heads_grad[first:last], values_all[:last], preferred_element_type=single
        )
        score_grad = (
            probs * (prob_grad - jnp.sum(probs * prob_grad, axis=-1, keepdims=True))
        ).astype(half)
        query_grads.append(
            jnp.einsum("hqk,khd->qhd", score_grad, keys_all[:last], preferred_element_type=single)
            * HEAD_DIM ** (-0.5)
        )
        key_grad = key_grad.at[:last].add(
            jnp.einsum("hqk,qhd->khd", score_grad, q_blk, preferred_element_type=single)
            * HEAD_DIM ** (-0.5)
        )
        value_grad = value_grad.at[:last].add(
            jnp.einsum(
                "hqk,qhd->khd",
                probs.astype(half),
                heads_grad[first:last],
                preferred_element_type=single,
            )
        )
    return (
        jnp.stack([jnp.concatenate(query_grads, 0), key_grad, value_grad])
        .reshape(3, seq, heads_local * HEAD_DIM)
        .astype(half)
    )


def expert_math(rows, grad_rows, gate, weights):
    out_grad = (grad_rows.astype(single) * gate).astype(half)
    gate_pre = mm(rows, weights[0])
    up_pre = mm(rows, weights[1])
    sigma = jax.nn.sigmoid(gate_pre)
    active = gate_pre * sigma
    hidden = (active * up_pre).astype(half)
    hidden_grad = mm(out_grad, weights[2])
    gate_pre_grad = (hidden_grad * up_pre * sigma * (1.0 + gate_pre * (1.0 - sigma))).astype(half)
    up_pre_grad = (hidden_grad * active).astype(half)
    expert_out = mm_nt(hidden, weights[2])
    in_grad = mm_nt(gate_pre_grad, weights[0]) + mm_nt(up_pre_grad, weights[1])
    weight_grads = jnp.stack(
        [
            mm_tn(rows, gate_pre_grad).astype(half),
            mm_tn(rows, up_pre_grad).astype(half),
            mm_tn(out_grad, hidden).astype(half),
        ]
    )
    return expert_out, in_grad, weight_grads


def per_device(
    tokens,
    segment_ids,
    routes,
    prev_logits,
    cotangent,
    proj_weight,
    out_weight,
    norm_gain,
    expert_weight,
    router,
    constant_vectors,
    gate_mixing,
):
    members = lax.axis_size("dp")
    groups = members // EXPERTS_FF
    cubes = [[g * EXPERTS_FF + i for i in range(EXPERTS_FF)] for g in range(groups)]
    core = lax.axis_index("tensor")
    d_rows, hh = out_weight.shape
    per_core = -(-CAPACITY // 2)
    padded = -(-(per_core + 3) // 16) * 16

    def exchange(blocks):
        return lax.all_to_all(blocks, "dp", 0, 0, axis_index_groups=cubes, tiled=True)

    pack = jnp.concatenate(
        [
            proj_weight.transpose(1, 0, 2).reshape(d_rows, 3 * hh),
            out_weight,
            norm_gain.T,
            constant_vectors.T,
            router,
        ],
        1,
    )
    full_pack = lax.all_gather(pack, "dp", axis=0, tiled=True)
    width = full_pack.shape[0]
    proj_full = full_pack[:, : 3 * hh]
    outw_own = full_pack[:, 3 * hh : 4 * hh]
    outw_other = swap(outw_own)
    rest = full_pack[:, 4 * hh :]
    gains = rest[:, :2].T.astype(single)
    const_f = rest[:, 2:4].T.astype(single)
    router_full = rest[:, 4:]
    sent_weight = jnp.broadcast_to(expert_weight[None], (groups,) + expert_weight.shape)
    sent_weight = sent_weight.reshape((members,) + expert_weight.shape[1:])
    my_weight = lax.all_to_all(sent_weight, "dp", 0, 0, tiled=True)
    weights_own = my_weight.transpose(1, 0, 2, 3).reshape(3, width, -1)
    weights_other = swap(weights_own)
    weights = jnp.concatenate([weights_own, weights_other], 2)

    ids = jnp.concatenate([segment_ids[0][:, None], routes[0]], 1)
    ids_all = in_order(ids, swap(ids))
    seg_keys = ids_all[:, 0]
    onehot = slot_onehot(ids_all[:, 1:], core, per_core, padded).reshape(EXPERTS_FF * padded, -1)
    dy_all = in_order(cotangent[0], swap(cotangent[0]))
    slot_dy = exchange(mm(onehot, dy_all).astype(half).reshape(EXPERTS_FF, padded, width))

    x_rows = tokens[0].astype(single)
    local_rows = x_rows.shape[0]
    x_all = in_order(tokens[0], swap(tokens[0])).astype(single)
    scale_all = rms_scale(x_all)
    full_one = (x_all * scale_all * gains[0]).astype(half)
    scale_one = half_of(scale_all, core)
    seq = full_one.shape[0]
    heads_local = hh // HEAD_DIM
    qkv = mm(full_one, proj_full).astype(half)
    queries, keys_all, values_all = (
        qkv[:, i * hh : (i + 1) * hh].reshape(seq, heads_local, HEAD_DIM) for i in range(3)
    )
    heads_out, log_totals = attention_forward(queries, keys_all, values_all, seg_keys)
    ho_own = half_of(heads_out, core)
    ho_other = swap(half_of(heads_out, 1 - core))
    resid = x_rows + mm_nt(ho_own, outw_own) + mm_nt(ho_other, outw_other)
    scale_two = rms_scale(resid)
    normed_two = (resid * scale_two * gains[1]).astype(half)
    two_rows = normed_two.astype(single)
    router_rows = mm(normed_two, router_full)
    prev_rows = prev_logits[0]
    logits = router_rows[:, :EXPERTS] + jnp.dot(prev_rows, gate_mixing, precision=HIGH)
    route_rows = routes[0]
    picks = (route_rows[:, :, None] == jnp.arange(EXPERTS, dtype=jnp.int32)[None, None, :]).astype(
        single
    )
    gates = softmax_last(jnp.sum(picks * logits[:, None, :], axis=-1))
    gate_low = gates.astype(half)

    gate_columns = jnp.sum(picks[:, :, :EXPERTS_FF] * gate_low.astype(single)[:, :, None], axis=1)
    spread = jnp.pad(gate_columns.astype(half), ((0, 0), (0, LANES - EXPERTS_FF)))
    both = jnp.concatenate([normed_two, spread], 1)
    both_all = in_order(both, swap(both))
    picked = mm(onehot, both_all).astype(half).reshape(EXPERTS_FF, padded, width + LANES)
    slot_gate = jnp.stack([picked[e, :, width + e] for e in range(EXPERTS_FF)])
    gate_row = jnp.pad(slot_gate, ((0, 0), (0, width - padded)))[:, None, :]
    row_number = lax.broadcasted_iota(jnp.int32, (1, padded, 1), 1)
    sent_rows = jnp.where(row_number == padded - 1, gate_row, picked[:, :, :width])
    got_rows = exchange(sent_rows)

    got_gate = got_rows[:, padded - 1, :padded].astype(single)
    count = EXPERTS_FF * padded
    gate_col = got_gate.reshape(count, 1)
    rows = got_rows.reshape(count, width)
    dy_rows = slot_dy.reshape(count, width)
    expert_out, in_grad, weight_grads = expert_math(rows, dy_rows, gate_col, weights)
    gated_out = (expert_out * gate_col).astype(half).reshape(EXPERTS_FF, padded, width)
    gate_dot = jnp.sum(dy_rows.astype(single) * expert_out, axis=-1).reshape(EXPERTS_FF, padded)
    dot_high = gate_dot.astype(half)
    dot_low = (gate_dot - dot_high.astype(single)).astype(half)
    lanes = ((0, 0), (0, width - padded))
    sent_grad = jnp.where(
        row_number == padded - 1,
        jnp.pad(dot_low, lanes)[:, None, :],
        jnp.where(
            row_number == padded - 2,
            jnp.pad(dot_high, lanes)[:, None, :],
            in_grad.astype(half).reshape(EXPERTS_FF, padded, width),
        ),
    )
    back_grad = exchange(sent_grad)
    back_out = exchange(gated_out)

    ff_half = weights_own.shape[2]
    grads_own = weight_grads[:, :, :ff_half].astype(single)
    grads_own = (grads_own + swap(weight_grads[:, :, ff_half:]).astype(single)).astype(half)
    grads_sent = grads_own.reshape(3, members, d_rows, ff_half).transpose(1, 0, 2, 3)
    grads_got = lax.all_to_all(grads_sent, "dp", 0, 0, tiled=True)
    expert_shard = jnp.sum(
        grads_got.reshape((groups, EXPERTS_FF) + grads_got.shape[1:]).astype(single), axis=0
    )

    dots = back_grad[:, padded - 2 :, :padded]
    eye = jnp.eye(EXPERTS_FF, dtype=half)
    dot_columns = jnp.concatenate(
        [dots[:, 0, :, None] * eye[:, None, :], dots[:, 1, :, None] * eye[:, None, :]], 2
    )
    dot_columns = jnp.pad(dot_columns, ((0, 0), (0, 0), (0, LANES - 2 * EXPERTS_FF)))
    back_both = jnp.concatenate([back_grad, dot_columns], 2).reshape(count, width + LANES)
    two_back = pair_sum(mm_tn(onehot, back_both))
    ffn_out = pair_sum(mm_tn(onehot, back_out.reshape(count, width)))
    two_grad_ffn = two_back[:, :width]
    expert_dot = (
        two_back[:, width : width + EXPERTS_FF]
        + two_back[:, width + EXPERTS_FF : width + 2 * EXPERTS_FF]
    )
    gate_grad_ffn = jnp.sum(picks[:, :, :EXPERTS_FF] * expert_dot[:, None, :], axis=-1)

    grad_rows = cotangent[0].astype(single)
    alphas = softmax_last(router_rows[:, EXPERTS:].reshape(local_rows, 2, 2))
    copy_weight = jnp.sum(gates * picks[:, :, EXPERTS_FF + 1], axis=1)
    const_weight = jnp.sum(gates[:, :, None] * picks[:, :, EXPERTS_FF + 2 :], axis=1)
    own_weight = copy_weight + jnp.sum(const_weight * alphas[:, :, 0], axis=1)
    vec_weight = const_weight * alphas[:, :, 1]
    other_out = own_weight[:, None] * two_rows + jnp.dot(vec_weight, const_f, precision=HIGH)
    mixed = (resid + ffn_out + other_out).astype(half)[None]
    own_dot = jnp.sum(grad_rows * two_rows, axis=-1)
    vec_dot = jnp.dot(grad_rows, const_f.T, precision=HIGH)
    value_dot = jnp.stack(
        [
            jnp.zeros_like(own_dot),
            own_dot,
            alphas[:, 0, 0] * own_dot + alphas[:, 0, 1] * vec_dot[:, 0],
            alphas[:, 1, 0] * own_dot + alphas[:, 1, 1] * vec_dot[:, 1],
        ],
        -1,
    )
    gate_grad = gate_grad_ffn + jnp.sum(picks[:, :, EXPERTS_FF:] * value_dot[:, None, :], axis=-1)
    alpha_grad = jnp.stack([const_weight * own_dot[:, None], const_weight * vec_dot], -1)
    mix_rows_grad = alphas * (alpha_grad - jnp.sum(alphas * alpha_grad, axis=-1, keepdims=True))
    const_vec_grad = jnp.dot(vec_weight.T, grad_rows, precision=HIGH)
    chosen_grad = gates * (gate_grad - jnp.sum(gates * gate_grad, axis=-1, keepdims=True))
    logit_grad = jnp.sum(picks * chosen_grad[:, :, None], axis=1)
    router_rows_grad = jnp.concatenate([logit_grad, mix_rows_grad.reshape(local_rows, 4)], -1)
    two_grad = (
        two_grad_ffn
        + own_weight[:, None] * grad_rows
        + jnp.dot(router_rows_grad, router_full.astype(single).T, precision=HIGH)
    )
    router_grad = jnp.dot(two_rows.T, router_rows_grad, precision=HIGH)
    prev_grad = jnp.dot(logit_grad, gate_mixing.T, precision=HIGH)
    mixing_grad = jnp.dot(prev_rows.T, logit_grad, precision=HIGH)
    weighted_two = two_grad * gains[1]
    resid_grad = grad_rows + scale_two * (
        weighted_two
        - resid * scale_two * scale_two * jnp.mean(weighted_two * resid, axis=-1, keepdims=True)
    )
    gain_two_grad = jnp.sum(two_grad * resid * scale_two, axis=0)
    attn_grad = resid_grad.astype(half)
    hg_own = mm(attn_grad, outw_own).astype(half)
    hg_other = swap(mm(attn_grad, outw_other).astype(half))
    heads_grad = in_order(hg_own, hg_other).reshape(seq, heads_local, HEAD_DIM)
    out_w_grad = mm_tn(attn_grad, ho_own) + swap(mm_tn(attn_grad, ho_other).astype(half)).astype(
        single
    )
    qkv_grad = attention_backward(queries, keys_all, values_all, seg_keys, log_totals, heads_grad)
    qkv_grad = jnp.concatenate([qkv_grad[0], qkv_grad[1], qkv_grad[2]], 1)
    one_part = mm_nt(qkv_grad, proj_full)
    gain_one_grad = jnp.sum(one_part * x_all * scale_all, axis=0)
    one_grad = pair_sum(one_part)
    proj_grad = mm_tn(full_one, qkv_grad)
    weighted_one = one_grad * gains[0]
    tokens_grad = resid_grad + scale_one * (
        weighted_one
        - x_rows * scale_one * scale_one * jnp.mean(weighted_one * x_rows, axis=-1, keepdims=True)
    )

    dense = jnp.concatenate([proj_grad, out_w_grad], 1).astype(half)
    dense = lax.all_to_all(dense.reshape(members, d_rows, 4 * hh), "dp", 0, 0, tiled=True)
    dense = jnp.sum(dense.astype(single), axis=0)
    proj_shard = dense[:, : 3 * hh].reshape(d_rows, 3, hh).transpose(1, 0, 2)
    outw_shard = dense[:, 3 * hh :]

    by_feature = jnp.concatenate(
        [gain_one_grad[:, None], gain_two_grad[:, None], const_vec_grad.T, router_grad], 1
    )
    columns = by_feature.shape[1]
    small = by_feature.reshape(members, d_rows * columns)
    mix = jnp.broadcast_to(mixing_grad.reshape(1, -1), (members, mixing_grad.size))
    small = jnp.concatenate([small, mix], 1)
    used = small.shape[1]
    wide = -(-used // (8 * LANES)) * 8 * LANES
    small = jnp.pad(small, ((0, 0), (0, wide - used))).reshape(members, wide // LANES, LANES)
    small = small + swap(small)
    small = jnp.sum(lax.all_to_all(small, "dp", 0, 0, tiled=True), axis=0).reshape(-1)
    features = small[: d_rows * columns].reshape(d_rows, columns)
    mixing_total = small[d_rows * columns : used].reshape(mixing_grad.shape)
    return (
        mixed,
        tokens_grad[None],
        prev_grad[None],
        proj_shard,
        outw_shard,
        features[:, :2].T,
        expert_shard,
        features[:, 4:],
        features[:, 2:4].T,
        mixing_total,
    )


def solution(mesh):
    return jax.shard_map(
        per_device,
        mesh=mesh,
        in_specs=(
            P("dp", "tensor", None),
            P("dp", "tensor"),
            P("dp", "tensor", None),
            P("dp", "tensor", None),
            P("dp", "tensor", None),
            P(None, "dp", "tensor"),
            P("dp", "tensor"),
            P(None, "dp"),
            P(None, None, "dp", "tensor"),
            P("dp", None),
            P(None, "dp"),
            P(),
        ),
        out_specs=(
            P("dp", "tensor", None),
            P("dp", "tensor", None),
            P("dp", "tensor", None),
            P(None, "dp", "tensor"),
            P("dp", "tensor"),
            P(None, "dp"),
            P(None, None, "dp", "tensor"),
            P("dp", None),
            P(None, "dp"),
            P(),
        ),
        check_vma=False,
    )
```

```python
import functools

import jax
import jax.numpy as jnp
from jax import lax
from jax.experimental import pallas as pl
from jax.experimental.pallas import tpu as pltpu
from jax.sharding import PartitionSpec as P

HEAD_DIM = 64
EXPERTS_FF = 8
EXPERTS = 12
CAPACITY = 341


EPS = 1e-05
HIGH = lax.Precision.HIGHEST
NEG = -1e30
LANES = 128
DOCS = 8
LOG2E = 1.4426950408889634
MESH = pl.DeviceIdType.MESH
single = jnp.float32
half = jnp.bfloat16


def rms_scale(rows):
    return lax.rsqrt(jnp.mean(rows * rows, axis=-1, keepdims=True) + EPS)


def softmax_last(values):
    peak = jnp.max(values, axis=-1, keepdims=True)
    expo = jnp.exp(values - peak)
    return expo / jnp.sum(expo, axis=-1, keepdims=True)


def mm(a, b):
    return jnp.dot(a, b, preferred_element_type=single)


def mm_nt(a, b):
    return lax.dot_general(a, b, (((1,), (1,)), ((), ())), preferred_element_type=single)


def mm_tn(a, b):
    return lax.dot_general(a, b, (((0,), (0,)), ((), ())), preferred_element_type=single)


def swap(x):
    return lax.ppermute(x, "tensor", [(0, 1), (1, 0)])


def in_order(own, other):
    first = lax.axis_index("tensor") == 0
    return jnp.concatenate([jnp.where(first, own, other), jnp.where(first, other, own)], 0)


def half_of(full, which):
    count = full.shape[0] // 2
    return lax.dynamic_slice_in_dim(full, which * count, count, 0)


def pair_sum(full):
    core = lax.axis_index("tensor")
    other = swap(half_of(full, 1 - core).astype(half))
    return half_of(full, core) + other.astype(single)


def slot_onehot(routes_all, core, per_core, padded):
    seq = routes_all.shape[0]
    experts = jnp.arange(EXPERTS_FF, dtype=jnp.int32)
    member = (routes_all[:, 0:1] == experts) | (routes_all[:, 1:2] == experts)
    chunk = min(128, seq)
    blocks = member.astype(half).reshape(seq // chunk, chunk, EXPERTS_FF)
    order = jnp.arange(chunk)
    strict = (order[None, :] < order[:, None]).astype(half)
    within = jnp.einsum("ij,bje->bie", strict, blocks, preferred_element_type=single)
    totals = jnp.sum(blocks.astype(single), axis=1)
    number = jnp.arange(seq // chunk)
    before = jnp.dot((number[None, :] < number[:, None]).astype(single), totals, precision=HIGH)
    position = (within + before[:, None, :]).reshape(seq, EXPERTS_FF).astype(jnp.int32)
    place = position - core * per_core
    kept = member & (position < CAPACITY) & (place >= 0) & (place < per_core)
    place = jnp.where(kept, place, -1).T
    slots = jnp.arange(padded, dtype=jnp.int32)
    return (place[:, None, :] == slots[None, :, None]).astype(half)


def fit(seq, want):
    return want if seq % want == 0 else seq

def block_bounds(seg, size):
    seq = seg.shape[0]
    member = (seg[:, None] == jnp.arange(DOCS, dtype=jnp.int32)).astype(jnp.int32)
    sizes = jnp.sum(member, axis=0)
    ends = jnp.cumsum(sizes)
    start = jnp.sum(member * (ends - sizes), axis=1)
    end = jnp.sum(member * ends, axis=1) - 1
    edges = start.reshape(-1, size)
    number = jnp.arange(seq // size, dtype=jnp.int32)
    low = edges[:, 0] // size
    plain = jnp.clip((edges[:, -1] + size - 1) // size, low, number)
    high = end.reshape(-1, size)[:, -1] // size
    clear = jnp.sum((edges[None, :, -1] <= number[:, None] * size).astype(jnp.int32), axis=1)
    clear = jnp.clip(clear, number + 1, high + 1)
    return jnp.stack([low, plain, high, clear]), start

def head_lanes(h, rows):
    lane = lax.broadcasted_iota(jnp.int32, (rows, LANES), 1)
    return (lane < HEAD_DIM) if h % 2 == 0 else (lane >= HEAD_DIM)

def fwd_kernel(heads, bounds, q_ref, k_ref, v_ref, start_ref, o_ref, lse_ref, s_ref, m_ref, l_ref, acc_ref, qm_ref):
    size = q_ref.shape[0]
    i = pl.program_id(0)
    low, plain = bounds[0, i], bounds[1, i]
    factor = LOG2E * HEAD_DIM ** -0.5
    for h in range(heads):
        pair = pl.ds(h // 2 * LANES, LANES)
        qm_ref[h] = jnp.where(head_lanes(h, size), q_ref[:, pair], 0).astype(half)
    m_ref[...] = jnp.full(m_ref.shape, NEG, single)
    l_ref[...] = jnp.zeros(l_ref.shape, single)
    acc_ref[...] = jnp.zeros(acc_ref.shape, single)

    def score(j, masked):
        rows = pl.ds(pl.multiple_of(j * size, size), size)
        if masked:
            row = i * size + lax.broadcasted_iota(jnp.int32, (size, size), 0)
            col = j * size + lax.broadcasted_iota(jnp.int32, (size, size), 1)
            allowed = (col <= row) & (col >= start_ref[...])
        for h in range(heads):
            s = mm_nt(qm_ref[h], k_ref[rows, pl.ds(h // 2 * LANES, LANES)])
            if masked:
                s = jnp.where(allowed, s, NEG)
            s_ref[h, j] = s
            m = m_ref[h]
            for c in range(size // LANES):
                m = jnp.maximum(m, s[:, c * LANES : (c + 1) * LANES])
            m_ref[h] = m

    pl.loop(low, plain)(lambda j: score(j, True))
    pl.loop(plain, i)(lambda j: score(j, False))
    score(i, True)
    for h in range(heads):
        m_ref[h] = jnp.broadcast_to(jnp.max(m_ref[h], axis=1, keepdims=True) * factor, (size, LANES))

    def gather(j):
        rows = pl.ds(pl.multiple_of(j * size, size), size)
        for h in range(heads):
            s = s_ref[h, j]
            m = m_ref[h]
            l = l_ref[h]
            parts = []
            for c in range(size // LANES):
                p = jnp.exp2(s[:, c * LANES : (c + 1) * LANES] * factor - m)
                l = l + p
                parts.append(p.astype(half))
            l_ref[h] = l
            acc_ref[h] += jnp.dot(jnp.concatenate(parts, 1), v_ref[rows, pl.ds(h // 2 * LANES, LANES)], preferred_element_type=single)

    pl.loop(low, i + 1)(gather)
    lane = lax.broadcasted_iota(jnp.int32, (size, LANES), 1)
    lse = jnp.zeros((size, LANES), single)
    for h in range(0, heads, 2):
        outs = []
        for k in (h, h + 1):
            l = jnp.sum(l_ref[k], axis=1, keepdims=True)
            outs.append(acc_ref[k] / l)
            lse = jnp.where(lane == k, m_ref[k] + jnp.log2(l), lse)
        o_ref[:, pl.ds(h // 2 * LANES, LANES)] = jnp.where(lane < HEAD_DIM, outs[0], outs[1])
    lse_ref[...] = lse

def attention_forward(qkv, seg_bounds, starts, size):
    seq = qkv.shape[0]
    hh = qkv.shape[1] // 3
    heads = hh // HEAD_DIM
    return pl.pallas_call(
        functools.partial(fwd_kernel, heads),
        grid_spec=pltpu.PrefetchScalarGridSpec(
            num_scalar_prefetch=1,
            grid=(seq // size,),
            in_specs=[
                pl.BlockSpec((size, hh), lambda i, b: (i, 0)),
                pl.BlockSpec((seq, hh), lambda i, b: (0, 1)),
                pl.BlockSpec((seq, hh), lambda i, b: (0, 2)),
                pl.BlockSpec((size, 1), lambda i, b: (i, 0)),
            ],
            out_specs=[
                pl.BlockSpec((size, hh), lambda i, b: (i, 0)),
                pl.BlockSpec((size, LANES), lambda i, b: (i, 0)),
            ],
            scratch_shapes=[
                pltpu.VMEM((heads, seq // size, size, size), single),
                pltpu.VMEM((heads, size, LANES), single),
                pltpu.VMEM((heads, size, LANES), single),
                pltpu.VMEM((heads, size, LANES), single),
                pltpu.VMEM((heads, size, LANES), half),
            ],
        ),
        out_shape=[
            jax.ShapeDtypeStruct((seq, hh), single),
            jax.ShapeDtypeStruct((seq, LANES), single),
        ],
        compiler_params=pltpu.CompilerParams(vmem_limit_bytes=48 << 20),
        cost_estimate=pl.CostEstimate(flops=4 * seq * seq * LANES * heads, bytes_accessed=16 * seq * hh, transcendentals=0),
    )(seg_bounds, qkv, qkv, qkv, starts[:, None])

def bwd_kernel(
    heads, bounds, q_ref, k_ref, v_ref, do_ref, o_ref, lse_ref, start_ref, out_ref, dq_ref, dk_ref, dv_ref, stat_ref
):
    size = k_ref.shape[0]
    j = pl.program_id(0)
    high, clear = bounds[2, j], bounds[3, j]
    factor = LOG2E * HEAD_DIM ** -0.5
    hh = k_ref.shape[1]

    @pl.when(j == 0)
    def _():
        dq_ref[...] = jnp.zeros(dq_ref.shape, single)
        feature = lax.broadcasted_iota(jnp.int32, (hh, LANES), 0)
        lane = lax.broadcasted_iota(jnp.int32, (hh, LANES), 1)
        pick = (feature // HEAD_DIM + 8 == lane).astype(half)

        @pl.loop(0, q_ref.shape[0] // size)
        def _(i):
            rows = pl.ds(pl.multiple_of(i * size, size), size)
            product = o_ref[rows, :] * do_ref[rows, :].astype(single)
            top = product.astype(half)
            low = (product - top.astype(single)).astype(half)
            both = mm(top, pick) + mm(low, pick) + lse_ref[rows, :]
            stat_ref[:, rows] = both.T[:16, :]

    dk_ref[...] = jnp.zeros(dk_ref.shape, single)
    dv_ref[...] = jnp.zeros(dv_ref.shape, single)

    def step(i, masked):
        rows = pl.ds(pl.multiple_of(i * size, size), size)
        if masked:
            key = j * size + lax.broadcasted_iota(jnp.int32, (size, size), 0)
            query = i * size + lax.broadcasted_iota(jnp.int32, (size, size), 1)
            allowed = (key <= query) & (key >= start_ref[:, rows])
        for pair in range(heads // 2):
            lanes = pl.ds(pair * LANES, LANES)
            k, v = k_ref[:, lanes], v_ref[:, lanes]
            q, do = q_ref[rows, lanes], do_ref[rows, lanes]
            ps, dss, qs, dos, ks = [], [], [], [], []
            for h in (2 * pair, 2 * pair + 1):
                mine = head_lanes(h, size)
                qm = jnp.where(mine, q, 0).astype(half)
                dom = jnp.where(mine, do, 0).astype(half)
                s = mm_nt(k, qm) * factor - stat_ref[pl.ds(h, 1), rows]
                if masked:
                    s = jnp.where(allowed, s, NEG)
                p = jnp.exp2(s)
                ds = p * (mm_nt(v, dom) - stat_ref[pl.ds(8 + h, 1), rows])
                ps.append(p.astype(half))
                dss.append(ds.astype(half))
                qs.append(qm)
                dos.append(dom)
                ks.append(jnp.where(mine, k, 0).astype(half))
            dv_ref[:, lanes] += jnp.dot(jnp.concatenate(ps, 1), jnp.concatenate(dos, 0), preferred_element_type=single)
            dk_ref[:, lanes] += jnp.dot(jnp.concatenate(dss, 1), jnp.concatenate(qs, 0), preferred_element_type=single)
            dq_ref[rows, lanes] += mm_tn(jnp.concatenate(dss, 0), jnp.concatenate(ks, 0))

    step(j, True)
    pl.loop(j + 1, clear)(lambda i: step(i, False))
    pl.loop(clear, high + 1)(lambda i: step(i, True))
    mine = pl.ds(pl.multiple_of(j * size, size), size)
    out_ref[mine, pl.ds(hh, hh)] = (dk_ref[...] * HEAD_DIM ** -0.5).astype(half)
    out_ref[mine, pl.ds(2 * hh, hh)] = dv_ref[...].astype(half)
    out_ref[mine, pl.ds(0, hh)] = (dq_ref[mine, :] * HEAD_DIM ** -0.5).astype(half)

def attention_backward(qkv, do, heads_out, lse, seg_bounds, starts, size):
    seq = qkv.shape[0]
    hh = qkv.shape[1] // 3
    heads = hh // HEAD_DIM
    return pl.pallas_call(
        functools.partial(bwd_kernel, heads),
        grid_spec=pltpu.PrefetchScalarGridSpec(
            num_scalar_prefetch=1,
            grid=(seq // size,),
            in_specs=[
                pl.BlockSpec((seq, hh), lambda j, b: (0, 0)),
                pl.BlockSpec((size, hh), lambda j, b: (j, 1)),
                pl.BlockSpec((size, hh), lambda j, b: (j, 2)),
                pl.BlockSpec((seq, hh), lambda j, b: (0, 0)),
                pl.BlockSpec((seq, hh), lambda j, b: (0, 0)),
                pl.BlockSpec((seq, LANES), lambda j, b: (0, 0)),
                pl.BlockSpec((1, seq), lambda j, b: (0, 0)),
            ],
            out_specs=pl.BlockSpec((seq, 3 * hh), lambda j, b: (0, 0)),
            scratch_shapes=[
                pltpu.VMEM((seq, hh), single),
                pltpu.VMEM((size, hh), single),
                pltpu.VMEM((size, hh), single),
                pltpu.VMEM((16, seq), single),
            ],
        ),
        out_shape=jax.ShapeDtypeStruct((seq, 3 * hh), half),
        compiler_params=pltpu.CompilerParams(vmem_limit_bytes=48 << 20),
        cost_estimate=pl.CostEstimate(flops=10 * seq * seq * LANES * heads, bytes_accessed=20 * seq * hh, transcendentals=0),
    )(seg_bounds, qkv, qkv, qkv, do, heads_out, lse, starts[None, :])


def gather_kernel(members, low, x_ref, o_ref, send_sem, recv_sem, own_sem):
    me = lax.axis_index("dp")
    high = members // low
    mine, row = lax.rem(me, low), me // low

    def beside(k):
        return row * low + lax.rem(mine + k, low)

    def across(k):
        return lax.rem(row + k, high) * low + mine

    peers = [beside(k) for k in range(1, low)] + [across(k) for k in range(1, high)]
    barrier = pltpu.get_barrier_semaphore()
    for peer in peers:
        pl.semaphore_signal(barrier, inc=1, device_id={"dp": peer}, device_id_type=MESH)
    pl.semaphore_wait(barrier, len(peers))

    def push(source, block, target, slot):
        copy = pltpu.make_async_remote_copy(
            src_ref=source,
            dst_ref=o_ref.at[block],
            send_sem=send_sem.at[slot],
            recv_sem=recv_sem.at[block],
            device_id={"dp": target},
            device_id_type=MESH,
        )
        copy.start()
        return copy

    def arrived(block):
        pltpu.make_async_remote_copy(
            src_ref=x_ref,
            dst_ref=o_ref.at[block],
            send_sem=send_sem.at[0],
            recv_sem=recv_sem.at[block],
            device_id={"dp": peers[0]},
            device_id_type=MESH,
        ).wait_recv()

    own = pltpu.make_async_copy(x_ref, o_ref.at[me], own_sem)
    own.start()
    sent = [push(x_ref, me, across(k), k) for k in range(1, high)]
    sent += [push(x_ref, me, beside(k), high + k) for k in range(1, low)]
    for k in range(1, high):
        block = across(high - k)
        arrived(block)
        for step in range(1, low):
            sent.append(push(o_ref.at[block], block, beside(step), high + k * low + step))
    for k in range(1, low):
        block = beside(low - k)
        arrived(block)
        for step in range(1, high):
            arrived(lax.rem(block + step * low, members))
    for copy in sent:
        copy.wait_send()
    own.wait()


def gather_all(x, members):
    low = 4 if members % 4 == 0 else 1
    high = members // low
    return pl.pallas_call(
        functools.partial(gather_kernel, members, low),
        out_shape=jax.ShapeDtypeStruct((members,) + x.shape, x.dtype),
        in_specs=[pl.BlockSpec(memory_space=pl.ANY)],
        out_specs=pl.BlockSpec(memory_space=pl.ANY),
        scratch_shapes=[
            pltpu.SemaphoreType.DMA((high * (low + 1),)),
            pltpu.SemaphoreType.DMA((members,)),
            pltpu.SemaphoreType.DMA,
        ],
        compiler_params=pltpu.CompilerParams(collective_id=0, has_side_effects=True),
        name="gather_all",
    )(x)


def exchange_kernel(count, *refs):
    size = EXPERTS_FF
    xs, os = refs[:count], refs[count : 2 * count]
    send_sem, recv_sem, own_sem = refs[2 * count :]
    me = lax.axis_index("dp")
    mine = lax.rem(me, size)
    base = me - mine
    barrier = pltpu.get_barrier_semaphore()
    for k in range(1, size):
        peer = base + lax.rem(mine + k, size)
        pl.semaphore_signal(barrier, inc=1, device_id={"dp": peer}, device_id_type=MESH)
    pl.semaphore_wait(barrier, size - 1)
    copies = []
    for a in range(count):
        for k in range(1, size):
            to = lax.rem(mine + k, size)
            copies.append(
                pltpu.make_async_remote_copy(
                    src_ref=xs[a].at[to],
                    dst_ref=os[a].at[mine],
                    send_sem=send_sem.at[a, k],
                    recv_sem=recv_sem.at[a, k],
                    device_id={"dp": base + to},
                    device_id_type=MESH,
                )
            )
        copies.append(pltpu.make_async_copy(xs[a].at[mine], os[a].at[mine], own_sem.at[a]))
    for copy in copies:
        copy.start()
    for copy in copies:
        copy.wait()


def exchange(number, *arrays):
    count = len(arrays)
    return pl.pallas_call(
        functools.partial(exchange_kernel, count),
        out_shape=[jax.ShapeDtypeStruct(x.shape, x.dtype) for x in arrays],
        in_specs=[pl.BlockSpec(memory_space=pl.ANY)] * count,
        out_specs=[pl.BlockSpec(memory_space=pl.ANY)] * count,
        scratch_shapes=[
            pltpu.SemaphoreType.DMA((count, EXPERTS_FF)),
            pltpu.SemaphoreType.DMA((count, EXPERTS_FF)),
            pltpu.SemaphoreType.DMA((count,)),
        ],
        compiler_params=pltpu.CompilerParams(collective_id=number, has_side_effects=True),
        name=f"exchange_{number}",
    )(*arrays)


def expert_kernel(
    padded,
    x_ref,
    dy_ref,
    own_ref,
    other_ref,
    out_ref,
    grad_ref,
    own_grad_ref,
    other_grad_ref,
    gate_ref,
    og_ref,
    xt_ref,
    ogt_ref,
    eo_ref,
    ig_ref,
    hid_ref,
    pg_ref,
    pu_ref,
    dot_ref,
):
    f = pl.program_id(0)
    sources = x_ref.shape[0]
    count, width = og_ref.shape
    chunk = count // 4
    x_all = x_ref.reshape(count, width)

    @pl.when(f == 0)
    def _():
        for s in range(sources):
            rows = pl.ds(s * padded, padded)
            gates = x_ref[s, padded - 16 :, : 2 * LANES].astype(single).T
            gate = jnp.broadcast_to(gates[:padded, 15:16], (padded, LANES))
            gate_ref[rows, :] = gate
            og_ref[rows, :] = (dy_ref[s].astype(single) * gate[:, :1]).astype(half)
        xt_ref[...] = x_all[...].T
        ogt_ref[...] = og_ref[...].T
        eo_ref[...] = jnp.zeros(eo_ref.shape, single)
        ig_ref[...] = jnp.zeros(ig_ref.shape, single)

    for w_ref, wg_ref in ((own_ref, own_grad_ref), (other_ref, other_grad_ref)):
        shape = wg_ref.shape[0], wg_ref.shape[2], wg_ref.shape[3]
        gate_w, up_w, down_w = (w_ref[:, k].reshape(width, shape[2]) for k in range(3))
        for r in range(4):
            rows = pl.ds(r * chunk, chunk)
            x = x_all[rows, :]
            og = og_ref[rows, :]
            pre = mm(x, gate_w)
            up = mm(x, up_w)
            hg = mm(og, down_w)
            sigma = jax.nn.sigmoid(pre)
            active = pre * sigma
            hidden = (active * up).astype(half)
            pg = (hg * up * (sigma * (1.0 + pre * (1.0 - sigma)))).astype(half)
            pu = (hg * active).astype(half)
            hid_ref[rows, :] = hidden
            pg_ref[rows, :] = pg
            pu_ref[rows, :] = pu
            eo_ref[rows, :] += mm_nt(hidden, down_w)
            ig_ref[rows, :] += mm_nt(pg, gate_w) + mm_nt(pu, up_w)
        wg_ref[:, 0] = mm(xt_ref[...], pg_ref[...]).astype(half).reshape(shape)
        wg_ref[:, 1] = mm(xt_ref[...], pu_ref[...]).astype(half).reshape(shape)
        wg_ref[:, 2] = mm(ogt_ref[...], hid_ref[...]).astype(half).reshape(shape)

    @pl.when(f == pl.num_programs(0) - 1)
    def _():
        dot_ref[...] = jnp.zeros(dot_ref.shape, single)
        ones = jnp.ones((16, width), half)
        for s in range(sources):
            rows = pl.ds(s * padded, padded)
            eo = eo_ref[rows, :]
            out_ref[s] = (eo * gate_ref[rows, :1]).astype(half)
            grad_ref[s] = ig_ref[rows, :].astype(half)
            product = eo * dy_ref[s].astype(single)
            top = product.astype(half)
            low = (product - top.astype(single)).astype(half)
            dot_ref[:, :padded] = mm_nt(ones, top) + mm_nt(ones, low)
            dots = dot_ref[...]
            high = dots.astype(half)
            rest = (dots - high.astype(single)).astype(half)
            row = lax.broadcasted_iota(jnp.int32, dots.shape, 0)
            tail = ig_ref[pl.ds((s + 1) * padded - 16, 16), : 2 * LANES].astype(half)
            tail = jnp.where(row == 14, high.astype(single), jnp.where(row == 15, rest.astype(single), tail.astype(single)))
            grad_ref[s, padded - 16 :, : 2 * LANES] = tail.astype(half)


def expert_step(x, dy, own, other, padded):
    sources, _, width = x.shape
    count = sources * padded
    m, _, r, ff = own.shape
    block = fit(ff, 256)
    whole = pl.BlockSpec((sources, padded, width), lambda f: (0, 0, 0))
    part = pl.BlockSpec((m, 3, r, block), lambda f: (0, 0, 0, f))
    return pl.pallas_call(
        functools.partial(expert_kernel, padded),
        grid=(ff // block,),
        in_specs=[whole, whole, part, part],
        out_specs=[whole, whole, part, part],
        out_shape=[
            jax.ShapeDtypeStruct(x.shape, half),
            jax.ShapeDtypeStruct(x.shape, half),
            jax.ShapeDtypeStruct(own.shape, half),
            jax.ShapeDtypeStruct(own.shape, half),
        ],
        scratch_shapes=[
            pltpu.VMEM((count, LANES), single),
            pltpu.VMEM((count, width), half),
            pltpu.VMEM((width, count), half),
            pltpu.VMEM((width, count), half),
            pltpu.VMEM((count, width), single),
            pltpu.VMEM((count, width), single),
            pltpu.VMEM((count, block), half),
            pltpu.VMEM((count, block), half),
            pltpu.VMEM((count, block), half),
            pltpu.VMEM((16, 2 * LANES), single),
        ],
        compiler_params=pltpu.CompilerParams(vmem_limit_bytes=60 << 20),
        cost_estimate=pl.CostEstimate(
            flops=18 * count * width * 2 * ff,
            bytes_accessed=4 * 6 * width * ff + 8 * count * width,
            transcendentals=0,
        ),
        name="expert_step",
    )(x, dy, own, other)


def per_device(
    tokens,
    segment_ids,
    routes,
    prev_logits,
    cotangent,
    proj_weight,
    out_weight,
    norm_gain,
    expert_weight,
    router,
    constant_vectors,
    gate_mixing,
):
    members = lax.axis_size("dp")
    groups = members // EXPERTS_FF
    core = lax.axis_index("tensor")
    d_rows, hh = out_weight.shape
    per_core = -(-CAPACITY // 2)
    padded = -(-(per_core + 3) // 16) * 16

    pack = jnp.concatenate(
        [
            proj_weight.transpose(1, 0, 2).reshape(d_rows, 3 * hh),
            out_weight,
            norm_gain.T,
            constant_vectors.T,
            router,
        ],
        1,
    )
    columns = pack.shape[1]
    pack = jnp.pad(pack, ((0, 0), (0, -columns % LANES)))
    full_pack, expert_weight = lax.optimization_barrier((gather_all(pack, members), expert_weight))
    full_pack = full_pack.reshape(members * d_rows, -1)[:, :columns]
    width = members * d_rows
    proj_full = full_pack[:, : 3 * hh]
    outw_own = full_pack[:, 3 * hh : 4 * hh]
    outw_other = swap(outw_own)
    rest = full_pack[:, 4 * hh :]
    gains = rest[:, :2].T.astype(single)
    const_f = rest[:, 2:4].T.astype(single)
    router_full = rest[:, 4:]
    sent_weight = jnp.broadcast_to(expert_weight[None], (groups,) + expert_weight.shape)
    sent_weight = sent_weight.reshape((members,) + expert_weight.shape[1:])
    my_weight = lax.all_to_all(sent_weight, "dp", 0, 0, tiled=True)
    if d_rows % 16:
        my_weight = my_weight.transpose(1, 0, 2, 3).reshape(1, 3, width, -1)
    other_weight = swap(my_weight)

    ids = jnp.concatenate([segment_ids[0][:, None], routes[0]], 1)
    ids_all = in_order(ids, swap(ids))
    seg_keys = ids_all[:, 0]
    onehot = slot_onehot(ids_all[:, 1:], core, per_core, padded).reshape(EXPERTS_FF * padded, -1)
    dy_all = in_order(cotangent[0], swap(cotangent[0]))
    sent_dy = mm(onehot, dy_all).astype(half).reshape(EXPERTS_FF, padded, width)

    x_rows = tokens[0].astype(single)
    local_rows = x_rows.shape[0]
    x_all = in_order(tokens[0], swap(tokens[0])).astype(single)
    scale_all = rms_scale(x_all)
    full_one = (x_all * scale_all * gains[0]).astype(half)
    scale_one = half_of(scale_all, core)
    seq = full_one.shape[0]
    qkv = mm(full_one, proj_full).astype(half)
    size = fit(seq, 256)
    bounds, starts = block_bounds(seg_keys, size)
    heads_full, lse = attention_forward(qkv, bounds, starts, size)
    heads_out = heads_full.astype(half)
    ho_own = half_of(heads_out, core)
    ho_other = swap(half_of(heads_out, 1 - core))
    resid = x_rows + mm_nt(ho_own, outw_own) + mm_nt(ho_other, outw_other)
    scale_two = rms_scale(resid)
    normed_two = (resid * scale_two * gains[1]).astype(half)
    two_rows = normed_two.astype(single)
    router_rows = mm(normed_two, router_full)
    prev_rows = prev_logits[0]
    logits = router_rows[:, :EXPERTS] + jnp.dot(prev_rows, gate_mixing, precision=HIGH)
    route_rows = routes[0]
    picks = (route_rows[:, :, None] == jnp.arange(EXPERTS, dtype=jnp.int32)[None, None, :]).astype(
        single
    )
    gates = softmax_last(jnp.sum(picks * logits[:, None, :], axis=-1))
    gate_low = gates.astype(half)

    gate_columns = jnp.sum(picks[:, :, :EXPERTS_FF] * gate_low.astype(single)[:, :, None], axis=1)
    spread = jnp.pad(gate_columns.astype(half), ((0, 0), (0, LANES - EXPERTS_FF)))
    both = jnp.concatenate([normed_two, spread], 1)
    both_all = in_order(both, swap(both))
    picked = mm(onehot, both_all).astype(half).reshape(EXPERTS_FF, padded, width + LANES)
    slot_gate = jnp.stack([picked[e, :, width + e] for e in range(EXPERTS_FF)])
    gate_row = jnp.pad(slot_gate, ((0, 0), (0, width - padded)))[:, None, :]
    row_number = lax.broadcasted_iota(jnp.int32, (1, padded, 1), 1)
    sent_rows = jnp.where(row_number == padded - 1, gate_row, picked[:, :, :width])
    got_rows, got_dy = exchange(1, sent_rows, sent_dy)

    count = EXPERTS_FF * padded
    gated_out, in_grad, grads_own, grads_other = expert_step(
        got_rows, got_dy, my_weight, other_weight, padded
    )
    back_grad, back_out = exchange(2, in_grad, gated_out)
    back_grad, grads_own = lax.optimization_barrier((back_grad, grads_own))

    grads_sent = (grads_own.astype(single) + swap(grads_other).astype(single)).astype(half)
    if d_rows % 16:
        grads_sent = grads_sent.reshape(3, members, d_rows, -1).transpose(1, 0, 2, 3)
    grads_got = lax.all_to_all(grads_sent, "dp", 0, 0, tiled=True)
    dots = back_grad[:, padded - 2 :, :padded]
    eye = jnp.eye(EXPERTS_FF, dtype=half)
    dot_columns = jnp.concatenate(
        [dots[:, 0, :, None] * eye[:, None, :], dots[:, 1, :, None] * eye[:, None, :]], 2
    )
    dot_columns = jnp.pad(dot_columns, ((0, 0), (0, 0), (0, LANES - 2 * EXPERTS_FF)))
    back_both = jnp.concatenate([back_grad, dot_columns], 2).reshape(count, width + LANES)
    two_back = pair_sum(mm_tn(onehot, back_both))
    ffn_out = pair_sum(mm_tn(onehot, back_out.reshape(count, width)))
    two_grad_ffn = two_back[:, :width]
    expert_dot = (
        two_back[:, width : width + EXPERTS_FF]
        + two_back[:, width + EXPERTS_FF : width + 2 * EXPERTS_FF]
    )
    gate_grad_ffn = jnp.sum(picks[:, :, :EXPERTS_FF] * expert_dot[:, None, :], axis=-1)

    grad_rows = cotangent[0].astype(single)
    alphas = softmax_last(router_rows[:, EXPERTS:].reshape(local_rows, 2, 2))
    copy_weight = jnp.sum(gates * picks[:, :, EXPERTS_FF + 1], axis=1)
    const_weight = jnp.sum(gates[:, :, None] * picks[:, :, EXPERTS_FF + 2 :], axis=1)
    own_weight = copy_weight + jnp.sum(const_weight * alphas[:, :, 0], axis=1)
    vec_weight = const_weight * alphas[:, :, 1]
    other_out = own_weight[:, None] * two_rows + jnp.dot(vec_weight, const_f, precision=HIGH)
    mixed = (resid + ffn_out + other_out).astype(half)[None]
    own_dot = jnp.sum(grad_rows * two_rows, axis=-1)
    vec_dot = jnp.dot(grad_rows, const_f.T, precision=HIGH)
    value_dot = jnp.stack(
        [
            jnp.zeros_like(own_dot),
            own_dot,
            alphas[:, 0, 0] * own_dot + alphas[:, 0, 1] * vec_dot[:, 0],
            alphas[:, 1, 0] * own_dot + alphas[:, 1, 1] * vec_dot[:, 1],
        ],
        -1,
    )
    gate_grad = gate_grad_ffn + jnp.sum(picks[:, :, EXPERTS_FF:] * value_dot[:, None, :], axis=-1)
    alpha_grad = jnp.stack([const_weight * own_dot[:, None], const_weight * vec_dot], -1)
    mix_rows_grad = alphas * (alpha_grad - jnp.sum(alphas * alpha_grad, axis=-1, keepdims=True))
    const_vec_grad = jnp.dot(vec_weight.T, grad_rows, precision=HIGH)
    chosen_grad = gates * (gate_grad - jnp.sum(gates * gate_grad, axis=-1, keepdims=True))
    logit_grad = jnp.sum(picks * chosen_grad[:, :, None], axis=1)
    router_rows_grad = jnp.concatenate([logit_grad, mix_rows_grad.reshape(local_rows, 4)], -1)
    two_grad = (
        two_grad_ffn
        + own_weight[:, None] * grad_rows
        + jnp.dot(router_rows_grad, router_full.astype(single).T, precision=HIGH)
    )
    router_grad = jnp.dot(two_rows.T, router_rows_grad, precision=HIGH)
    prev_grad = jnp.dot(logit_grad, gate_mixing.T, precision=HIGH)
    mixing_grad = jnp.dot(prev_rows.T, logit_grad, precision=HIGH)
    weighted_two = two_grad * gains[1]
    resid_grad = grad_rows + scale_two * (
        weighted_two
        - resid * scale_two * scale_two * jnp.mean(weighted_two * resid, axis=-1, keepdims=True)
    )
    gain_two_grad = jnp.sum(two_grad * resid * scale_two, axis=0)
    attn_grad = resid_grad.astype(half)
    hg_own = mm(attn_grad, outw_own).astype(half)
    hg_other = swap(mm(attn_grad, outw_other).astype(half))
    heads_grad = in_order(hg_own, hg_other)
    out_w_grad = mm_tn(attn_grad, ho_own) + swap(mm_tn(attn_grad, ho_other).astype(half)).astype(
        single
    )
    qkv_grad = attention_backward(qkv, heads_grad, heads_full, lse, bounds, starts, size)
    one_part = mm_nt(qkv_grad, proj_full)
    gain_one_grad = jnp.sum(one_part * x_all * scale_all, axis=0)
    one_grad = pair_sum(one_part)
    proj_grad = mm_tn(full_one, qkv_grad)
    weighted_one = one_grad * gains[0]
    tokens_grad = resid_grad + scale_one * (
        weighted_one
        - x_rows * scale_one * scale_one * jnp.mean(weighted_one * x_rows, axis=-1, keepdims=True)
    )

    dense = jnp.concatenate([proj_grad, out_w_grad], 1).astype(half)
    dense, grads_got = lax.optimization_barrier((dense, grads_got))
    dense = lax.all_to_all(dense.reshape(members, d_rows, 4 * hh), "dp", 0, 0, tiled=True)
    dense = jnp.sum(dense.astype(single), axis=0)
    proj_shard = dense[:, : 3 * hh].reshape(d_rows, 3, hh).transpose(1, 0, 2)
    outw_shard = dense[:, 3 * hh :]

    expert_shard = jnp.sum(
        grads_got.reshape((groups, EXPERTS_FF) + grads_got.shape[1:]).astype(single), axis=0
    )

    by_feature = jnp.concatenate(
        [gain_one_grad[:, None], gain_two_grad[:, None], const_vec_grad.T, router_grad], 1
    )
    columns = by_feature.shape[1]
    small = by_feature.reshape(members, d_rows * columns)
    mix = jnp.broadcast_to(mixing_grad.reshape(1, -1), (members, mixing_grad.size))
    small = jnp.concatenate([small, mix], 1)
    used = small.shape[1]
    wide = -(-used // (8 * LANES)) * 8 * LANES
    small = jnp.pad(small, ((0, 0), (0, wide - used))).reshape(members, wide // LANES, LANES)
    small = small + swap(small)
    small = jnp.sum(lax.all_to_all(small, "dp", 0, 0, tiled=True), axis=0).reshape(-1)
    features = small[: d_rows * columns].reshape(d_rows, columns)
    mixing_total = small[d_rows * columns : used].reshape(mixing_grad.shape)
    return (
        mixed,
        tokens_grad[None],
        prev_grad[None],
        proj_shard,
        outw_shard,
        features[:, :2].T,
        expert_shard,
        features[:, 4:],
        features[:, 2:4].T,
        mixing_total,
    )


def solution(mesh):
    return jax.shard_map(
        per_device,
        mesh=mesh,
        in_specs=(
            P("dp", "tensor", None),
            P("dp", "tensor"),
            P("dp", "tensor", None),
            P("dp", "tensor", None),
            P("dp", "tensor", None),
            P(None, "dp", "tensor"),
            P("dp", "tensor"),
            P(None, "dp"),
            P(None, None, "dp", "tensor"),
            P("dp", None),
            P(None, "dp"),
            P(),
        ),
        out_specs=(
            P("dp", "tensor", None),
            P("dp", "tensor", None),
            P("dp", "tensor", None),
            P(None, "dp", "tensor"),
            P("dp", "tensor"),
            P(None, "dp"),
            P(None, None, "dp", "tensor"),
            P("dp", None),
            P(None, "dp"),
            P(),
        ),
        check_vma=False,
    )
```

```python
import functools

import jax
import jax.numpy as jnp
from jax import lax
from jax.experimental import pallas as pl
from jax.experimental.pallas import tpu as pltpu
from jax.sharding import PartitionSpec as P

HEAD_DIM = 64
EXPERTS_FF = 8
EXPERTS = 12
CAPACITY = 341


EPS = 1e-05
HIGH = lax.Precision.HIGHEST
NEG = -1e30
LANES = 128
DOCS = 8
LOG2E = 1.4426950408889634
MESH = pl.DeviceIdType.MESH
single = jnp.float32
half = jnp.bfloat16


def rms_scale(rows):
    return lax.rsqrt(jnp.mean(rows * rows, axis=-1, keepdims=True) + EPS)


def softmax_last(values):
    peak = jnp.max(values, axis=-1, keepdims=True)
    expo = jnp.exp(values - peak)
    return expo / jnp.sum(expo, axis=-1, keepdims=True)


def mm(a, b):
    return jnp.dot(a, b, preferred_element_type=single)


def mm_nt(a, b):
    return lax.dot_general(a, b, (((1,), (1,)), ((), ())), preferred_element_type=single)


def mm_tn(a, b):
    return lax.dot_general(a, b, (((0,), (0,)), ((), ())), preferred_element_type=single)


def swap(x):
    return lax.ppermute(x, "tensor", [(0, 1), (1, 0)])


def in_order(own, other):
    first = lax.axis_index("tensor") == 0
    return jnp.concatenate([jnp.where(first, own, other), jnp.where(first, other, own)], 0)


def half_of(full, which):
    count = full.shape[0] // 2
    return lax.dynamic_slice_in_dim(full, which * count, count, 0)


def pair_sum(full):
    core = lax.axis_index("tensor")
    other = swap(half_of(full, 1 - core).astype(half))
    return half_of(full, core) + other.astype(single)


def fit(seq, want):
    return want if seq % want == 0 else seq

def block_bounds(start, end, size):
    edges = start.reshape(-1, size)
    number = jnp.arange(edges.shape[0], dtype=jnp.int32)
    low = edges[:, 0] // size
    plain = jnp.clip((edges[:, -1] + size - 1) // size, low, number)
    high = end.reshape(-1, size)[:, -1] // size
    clear = jnp.sum((edges[None, :, -1] <= number[:, None] * size).astype(jnp.int32), axis=1)
    clear = jnp.clip(clear, number + 1, high + 1)
    return jnp.stack([low, plain, high, clear])


def head_lanes(h, rows):
    lane = lax.broadcasted_iota(jnp.int32, (rows, LANES), 1)
    return (lane < HEAD_DIM) if h % 2 == 0 else (lane >= HEAD_DIM)

def fwd_kernel(heads, bounds, q_ref, k_ref, v_ref, start_ref, o_ref, low_ref, lse_ref, s_ref, m_ref, l_ref, acc_ref, qm_ref):
    size = q_ref.shape[0]
    i = pl.program_id(0)
    low, plain = bounds[0, i], bounds[1, i]
    factor = LOG2E * HEAD_DIM ** -0.5
    for h in range(heads):
        pair = pl.ds(h // 2 * LANES, LANES)
        qm_ref[h] = jnp.where(head_lanes(h, size), q_ref[:, pair], 0).astype(half)
    m_ref[...] = jnp.full(m_ref.shape, NEG, single)
    l_ref[...] = jnp.zeros(l_ref.shape, single)
    acc_ref[...] = jnp.zeros(acc_ref.shape, single)

    def score(j, masked):
        rows = pl.ds(pl.multiple_of(j * size, size), size)
        if masked:
            row = i * size + lax.broadcasted_iota(jnp.int32, (size, size), 0)
            col = j * size + lax.broadcasted_iota(jnp.int32, (size, size), 1)
            allowed = (col <= row) & (col >= start_ref[...])
        for h in range(heads):
            s = mm_nt(qm_ref[h], k_ref[rows, pl.ds(h // 2 * LANES, LANES)])
            if masked:
                s = jnp.where(allowed, s, NEG)
            s_ref[h, j] = s
            m = m_ref[h]
            for c in range(size // LANES):
                m = jnp.maximum(m, s[:, c * LANES : (c + 1) * LANES])
            m_ref[h] = m

    pl.loop(low, plain)(lambda j: score(j, True))
    pl.loop(plain, i)(lambda j: score(j, False))
    score(i, True)
    for h in range(heads):
        m_ref[h] = jnp.broadcast_to(jnp.max(m_ref[h], axis=1, keepdims=True) * factor, (size, LANES))

    def gather(j):
        rows = pl.ds(pl.multiple_of(j * size, size), size)
        for h in range(heads):
            s = s_ref[h, j]
            m = m_ref[h]
            l = l_ref[h]
            parts = []
            for c in range(size // LANES):
                p = jnp.exp2(s[:, c * LANES : (c + 1) * LANES] * factor - m)
                l = l + p
                parts.append(p.astype(half))
            l_ref[h] = l
            acc_ref[h] += jnp.dot(jnp.concatenate(parts, 1), v_ref[rows, pl.ds(h // 2 * LANES, LANES)], preferred_element_type=single)

    pl.loop(low, i + 1)(gather)
    lane = lax.broadcasted_iota(jnp.int32, (size, LANES), 1)
    lse = jnp.zeros((size, LANES), single)
    for h in range(0, heads, 2):
        outs = []
        for k in (h, h + 1):
            l = jnp.sum(l_ref[k], axis=1, keepdims=True)
            outs.append(acc_ref[k] / l)
            lse = jnp.where(lane == k, m_ref[k] + jnp.log2(l), lse)
        out = jnp.where(lane < HEAD_DIM, outs[0], outs[1])
        o_ref[:, pl.ds(h // 2 * LANES, LANES)] = out
        low_ref[:, pl.ds(h // 2 * LANES, LANES)] = out.astype(half)
    lse_ref[...] = lse

def attention_forward(qkv, seg_bounds, starts, size):
    seq = qkv.shape[0]
    hh = qkv.shape[1] // 3
    heads = hh // HEAD_DIM
    return pl.pallas_call(
        functools.partial(fwd_kernel, heads),
        grid_spec=pltpu.PrefetchScalarGridSpec(
            num_scalar_prefetch=1,
            grid=(seq // size,),
            in_specs=[
                pl.BlockSpec((size, hh), lambda i, b: (i, 0)),
                pl.BlockSpec((seq, hh), lambda i, b: (0, 1)),
                pl.BlockSpec((seq, hh), lambda i, b: (0, 2)),
                pl.BlockSpec((size, 1), lambda i, b: (i, 0)),
            ],
            out_specs=[
                pl.BlockSpec((size, hh), lambda i, b: (i, 0)),
                pl.BlockSpec((size, hh), lambda i, b: (i, 0)),
                pl.BlockSpec((size, LANES), lambda i, b: (i, 0)),
            ],
            scratch_shapes=[
                pltpu.VMEM((heads, seq // size, size, size), single),
                pltpu.VMEM((heads, size, LANES), single),
                pltpu.VMEM((heads, size, LANES), single),
                pltpu.VMEM((heads, size, LANES), single),
                pltpu.VMEM((heads, size, LANES), half),
            ],
        ),
        out_shape=[
            jax.ShapeDtypeStruct((seq, hh), single),
            jax.ShapeDtypeStruct((seq, hh), half),
            jax.ShapeDtypeStruct((seq, LANES), single),
        ],
        compiler_params=pltpu.CompilerParams(vmem_limit_bytes=48 << 20),
        cost_estimate=pl.CostEstimate(flops=4 * seq * seq * LANES * heads, bytes_accessed=16 * seq * hh, transcendentals=0),
    )(seg_bounds, qkv, qkv, qkv, starts[:, None])

def bwd_kernel(
    heads, bounds, q_ref, k_ref, v_ref, do_ref, o_ref, lse_ref, start_ref, out_ref, dq_ref, dk_ref, dv_ref, stat_ref
):
    size = k_ref.shape[0]
    j = pl.program_id(0)
    high, clear = bounds[2, j], bounds[3, j]
    factor = LOG2E * HEAD_DIM ** -0.5
    hh = k_ref.shape[1]

    @pl.when(j == 0)
    def _():
        dq_ref[...] = jnp.zeros(dq_ref.shape, single)
        feature = lax.broadcasted_iota(jnp.int32, (hh, LANES), 0)
        lane = lax.broadcasted_iota(jnp.int32, (hh, LANES), 1)
        pick = (feature // HEAD_DIM + 8 == lane).astype(half)

        @pl.loop(0, q_ref.shape[0] // size)
        def _(i):
            rows = pl.ds(pl.multiple_of(i * size, size), size)
            product = o_ref[rows, :] * do_ref[rows, :].astype(single)
            top = product.astype(half)
            low = (product - top.astype(single)).astype(half)
            both = mm(top, pick) + mm(low, pick) + lse_ref[rows, :]
            stat_ref[:, rows] = both.T[:16, :]

    dk_ref[...] = jnp.zeros(dk_ref.shape, single)
    dv_ref[...] = jnp.zeros(dv_ref.shape, single)

    def step(i, masked):
        rows = pl.ds(pl.multiple_of(i * size, size), size)
        if masked:
            key = j * size + lax.broadcasted_iota(jnp.int32, (size, size), 0)
            query = i * size + lax.broadcasted_iota(jnp.int32, (size, size), 1)
            allowed = (key <= query) & (key >= start_ref[:, rows])
        for pair in range(heads // 2):
            lanes = pl.ds(pair * LANES, LANES)
            k, v = k_ref[:, lanes], v_ref[:, lanes]
            q, do = q_ref[rows, lanes], do_ref[rows, lanes]
            ps, dss, qs, dos, ks = [], [], [], [], []
            for h in (2 * pair, 2 * pair + 1):
                mine = head_lanes(h, size)
                qm = jnp.where(mine, q, 0).astype(half)
                dom = jnp.where(mine, do, 0).astype(half)
                s = mm_nt(k, qm) * factor - stat_ref[pl.ds(h, 1), rows]
                if masked:
                    s = jnp.where(allowed, s, NEG)
                p = jnp.exp2(s)
                ds = p * (mm_nt(v, dom) - stat_ref[pl.ds(8 + h, 1), rows])
                ps.append(p.astype(half))
                dss.append(ds.astype(half))
                qs.append(qm)
                dos.append(dom)
                ks.append(jnp.where(mine, k, 0).astype(half))
            dv_ref[:, lanes] += jnp.dot(jnp.concatenate(ps, 1), jnp.concatenate(dos, 0), preferred_element_type=single)
            dk_ref[:, lanes] += jnp.dot(jnp.concatenate(dss, 1), jnp.concatenate(qs, 0), preferred_element_type=single)
            dq_ref[rows, lanes] += mm_tn(jnp.concatenate(dss, 0), jnp.concatenate(ks, 0))

    step(j, True)
    pl.loop(j + 1, clear)(lambda i: step(i, False))
    pl.loop(clear, high + 1)(lambda i: step(i, True))
    mine = pl.ds(pl.multiple_of(j * size, size), size)
    out_ref[mine, pl.ds(hh, hh)] = (dk_ref[...] * HEAD_DIM ** -0.5).astype(half)
    out_ref[mine, pl.ds(2 * hh, hh)] = dv_ref[...].astype(half)
    out_ref[mine, pl.ds(0, hh)] = (dq_ref[mine, :] * HEAD_DIM ** -0.5).astype(half)

def attention_backward(qkv, do, heads_out, lse, seg_bounds, starts, size):
    seq = qkv.shape[0]
    hh = qkv.shape[1] // 3
    heads = hh // HEAD_DIM
    return pl.pallas_call(
        functools.partial(bwd_kernel, heads),
        grid_spec=pltpu.PrefetchScalarGridSpec(
            num_scalar_prefetch=1,
            grid=(seq // size,),
            in_specs=[
                pl.BlockSpec((seq, hh), lambda j, b: (0, 0)),
                pl.BlockSpec((size, hh), lambda j, b: (j, 1)),
                pl.BlockSpec((size, hh), lambda j, b: (j, 2)),
                pl.BlockSpec((seq, hh), lambda j, b: (0, 0)),
                pl.BlockSpec((seq, hh), lambda j, b: (0, 0)),
                pl.BlockSpec((seq, LANES), lambda j, b: (0, 0)),
                pl.BlockSpec((1, seq), lambda j, b: (0, 0)),
            ],
            out_specs=pl.BlockSpec((seq, 3 * hh), lambda j, b: (0, 0)),
            scratch_shapes=[
                pltpu.VMEM((seq, hh), single),
                pltpu.VMEM((size, hh), single),
                pltpu.VMEM((size, hh), single),
                pltpu.VMEM((16, seq), single),
            ],
        ),
        out_shape=jax.ShapeDtypeStruct((seq, 3 * hh), half),
        compiler_params=pltpu.CompilerParams(vmem_limit_bytes=48 << 20),
        cost_estimate=pl.CostEstimate(flops=10 * seq * seq * LANES * heads, bytes_accessed=20 * seq * hh, transcendentals=0),
    )(seg_bounds, qkv, qkv, qkv, do, heads_out, lse, starts[None, :])


def start_kernel(
    members,
    low,
    per_core,
    padded,
    pack_ref,
    tok_ref,
    dy_ref,
    ids_ref,
    full_ref,
    all_ref,
    got_ref,
    hot_ref,
    info_ref,
    ids_all_ref,
    dy_all_ref,
    stage_ref,
    place_ref,
    send_sem,
    recv_sem,
    own_sem,
    swap_send,
    swap_recv,
    dy_send,
    dy_recv,
):
    size = EXPERTS_FF
    me = lax.axis_index("dp")
    core = lax.axis_index("tensor")
    high = members // low
    inside, row = lax.rem(me, low), me // low
    mine = lax.rem(me, size)
    base = me - mine
    local = tok_ref.shape[0]
    seq = 2 * local
    partner = {"tensor": 1 - core}

    def beside(k):
        return row * low + lax.rem(inside + k, low)

    def across(k):
        return lax.rem(row + k, high) * low + inside

    peers = [beside(k) for k in range(1, low)] + [across(k) for k in range(1, high)]
    peers += [base + lax.rem(mine + k, size) for k in range(1, size)]
    barrier = pltpu.get_barrier_semaphore()
    for peer in peers:
        pl.semaphore_signal(barrier, inc=1, device_id={"dp": peer}, device_id_type=MESH)
    pl.semaphore_signal(barrier, inc=1, device_id=partner, device_id_type=MESH)
    pl.semaphore_wait(barrier, len(peers) + 1)

    def remote(src, dst, send, recv, device):
        return pltpu.make_async_remote_copy(
            src_ref=src,
            dst_ref=dst,
            send_sem=send,
            recv_sem=recv,
            device_id=device,
            device_id_type=MESH,
        )

    def push(source, block, target, slot):
        copy = remote(
            source, full_ref.at[block], send_sem.at[slot], recv_sem.at[block], {"dp": target}
        )
        copy.start()
        return copy

    def arrived(block):
        remote(
            pack_ref, full_ref.at[block], send_sem.at[0], recv_sem.at[block], {"dp": peers[0]}
        ).wait_recv()

    sent = [push(pack_ref, me, across(k), k) for k in range(1, high)]
    sent += [push(pack_ref, me, beside(k), high + k) for k in range(1, low)]
    own_rows = pl.ds(pl.multiple_of(core * local, local), local)
    swaps = [
        remote(ids_ref, ids_all_ref.at[core], swap_send.at[0], swap_recv.at[0], partner),
        remote(dy_ref, dy_all_ref.at[own_rows], swap_send.at[1], swap_recv.at[1], partner),
        remote(tok_ref, all_ref.at[own_rows], swap_send.at[2], swap_recv.at[2], partner),
    ]
    owns = [
        pltpu.make_async_copy(ids_ref, ids_all_ref.at[core], own_sem.at[0]),
        pltpu.make_async_copy(dy_ref, dy_all_ref.at[own_rows], own_sem.at[1]),
        pltpu.make_async_copy(tok_ref, all_ref.at[own_rows], own_sem.at[2]),
        pltpu.make_async_copy(pack_ref, full_ref.at[me], own_sem.at[3]),
    ]
    for copy in swaps + owns:
        copy.start()

    swaps[0].wait()
    owns[0].wait()
    ids = jnp.concatenate([ids_all_ref[0], ids_all_ref[1]], 1)
    seg = ids[:1]
    number = lax.broadcasted_iota(jnp.int32, (8, seq), 0)
    starts = jnp.zeros((1, seq), jnp.int32)
    ends = jnp.zeros((1, seq), jnp.int32)
    total = jnp.zeros((1, 1), jnp.int32)
    for d in range(DOCS):
        here = seg == d
        starts = jnp.where(here, total, starts)
        total = total + jnp.sum(here.astype(jnp.int32), axis=1, keepdims=True)
        ends = jnp.where(here, total - 1, ends)
    row16 = lax.broadcasted_iota(jnp.int32, (16, LANES), 0)
    first = lax.broadcasted_iota(jnp.int32, (LANES, LANES), 0)
    second = lax.broadcasted_iota(jnp.int32, (LANES, LANES), 1)
    upper = (first < second).astype(half)
    before = jnp.zeros((16, 1), single)
    for c in range(seq // LANES):
        lanes = slice(c * LANES, (c + 1) * LANES)
        member = (ids[1:2, lanes] == row16) | (ids[2:3, lanes] == row16)
        member = jnp.where(member & (row16 < size), 1.0, 0.0)
        position = mm(member.astype(half), upper) + before
        before = before + jnp.sum(member, axis=1, keepdims=True)
        place = position - (core * per_core).astype(single)
        kept = (member > 0.5) & (position < CAPACITY) & (place >= 0) & (place < per_core)
        place_ref[:, lanes] = jnp.where(kept, place, -1.0).astype(jnp.int32)
    slot = lax.broadcasted_iota(jnp.int32, (padded, seq), 0)
    for e in range(size):
        hot_ref[e * padded : (e + 1) * padded, :] = jnp.where(
            place_ref[e : e + 1, :] == slot, 1.0, 0.0
        ).astype(half)

    info = jnp.where(number == 0, starts, jnp.where(number == 1, ends, -1))
    for k in range(2):
        chosen = jnp.full((1, seq), -1, jnp.int32)
        for e in range(size):
            place = place_ref[e : e + 1, :]
            chosen = jnp.where(
                (ids[k + 1 : k + 2] == e) & (place >= 0), place + e * padded, chosen
            )
        info = jnp.where(number == k + 2, chosen, info)
    info_ref[...] = info

    for k in range(1, high):
        block = across(high - k)
        arrived(block)
        for step in range(1, low):
            sent.append(push(full_ref.at[block], block, beside(step), high + k * low + step))

    swaps[1].wait()
    owns[1].wait()
    for pair in [(1, 2), (3, 4), (5, 6), (7, 0)]:
        slots = [
            pl.ds(pl.multiple_of(lax.rem(mine + k, size) * padded, 16), padded) for k in pair
        ]
        rows = mm(jnp.concatenate([hot_ref[s, :] for s in slots], 0), dy_all_ref[...])
        for place, k in enumerate(pair):
            to = lax.rem(mine + k, size)
            stage_ref[to] = rows[place * padded : (place + 1) * padded].astype(half)
            if k:
                copy = remote(
                    stage_ref.at[to], got_ref.at[mine], dy_send.at[k], dy_recv.at[k], {"dp": base + to}
                )
            else:
                copy = pltpu.make_async_copy(stage_ref.at[to], got_ref.at[mine], own_sem.at[4])
            copy.start()
            owns.append(copy)
    for k in range(1, low):
        block = beside(low - k)
        arrived(block)
        for step in range(1, high):
            arrived(lax.rem(block + step * low, members))
    for copy in sent:
        copy.wait_send()
    for copy in owns[2:]:
        copy.wait()
    swaps[2].wait()


def start(pack, tokens, dy, ids, members, per_core, padded):
    low = 4 if members % 4 == 0 else 1
    high = members // low
    local, width = tokens.shape
    count = EXPERTS_FF * padded
    any_spec = pl.BlockSpec(memory_space=pl.ANY)
    vmem = pl.BlockSpec(memory_space=pltpu.VMEM)
    dma = pltpu.SemaphoreType.DMA
    return pl.pallas_call(
        functools.partial(start_kernel, members, low, per_core, padded),
        out_shape=[
            jax.ShapeDtypeStruct((members,) + pack.shape, half),
            jax.ShapeDtypeStruct((2 * local, width), half),
            jax.ShapeDtypeStruct((EXPERTS_FF, padded, width), half),
            jax.ShapeDtypeStruct((count, 2 * local), half),
            jax.ShapeDtypeStruct((8, 2 * local), jnp.int32),
        ],
        in_specs=[any_spec] * 4,
        out_specs=[any_spec] * 3 + [vmem] * 2,
        scratch_shapes=[
            pltpu.VMEM((2, 8, local), jnp.int32),
            pltpu.VMEM((2 * local, width), half),
            pltpu.VMEM((EXPERTS_FF, padded, width), half),
            pltpu.VMEM((16, 2 * local), jnp.int32),
            dma((high * (low + 1),)),
            dma((members,)),
            dma((5,)),
            dma((3,)),
            dma((3,)),
            dma((EXPERTS_FF,)),
            dma((EXPERTS_FF,)),
        ],
        compiler_params=pltpu.CompilerParams(
            collective_id=0, has_side_effects=True, vmem_limit_bytes=40 << 20
        ),
        name="start",
    )(pack, tokens, dy, ids)


def middle_kernel(
    members,
    padded,
    w_ref,
    in_ref,
    ho_ref,
    tok_ref,
    own_w_ref,
    other_w_ref,
    gain_ref,
    router_ref,
    prev_ref,
    routes_ref,
    hot_ref,
    ox_ref,
    ow_ref,
    pw_ref,
    pin_ref,
    resid_ref,
    normed_ref,
    misc_ref,
    ho_in_ref,
    both_ref,
    acc_ref,
    stage_ref,
    row_ref,
    send_sem,
    x_sem,
    w_sem,
    pass_sem,
    pair_sem,
    own_sem,
    swap_send,
    swap_recv,
):
    size = EXPERTS_FF
    groups = members // size
    me = lax.axis_index("dp")
    core = lax.axis_index("tensor")
    mine = lax.rem(me, size)
    base = me - mine
    local, width = tok_ref.shape
    partner = {"tensor": 1 - core}

    def member(g, k):
        return lax.rem(base + g * size, members) + lax.rem(mine + k, size)

    barrier = pltpu.get_barrier_semaphore()
    for g in range(groups):
        for k in range(size):
            if g or k:
                pl.semaphore_signal(
                    barrier, inc=1, device_id={"dp": member(g, k)}, device_id_type=MESH
                )
    pl.semaphore_signal(barrier, inc=1, device_id=partner, device_id_type=MESH)
    pl.semaphore_wait(barrier, members)

    def remote(src, dst, send, recv, device):
        return pltpu.make_async_remote_copy(
            src_ref=src,
            dst_ref=dst,
            send_sem=send,
            recv_sem=recv,
            device_id=device,
            device_id_type=MESH,
        )

    def send_w(g, k):
        to = member(g, k)
        copy = remote(
            w_ref.at[to], ow_ref.at[me], send_sem.at[g * size + k], w_sem.at[me], {"dp": to}
        )
        copy.start()
        return copy

    def send_pair(block):
        copy = remote(
            ow_ref.at[block], pw_ref.at[block], pass_sem.at[block], pair_sem.at[block], partner
        )
        copy.start()
        return copy

    own_rows = pl.ds(pl.multiple_of(core * local, local), local)
    other_rows = pl.ds(pl.multiple_of((1 - core) * local, local), local)
    heads = remote(ho_ref.at[other_rows], ho_in_ref, swap_send.at[0], swap_recv.at[0], partner)
    heads.start()
    pair_in = remote(in_ref, pin_ref, swap_send.at[2], swap_recv.at[2], partner)
    pair_in.start()
    own_w = pltpu.make_async_copy(w_ref.at[me], ow_ref.at[me], own_sem.at[1])
    own_w.start()
    sent_w = []
    for k in range(size):
        for g in range(1, groups):
            sent_w.append(send_w(g, k))
        if k:
            sent_w.append(send_w(0, k))

    step = fit(local, 256)
    heads.wait()

    @pl.loop(0, local // step)
    def _(r):
        rows = pl.ds(pl.multiple_of(r * step, step), step)
        mine_rows = pl.ds(pl.multiple_of(core * local + r * step, step), step)
        resid = tok_ref[rows, :].astype(single)
        resid += mm_nt(ho_ref[mine_rows, :], own_w_ref[...])
        resid += mm_nt(ho_in_ref[rows, :], other_w_ref[...])
        resid_ref[rows, :] = resid
        normed = (resid * rms_scale(resid) * gain_ref[1:2, :]).astype(half)
        normed_ref[rows, :] = normed
        router = mm(normed, router_ref[...])
        lane = lax.broadcasted_iota(jnp.int32, (step, LANES), 1)
        logits = jnp.where(lane < EXPERTS, router + prev_ref[rows, :], 0.0)
        hits = [lane == routes_ref[rows, k : k + 1] for k in range(2)]
        picked = [jnp.sum(jnp.where(hit, logits, 0.0), axis=1, keepdims=True) for hit in hits]
        peak = jnp.maximum(picked[0], picked[1])
        expo = [jnp.exp(p - peak) for p in picked]
        total = expo[0] + expo[1]
        gates = [e / total for e in expo]
        misc_ref[rows, :] = jnp.where(lane == 0, gates[0], jnp.where(lane == 1, gates[1], router))
        spread = sum(
            jnp.where(hit & (lane < size), gate.astype(half).astype(single), 0.0)
            for hit, gate in zip(hits, gates)
        )
        both_ref[mine_rows, pl.ds(0, width)] = normed
        both_ref[mine_rows, pl.ds(width, LANES)] = spread.astype(half)

    swap_rows = remote(
        both_ref.at[own_rows], both_ref.at[own_rows], swap_send.at[1], swap_recv.at[1], partner
    )
    swap_rows.start()

    pairs = [(1, 2), (3, 4), (5, 6), (7, 0)]
    for number, pair in enumerate(pairs):
        slots = [
            pl.ds(pl.multiple_of(lax.rem(mine + k, size) * padded, 16), padded) for k in pair
        ]
        hot = jnp.concatenate([hot_ref[s, own_rows] for s in slots], 0)
        acc_ref[number] = mm(hot, both_ref[own_rows, :])
    swap_rows.wait_recv()
    sent_x = []
    row_ref[...] = jnp.zeros(row_ref.shape, single)
    for number, pair in enumerate(pairs):
        slots = [
            pl.ds(pl.multiple_of(lax.rem(mine + k, size) * padded, 16), padded) for k in pair
        ]
        hot = jnp.concatenate([hot_ref[s, other_rows] for s in slots], 0)
        acc_ref[number] += mm(hot, both_ref[other_rows, :])
        for place, k in enumerate(pair):
            to = lax.rem(mine + k, size)
            start = place * padded
            tail = acc_ref[number, start : start + padded, width:].astype(half)
            lane = lax.broadcasted_iota(jnp.int32, (16, LANES), 1)
            row_ref[:, :padded] = mm_nt((lane == to).astype(half), tail)
            stage_ref[to] = acc_ref[number, start : start + padded, :width].astype(half)
            last = acc_ref[number, start + padded - 16 : start + padded, : 2 * LANES]
            row = lax.broadcasted_iota(jnp.int32, (16, 2 * LANES), 0)
            last = jnp.where(row == 15, row_ref[...], last)
            stage_ref[to, padded - 16 :, : 2 * LANES] = last.astype(half)
            if k:
                copy = remote(
                    stage_ref.at[to],
                    ox_ref.at[mine],
                    send_sem.at[members + k],
                    x_sem.at[k],
                    {"dp": base + to},
                )
            else:
                copy = pltpu.make_async_copy(stage_ref.at[to], ox_ref.at[mine], own_sem.at[0])
            copy.start()
            sent_x.append(copy)

    own_w.wait()
    passed = [send_pair(me)]
    for k in range(size):
        for g in range(groups):
            if g or k:
                block = member((groups - g) % groups, (size - k) % size)
                remote(
                    w_ref.at[0], ow_ref.at[block], send_sem.at[0], w_sem.at[block], partner
                ).wait_recv()
                passed.append(send_pair(block))
    pair_in.wait()
    swap_rows.wait_send()
    for copy in sent_x:
        copy.wait()
    for copy in sent_w:
        copy.wait_send()
    for copy in passed:
        copy.wait()


def middle(w, inward, heads, tokens, own_w, other_w, gains, router, prev, routes, hot, padded):
    members = w.shape[0]
    local, width = tokens.shape
    seq = heads.shape[0]
    any_spec = pl.BlockSpec(memory_space=pl.ANY)
    vmem = pl.BlockSpec(memory_space=pltpu.VMEM)
    dma = pltpu.SemaphoreType.DMA
    return pl.pallas_call(
        functools.partial(middle_kernel, members, padded),
        out_shape=[
            jax.ShapeDtypeStruct((EXPERTS_FF, padded, width), half),
            jax.ShapeDtypeStruct(w.shape, half),
            jax.ShapeDtypeStruct(w.shape, half),
            jax.ShapeDtypeStruct(inward.shape, half),
            jax.ShapeDtypeStruct((local, width), single),
            jax.ShapeDtypeStruct((local, width), half),
            jax.ShapeDtypeStruct((local, LANES), single),
        ],
        in_specs=[any_spec] * 2 + [vmem] * 9,
        out_specs=[any_spec] * 4 + [vmem] * 3,
        scratch_shapes=[
            pltpu.VMEM((local, heads.shape[1]), half),
            pltpu.VMEM((seq, width + LANES), half),
            pltpu.VMEM((EXPERTS_FF // 2, 2 * padded, width + LANES), single),
            pltpu.VMEM((EXPERTS_FF, padded, width), half),
            pltpu.VMEM((16, 2 * LANES), single),
            dma((members + EXPERTS_FF,)),
            dma((EXPERTS_FF,)),
            dma((members,)),
            dma((members,)),
            dma((members,)),
            dma((2,)),
            dma((3,)),
            dma((3,)),
        ],
        compiler_params=pltpu.CompilerParams(
            collective_id=1, has_side_effects=True, vmem_limit_bytes=50 << 20
        ),
        name="middle",
    )(w, inward, heads, tokens, own_w, other_w, gains, router, prev, routes, hot)


def expert_kernel(
    padded,
    x_ref,
    dy_ref,
    own_in_ref,
    own_down_ref,
    other_in_ref,
    other_down_ref,
    out_ref,
    grad_ref,
    og_ref,
    hid_ref,
    pg_ref,
    pu_ref,
    gate_ref,
    eo_ref,
    ig_ref,
    dot_ref,
):
    f = pl.program_id(0)
    sources = x_ref.shape[0]
    count, width = og_ref.shape
    chunk = count // 4
    x_all = x_ref.reshape(count, width)
    block = hid_ref.shape[2]

    @pl.when(f == 0)
    def _():
        for s in range(sources):
            rows = pl.ds(s * padded, padded)
            gates = x_ref[s, padded - 16 :, : 2 * LANES].astype(single).T
            gate = jnp.broadcast_to(gates[:padded, 15:16], (padded, LANES))
            gate_ref[rows, :] = gate
            og_ref[rows, :] = (dy_ref[s].astype(single) * gate[:, :1]).astype(half)
        eo_ref[...] = jnp.zeros(eo_ref.shape, single)
        ig_ref[...] = jnp.zeros(ig_ref.shape, single)

    for part, (in_ref, down_ref) in enumerate(
        ((own_in_ref, own_down_ref), (other_in_ref, other_down_ref))
    ):
        gate_w, up_w = (in_ref[:, k].reshape(width, block) for k in range(2))
        down_w = down_ref[...].reshape(width, block)
        for r in range(4):
            rows = pl.ds(r * chunk, chunk)
            x = x_all[rows, :]
            og = og_ref[rows, :]
            pre = mm(x, gate_w)
            up = mm(x, up_w)
            hg = mm(og, down_w)
            sigma = jax.nn.sigmoid(pre)
            active = pre * sigma
            hidden = (active * up).astype(half)
            pg = (hg * up * (sigma * (1.0 + pre * (1.0 - sigma)))).astype(half)
            pu = (hg * active).astype(half)
            hid_ref[part, rows, :] = hidden
            pg_ref[part, rows, :] = pg
            pu_ref[part, rows, :] = pu
            eo_ref[rows, :] += mm_nt(hidden, down_w)
            ig_ref[rows, :] += mm_nt(pg, gate_w) + mm_nt(pu, up_w)

    @pl.when(f == pl.num_programs(0) - 1)
    def _():
        dot_ref[...] = jnp.zeros(dot_ref.shape, single)
        ones = jnp.ones((16, width), half)
        for s in range(sources):
            rows = pl.ds(s * padded, padded)
            eo = eo_ref[rows, :]
            out_ref[s] = (eo * gate_ref[rows, :1]).astype(half)
            grad_ref[s] = ig_ref[rows, :].astype(half)
            product = eo * dy_ref[s].astype(single)
            top = product.astype(half)
            low = (product - top.astype(single)).astype(half)
            dot_ref[:, :padded] = mm_nt(ones, top) + mm_nt(ones, low)
            dots = dot_ref[...]
            high = dots.astype(half).astype(single)
            row = lax.broadcasted_iota(jnp.int32, dots.shape, 0)
            tail = ig_ref[pl.ds((s + 1) * padded - 16, 16), : 2 * LANES]
            tail = jnp.where(row == 14, high, jnp.where(row == 15, dots - high, tail))
            grad_ref[s, padded - 16 :, : 2 * LANES] = tail.astype(half)


def expert_step(x, dy, own_in, own_down, other_in, other_down, padded):
    sources, _, width = x.shape
    count = sources * padded
    m, _, r, ff = own_in.shape
    block = fit(ff, 256)
    whole = pl.BlockSpec((sources, padded, width), lambda f: (0, 0, 0))
    two = pl.BlockSpec((m, 2, r, block), lambda f: (0, 0, 0, f))
    one = pl.BlockSpec((m, r, block), lambda f: (0, 0, f))
    wide = pl.BlockSpec((2, count, block), lambda f: (0, 0, f))
    return pl.pallas_call(
        functools.partial(expert_kernel, padded),
        grid=(ff // block,),
        in_specs=[whole, whole, two, one, two, one],
        out_specs=[whole, whole, pl.BlockSpec((count, width), lambda f: (0, 0)), wide, wide, wide],
        out_shape=[
            jax.ShapeDtypeStruct(x.shape, half),
            jax.ShapeDtypeStruct(x.shape, half),
            jax.ShapeDtypeStruct((count, width), half),
            jax.ShapeDtypeStruct((2, count, ff), half),
            jax.ShapeDtypeStruct((2, count, ff), half),
            jax.ShapeDtypeStruct((2, count, ff), half),
        ],
        scratch_shapes=[
            pltpu.VMEM((count, LANES), single),
            pltpu.VMEM((count, width), single),
            pltpu.VMEM((count, width), single),
            pltpu.VMEM((16, 2 * LANES), single),
        ],
        compiler_params=pltpu.CompilerParams(vmem_limit_bytes=58 << 20),
        cost_estimate=pl.CostEstimate(
            flops=12 * count * width * 2 * ff,
            bytes_accessed=2 * 6 * width * ff + 20 * count * ff,
            transcendentals=0,
        ),
        name="expert_step",
    )(x, dy, own_in, own_down, other_in, other_down)


def split(x):
    high = x.astype(half)
    return high, (x - high.astype(single)).astype(half)


def slot_rows(columns, count):
    slot = lax.broadcasted_iota(jnp.int32, (columns.shape[0], count), 1)
    hit = (columns[:, 2:3] == slot) | (columns[:, 3:4] == slot)
    return jnp.where(hit, 1.0, 0.0).astype(half)


def lane_sum(x):
    return jnp.sum(x, axis=1, keepdims=True)


def back_kernel(
    padded,
    back_ref,
    info_ref,
    resid_ref,
    normed_ref,
    misc_ref,
    dy_ref,
    routes_ref,
    gain_ref,
    const_ref,
    router_ref,
    own_w_ref,
    other_w_ref,
    prev_ref,
    mix_ref,
    rgrad_ref,
    attn_ref,
    heads_ref,
    base_ref,
    pgrad_ref,
    small_ref,
    mgrad_ref,
    ext_ref,
    out_ref,
    in_ref,
    hg_ref,
    send_sem,
    recv_sem,
):
    core = lax.axis_index("tensor")
    partner = {"tensor": 1 - core}
    sources, _, width = back_ref.shape
    count = sources * padded
    local = dy_ref.shape[0]
    step = fit(local, 256)
    barrier = pltpu.get_barrier_semaphore()
    pl.semaphore_signal(barrier, inc=1, device_id=partner, device_id_type=MESH)
    pl.semaphore_wait(barrier, 1)

    def remote(src, dst, number):
        return pltpu.make_async_remote_copy(
            src_ref=src,
            dst_ref=dst,
            send_sem=send_sem.at[number],
            recv_sem=recv_sem.at[number],
            device_id=partner,
            device_id_type=MESH,
        )

    own_rows = pl.ds(pl.multiple_of(core * local, local), local)
    lane = lax.broadcasted_iota(jnp.int32, (step, LANES), 1)
    for s in range(sources):
        dots = back_ref[s, padded - 16 :, : 2 * LANES].astype(single).T
        number = lax.broadcasted_iota(jnp.int32, (padded, LANES), 1)
        ext = jnp.where(
            number == s,
            dots[:padded, 14:15],
            jnp.where(number == s + EXPERTS_FF, dots[:padded, 15:16], 0.0),
        )
        ext_ref[pl.ds(s * padded, padded), :] = ext.astype(half)
    back_all = back_ref.reshape(count, width)

    @pl.loop(0, local // step)
    def _(r):
        rows = pl.ds(pl.multiple_of(r * step, step), step)
        there = pl.ds(pl.multiple_of((1 - core) * local + r * step, step), step)
        hot = slot_rows(info_ref[there, :], count)
        out_ref[rows, pl.ds(0, width)] = mm(hot, back_all[...]).astype(half)
        out_ref[rows, pl.ds(width, LANES)] = mm(hot, ext_ref[...]).astype(half)

    sums = remote(out_ref, in_ref, 0)
    sums.start()
    small_ref[...] = jnp.zeros(small_ref.shape, single)
    mgrad_ref[...] = jnp.zeros(mgrad_ref.shape, single)

    @pl.loop(0, local // step)
    def _(r):
        rows = pl.ds(pl.multiple_of(r * step, step), step)
        here = pl.ds(pl.multiple_of(core * local + r * step, step), step)
        hot = slot_rows(info_ref[here, :], count)
        rgrad_ref[rows, :] = mm(hot, back_all[...])
        pgrad_ref[rows, :] = mm(hot, ext_ref[...])

    sums.wait()

    @pl.loop(0, local // step)
    def _(r):
        rows = pl.ds(pl.multiple_of(r * step, step), step)
        here = pl.ds(pl.multiple_of(core * local + r * step, step), step)
        dy = dy_ref[rows, :].astype(single)
        normed = normed_ref[rows, :].astype(single)
        resid = resid_ref[rows, :]
        misc = misc_ref[rows, :]
        expert_dot = pgrad_ref[rows, :] + in_ref[rows, pl.ds(width, LANES)].astype(single)
        own_dot = lane_sum(dy * normed)
        vec_dot = [lane_sum(dy * const_ref[j : j + 1, :]) for j in range(2)]
        gates = [misc[:, k : k + 1] for k in range(2)]
        routes = [routes_ref[rows, k : k + 1] for k in range(2)]
        alphas = []
        for j in range(2):
            columns = [misc[:, EXPERTS + 2 * j + m : EXPERTS + 2 * j + m + 1] for m in range(2)]
            peak = jnp.maximum(columns[0], columns[1])
            expo = [jnp.exp(c - peak) for c in columns]
            total = expo[0] + expo[1]
            alphas.append([e / total for e in expo])
        gate_grads = []
        for k in range(2):
            hit = (lane == routes[k]) | (lane == routes[k] + EXPERTS_FF)
            dot = lane_sum(jnp.where(hit & (routes[k] < EXPERTS_FF), expert_dot, 0.0))
            dot += jnp.where(routes[k] == EXPERTS_FF + 1, own_dot, 0.0)
            for j in range(2):
                value = alphas[j][0] * own_dot + alphas[j][1] * vec_dot[j]
                dot += jnp.where(routes[k] == EXPERTS_FF + 2 + j, value, 0.0)
            gate_grads.append(dot)
        centre = gates[0] * gate_grads[0] + gates[1] * gate_grads[1]
        chosen = [gates[k] * (gate_grads[k] - centre) for k in range(2)]
        router_grad = jnp.zeros((step, LANES), single)
        own_weight = jnp.zeros((step, 1), single)
        for k in range(2):
            router_grad = jnp.where(lane == routes[k], chosen[k], router_grad)
            own_weight += jnp.where(routes[k] == EXPERTS_FF + 1, gates[k], 0.0)
        logit_grad = router_grad
        vec_lanes = jnp.zeros((step, LANES), single)
        other = jnp.zeros((step, width), single)
        for j in range(2):
            weight = sum(jnp.where(routes[k] == EXPERTS_FF + 2 + j, gates[k], 0.0) for k in range(2))
            grads = [weight * own_dot, weight * vec_dot[j]]
            mean = alphas[j][0] * grads[0] + alphas[j][1] * grads[1]
            for m in range(2):
                router_grad = jnp.where(
                    lane == EXPERTS + 2 * j + m, alphas[j][m] * (grads[m] - mean), router_grad
                )
            own_weight += weight * alphas[j][0]
            vec_weight = weight * alphas[j][1]
            vec_lanes = jnp.where(lane == 16 + j, vec_weight, vec_lanes)
            other += vec_weight * const_ref[j : j + 1, :]
        base_ref[rows, :] = resid + own_weight * normed + other
        rg_high, rg_low = split(router_grad)
        two_grad = rgrad_ref[rows, :] + in_ref[rows, pl.ds(0, width)].astype(single)
        two_grad += own_weight * dy
        two_grad += mm_nt(rg_high, router_ref[...]) + mm_nt(rg_low, router_ref[...])
        normed_low = normed_ref[rows, :]
        vec_high, vec_low = split(vec_lanes)
        small_ref[...] += (
            mm_tn(rg_high, normed_low)
            + mm_tn(rg_low, normed_low)
            + mm_tn(vec_high, dy_ref[rows, :])
            + mm_tn(vec_low, dy_ref[rows, :])
        )[:24]
        scale = rms_scale(resid)
        gain_part = jnp.sum(two_grad * resid * scale, axis=0, keepdims=True)
        small_ref[19:20, :] += gain_part
        weighted = two_grad * gain_ref[1:2, :]
        mean = jnp.mean(weighted * resid, axis=-1, keepdims=True)
        grad = dy + scale * (weighted - resid * scale * scale * mean)
        rgrad_ref[rows, :] = grad
        low = grad.astype(half)
        attn_ref[here, :] = low
        heads_ref[here, :] = mm(low, own_w_ref[...]).astype(half)
        hg_ref[rows, :] = mm(low, other_w_ref[...]).astype(half)
        lg_high, lg_low = split(logit_grad)
        mix_high, mix_low = split(mix_ref[...])
        pgrad_ref[rows, :] = (
            mm_nt(lg_high, mix_high) + mm_nt(lg_high, mix_low) + mm_nt(lg_low, mix_high)
        )
        prev_high, prev_low = split(prev_ref[rows, :])
        mgrad_ref[...] += (
            mm_tn(prev_high, lg_high) + mm_tn(prev_high, lg_low) + mm_tn(prev_low, lg_high)
        )

    for i in range(EXPERTS):
        place = pl.ds(i % 6 * LANES, LANES)
        small_ref[20 + i // 6 : 21 + i // 6, place] = mgrad_ref[i : i + 1, :]

    heads = remote(hg_ref, heads_ref.at[own_rows], 1)
    heads.start()
    attn = remote(attn_ref.at[own_rows], attn_ref.at[own_rows], 2)
    attn.start()
    heads.wait()
    attn.wait()


def backward_middle(
    back, info, resid, normed, misc, dy, routes, gains, const, router, own_w, other_w, prev, mix, padded
):
    local, width = dy.shape
    seq = info.shape[0]
    hh = own_w.shape[1]
    count = EXPERTS_FF * padded
    vmem = pl.BlockSpec(memory_space=pltpu.VMEM)
    return pl.pallas_call(
        functools.partial(back_kernel, padded),
        out_shape=[
            jax.ShapeDtypeStruct((local, width), single),
            jax.ShapeDtypeStruct((seq, width), half),
            jax.ShapeDtypeStruct((seq, hh), half),
            jax.ShapeDtypeStruct((local, width), single),
            jax.ShapeDtypeStruct((local, LANES), single),
            jax.ShapeDtypeStruct((24, width), single),
            jax.ShapeDtypeStruct((LANES, LANES), single),
        ],
        in_specs=[vmem] * 14,
        out_specs=[vmem] * 7,
        scratch_shapes=[
            pltpu.VMEM((count, LANES), half),
            pltpu.VMEM((local, width + LANES), half),
            pltpu.VMEM((local, width + LANES), half),
            pltpu.VMEM((local, hh), half),
            pltpu.SemaphoreType.DMA((3,)),
            pltpu.SemaphoreType.DMA((3,)),
        ],
        compiler_params=pltpu.CompilerParams(
            collective_id=2, has_side_effects=True, vmem_limit_bytes=56 << 20
        ),
        name="backward_middle",
    )(back, info, resid, normed, misc, dy, routes, gains, const, router, own_w, other_w, prev, mix)


def weight_kernel(
    x_ref, og_ref, hid_ref, pg_ref, pu_ref, out_ref, xt_ref, ogt_ref, send_ref, got_ref, send_sem, recv_sem
):
    f = pl.program_id(0)
    partner = {"tensor": 1 - lax.axis_index("tensor")}
    shape = out_ref.shape[0], out_ref.shape[2], out_ref.shape[3]

    @pl.when(f == 0)
    def _():
        barrier = pltpu.get_barrier_semaphore()
        pl.semaphore_signal(barrier, inc=1, device_id=partner, device_id_type=MESH)
        pl.semaphore_wait(barrier, 1)
        xt_ref[...] = x_ref[...].T
        ogt_ref[...] = og_ref[...].T

    def remote(number):
        return pltpu.make_async_remote_copy(
            src_ref=send_ref.at[number],
            dst_ref=got_ref.at[number],
            send_sem=send_sem.at[number],
            recv_sem=recv_sem.at[number],
            device_id=partner,
            device_id_type=MESH,
        )

    factors = (xt_ref, pg_ref), (xt_ref, pu_ref), (ogt_ref, hid_ref)
    for k, (left, right) in enumerate(factors):
        send_ref[f, k] = mm(left[...], right[1]).astype(half)
    remote(f).start()
    grads = [mm(left[...], right[0]) for left, right in factors]
    remote(f).wait_recv()
    for k in range(3):
        total = grads[k] + got_ref[f, k].astype(single)
        out_ref[:, k] = total.astype(half).reshape(shape)

    @pl.when(f == pl.num_programs(0) - 1)
    def _():
        for number in range(send_ref.shape[0]):
            remote(number).wait_send()


def weight_step(x, og, hidden, pg, pu, m):
    count, width = og.shape
    ff = hidden.shape[2]
    block = fit(ff, 256)
    steps = ff // block
    whole = pl.BlockSpec((count, width), lambda f: (0, 0))
    wide = pl.BlockSpec((2, count, block), lambda f: (0, 0, f))
    part = pl.BlockSpec((m, 3, width // m, block), lambda f: (0, 0, 0, f))
    return pl.pallas_call(
        weight_kernel,
        grid=(steps,),
        in_specs=[whole, whole, wide, wide, wide],
        out_specs=part,
        out_shape=jax.ShapeDtypeStruct((m, 3, width // m, ff), half),
        scratch_shapes=[
            pltpu.VMEM((width, count), half),
            pltpu.VMEM((width, count), half),
            pltpu.VMEM((steps, 3, width, block), half),
            pltpu.VMEM((steps, 3, width, block), half),
            pltpu.SemaphoreType.DMA((steps,)),
            pltpu.SemaphoreType.DMA((steps,)),
        ],
        compiler_params=pltpu.CompilerParams(
            collective_id=3, has_side_effects=True, vmem_limit_bytes=56 << 20
        ),
        cost_estimate=pl.CostEstimate(
            flops=12 * count * width * ff,
            bytes_accessed=12 * width * ff + 12 * count * ff,
            transcendentals=0,
        ),
        name="weight_step",
    )(x, og, hidden, pg, pu)


def tail_kernel(
    members,
    low,
    padded,
    eo_ref,
    qkv_ref,
    one_ref,
    proj_ref,
    outg_ref,
    x_ref,
    base_ref,
    resid_ref,
    info_ref,
    gain_ref,
    small_ref,
    dense_out_ref,
    tokens_ref,
    mixed_ref,
    small_out_ref,
    dense_ref,
    first_ref,
    stage_ref,
    second_ref,
    eo_in_ref,
    one_out_ref,
    one_in_ref,
    ffn_out_ref,
    ffn_in_ref,
    ffn_ref,
    mine_ref,
    pair_ref,
    near_ref,
    far_ref,
    send1,
    recv1,
    send2,
    recv2,
    eo_send,
    eo_recv,
    pair_send,
    pair_recv,
    near_send,
    near_recv,
    far_send,
    far_recv,
    own_sem,
):
    size = EXPERTS_FF
    me = lax.axis_index("dp")
    core = lax.axis_index("tensor")
    high = members // low
    inside, row = lax.rem(me, low), me // low
    mine = lax.rem(me, size)
    base = me - mine
    local, width = base_ref.shape
    count = size * padded
    d_rows = dense_out_ref.shape[0]
    hh3 = qkv_ref.shape[1]
    step = fit(local, 256)
    partner = {"tensor": 1 - core}

    def beside(k):
        return row * low + lax.rem(inside + k, low)

    def across(k):
        return lax.rem(row + k, high) * low + inside

    peers = [beside(k) for k in range(1, low)] + [across(k) for k in range(1, high)]
    peers += [base + lax.rem(mine + k, size) for k in range(1, size)]
    barrier = pltpu.get_barrier_semaphore()
    for peer in peers:
        pl.semaphore_signal(barrier, inc=1, device_id={"dp": peer}, device_id_type=MESH)
    pl.semaphore_signal(barrier, inc=1, device_id=partner, device_id_type=MESH)
    pl.semaphore_wait(barrier, len(peers) + 1)

    def remote(src, dst, send, recv, device):
        return pltpu.make_async_remote_copy(
            src_ref=src,
            dst_ref=dst,
            send_sem=send,
            recv_sem=recv,
            device_id=device,
            device_id_type=MESH,
        )

    eo = []
    for k in range(1, size):
        to = lax.rem(mine + k, size)
        eo.append(
            remote(
                eo_ref.at[to], eo_in_ref.at[mine], eo_send.at[k], eo_recv.at[k], {"dp": base + to}
            )
        )
    eo.append(pltpu.make_async_copy(eo_ref.at[mine], eo_in_ref.at[mine], own_sem))
    for copy in eo:
        copy.start()

    sent = []
    chunks = 2
    rows_each = width // chunks
    for c in range(chunks):
        lanes = pl.ds(c * rows_each, rows_each)
        grad = mm_tn(one_ref[:, lanes], qkv_ref[...])
        for j in range(members // chunks):
            owner = c * (members // chunks) + j
            dense_ref[owner, :, :hh3] = grad[j * d_rows : (j + 1) * d_rows].astype(half)
            dense_ref[owner, :, hh3:] = outg_ref[owner * d_rows : (owner + 1) * d_rows, :]
        for h in range(c * high // chunks, (c + 1) * high // chunks):
            for k in range(1, low):
                copy = remote(
                    dense_ref.at[h * low + lax.rem(inside + k, low)],
                    first_ref.at[k - 1, h],
                    send1.at[k - 1, h],
                    recv1.at[k - 1, h],
                    {"dp": beside(k)},
                )
                copy.start()
                sent.append(copy)

    def one_part(rows):
        part = mm_nt(qkv_ref[rows, :], proj_ref[...])
        x = x_ref[rows, :].astype(single)
        mine_ref[18:19, :] += jnp.sum(part * x * rms_scale(x), axis=0, keepdims=True)
        return part

    mine_ref[...] = small_ref[...]

    @pl.loop(0, local // step)
    def _(r):
        rows = pl.ds(pl.multiple_of(r * step, step), step)
        there = pl.ds(pl.multiple_of((1 - core) * local + r * step, step), step)
        one_out_ref[rows, :] = one_part(there).astype(half)

    one_sent = remote(one_out_ref, one_in_ref, pair_send.at[0], pair_recv.at[0], partner)
    one_sent.start()

    @pl.loop(0, local // step)
    def _(r):
        rows = pl.ds(pl.multiple_of(r * step, step), step)
        here = pl.ds(pl.multiple_of(core * local + r * step, step), step)
        tokens_ref[rows, :] = one_part(here)

    pair = remote(mine_ref, pair_ref, pair_send.at[1], pair_recv.at[1], partner)
    pair.start()
    pair.wait()
    near_ref[inside] = mine_ref[...] + pair_ref[...]
    near = []
    for k in range(1, low):
        near.append(
            remote(
                near_ref.at[inside],
                near_ref.at[inside],
                near_send.at[k],
                near_recv.at[inside],
                {"dp": beside(k)},
            )
        )
        near[-1].start()

    for j in range(1, high + 1):
        h = lax.rem(row + j, high)
        total = dense_ref[h * low + inside].astype(single)
        for k in range(low - 1):
            remote(
                dense_ref.at[0], first_ref.at[k, h], send1.at[k, h], recv1.at[k, h], partner
            ).wait_recv()
            total += first_ref[k, h].astype(single)
        if j < high:
            stage_ref[j - 1] = total.astype(half)
            copy = remote(
                stage_ref.at[j - 1],
                second_ref.at[j - 1],
                send2.at[j - 1],
                recv2.at[j - 1],
                {"dp": across(j)},
            )
            copy.start()
            sent.append(copy)
        else:
            dense_out_ref[...] = total
    for k in range(1, low):
        block = lax.rem(inside + k, low)
        remote(
            mine_ref, near_ref.at[block], near_send.at[0], near_recv.at[block], partner
        ).wait_recv()
    total = near_ref[0]
    for k in range(1, low):
        total = total + near_ref[k]
    far_ref[row] = total
    far = []
    for k in range(1, high):
        far.append(
            remote(
                far_ref.at[row], far_ref.at[row], far_send.at[k], far_recv.at[row], {"dp": across(k)}
            )
        )
        far[-1].start()

    for copy in eo:
        copy.wait()
    eo_all = eo_in_ref.reshape(count, width)

    @pl.loop(0, local // step)
    def _(r):
        rows = pl.ds(pl.multiple_of(r * step, step), step)
        there = pl.ds(pl.multiple_of((1 - core) * local + r * step, step), step)
        ffn_out_ref[rows, :] = mm(slot_rows(info_ref[there, :], count), eo_all[...]).astype(half)

    ffn_sent = remote(ffn_out_ref, ffn_in_ref, pair_send.at[2], pair_recv.at[2], partner)
    ffn_sent.start()

    @pl.loop(0, local // step)
    def _(r):
        rows = pl.ds(pl.multiple_of(r * step, step), step)
        here = pl.ds(pl.multiple_of(core * local + r * step, step), step)
        ffn_ref[rows, :] = mm(slot_rows(info_ref[here, :], count), eo_all[...])

    one_sent.wait()

    @pl.loop(0, local // step)
    def _(r):
        rows = pl.ds(pl.multiple_of(r * step, step), step)
        here = pl.ds(pl.multiple_of(core * local + r * step, step), step)
        x = x_ref[here, :].astype(single)
        scale = rms_scale(x)
        weighted = (tokens_ref[rows, :] + one_in_ref[rows, :].astype(single)) * gain_ref[0:1, :]
        mean = jnp.mean(weighted * x, axis=-1, keepdims=True)
        tokens_ref[rows, :] = resid_ref[rows, :] + scale * (weighted - x * scale * scale * mean)

    ffn_sent.wait()

    @pl.loop(0, local // step)
    def _(r):
        rows = pl.ds(pl.multiple_of(r * step, step), step)
        total = base_ref[rows, :] + ffn_ref[rows, :] + ffn_in_ref[rows, :].astype(single)
        mixed_ref[rows, :] = total.astype(half)

    for j in range(1, high):
        remote(
            stage_ref.at[0], second_ref.at[j - 1], send2.at[j - 1], recv2.at[j - 1], partner
        ).wait_recv()
        dense_out_ref[...] += second_ref[j - 1].astype(single)
    for k in range(1, high):
        block = lax.rem(row + k, high)
        remote(
            mine_ref, far_ref.at[block], far_send.at[0], far_recv.at[block], partner
        ).wait_recv()
    total = far_ref[0]
    for k in range(1, high):
        total = total + far_ref[k]
    small_out_ref[...] = total
    for copy in sent + near + far:
        copy.wait_send()


def tail(members, eo, qkv, one, proj, outg, x, base, resid, info, gains, small, padded):
    low = 4
    high = members // low
    local, width = base.shape
    d_rows = width // members
    wide = qkv.shape[1] + outg.shape[1]
    vmem = pl.BlockSpec(memory_space=pltpu.VMEM)
    dma = pltpu.SemaphoreType.DMA
    rows_half = pltpu.VMEM((local, width), half)
    small_one = pltpu.VMEM(small.shape, single)
    return pl.pallas_call(
        functools.partial(tail_kernel, members, low, padded),
        out_shape=[
            jax.ShapeDtypeStruct((d_rows, wide), single),
            jax.ShapeDtypeStruct((local, width), single),
            jax.ShapeDtypeStruct((local, width), half),
            jax.ShapeDtypeStruct(small.shape, single),
        ],
        in_specs=[pl.BlockSpec(memory_space=pl.ANY)] + [vmem] * 10,
        out_specs=[vmem] * 4,
        scratch_shapes=[
            pltpu.VMEM((members, d_rows, wide), half),
            pltpu.VMEM((low - 1, high, d_rows, wide), half),
            pltpu.VMEM((high - 1, d_rows, wide), half),
            pltpu.VMEM((high - 1, d_rows, wide), half),
            pltpu.VMEM(eo.shape, half),
            rows_half,
            rows_half,
            rows_half,
            rows_half,
            pltpu.VMEM((local, width), single),
            small_one,
            small_one,
            pltpu.VMEM((low,) + small.shape, single),
            pltpu.VMEM((high,) + small.shape, single),
            dma((low - 1, high)),
            dma((low - 1, high)),
            dma((high - 1,)),
            dma((high - 1,)),
            dma((EXPERTS_FF,)),
            dma((EXPERTS_FF,)),
            dma((3,)),
            dma((3,)),
            dma((low,)),
            dma((low,)),
            dma((high,)),
            dma((high,)),
            dma,
        ],
        compiler_params=pltpu.CompilerParams(
            collective_id=4, has_side_effects=True, vmem_limit_bytes=60 << 20
        ),
        name="tail",
    )(eo, qkv, one, proj, outg, x, base, resid, info, gains, small)


def per_device(
    tokens,
    segment_ids,
    routes,
    prev_logits,
    cotangent,
    proj_weight,
    out_weight,
    norm_gain,
    expert_weight,
    router,
    constant_vectors,
    gate_mixing,
):
    members = lax.axis_size("dp")
    groups = members // EXPERTS_FF
    cubes = [[g * EXPERTS_FF + i for i in range(EXPERTS_FF)] for g in range(groups)]
    core = lax.axis_index("tensor")
    d_rows, hh = out_weight.shape
    per_core = -(-CAPACITY // 2)
    padded = -(-(per_core + 3) // 16) * 16

    def in_group(blocks):
        return lax.all_to_all(blocks, "dp", 0, 0, axis_index_groups=cubes, tiled=True)

    def plain_tail(eo, qkv, one, proj, outg, x, base, resid, gains, small):
        ffn = pair_sum(mm_tn(onehot, in_group(eo).reshape(-1, width)))
        part = mm_nt(qkv, proj)
        scale = rms_scale(x)
        small = small.at[18].set(jnp.sum(part * x * scale, axis=0))
        weighted = pair_sum(part) * gains[0]
        x, scale = half_of(x, core), half_of(scale, core)
        mean = jnp.mean(weighted * x, axis=-1, keepdims=True)
        tokens_grad = resid + scale * (weighted - x * scale * scale * mean)
        dense = jnp.concatenate([mm_tn(one, qkv).astype(half), outg], 1)
        dense = lax.all_to_all(dense.reshape(members, d_rows, -1), "dp", 0, 0, tiled=True)
        dense = jnp.sum(dense.astype(single), axis=0)
        return dense, tokens_grad, (base + ffn).astype(half), lax.psum(small, ("dp", "tensor"))

    pack = jnp.concatenate(
        [
            proj_weight.transpose(1, 0, 2).reshape(d_rows, 3 * hh),
            out_weight,
            norm_gain.T,
            constant_vectors.T,
            router,
        ],
        1,
    )
    columns = pack.shape[1]
    pack = jnp.pad(pack, ((0, 0), (0, -columns % LANES)))
    ids = jnp.concatenate([segment_ids, routes[0].T], 0)
    ids = jnp.pad(ids, ((0, 5), (0, 0)))
    full_pack, tokens_all, got_dy, onehot, info = start(
        pack, tokens[0], cotangent[0], ids, members, per_core, padded
    )
    full_pack, expert_weight = lax.optimization_barrier((full_pack, expert_weight))
    full_pack = full_pack.reshape(members * d_rows, -1)[:, :columns]
    width = members * d_rows
    proj_full = full_pack[:, : 3 * hh]
    outw_own = full_pack[:, 3 * hh : 4 * hh]
    outw_other = swap(outw_own)
    rest = full_pack[:, 4 * hh :]
    gains = rest[:, :2].T.astype(single)
    const_f = rest[:, 2:4].T.astype(single)
    router_full = rest[:, 4:]
    in_weight = jnp.broadcast_to(
        expert_weight[None, :, :2], (groups, EXPERTS_FF, 2) + expert_weight.shape[2:]
    ).reshape((members, 2) + expert_weight.shape[2:])
    down_weight = jnp.broadcast_to(
        expert_weight[None, :, 2], (groups, EXPERTS_FF) + expert_weight.shape[2:]
    ).reshape((members,) + expert_weight.shape[2:])
    my_in = lax.all_to_all(in_weight, "dp", 0, 0, tiled=True)
    if d_rows % 16:
        my_in = my_in.transpose(1, 0, 2, 3).reshape(1, 2, width, -1)

    x_rows = tokens[0].astype(single)
    local_rows = x_rows.shape[0]
    x_all = tokens_all.astype(single)
    scale_all = rms_scale(x_all)
    full_one = (x_all * scale_all * gains[0]).astype(half)
    scale_one = half_of(scale_all, core)
    seq = full_one.shape[0]
    qkv = mm(full_one, proj_full).astype(half)
    size = fit(seq, 256)
    starts = info[0]
    bounds = block_bounds(starts, info[1], size)
    columns = info.T
    heads_full, heads_out, lse = attention_forward(qkv, bounds, starts, size)
    prev_rows = prev_logits[0]
    mixed_prev = jnp.dot(prev_rows, gate_mixing, precision=HIGH)
    mixed_prev = jnp.pad(mixed_prev, ((0, 0), (0, LANES - EXPERTS)))
    router_wide = jnp.pad(router_full, ((0, 0), (0, LANES - router_full.shape[1])))
    got_rows, my_down, other_down, other_in, resid, normed_two, misc = middle(
        down_weight,
        my_in,
        heads_out,
        tokens[0],
        outw_own,
        outw_other,
        gains,
        router_wide,
        mixed_prev,
        routes[0],
        onehot,
        padded,
    )
    if d_rows % 16:
        my_down = my_down.reshape(1, width, -1)
        other_down = other_down.reshape(1, width, -1)

    count = EXPERTS_FF * padded
    gated_out, in_grad, out_grad, hidden, pg, pu = expert_step(
        got_rows, got_dy, my_in, my_down, other_in, other_down, padded
    )
    back_grad = in_group(in_grad)
    grads_sent = weight_step(
        got_rows.reshape(count, width), out_grad, hidden, pg, pu, my_in.shape[0]
    )
    back_grad, grads_sent = lax.optimization_barrier((back_grad, grads_sent))
    if d_rows % 16:
        grads_sent = grads_sent.reshape(3, members, d_rows, -1).transpose(1, 0, 2, 3)
    grads_got = lax.all_to_all(grads_sent, "dp", 0, 0, tiled=True)

    mix_wide = jnp.pad(gate_mixing, ((0, LANES - EXPERTS), (0, LANES - EXPERTS)))
    prev_wide = jnp.pad(prev_rows, ((0, 0), (0, LANES - EXPERTS)))
    resid_grad, attn_all, heads_grad, base, prev_grad, small, mixing_grad = backward_middle(
        back_grad,
        columns,
        resid,
        normed_two,
        misc,
        cotangent[0],
        routes[0],
        gains,
        const_f,
        router_wide,
        outw_own,
        outw_other,
        prev_wide,
        mix_wide,
        padded,
    )
    out_w_grad = mm_tn(attn_all, heads_out)
    qkv_grad = attention_backward(qkv, heads_grad, heads_full, lse, bounds, starts, size)
    qkv_grad, grads_got = lax.optimization_barrier((qkv_grad, grads_got))
    out_w_grad = out_w_grad.astype(half)
    if d_rows % 16 or members != 16:
        outs = plain_tail(
            gated_out, qkv_grad, full_one, proj_full, out_w_grad, x_all, base, resid_grad, gains, small
        )
    else:
        outs = tail(
            members,
            gated_out,
            qkv_grad,
            full_one,
            proj_full,
            out_w_grad,
            tokens_all,
            base,
            resid_grad,
            columns,
            gains,
            small,
            padded,
        )
    dense, tokens_grad, mixed, small = outs
    expert_shard = jnp.sum(
        grads_got.reshape((groups, EXPERTS_FF) + grads_got.shape[1:]).astype(single), axis=0
    )
    proj_shard = dense[:, : 3 * hh].reshape(d_rows, 3, hh).transpose(1, 0, 2)
    outw_shard = dense[:, 3 * hh :]
    mixing_total = small[20:22].reshape(EXPERTS, LANES)[:, :EXPERTS]
    features = lax.dynamic_slice_in_dim(small, lax.axis_index("dp") * d_rows, d_rows, 1)
    return (
        mixed[None],
        tokens_grad[None],
        prev_grad[None, :, :EXPERTS],
        proj_shard,
        outw_shard,
        features[18:20],
        expert_shard,
        features[:16].T,
        features[16:18],
        mixing_total,
    )


def solution(mesh):
    return jax.shard_map(
        per_device,
        mesh=mesh,
        in_specs=(
            P("dp", "tensor", None),
            P("dp", "tensor"),
            P("dp", "tensor", None),
            P("dp", "tensor", None),
            P("dp", "tensor", None),
            P(None, "dp", "tensor"),
            P("dp", "tensor"),
            P(None, "dp"),
            P(None, None, "dp", "tensor"),
            P("dp", None),
            P(None, "dp"),
            P(),
        ),
        out_specs=(
            P("dp", "tensor", None),
            P("dp", "tensor", None),
            P("dp", "tensor", None),
            P(None, "dp", "tensor"),
            P("dp", "tensor"),
            P(None, "dp"),
            P(None, None, "dp", "tensor"),
            P("dp", None),
            P(None, "dp"),
            P(),
        ),
        check_vma=False,
    )
```

```python
import functools

import jax
import jax.numpy as jnp
from jax import lax
from jax.experimental import pallas as pl
from jax.experimental.pallas import tpu as pltpu
from jax.sharding import PartitionSpec as P

HEAD_DIM = 64
EXPERTS_FF = 8
EXPERTS = 12
CAPACITY = 341


EPS = 1e-05
HIGH = lax.Precision.HIGHEST
NEG = -1e30
LANES = 128
DOCS = 8
LOG2E = 1.4426950408889634
MESH = pl.DeviceIdType.MESH
single = jnp.float32
half = jnp.bfloat16


def rms_scale(rows):
    return lax.rsqrt(jnp.mean(rows * rows, axis=-1, keepdims=True) + EPS)


def softmax_last(values):
    peak = jnp.max(values, axis=-1, keepdims=True)
    expo = jnp.exp(values - peak)
    return expo / jnp.sum(expo, axis=-1, keepdims=True)


def mm(a, b):
    return jnp.dot(a, b, preferred_element_type=single)


def mm_nt(a, b):
    return lax.dot_general(a, b, (((1,), (1,)), ((), ())), preferred_element_type=single)


def mm_tn(a, b):
    return lax.dot_general(a, b, (((0,), (0,)), ((), ())), preferred_element_type=single)


def swap(x):
    return lax.ppermute(x, "tensor", [(0, 1), (1, 0)])


def in_order(own, other):
    first = lax.axis_index("tensor") == 0
    return jnp.concatenate([jnp.where(first, own, other), jnp.where(first, other, own)], 0)


def half_of(full, which):
    count = full.shape[0] // 2
    return lax.dynamic_slice_in_dim(full, which * count, count, 0)


def pair_sum(full):
    core = lax.axis_index("tensor")
    other = swap(half_of(full, 1 - core).astype(half))
    return half_of(full, core) + other.astype(single)


def fit(seq, want):
    return want if seq % want == 0 else seq

def block_bounds(start, end, size):
    edges = start.reshape(-1, size)
    number = jnp.arange(edges.shape[0], dtype=jnp.int32)
    low = edges[:, 0] // size
    plain = jnp.clip((edges[:, -1] + size - 1) // size, low, number)
    high = end.reshape(-1, size)[:, -1] // size
    clear = jnp.sum((edges[None, :, -1] <= number[:, None] * size).astype(jnp.int32), axis=1)
    clear = jnp.clip(clear, number + 1, high + 1)
    return jnp.stack([low, plain, high, clear])


def head_lanes(h, rows):
    lane = lax.broadcasted_iota(jnp.int32, (rows, LANES), 1)
    return (lane < HEAD_DIM) if h % 2 == 0 else (lane >= HEAD_DIM)

def fwd_kernel(heads, bounds, q_ref, k_ref, v_ref, start_ref, o_ref, low_ref, lse_ref, s_ref, m_ref, l_ref, acc_ref, qm_ref):
    size = q_ref.shape[0]
    i = pl.program_id(0)
    low, plain = bounds[0, i], bounds[1, i]
    factor = LOG2E * HEAD_DIM ** -0.5
    for h in range(heads):
        pair = pl.ds(h // 2 * LANES, LANES)
        qm_ref[h] = jnp.where(head_lanes(h, size), q_ref[:, pair], 0).astype(half)
    m_ref[...] = jnp.full(m_ref.shape, NEG, single)
    l_ref[...] = jnp.zeros(l_ref.shape, single)
    acc_ref[...] = jnp.zeros(acc_ref.shape, single)

    def score(j, masked):
        rows = pl.ds(pl.multiple_of(j * size, size), size)
        if masked:
            row = i * size + lax.broadcasted_iota(jnp.int32, (size, size), 0)
            col = j * size + lax.broadcasted_iota(jnp.int32, (size, size), 1)
            allowed = (col <= row) & (col >= start_ref[...])
        for h in range(heads):
            s = mm_nt(qm_ref[h], k_ref[rows, pl.ds(h // 2 * LANES, LANES)])
            if masked:
                s = jnp.where(allowed, s, NEG)
            s_ref[h, j] = s
            m = m_ref[h]
            for c in range(size // LANES):
                m = jnp.maximum(m, s[:, c * LANES : (c + 1) * LANES])
            m_ref[h] = m

    pl.loop(low, plain)(lambda j: score(j, True))
    pl.loop(plain, i)(lambda j: score(j, False))
    score(i, True)
    for h in range(heads):
        m_ref[h] = jnp.broadcast_to(jnp.max(m_ref[h], axis=1, keepdims=True) * factor, (size, LANES))

    def gather(j):
        rows = pl.ds(pl.multiple_of(j * size, size), size)
        for h in range(heads):
            s = s_ref[h, j]
            m = m_ref[h]
            l = l_ref[h]
            parts = []
            for c in range(size // LANES):
                p = jnp.exp2(s[:, c * LANES : (c + 1) * LANES] * factor - m)
                l = l + p
                parts.append(p.astype(half))
            l_ref[h] = l
            acc_ref[h] += jnp.dot(jnp.concatenate(parts, 1), v_ref[rows, pl.ds(h // 2 * LANES, LANES)], preferred_element_type=single)

    pl.loop(low, i + 1)(gather)
    lane = lax.broadcasted_iota(jnp.int32, (size, LANES), 1)
    lse = jnp.zeros((size, LANES), single)
    for h in range(0, heads, 2):
        outs = []
        for k in (h, h + 1):
            l = jnp.sum(l_ref[k], axis=1, keepdims=True)
            outs.append(acc_ref[k] / l)
            lse = jnp.where(lane == k, m_ref[k] + jnp.log2(l), lse)
        out = jnp.where(lane < HEAD_DIM, outs[0], outs[1])
        o_ref[:, pl.ds(h // 2 * LANES, LANES)] = out
        low_ref[:, pl.ds(h // 2 * LANES, LANES)] = out.astype(half)
    lse_ref[...] = lse

def attention_forward(qkv, seg_bounds, starts, size):
    seq = qkv.shape[0]
    hh = qkv.shape[1] // 3
    heads = hh // HEAD_DIM
    return pl.pallas_call(
        functools.partial(fwd_kernel, heads),
        grid_spec=pltpu.PrefetchScalarGridSpec(
            num_scalar_prefetch=1,
            grid=(seq // size,),
            in_specs=[
                pl.BlockSpec((size, hh), lambda i, b: (i, 0)),
                pl.BlockSpec((seq, hh), lambda i, b: (0, 1)),
                pl.BlockSpec((seq, hh), lambda i, b: (0, 2)),
                pl.BlockSpec((size, 1), lambda i, b: (i, 0)),
            ],
            out_specs=[
                pl.BlockSpec((size, hh), lambda i, b: (i, 0)),
                pl.BlockSpec((size, hh), lambda i, b: (i, 0)),
                pl.BlockSpec((size, LANES), lambda i, b: (i, 0)),
            ],
            scratch_shapes=[
                pltpu.VMEM((heads, seq // size, size, size), single),
                pltpu.VMEM((heads, size, LANES), single),
                pltpu.VMEM((heads, size, LANES), single),
                pltpu.VMEM((heads, size, LANES), single),
                pltpu.VMEM((heads, size, LANES), half),
            ],
        ),
        out_shape=[
            jax.ShapeDtypeStruct((seq, hh), single),
            jax.ShapeDtypeStruct((seq, hh), half),
            jax.ShapeDtypeStruct((seq, LANES), single),
        ],
        compiler_params=pltpu.CompilerParams(vmem_limit_bytes=48 << 20),
        cost_estimate=pl.CostEstimate(flops=4 * seq * seq * LANES * heads, bytes_accessed=16 * seq * hh, transcendentals=0),
    )(seg_bounds, qkv, qkv, qkv, starts[:, None])

def bwd_kernel(
    heads, bounds, q_ref, k_ref, v_ref, do_ref, o_ref, lse_ref, start_ref, out_ref, dq_ref, dk_ref, dv_ref, stat_ref
):
    size = k_ref.shape[0]
    j = pl.program_id(0)
    high, clear = bounds[2, j], bounds[3, j]
    factor = LOG2E * HEAD_DIM ** -0.5
    hh = k_ref.shape[1]

    @pl.when(j == 0)
    def _():
        dq_ref[...] = jnp.zeros(dq_ref.shape, single)
        feature = lax.broadcasted_iota(jnp.int32, (hh, LANES), 0)
        lane = lax.broadcasted_iota(jnp.int32, (hh, LANES), 1)
        pick = (feature // HEAD_DIM + 8 == lane).astype(half)

        @pl.loop(0, q_ref.shape[0] // size)
        def _(i):
            rows = pl.ds(pl.multiple_of(i * size, size), size)
            product = o_ref[rows, :] * do_ref[rows, :].astype(single)
            top = product.astype(half)
            low = (product - top.astype(single)).astype(half)
            both = mm(top, pick) + mm(low, pick) + lse_ref[rows, :]
            stat_ref[:, rows] = both.T[:16, :]

    dk_ref[...] = jnp.zeros(dk_ref.shape, single)
    dv_ref[...] = jnp.zeros(dv_ref.shape, single)

    def step(i, masked):
        rows = pl.ds(pl.multiple_of(i * size, size), size)
        if masked:
            key = j * size + lax.broadcasted_iota(jnp.int32, (size, size), 0)
            query = i * size + lax.broadcasted_iota(jnp.int32, (size, size), 1)
            allowed = (key <= query) & (key >= start_ref[:, rows])
        for pair in range(heads // 2):
            lanes = pl.ds(pair * LANES, LANES)
            k, v = k_ref[:, lanes], v_ref[:, lanes]
            q, do = q_ref[rows, lanes], do_ref[rows, lanes]
            ps, dss, qs, dos, ks = [], [], [], [], []
            for h in (2 * pair, 2 * pair + 1):
                mine = head_lanes(h, size)
                qm = jnp.where(mine, q, 0).astype(half)
                dom = jnp.where(mine, do, 0).astype(half)
                s = mm_nt(k, qm) * factor - stat_ref[pl.ds(h, 1), rows]
                if masked:
                    s = jnp.where(allowed, s, NEG)
                p = jnp.exp2(s)
                ds = p * (mm_nt(v, dom) - stat_ref[pl.ds(8 + h, 1), rows])
                ps.append(p.astype(half))
                dss.append(ds.astype(half))
                qs.append(qm)
                dos.append(dom)
                ks.append(jnp.where(mine, k, 0).astype(half))
            dv_ref[:, lanes] += jnp.dot(jnp.concatenate(ps, 1), jnp.concatenate(dos, 0), preferred_element_type=single)
            dk_ref[:, lanes] += jnp.dot(jnp.concatenate(dss, 1), jnp.concatenate(qs, 0), preferred_element_type=single)
            dq_ref[rows, lanes] += mm_tn(jnp.concatenate(dss, 0), jnp.concatenate(ks, 0))

    step(j, True)
    pl.loop(j + 1, clear)(lambda i: step(i, False))
    pl.loop(clear, high + 1)(lambda i: step(i, True))
    mine = pl.ds(pl.multiple_of(j * size, size), size)
    out_ref[mine, pl.ds(hh, hh)] = (dk_ref[...] * HEAD_DIM ** -0.5).astype(half)
    out_ref[mine, pl.ds(2 * hh, hh)] = dv_ref[...].astype(half)
    out_ref[mine, pl.ds(0, hh)] = (dq_ref[mine, :] * HEAD_DIM ** -0.5).astype(half)

def attention_backward(qkv, do, heads_out, lse, seg_bounds, starts, size):
    seq = qkv.shape[0]
    hh = qkv.shape[1] // 3
    heads = hh // HEAD_DIM
    return pl.pallas_call(
        functools.partial(bwd_kernel, heads),
        grid_spec=pltpu.PrefetchScalarGridSpec(
            num_scalar_prefetch=1,
            grid=(seq // size,),
            in_specs=[
                pl.BlockSpec((seq, hh), lambda j, b: (0, 0)),
                pl.BlockSpec((size, hh), lambda j, b: (j, 1)),
                pl.BlockSpec((size, hh), lambda j, b: (j, 2)),
                pl.BlockSpec((seq, hh), lambda j, b: (0, 0)),
                pl.BlockSpec((seq, hh), lambda j, b: (0, 0)),
                pl.BlockSpec((seq, LANES), lambda j, b: (0, 0)),
                pl.BlockSpec((1, seq), lambda j, b: (0, 0)),
            ],
            out_specs=pl.BlockSpec((seq, 3 * hh), lambda j, b: (0, 0)),
            scratch_shapes=[
                pltpu.VMEM((seq, hh), single),
                pltpu.VMEM((size, hh), single),
                pltpu.VMEM((size, hh), single),
                pltpu.VMEM((16, seq), single),
            ],
        ),
        out_shape=jax.ShapeDtypeStruct((seq, 3 * hh), half),
        compiler_params=pltpu.CompilerParams(vmem_limit_bytes=48 << 20),
        cost_estimate=pl.CostEstimate(flops=10 * seq * seq * LANES * heads, bytes_accessed=20 * seq * hh, transcendentals=0),
    )(seg_bounds, qkv, qkv, qkv, do, heads_out, lse, starts[None, :])


def start_kernel(
    members,
    low,
    per_core,
    padded,
    pack_ref,
    tok_ref,
    dy_ref,
    ids_ref,
    w_ref,
    full_ref,
    all_ref,
    got_ref,
    hot_ref,
    info_ref,
    down_ref,
    ids_all_ref,
    dy_all_ref,
    stage_ref,
    place_ref,
    send_sem,
    recv_sem,
    own_sem,
    swap_send,
    swap_recv,
    dy_send,
    dy_recv,
    down_send,
    down_recv,
):
    size = EXPERTS_FF
    me = lax.axis_index("dp")
    core = lax.axis_index("tensor")
    high = members // low
    inside, row = lax.rem(me, low), me // low
    mine = lax.rem(me, size)
    base = me - mine
    local = tok_ref.shape[0]
    seq = 2 * local
    partner = {"tensor": 1 - core}

    def beside(k):
        return row * low + lax.rem(inside + k, low)

    def across(k):
        return lax.rem(row + k, high) * low + inside

    peers = [beside(k) for k in range(1, low)] + [across(k) for k in range(1, high)]
    peers += [base + lax.rem(mine + k, size) for k in range(1, size)]
    groups = members // size

    def device_at(g, k):
        return lax.rem(base + g * size, members) + lax.rem(mine + k, size)

    distant = [(g, k) for g in range(1, groups) for k in range(size)]
    peers += [device_at(g, k) for g, k in distant]
    barrier = pltpu.get_barrier_semaphore()
    for peer in peers:
        pl.semaphore_signal(barrier, inc=1, device_id={"dp": peer}, device_id_type=MESH)
    pl.semaphore_signal(barrier, inc=1, device_id=partner, device_id_type=MESH)
    pl.semaphore_wait(barrier, len(peers) + 1)

    def remote(src, dst, send, recv, device):
        return pltpu.make_async_remote_copy(
            src_ref=src,
            dst_ref=dst,
            send_sem=send,
            recv_sem=recv,
            device_id=device,
            device_id_type=MESH,
        )

    def push(source, block, target, slot):
        copy = remote(
            source, full_ref.at[block], send_sem.at[slot], recv_sem.at[block], {"dp": target}
        )
        copy.start()
        return copy

    def arrived(block):
        remote(
            pack_ref, full_ref.at[block], send_sem.at[0], recv_sem.at[block], {"dp": peers[0]}
        ).wait_recv()

    sent = [push(pack_ref, me, across(k), k) for k in range(1, high)]
    sent += [push(pack_ref, me, beside(k), high + k) for k in range(1, low)]
    own_rows = pl.ds(pl.multiple_of(core * local, local), local)
    swaps = [
        remote(ids_ref, ids_all_ref.at[core], swap_send.at[0], swap_recv.at[0], partner),
        remote(dy_ref, dy_all_ref.at[own_rows], swap_send.at[1], swap_recv.at[1], partner),
        remote(tok_ref, all_ref.at[own_rows], swap_send.at[2], swap_recv.at[2], partner),
    ]
    owns = [
        pltpu.make_async_copy(ids_ref, ids_all_ref.at[core], own_sem.at[0]),
        pltpu.make_async_copy(dy_ref, dy_all_ref.at[own_rows], own_sem.at[1]),
        pltpu.make_async_copy(tok_ref, all_ref.at[own_rows], own_sem.at[2]),
        pltpu.make_async_copy(pack_ref, full_ref.at[me], own_sem.at[3]),
    ]
    for copy in swaps + owns:
        copy.start()

    swaps[0].wait()
    owns[0].wait()
    ids = jnp.concatenate([ids_all_ref[0], ids_all_ref[1]], 1)
    seg = ids[:1]
    number = lax.broadcasted_iota(jnp.int32, (8, seq), 0)
    starts = jnp.zeros((1, seq), jnp.int32)
    ends = jnp.zeros((1, seq), jnp.int32)
    total = jnp.zeros((1, 1), jnp.int32)
    for d in range(DOCS):
        here = seg == d
        starts = jnp.where(here, total, starts)
        total = total + jnp.sum(here.astype(jnp.int32), axis=1, keepdims=True)
        ends = jnp.where(here, total - 1, ends)
    row16 = lax.broadcasted_iota(jnp.int32, (16, LANES), 0)
    first = lax.broadcasted_iota(jnp.int32, (LANES, LANES), 0)
    second = lax.broadcasted_iota(jnp.int32, (LANES, LANES), 1)
    upper = (first < second).astype(half)
    before = jnp.zeros((16, 1), single)
    for c in range(seq // LANES):
        lanes = slice(c * LANES, (c + 1) * LANES)
        member = (ids[1:2, lanes] == row16) | (ids[2:3, lanes] == row16)
        member = jnp.where(member & (row16 < size), 1.0, 0.0)
        position = mm(member.astype(half), upper) + before
        before = before + jnp.sum(member, axis=1, keepdims=True)
        place = position - (core * per_core).astype(single)
        kept = (member > 0.5) & (position < CAPACITY) & (place >= 0) & (place < per_core)
        place_ref[:, lanes] = jnp.where(kept, place, -1.0).astype(jnp.int32)
    slot = lax.broadcasted_iota(jnp.int32, (padded, seq), 0)
    for e in range(size):
        hot_ref[e * padded : (e + 1) * padded, :] = jnp.where(
            place_ref[e : e + 1, :] == slot, 1.0, 0.0
        ).astype(half)

    info = jnp.where(number == 0, starts, jnp.where(number == 1, ends, -1))
    for k in range(2):
        chosen = jnp.full((1, seq), -1, jnp.int32)
        for e in range(size):
            place = place_ref[e : e + 1, :]
            chosen = jnp.where(
                (ids[k + 1 : k + 2] == e) & (place >= 0), place + e * padded, chosen
            )
        info = jnp.where(number == k + 2, chosen, info)
    info_ref[...] = info

    for k in range(1, high):
        block = across(high - k)
        arrived(block)
        for step in range(1, low):
            sent.append(push(full_ref.at[block], block, beside(step), high + k * low + step))

    for g, k in distant:
        copy = remote(
            w_ref.at[lax.rem(mine + k, size), 2],
            down_ref.at[me],
            down_send.at[(g - 1) * size + k],
            down_recv.at[me],
            {"dp": device_at(g, k)},
        )
        copy.start()
        sent.append(copy)

    swaps[1].wait()
    owns[1].wait()
    for pair in [(1, 2), (3, 4), (5, 6), (7, 0)]:
        slots = [
            pl.ds(pl.multiple_of(lax.rem(mine + k, size) * padded, 16), padded) for k in pair
        ]
        rows = mm(jnp.concatenate([hot_ref[s, :] for s in slots], 0), dy_all_ref[...])
        for place, k in enumerate(pair):
            to = lax.rem(mine + k, size)
            stage_ref[to] = rows[place * padded : (place + 1) * padded].astype(half)
            if k:
                copy = remote(
                    stage_ref.at[to], got_ref.at[mine], dy_send.at[k], dy_recv.at[k], {"dp": base + to}
                )
            else:
                copy = pltpu.make_async_copy(stage_ref.at[to], got_ref.at[mine], own_sem.at[4])
            copy.start()
            owns.append(copy)
    for k in range(1, low):
        block = beside(low - k)
        arrived(block)
        for step in range(1, high):
            arrived(lax.rem(block + step * low, members))
    for g, k in distant:
        block = device_at(groups - g, size - k)
        remote(
            w_ref.at[0, 2], down_ref.at[block], down_send.at[0], down_recv.at[block], partner
        ).wait_recv()
    for copy in sent:
        copy.wait_send()
    for copy in owns[2:]:
        copy.wait()
    swaps[2].wait()


def start(pack, tokens, dy, ids, w, members, per_core, padded):
    low = 4 if members % 4 == 0 else 1
    high = members // low
    local, width = tokens.shape
    count = EXPERTS_FF * padded
    any_spec = pl.BlockSpec(memory_space=pl.ANY)
    vmem = pl.BlockSpec(memory_space=pltpu.VMEM)
    dma = pltpu.SemaphoreType.DMA
    return pl.pallas_call(
        functools.partial(start_kernel, members, low, per_core, padded),
        out_shape=[
            jax.ShapeDtypeStruct((members,) + pack.shape, half),
            jax.ShapeDtypeStruct((2 * local, width), half),
            jax.ShapeDtypeStruct((EXPERTS_FF, padded, width), half),
            jax.ShapeDtypeStruct((count, 2 * local), half),
            jax.ShapeDtypeStruct((8, 2 * local), jnp.int32),
            jax.ShapeDtypeStruct((members,) + w.shape[2:], half),
        ],
        in_specs=[any_spec] * 5,
        out_specs=[any_spec] * 3 + [vmem] * 2 + [any_spec],
        scratch_shapes=[
            pltpu.VMEM((2, 8, local), jnp.int32),
            pltpu.VMEM((2 * local, width), half),
            pltpu.VMEM((EXPERTS_FF, padded, width), half),
            pltpu.VMEM((16, 2 * local), jnp.int32),
            dma((high * (low + 1),)),
            dma((members,)),
            dma((5,)),
            dma((3,)),
            dma((3,)),
            dma((EXPERTS_FF,)),
            dma((EXPERTS_FF,)),
            dma((members,)),
            dma((members,)),
        ],
        compiler_params=pltpu.CompilerParams(
            collective_id=0, has_side_effects=True, vmem_limit_bytes=40 << 20
        ),
        name="start",
    )(pack, tokens, dy, ids, w)


def experts_kernel(
    members,
    padded,
    w_ref,
    far_ref,
    in_ref,
    dy_hbm_ref,
    ho_ref,
    tok_ref,
    own_w_ref,
    other_w_ref,
    gain_ref,
    router_ref,
    prev_ref,
    routes_ref,
    hot_ref,
    back_ref,
    out_ref,
    x_ref,
    og_ref,
    hid_ref,
    pg_ref,
    pu_ref,
    resid_ref,
    normed_ref,
    misc_ref,
    ho_in_ref,
    both_ref,
    acc_ref,
    stage_ref,
    row_ref,
    win_ref,
    down_ref,
    dy_ref,
    ig_ref,
    spill_ref,
    gate_ref,
    dot_ref,
    x_send,
    x_recv,
    w_send,
    w_recv,
    pass_send,
    pass_recv,
    own_sem,
    far_sem,
    swap_send,
    swap_recv,
    ig_send,
    ig_recv,
    spill_sem,
):
    size = EXPERTS_FF
    groups = members // size
    me = lax.axis_index("dp")
    core = lax.axis_index("tensor")
    mine = lax.rem(me, size)
    base = me - mine
    local, width = tok_ref.shape
    partner = {"tensor": 1 - core}
    near = [base + lax.rem(mine + k, size) for k in range(1, size)]
    barrier = pltpu.get_barrier_semaphore()
    for peer in near:
        pl.semaphore_signal(barrier, inc=1, device_id={"dp": peer}, device_id_type=MESH)
    pl.semaphore_signal(barrier, inc=1, device_id=partner, device_id_type=MESH)
    pl.semaphore_wait(barrier, size)

    def remote(src, dst, send, recv, device):
        return pltpu.make_async_remote_copy(
            src_ref=src,
            dst_ref=dst,
            send_sem=send,
            recv_sem=recv,
            device_id=device,
            device_id_type=MESH,
        )

    own_rows = pl.ds(pl.multiple_of(core * local, local), local)
    other_rows = pl.ds(pl.multiple_of((1 - core) * local, local), local)
    heads = remote(ho_ref.at[other_rows], ho_in_ref, swap_send.at[0], swap_recv.at[0], partner)
    heads.start()
    waits = []
    for k in range(1, size):
        to = lax.rem(mine + k, size)
        copy = remote(
            w_ref.at[to, 2], down_ref.at[0, me], w_send.at[k], w_recv.at[k], {"dp": base + to}
        )
        copy.start()
        waits.append(copy)
    pair_in = remote(in_ref, win_ref.at[1], swap_send.at[2], swap_recv.at[2], partner)
    pair_in.start()
    local_in = pltpu.make_async_copy(in_ref, win_ref.at[0], own_sem.at[1])
    local_in.start()
    local_dy = pltpu.make_async_copy(dy_hbm_ref, dy_ref, own_sem.at[2])
    local_dy.start()
    own_w = pltpu.make_async_copy(w_ref.at[mine, 2], down_ref.at[0, me], own_sem.at[3])
    own_w.start()
    far = []
    for g in range(1, groups):
        blocks = pl.ds(lax.rem(base + g * size, members), size)
        copy = pltpu.make_async_copy(far_ref.at[blocks], down_ref.at[0, blocks], far_sem.at[g])
        copy.start()
        far.append(copy)

    step = fit(local, 256)
    heads.wait()

    @pl.loop(0, local // step)
    def _(r):
        rows = pl.ds(pl.multiple_of(r * step, step), step)
        mine_rows = pl.ds(pl.multiple_of(core * local + r * step, step), step)
        resid = tok_ref[rows, :].astype(single)
        resid += mm_nt(ho_ref[mine_rows, :], own_w_ref[...])
        resid += mm_nt(ho_in_ref[rows, :], other_w_ref[...])
        resid_ref[rows, :] = resid
        normed = (resid * rms_scale(resid) * gain_ref[1:2, :]).astype(half)
        normed_ref[rows, :] = normed
        router = mm(normed, router_ref[...])
        lane = lax.broadcasted_iota(jnp.int32, (step, LANES), 1)
        logits = jnp.where(lane < EXPERTS, router + prev_ref[rows, :], 0.0)
        hits = [lane == routes_ref[rows, k : k + 1] for k in range(2)]
        picked = [jnp.sum(jnp.where(hit, logits, 0.0), axis=1, keepdims=True) for hit in hits]
        peak = jnp.maximum(picked[0], picked[1])
        expo = [jnp.exp(p - peak) for p in picked]
        total = expo[0] + expo[1]
        gates = [e / total for e in expo]
        misc_ref[rows, :] = jnp.where(lane == 0, gates[0], jnp.where(lane == 1, gates[1], router))
        spread = sum(
            jnp.where(hit & (lane < size), gate.astype(half).astype(single), 0.0)
            for hit, gate in zip(hits, gates)
        )
        both_ref[mine_rows, pl.ds(0, width)] = normed
        both_ref[mine_rows, pl.ds(width, LANES)] = spread.astype(half)

    swap_rows = remote(
        both_ref.at[own_rows], both_ref.at[own_rows], swap_send.at[1], swap_recv.at[1], partner
    )
    swap_rows.start()

    pairs = [(1, 0), (2, 3), (4, 5), (6, 7)]
    for number, pair in enumerate(pairs):
        slots = [
            pl.ds(pl.multiple_of(lax.rem(mine + k, size) * padded, 16), padded) for k in pair
        ]
        hot = jnp.concatenate([hot_ref[s, own_rows] for s in slots], 0)
        acc_ref[number] = mm(hot, both_ref[own_rows, :])
    swap_rows.wait_recv()
    row_ref[...] = jnp.zeros(row_ref.shape, single)
    own_x = None
    for number, pair in enumerate(pairs):
        slots = [
            pl.ds(pl.multiple_of(lax.rem(mine + k, size) * padded, 16), padded) for k in pair
        ]
        hot = jnp.concatenate([hot_ref[s, other_rows] for s in slots], 0)
        acc_ref[number] += mm(hot, both_ref[other_rows, :])
        for place, k in enumerate(pair):
            to = lax.rem(mine + k, size)
            first = place * padded
            tail = acc_ref[number, first : first + padded, width:].astype(half)
            lane = lax.broadcasted_iota(jnp.int32, (16, LANES), 1)
            row_ref[:, :padded] = mm_nt((lane == to).astype(half), tail)
            stage_ref[to] = acc_ref[number, first : first + padded, :width].astype(half)
            last = acc_ref[number, first + padded - 16 : first + padded, : 2 * LANES]
            row = lax.broadcasted_iota(jnp.int32, (16, 2 * LANES), 0)
            last = jnp.where(row == 15, row_ref[...], last)
            stage_ref[to, padded - 16 :, : 2 * LANES] = last.astype(half)
            if k:
                copy = remote(
                    stage_ref.at[to], x_ref.at[mine], x_send.at[k], x_recv.at[k], {"dp": base + to}
                )
                waits.append(copy)
            else:
                copy = pltpu.make_async_copy(stage_ref.at[to], x_ref.at[mine], own_sem.at[0])
                own_x = copy
            copy.start()

    own_w.wait()
    for copy in far:
        copy.wait()
    passed = []
    for g in range(1, groups):
        blocks = pl.ds(lax.rem(base + g * size, members), size)
        passed.append(
            remote(
                down_ref.at[0, blocks],
                down_ref.at[1, blocks],
                pass_send.at[size + g],
                pass_recv.at[size + g],
                partner,
            )
        )
        passed[-1].start()
    for k in range(size):
        block = base + lax.rem(mine + size - k, size)
        if k:
            waits[k - 1].wait_recv()
        passed.append(
            remote(
                down_ref.at[0, block],
                down_ref.at[1, block],
                pass_send.at[k],
                pass_recv.at[k],
                partner,
            )
        )
        passed[-1].start()
    local_in.wait()
    local_dy.wait()
    pair_in.wait_recv()
    for copy in passed:
        copy.wait_recv()

    ff = in_ref.shape[3]
    block = fit(ff, 256)
    steps = ff // block
    rows2 = 2 * padded
    dot_ref[...] = jnp.zeros(dot_ref.shape, single)

    def spill(slot, array, place, source, part, f):
        out = (hid_ref, pg_ref, pu_ref)[array]
        rows = pl.ds(pl.multiple_of(source * padded, 16), padded)
        return pltpu.make_async_copy(
            spill_ref.at[slot, array, pl.ds(place * padded, padded)],
            out.at[part, rows, pl.ds(f * block, block)],
            spill_sem.at[slot, array, place],
        )

    def give_back(k, source):
        return remote(
            ig_ref.at[source], back_ref.at[mine], ig_send.at[k], ig_recv.at[k], {"dp": base + source}
        )

    @pl.loop(0, size // 2)
    def _(q):
        ks = [2 * q, 2 * q + 1]
        sources = [lax.rem(mine + size - k, size) for k in ks]

        @pl.when(q == 0)
        def _():
            pltpu.make_async_copy(stage_ref.at[0], x_ref.at[0], own_sem.at[0]).wait()

        @pl.when(q > 0)
        def _():
            remote(
                stage_ref.at[0], x_ref.at[0], x_send.at[0], x_recv.at[2 * q], partner
            ).wait_recv()

        remote(
            stage_ref.at[0], x_ref.at[0], x_send.at[0], x_recv.at[2 * q + 1], partner
        ).wait_recv()
        for place, source in enumerate(sources):
            rows = pl.ds(place * padded, padded)
            gates = x_ref[source, padded - 16 :, : 2 * LANES].astype(single).T
            gate = jnp.broadcast_to(gates[:padded, 15:16], (padded, LANES))
            gate_ref[rows, :] = gate
            og_ref[source] = (dy_ref[source].astype(single) * gate[:, :1]).astype(half)
        for number in range(2):
            acc_ref[number, :, :width] = jnp.zeros((rows2, width), single)

        @pl.loop(0, 2)
        def _(part):
            for f in range(steps):
                lanes = pl.ds(f * block, block)
                slot = f % 2
                if f >= 2:
                    for array in range(3):
                        for place, source in enumerate(sources):
                            spill(slot, array, place, source, part, f - 2).wait()
                gate_w = win_ref[part, :, 0, :, lanes].reshape(width, block)
                up_w = win_ref[part, :, 1, :, lanes].reshape(width, block)
                down_w = down_ref[part, :, :, lanes].reshape(width, block)
                x = jnp.concatenate([x_ref[source] for source in sources], 0)
                og = jnp.concatenate([og_ref[source] for source in sources], 0)
                pre = mm(x, gate_w)
                up = mm(x, up_w)
                hg = mm(og, down_w)
                sigma = jax.nn.sigmoid(pre)
                active = pre * sigma
                hidden = (active * up).astype(half)
                pg = (hg * up * (sigma * (1.0 + pre * (1.0 - sigma)))).astype(half)
                pu = (hg * active).astype(half)
                spill_ref[slot, 0] = hidden
                spill_ref[slot, 1] = pg
                spill_ref[slot, 2] = pu
                acc_ref[0, :, :width] += mm_nt(hidden, down_w)
                acc_ref[1, :, :width] += mm_nt(pg, gate_w) + mm_nt(pu, up_w)
                for array in range(3):
                    for place, source in enumerate(sources):
                        spill(slot, array, place, source, part, f).start()
            for f in range(max(0, steps - 2), steps):
                for array in range(3):
                    for place, source in enumerate(sources):
                        spill(f % 2, array, place, source, part, f).wait()

        ones = jnp.ones((16, width), half)
        for place, source in enumerate(sources):
            rows = pl.ds(place * padded, padded)
            eo = acc_ref[0, rows, :width]
            out_ref[source] = (eo * gate_ref[rows, :1]).astype(half)
            ig_ref[source] = acc_ref[1, rows, :width].astype(half)
            product = eo * dy_ref[source].astype(single)
            top = product.astype(half)
            low = (product - top.astype(single)).astype(half)
            dot_ref[:, :padded] = mm_nt(ones, top) + mm_nt(ones, low)
            dots = dot_ref[...]
            high = dots.astype(half).astype(single)
            row = lax.broadcasted_iota(jnp.int32, dots.shape, 0)
            last = acc_ref[1, pl.ds((place + 1) * padded - 16, 16), : 2 * LANES]
            last = jnp.where(row == 14, high, jnp.where(row == 15, dots - high, last))
            ig_ref[source, padded - 16 :, : 2 * LANES] = last.astype(half)

        @pl.when(q == 0)
        def _():
            pltpu.make_async_copy(ig_ref.at[mine], back_ref.at[mine], own_sem.at[0]).start()

        @pl.when(q > 0)
        def _():
            give_back(2 * q, sources[0]).start()

        give_back(2 * q + 1, sources[1]).start()

    pltpu.make_async_copy(ig_ref.at[mine], back_ref.at[mine], own_sem.at[0]).wait()
    for k in range(1, size):
        give_back(k, lax.rem(mine + size - k, size)).wait()
    heads_done = [swap_rows, pair_in]
    for copy in waits + passed + heads_done:
        copy.wait_send()


def experts(
    w, far, inward, dy, heads, tokens, own_w, other_w, gains, router, prev, routes, hot, padded
):
    members, _, d_rows, ff = inward.shape
    local, width = tokens.shape
    seq = heads.shape[0]
    size = EXPERTS_FF
    block = fit(ff, 256)
    any_spec = pl.BlockSpec(memory_space=pl.ANY)
    vmem = pl.BlockSpec(memory_space=pltpu.VMEM)
    dma = pltpu.SemaphoreType.DMA
    rows = jax.ShapeDtypeStruct((size, padded, width), half)
    wide = jax.ShapeDtypeStruct((2, size * padded, ff), half)
    return pl.pallas_call(
        functools.partial(experts_kernel, members, padded),
        out_shape=[
            rows,
            rows,
            rows,
            rows,
            wide,
            wide,
            wide,
            jax.ShapeDtypeStruct((local, width), single),
            jax.ShapeDtypeStruct((local, width), half),
            jax.ShapeDtypeStruct((local, LANES), single),
        ],
        in_specs=[any_spec] * 4 + [vmem] * 9,
        out_specs=[any_spec] + [vmem] * 3 + [any_spec] * 3 + [vmem] * 3,
        scratch_shapes=[
            pltpu.VMEM((local, heads.shape[1]), half),
            pltpu.VMEM((seq, width + LANES), half),
            pltpu.VMEM((size // 2, 2 * padded, width + LANES), single),
            pltpu.VMEM((size, padded, width), half),
            pltpu.VMEM((16, 2 * LANES), single),
            pltpu.VMEM((2,) + inward.shape, half),
            pltpu.VMEM((2, members, d_rows, ff), half),
            pltpu.VMEM((size, padded, width), half),
            pltpu.VMEM((size, padded, width), half),
            pltpu.VMEM((2, 3, 2 * padded, block), half),
            pltpu.VMEM((2 * padded, LANES), single),
            pltpu.VMEM((16, 2 * LANES), single),
            dma((size,)),
            dma((size,)),
            dma((size,)),
            dma((size,)),
            dma((size + members // size,)),
            dma((size + members // size,)),
            dma((4,)),
            dma((members // size,)),
            dma((3,)),
            dma((3,)),
            dma((size,)),
            dma((size,)),
            dma((2, 3, 2)),
        ],
        compiler_params=pltpu.CompilerParams(
            collective_id=1, has_side_effects=True, vmem_limit_bytes=62 << 20
        ),
        name="experts",
    )(w, far, inward, dy, heads, tokens, own_w, other_w, gains, router, prev, routes, hot)


def split(x):
    high = x.astype(half)
    return high, (x - high.astype(single)).astype(half)


def slot_rows(columns, count):
    slot = lax.broadcasted_iota(jnp.int32, (columns.shape[0], count), 1)
    hit = (columns[:, 2:3] == slot) | (columns[:, 3:4] == slot)
    return jnp.where(hit, 1.0, 0.0).astype(half)


def lane_sum(x):
    return jnp.sum(x, axis=1, keepdims=True)


def back_kernel(
    padded,
    back_ref,
    info_ref,
    resid_ref,
    normed_ref,
    misc_ref,
    dy_ref,
    routes_ref,
    gain_ref,
    const_ref,
    router_ref,
    own_w_ref,
    other_w_ref,
    prev_ref,
    mix_ref,
    rgrad_ref,
    attn_ref,
    heads_ref,
    base_ref,
    pgrad_ref,
    small_ref,
    mgrad_ref,
    ext_ref,
    out_ref,
    in_ref,
    hg_ref,
    send_sem,
    recv_sem,
):
    core = lax.axis_index("tensor")
    partner = {"tensor": 1 - core}
    sources, _, width = back_ref.shape
    count = sources * padded
    local = dy_ref.shape[0]
    step = fit(local, 256)
    barrier = pltpu.get_barrier_semaphore()
    pl.semaphore_signal(barrier, inc=1, device_id=partner, device_id_type=MESH)
    pl.semaphore_wait(barrier, 1)

    def remote(src, dst, number):
        return pltpu.make_async_remote_copy(
            src_ref=src,
            dst_ref=dst,
            send_sem=send_sem.at[number],
            recv_sem=recv_sem.at[number],
            device_id=partner,
            device_id_type=MESH,
        )

    own_rows = pl.ds(pl.multiple_of(core * local, local), local)
    lane = lax.broadcasted_iota(jnp.int32, (step, LANES), 1)
    for s in range(sources):
        dots = back_ref[s, padded - 16 :, : 2 * LANES].astype(single).T
        number = lax.broadcasted_iota(jnp.int32, (padded, LANES), 1)
        ext = jnp.where(
            number == s,
            dots[:padded, 14:15],
            jnp.where(number == s + EXPERTS_FF, dots[:padded, 15:16], 0.0),
        )
        ext_ref[pl.ds(s * padded, padded), :] = ext.astype(half)
    back_all = back_ref.reshape(count, width)

    @pl.loop(0, local // step)
    def _(r):
        rows = pl.ds(pl.multiple_of(r * step, step), step)
        there = pl.ds(pl.multiple_of((1 - core) * local + r * step, step), step)
        hot = slot_rows(info_ref[there, :], count)
        out_ref[rows, pl.ds(0, width)] = mm(hot, back_all[...]).astype(half)
        out_ref[rows, pl.ds(width, LANES)] = mm(hot, ext_ref[...]).astype(half)

    sums = remote(out_ref, in_ref, 0)
    sums.start()
    small_ref[...] = jnp.zeros(small_ref.shape, single)
    mgrad_ref[...] = jnp.zeros(mgrad_ref.shape, single)

    @pl.loop(0, local // step)
    def _(r):
        rows = pl.ds(pl.multiple_of(r * step, step), step)
        here = pl.ds(pl.multiple_of(core * local + r * step, step), step)
        hot = slot_rows(info_ref[here, :], count)
        rgrad_ref[rows, :] = mm(hot, back_all[...])
        pgrad_ref[rows, :] = mm(hot, ext_ref[...])

    sums.wait()

    @pl.loop(0, local // step)
    def _(r):
        rows = pl.ds(pl.multiple_of(r * step, step), step)
        here = pl.ds(pl.multiple_of(core * local + r * step, step), step)
        dy = dy_ref[rows, :].astype(single)
        normed = normed_ref[rows, :].astype(single)
        resid = resid_ref[rows, :]
        misc = misc_ref[rows, :]
        expert_dot = pgrad_ref[rows, :] + in_ref[rows, pl.ds(width, LANES)].astype(single)
        own_dot = lane_sum(dy * normed)
        vec_dot = [lane_sum(dy * const_ref[j : j + 1, :]) for j in range(2)]
        gates = [misc[:, k : k + 1] for k in range(2)]
        routes = [routes_ref[rows, k : k + 1] for k in range(2)]
        alphas = []
        for j in range(2):
            columns = [misc[:, EXPERTS + 2 * j + m : EXPERTS + 2 * j + m + 1] for m in range(2)]
            peak = jnp.maximum(columns[0], columns[1])
            expo = [jnp.exp(c - peak) for c in columns]
            total = expo[0] + expo[1]
            alphas.append([e / total for e in expo])
        gate_grads = []
        for k in range(2):
            hit = (lane == routes[k]) | (lane == routes[k] + EXPERTS_FF)
            dot = lane_sum(jnp.where(hit & (routes[k] < EXPERTS_FF), expert_dot, 0.0))
            dot += jnp.where(routes[k] == EXPERTS_FF + 1, own_dot, 0.0)
            for j in range(2):
                value = alphas[j][0] * own_dot + alphas[j][1] * vec_dot[j]
                dot += jnp.where(routes[k] == EXPERTS_FF + 2 + j, value, 0.0)
            gate_grads.append(dot)
        centre = gates[0] * gate_grads[0] + gates[1] * gate_grads[1]
        chosen = [gates[k] * (gate_grads[k] - centre) for k in range(2)]
        router_grad = jnp.zeros((step, LANES), single)
        own_weight = jnp.zeros((step, 1), single)
        for k in range(2):
            router_grad = jnp.where(lane == routes[k], chosen[k], router_grad)
            own_weight += jnp.where(routes[k] == EXPERTS_FF + 1, gates[k], 0.0)
        logit_grad = router_grad
        vec_lanes = jnp.zeros((step, LANES), single)
        other = jnp.zeros((step, width), single)
        for j in range(2):
            weight = sum(jnp.where(routes[k] == EXPERTS_FF + 2 + j, gates[k], 0.0) for k in range(2))
            grads = [weight * own_dot, weight * vec_dot[j]]
            mean = alphas[j][0] * grads[0] + alphas[j][1] * grads[1]
            for m in range(2):
                router_grad = jnp.where(
                    lane == EXPERTS + 2 * j + m, alphas[j][m] * (grads[m] - mean), router_grad
                )
            own_weight += weight * alphas[j][0]
            vec_weight = weight * alphas[j][1]
            vec_lanes = jnp.where(lane == 16 + j, vec_weight, vec_lanes)
            other += vec_weight * const_ref[j : j + 1, :]
        base_ref[rows, :] = resid + own_weight * normed + other
        rg_high, rg_low = split(router_grad)
        two_grad = rgrad_ref[rows, :] + in_ref[rows, pl.ds(0, width)].astype(single)
        two_grad += own_weight * dy
        two_grad += mm_nt(rg_high, router_ref[...]) + mm_nt(rg_low, router_ref[...])
        normed_low = normed_ref[rows, :]
        vec_high, vec_low = split(vec_lanes)
        small_ref[...] += (
            mm_tn(rg_high, normed_low)
            + mm_tn(rg_low, normed_low)
            + mm_tn(vec_high, dy_ref[rows, :])
            + mm_tn(vec_low, dy_ref[rows, :])
        )[:24]
        scale = rms_scale(resid)
        gain_part = jnp.sum(two_grad * resid * scale, axis=0, keepdims=True)
        small_ref[19:20, :] += gain_part
        weighted = two_grad * gain_ref[1:2, :]
        mean = jnp.mean(weighted * resid, axis=-1, keepdims=True)
        grad = dy + scale * (weighted - resid * scale * scale * mean)
        rgrad_ref[rows, :] = grad
        low = grad.astype(half)
        attn_ref[here, :] = low
        heads_ref[here, :] = mm(low, own_w_ref[...]).astype(half)
        hg_ref[rows, :] = mm(low, other_w_ref[...]).astype(half)
        lg_high, lg_low = split(logit_grad)
        mix_high, mix_low = split(mix_ref[...])
        pgrad_ref[rows, :] = (
            mm_nt(lg_high, mix_high) + mm_nt(lg_high, mix_low) + mm_nt(lg_low, mix_high)
        )
        prev_high, prev_low = split(prev_ref[rows, :])
        mgrad_ref[...] += (
            mm_tn(prev_high, lg_high) + mm_tn(prev_high, lg_low) + mm_tn(prev_low, lg_high)
        )

    for i in range(EXPERTS):
        place = pl.ds(i % 6 * LANES, LANES)
        small_ref[20 + i // 6 : 21 + i // 6, place] = mgrad_ref[i : i + 1, :]

    heads = remote(hg_ref, heads_ref.at[own_rows], 1)
    heads.start()
    attn = remote(attn_ref.at[own_rows], attn_ref.at[own_rows], 2)
    attn.start()
    heads.wait()
    attn.wait()


def backward_middle(
    back, info, resid, normed, misc, dy, routes, gains, const, router, own_w, other_w, prev, mix, padded
):
    local, width = dy.shape
    seq = info.shape[0]
    hh = own_w.shape[1]
    count = EXPERTS_FF * padded
    vmem = pl.BlockSpec(memory_space=pltpu.VMEM)
    return pl.pallas_call(
        functools.partial(back_kernel, padded),
        out_shape=[
            jax.ShapeDtypeStruct((local, width), single),
            jax.ShapeDtypeStruct((seq, width), half),
            jax.ShapeDtypeStruct((seq, hh), half),
            jax.ShapeDtypeStruct((local, width), single),
            jax.ShapeDtypeStruct((local, LANES), single),
            jax.ShapeDtypeStruct((24, width), single),
            jax.ShapeDtypeStruct((LANES, LANES), single),
        ],
        in_specs=[vmem] * 14,
        out_specs=[vmem] * 7,
        scratch_shapes=[
            pltpu.VMEM((count, LANES), half),
            pltpu.VMEM((local, width + LANES), half),
            pltpu.VMEM((local, width + LANES), half),
            pltpu.VMEM((local, hh), half),
            pltpu.SemaphoreType.DMA((3,)),
            pltpu.SemaphoreType.DMA((3,)),
        ],
        compiler_params=pltpu.CompilerParams(
            collective_id=2, has_side_effects=True, vmem_limit_bytes=56 << 20
        ),
        name="backward_middle",
    )(back, info, resid, normed, misc, dy, routes, gains, const, router, own_w, other_w, prev, mix)


def weight_kernel(
    x_ref,
    og_ref,
    hid_ref,
    pg_ref,
    pu_ref,
    out_ref,
    xt_ref,
    ogt_ref,
    send_ref,
    got_ref,
    own_ref,
    send_sem,
    recv_sem,
):
    f = pl.program_id(0)
    partner = {"tensor": 1 - lax.axis_index("tensor")}
    shape = out_ref.shape[0], out_ref.shape[2], out_ref.shape[3]

    @pl.when(f == 0)
    def _():
        barrier = pltpu.get_barrier_semaphore()
        pl.semaphore_signal(barrier, inc=1, device_id=partner, device_id_type=MESH)
        pl.semaphore_wait(barrier, 1)
        xt_ref[...] = x_ref[...].T
        ogt_ref[...] = og_ref[...].T

    def remote(number):
        return pltpu.make_async_remote_copy(
            src_ref=send_ref.at[number],
            dst_ref=got_ref.at[number],
            send_sem=send_sem.at[number],
            recv_sem=recv_sem.at[number],
            device_id=partner,
            device_id_type=MESH,
        )

    factors = (xt_ref, pg_ref), (xt_ref, pu_ref), (ogt_ref, hid_ref)
    for k, (left, right) in enumerate(factors):
        send_ref[f, k] = mm(left[...], right[1]).astype(half)
    remote(f).start()
    for k, (left, right) in enumerate(factors):
        own_ref[k] = mm(left[...], right[0])
    remote(f).wait_recv()
    for k in range(3):
        total = own_ref[k] + got_ref[f, k].astype(single)
        out_ref[:, k] = total.astype(half).reshape(shape)

    @pl.when(f == pl.num_programs(0) - 1)
    def _():
        for number in range(send_ref.shape[0]):
            remote(number).wait_send()


def weight_step(x, og, hidden, pg, pu, m):
    count, width = og.shape
    ff = hidden.shape[2]
    block = fit(ff, 256)
    steps = ff // block
    whole = pl.BlockSpec((count, width), lambda f: (0, 0))
    wide = pl.BlockSpec((2, count, block), lambda f: (0, 0, f))
    part = pl.BlockSpec((m, 3, width // m, block), lambda f: (0, 0, 0, f))
    return pl.pallas_call(
        weight_kernel,
        grid=(steps,),
        in_specs=[whole, whole, wide, wide, wide],
        out_specs=part,
        out_shape=jax.ShapeDtypeStruct((m, 3, width // m, ff), half),
        scratch_shapes=[
            pltpu.VMEM((width, count), half),
            pltpu.VMEM((width, count), half),
            pltpu.VMEM((steps, 3, width, block), half),
            pltpu.VMEM((steps, 3, width, block), half),
            pltpu.VMEM((3, width, block), single),
            pltpu.SemaphoreType.DMA((steps,)),
            pltpu.SemaphoreType.DMA((steps,)),
        ],
        compiler_params=pltpu.CompilerParams(
            collective_id=3, has_side_effects=True, vmem_limit_bytes=56 << 20
        ),
        cost_estimate=pl.CostEstimate(
            flops=12 * count * width * ff,
            bytes_accessed=12 * width * ff + 12 * count * ff,
            transcendentals=0,
        ),
        name="weight_step",
    )(x, og, hidden, pg, pu)


def tail_kernel(
    members,
    low,
    padded,
    eo_ref,
    qkv_ref,
    one_ref,
    proj_ref,
    outg_ref,
    x_ref,
    base_ref,
    resid_ref,
    info_ref,
    gain_ref,
    small_ref,
    dense_out_ref,
    tokens_ref,
    mixed_ref,
    small_out_ref,
    dense_ref,
    first_ref,
    stage_ref,
    second_ref,
    one_out_ref,
    one_in_ref,
    ffn_out_ref,
    ffn_in_ref,
    ffn_ref,
    mine_ref,
    pair_ref,
    near_ref,
    far_ref,
    send1,
    recv1,
    send2,
    recv2,
    pair_send,
    pair_recv,
    near_send,
    near_recv,
    far_send,
    far_recv,
):
    size = EXPERTS_FF
    me = lax.axis_index("dp")
    core = lax.axis_index("tensor")
    high = members // low
    inside, row = lax.rem(me, low), me // low
    local, width = base_ref.shape
    count = size * padded
    d_rows = dense_out_ref.shape[0]
    hh3 = qkv_ref.shape[1]
    step = fit(local, 256)
    partner = {"tensor": 1 - core}

    def beside(k):
        return row * low + lax.rem(inside + k, low)

    def across(k):
        return lax.rem(row + k, high) * low + inside

    peers = [beside(k) for k in range(1, low)] + [across(k) for k in range(1, high)]
    barrier = pltpu.get_barrier_semaphore()
    for peer in peers:
        pl.semaphore_signal(barrier, inc=1, device_id={"dp": peer}, device_id_type=MESH)
    pl.semaphore_signal(barrier, inc=1, device_id=partner, device_id_type=MESH)
    pl.semaphore_wait(barrier, len(peers) + 1)

    def remote(src, dst, send, recv, device):
        return pltpu.make_async_remote_copy(
            src_ref=src,
            dst_ref=dst,
            send_sem=send,
            recv_sem=recv,
            device_id=device,
            device_id_type=MESH,
        )

    sent = []
    chunks = 2
    rows_each = width // chunks
    for c in range(chunks):
        lanes = pl.ds(c * rows_each, rows_each)
        grad = mm_tn(one_ref[:, lanes], qkv_ref[...])
        for j in range(members // chunks):
            owner = c * (members // chunks) + j
            dense_ref[owner, :, :hh3] = grad[j * d_rows : (j + 1) * d_rows].astype(half)
            dense_ref[owner, :, hh3:] = outg_ref[owner * d_rows : (owner + 1) * d_rows, :]
        for h in range(c * high // chunks, (c + 1) * high // chunks):
            for k in range(1, low):
                copy = remote(
                    dense_ref.at[h * low + lax.rem(inside + k, low)],
                    first_ref.at[k - 1, h],
                    send1.at[k - 1, h],
                    recv1.at[k - 1, h],
                    {"dp": beside(k)},
                )
                copy.start()
                sent.append(copy)

    def one_part(rows):
        part = mm_nt(qkv_ref[rows, :], proj_ref[...])
        x = x_ref[rows, :].astype(single)
        mine_ref[18:19, :] += jnp.sum(part * x * rms_scale(x), axis=0, keepdims=True)
        return part

    mine_ref[...] = small_ref[...]

    @pl.loop(0, local // step)
    def _(r):
        rows = pl.ds(pl.multiple_of(r * step, step), step)
        there = pl.ds(pl.multiple_of((1 - core) * local + r * step, step), step)
        one_out_ref[rows, :] = one_part(there).astype(half)

    one_sent = remote(one_out_ref, one_in_ref, pair_send.at[0], pair_recv.at[0], partner)
    one_sent.start()

    @pl.loop(0, local // step)
    def _(r):
        rows = pl.ds(pl.multiple_of(r * step, step), step)
        here = pl.ds(pl.multiple_of(core * local + r * step, step), step)
        tokens_ref[rows, :] = one_part(here)

    eo_all = eo_ref.reshape(count, width)

    @pl.loop(0, local // step)
    def _(r):
        rows = pl.ds(pl.multiple_of(r * step, step), step)
        there = pl.ds(pl.multiple_of((1 - core) * local + r * step, step), step)
        ffn_out_ref[rows, :] = mm(slot_rows(info_ref[there, :], count), eo_all[...]).astype(half)

    ffn_sent = remote(ffn_out_ref, ffn_in_ref, pair_send.at[2], pair_recv.at[2], partner)
    ffn_sent.start()

    @pl.loop(0, local // step)
    def _(r):
        rows = pl.ds(pl.multiple_of(r * step, step), step)
        here = pl.ds(pl.multiple_of(core * local + r * step, step), step)
        ffn_ref[rows, :] = mm(slot_rows(info_ref[here, :], count), eo_all[...])

    pair = remote(mine_ref, pair_ref, pair_send.at[1], pair_recv.at[1], partner)
    pair.start()
    pair.wait()
    near_ref[inside] = mine_ref[...] + pair_ref[...]
    near = []
    for k in range(1, low):
        near.append(
            remote(
                near_ref.at[inside],
                near_ref.at[inside],
                near_send.at[k],
                near_recv.at[inside],
                {"dp": beside(k)},
            )
        )
        near[-1].start()

    for j in range(1, high + 1):
        h = lax.rem(row + j, high)
        for k in range(low - 1):
            remote(
                dense_ref.at[0], first_ref.at[k, h], send1.at[k, h], recv1.at[k, h], partner
            ).wait_recv()
        total = dense_ref[h * low + inside].astype(single)
        for k in range(low - 1):
            total += first_ref[k, h].astype(single)
        if j < high:
            stage_ref[j - 1] = total.astype(half)
            copy = remote(
                stage_ref.at[j - 1],
                second_ref.at[j - 1],
                send2.at[j - 1],
                recv2.at[j - 1],
                {"dp": across(j)},
            )
            copy.start()
            sent.append(copy)
        else:
            dense_out_ref[...] = total
    for k in range(1, low):
        block = lax.rem(inside + k, low)
        remote(
            mine_ref, near_ref.at[block], near_send.at[0], near_recv.at[block], partner
        ).wait_recv()
    total = near_ref[0]
    for k in range(1, low):
        total = total + near_ref[k]
    far_ref[row] = total
    far = []
    for k in range(1, high):
        far.append(
            remote(
                far_ref.at[row], far_ref.at[row], far_send.at[k], far_recv.at[row], {"dp": across(k)}
            )
        )
        far[-1].start()

    one_sent.wait()

    @pl.loop(0, local // step)
    def _(r):
        rows = pl.ds(pl.multiple_of(r * step, step), step)
        here = pl.ds(pl.multiple_of(core * local + r * step, step), step)
        x = x_ref[here, :].astype(single)
        scale = rms_scale(x)
        weighted = (tokens_ref[rows, :] + one_in_ref[rows, :].astype(single)) * gain_ref[0:1, :]
        mean = jnp.mean(weighted * x, axis=-1, keepdims=True)
        tokens_ref[rows, :] = resid_ref[rows, :] + scale * (weighted - x * scale * scale * mean)

    ffn_sent.wait()

    @pl.loop(0, local // step)
    def _(r):
        rows = pl.ds(pl.multiple_of(r * step, step), step)
        total = base_ref[rows, :] + ffn_ref[rows, :] + ffn_in_ref[rows, :].astype(single)
        mixed_ref[rows, :] = total.astype(half)

    for j in range(1, high):
        remote(
            stage_ref.at[0], second_ref.at[j - 1], send2.at[j - 1], recv2.at[j - 1], partner
        ).wait_recv()
        dense_out_ref[...] += second_ref[j - 1].astype(single)
    for k in range(1, high):
        block = lax.rem(row + k, high)
        remote(
            mine_ref, far_ref.at[block], far_send.at[0], far_recv.at[block], partner
        ).wait_recv()
    total = far_ref[0]
    for k in range(1, high):
        total = total + far_ref[k]
    small_out_ref[...] = total
    for copy in sent + near + far:
        copy.wait_send()


def tail(members, eo, qkv, one, proj, outg, x, base, resid, info, gains, small, padded):
    low = 4
    high = members // low
    local, width = base.shape
    d_rows = width // members
    wide = qkv.shape[1] + outg.shape[1]
    vmem = pl.BlockSpec(memory_space=pltpu.VMEM)
    dma = pltpu.SemaphoreType.DMA
    rows_half = pltpu.VMEM((local, width), half)
    small_one = pltpu.VMEM(small.shape, single)
    return pl.pallas_call(
        functools.partial(tail_kernel, members, low, padded),
        out_shape=[
            jax.ShapeDtypeStruct((d_rows, wide), single),
            jax.ShapeDtypeStruct((local, width), single),
            jax.ShapeDtypeStruct((local, width), half),
            jax.ShapeDtypeStruct(small.shape, single),
        ],
        in_specs=[vmem] * 11,
        out_specs=[vmem] * 4,
        scratch_shapes=[
            pltpu.VMEM((members, d_rows, wide), half),
            pltpu.VMEM((low - 1, high, d_rows, wide), half),
            pltpu.VMEM((high - 1, d_rows, wide), half),
            pltpu.VMEM((high - 1, d_rows, wide), half),
            rows_half,
            rows_half,
            rows_half,
            rows_half,
            pltpu.VMEM((local, width), single),
            small_one,
            small_one,
            pltpu.VMEM((low,) + small.shape, single),
            pltpu.VMEM((high,) + small.shape, single),
            dma((low - 1, high)),
            dma((low - 1, high)),
            dma((high - 1,)),
            dma((high - 1,)),
            dma((3,)),
            dma((3,)),
            dma((low,)),
            dma((low,)),
            dma((high,)),
            dma((high,)),
        ],
        compiler_params=pltpu.CompilerParams(
            collective_id=4, has_side_effects=True, vmem_limit_bytes=60 << 20
        ),
        name="tail",
    )(eo, qkv, one, proj, outg, x, base, resid, info, gains, small)


def per_device(
    tokens,
    segment_ids,
    routes,
    prev_logits,
    cotangent,
    proj_weight,
    out_weight,
    norm_gain,
    expert_weight,
    router,
    constant_vectors,
    gate_mixing,
):
    members = lax.axis_size("dp")
    groups = members // EXPERTS_FF
    cubes = [[g * EXPERTS_FF + i for i in range(EXPERTS_FF)] for g in range(groups)]
    core = lax.axis_index("tensor")
    d_rows, hh = out_weight.shape
    per_core = -(-CAPACITY // 2)
    padded = -(-(per_core + 3) // 16) * 16

    def in_group(blocks):
        return lax.all_to_all(blocks, "dp", 0, 0, axis_index_groups=cubes, tiled=True)

    def plain_tail(eo, qkv, one, proj, outg, x, base, resid, gains, small):
        ffn = pair_sum(mm_tn(onehot, eo.reshape(-1, width)))
        part = mm_nt(qkv, proj)
        scale = rms_scale(x)
        small = small.at[18].set(jnp.sum(part * x * scale, axis=0))
        weighted = pair_sum(part) * gains[0]
        x, scale = half_of(x, core), half_of(scale, core)
        mean = jnp.mean(weighted * x, axis=-1, keepdims=True)
        tokens_grad = resid + scale * (weighted - x * scale * scale * mean)
        dense = jnp.concatenate([mm_tn(one, qkv).astype(half), outg], 1)
        dense = lax.all_to_all(dense.reshape(members, d_rows, -1), "dp", 0, 0, tiled=True)
        dense = jnp.sum(dense.astype(single), axis=0)
        return dense, tokens_grad, (base + ffn).astype(half), lax.psum(small, ("dp", "tensor"))

    pack = jnp.concatenate(
        [
            proj_weight.transpose(1, 0, 2).reshape(d_rows, 3 * hh),
            out_weight,
            norm_gain.T,
            constant_vectors.T,
            router,
        ],
        1,
    )
    columns = pack.shape[1]
    pack = jnp.pad(pack, ((0, 0), (0, -columns % LANES)))
    ids = jnp.concatenate([segment_ids, routes[0].T], 0)
    ids = jnp.pad(ids, ((0, 5), (0, 0)))
    full_pack, tokens_all, got_dy, onehot, info, far_down = start(
        pack, tokens[0], cotangent[0], ids, expert_weight, members, per_core, padded
    )
    full_pack, expert_weight = lax.optimization_barrier((full_pack, expert_weight))
    full_pack = full_pack.reshape(members * d_rows, -1)[:, :columns]
    width = members * d_rows
    proj_full = full_pack[:, : 3 * hh]
    outw_own = full_pack[:, 3 * hh : 4 * hh]
    outw_other = swap(outw_own)
    rest = full_pack[:, 4 * hh :]
    gains = rest[:, :2].T.astype(single)
    const_f = rest[:, 2:4].T.astype(single)
    router_full = rest[:, 4:]
    in_weight = jnp.broadcast_to(
        expert_weight[None, :, :2], (groups, EXPERTS_FF, 2) + expert_weight.shape[2:]
    ).reshape((members, 2) + expert_weight.shape[2:])
    my_in = lax.all_to_all(in_weight, "dp", 0, 0, tiled=True)

    x_rows = tokens[0].astype(single)
    local_rows = x_rows.shape[0]
    x_all = tokens_all.astype(single)
    scale_all = rms_scale(x_all)
    full_one = (x_all * scale_all * gains[0]).astype(half)
    scale_one = half_of(scale_all, core)
    seq = full_one.shape[0]
    qkv = mm(full_one, proj_full).astype(half)
    size = fit(seq, 256)
    starts = info[0]
    bounds = block_bounds(starts, info[1], size)
    columns = info.T
    heads_full, heads_out, lse = attention_forward(qkv, bounds, starts, size)
    prev_rows = prev_logits[0]
    mixed_prev = jnp.dot(prev_rows, gate_mixing, precision=HIGH)
    mixed_prev = jnp.pad(mixed_prev, ((0, 0), (0, LANES - EXPERTS)))
    router_wide = jnp.pad(router_full, ((0, 0), (0, LANES - router_full.shape[1])))
    back_grad, gated_out, got_rows, out_grad, hidden, pg, pu, resid, normed_two, misc = experts(
        expert_weight,
        far_down,
        my_in,
        got_dy,
        heads_out,
        tokens[0],
        outw_own,
        outw_other,
        gains,
        router_wide,
        mixed_prev,
        routes[0],
        onehot,
        padded,
    )
    count = EXPERTS_FF * padded
    grads_sent = weight_step(
        got_rows.reshape(count, width),
        out_grad.reshape(count, width),
        hidden,
        pg,
        pu,
        1 if d_rows % 16 else members,
    )
    back_out = in_group(gated_out)
    back_grad, grads_sent, back_out = lax.optimization_barrier((back_grad, grads_sent, back_out))
    if d_rows % 16:
        grads_sent = grads_sent.reshape(3, members, d_rows, -1).transpose(1, 0, 2, 3)
    grads_got = lax.all_to_all(grads_sent, "dp", 0, 0, tiled=True)

    mix_wide = jnp.pad(gate_mixing, ((0, LANES - EXPERTS), (0, LANES - EXPERTS)))
    prev_wide = jnp.pad(prev_rows, ((0, 0), (0, LANES - EXPERTS)))
    resid_grad, attn_all, heads_grad, base, prev_grad, small, mixing_grad = backward_middle(
        back_grad,
        columns,
        resid,
        normed_two,
        misc,
        cotangent[0],
        routes[0],
        gains,
        const_f,
        router_wide,
        outw_own,
        outw_other,
        prev_wide,
        mix_wide,
        padded,
    )
    out_w_grad = mm_tn(attn_all, heads_out)
    qkv_grad = attention_backward(qkv, heads_grad, heads_full, lse, bounds, starts, size)
    qkv_grad, grads_got = lax.optimization_barrier((qkv_grad, grads_got))
    out_w_grad = out_w_grad.astype(half)
    if d_rows % 16 or members != 16:
        outs = plain_tail(
            back_out, qkv_grad, full_one, proj_full, out_w_grad, x_all, base, resid_grad, gains, small
        )
    else:
        outs = tail(
            members,
            back_out,
            qkv_grad,
            full_one,
            proj_full,
            out_w_grad,
            tokens_all,
            base,
            resid_grad,
            columns,
            gains,
            small,
            padded,
        )
    dense, tokens_grad, mixed, small = outs
    expert_shard = jnp.sum(
        grads_got.reshape((groups, EXPERTS_FF) + grads_got.shape[1:]).astype(single), axis=0
    )
    proj_shard = dense[:, : 3 * hh].reshape(d_rows, 3, hh).transpose(1, 0, 2)
    outw_shard = dense[:, 3 * hh :]
    mixing_total = small[20:22].reshape(EXPERTS, LANES)[:, :EXPERTS]
    features = lax.dynamic_slice_in_dim(small, lax.axis_index("dp") * d_rows, d_rows, 1)
    return (
        mixed[None],
        tokens_grad[None],
        prev_grad[None, :, :EXPERTS],
        proj_shard,
        outw_shard,
        features[18:20],
        expert_shard,
        features[:16].T,
        features[16:18],
        mixing_total,
    )


def solution(mesh):
    return jax.shard_map(
        per_device,
        mesh=mesh,
        in_specs=(
            P("dp", "tensor", None),
            P("dp", "tensor"),
            P("dp", "tensor", None),
            P("dp", "tensor", None),
            P("dp", "tensor", None),
            P(None, "dp", "tensor"),
            P("dp", "tensor"),
            P(None, "dp"),
            P(None, None, "dp", "tensor"),
            P("dp", None),
            P(None, "dp"),
            P(),
        ),
        out_specs=(
            P("dp", "tensor", None),
            P("dp", "tensor", None),
            P("dp", "tensor", None),
            P(None, "dp", "tensor"),
            P("dp", "tensor"),
            P(None, "dp"),
            P(None, None, "dp", "tensor"),
            P("dp", None),
            P(None, "dp"),
            P(),
        ),
        check_vma=False,
    )
```

```python
import functools

import jax
import jax.numpy as jnp
from jax import lax
from jax.experimental import pallas as pl
from jax.experimental.pallas import tpu as pltpu
from jax.sharding import PartitionSpec as P

HEAD_DIM = 64
EXPERTS_FF = 8
EXPERTS = 12
CAPACITY = 341


EPS = 1e-05
HIGH = lax.Precision.HIGHEST
NEG = -1e30
LANES = 128
DOCS = 8
LOG2E = 1.4426950408889634
MESH = pl.DeviceIdType.MESH
single = jnp.float32
half = jnp.bfloat16


def rms_scale(rows):
    return lax.rsqrt(jnp.mean(rows * rows, axis=-1, keepdims=True) + EPS)


def softmax_last(values):
    peak = jnp.max(values, axis=-1, keepdims=True)
    expo = jnp.exp(values - peak)
    return expo / jnp.sum(expo, axis=-1, keepdims=True)


def mm(a, b):
    return jnp.dot(a, b, preferred_element_type=single)


def mm_nt(a, b):
    return lax.dot_general(a, b, (((1,), (1,)), ((), ())), preferred_element_type=single)


def mm_tn(a, b):
    return lax.dot_general(a, b, (((0,), (0,)), ((), ())), preferred_element_type=single)


def swap(x):
    return lax.ppermute(x, "tensor", [(0, 1), (1, 0)])


def in_order(own, other):
    first = lax.axis_index("tensor") == 0
    return jnp.concatenate([jnp.where(first, own, other), jnp.where(first, other, own)], 0)


def half_of(full, which):
    count = full.shape[0] // 2
    return lax.dynamic_slice_in_dim(full, which * count, count, 0)


def pair_sum(full):
    core = lax.axis_index("tensor")
    other = swap(half_of(full, 1 - core).astype(half))
    return half_of(full, core) + other.astype(single)


def fit(seq, want):
    return want if seq % want == 0 else seq

def block_bounds(start, end, size):
    edges = start.reshape(-1, size)
    number = jnp.arange(edges.shape[0], dtype=jnp.int32)
    low = edges[:, 0] // size
    plain = jnp.clip((edges[:, -1] + size - 1) // size, low, number)
    high = end.reshape(-1, size)[:, -1] // size
    clear = jnp.sum((edges[None, :, -1] <= number[:, None] * size).astype(jnp.int32), axis=1)
    clear = jnp.clip(clear, number + 1, high + 1)
    return jnp.stack([low, plain, high, clear])


def head_lanes(h, rows):
    lane = lax.broadcasted_iota(jnp.int32, (rows, LANES), 1)
    return (lane < HEAD_DIM) if h % 2 == 0 else (lane >= HEAD_DIM)

def fwd_kernel(heads, bounds, q_ref, k_ref, v_ref, start_ref, o_ref, low_ref, lse_ref, s_ref, m_ref, l_ref, acc_ref, qm_ref):
    size = q_ref.shape[0]
    i = pl.program_id(0)
    low, plain = bounds[0, i], bounds[1, i]
    factor = LOG2E * HEAD_DIM ** -0.5
    for h in range(heads):
        pair = pl.ds(h // 2 * LANES, LANES)
        qm_ref[h] = jnp.where(head_lanes(h, size), q_ref[:, pair], 0).astype(half)
    m_ref[...] = jnp.full(m_ref.shape, NEG, single)
    l_ref[...] = jnp.zeros(l_ref.shape, single)
    acc_ref[...] = jnp.zeros(acc_ref.shape, single)

    def score(j, masked):
        rows = pl.ds(pl.multiple_of(j * size, size), size)
        if masked:
            row = i * size + lax.broadcasted_iota(jnp.int32, (size, size), 0)
            col = j * size + lax.broadcasted_iota(jnp.int32, (size, size), 1)
            allowed = (col <= row) & (col >= start_ref[...])
        for h in range(heads):
            s = mm_nt(qm_ref[h], k_ref[rows, pl.ds(h // 2 * LANES, LANES)])
            if masked:
                s = jnp.where(allowed, s, NEG)
            s_ref[h, j] = s
            m = m_ref[h]
            for c in range(size // LANES):
                m = jnp.maximum(m, s[:, c * LANES : (c + 1) * LANES])
            m_ref[h] = m

    pl.loop(low, plain)(lambda j: score(j, True))
    pl.loop(plain, i)(lambda j: score(j, False))
    score(i, True)
    for h in range(heads):
        m_ref[h] = jnp.broadcast_to(jnp.max(m_ref[h], axis=1, keepdims=True) * factor, (size, LANES))

    def gather(j):
        rows = pl.ds(pl.multiple_of(j * size, size), size)
        for h in range(heads):
            s = s_ref[h, j]
            m = m_ref[h]
            l = l_ref[h]
            parts = []
            for c in range(size // LANES):
                p = jnp.exp2(s[:, c * LANES : (c + 1) * LANES] * factor - m)
                l = l + p
                parts.append(p.astype(half))
            l_ref[h] = l
            acc_ref[h] += jnp.dot(jnp.concatenate(parts, 1), v_ref[rows, pl.ds(h // 2 * LANES, LANES)], preferred_element_type=single)

    pl.loop(low, i + 1)(gather)
    lane = lax.broadcasted_iota(jnp.int32, (size, LANES), 1)
    lse = jnp.zeros((size, LANES), single)
    for h in range(0, heads, 2):
        outs = []
        for k in (h, h + 1):
            l = jnp.sum(l_ref[k], axis=1, keepdims=True)
            outs.append(acc_ref[k] / l)
            lse = jnp.where(lane == k, m_ref[k] + jnp.log2(l), lse)
        out = jnp.where(lane < HEAD_DIM, outs[0], outs[1])
        o_ref[:, pl.ds(h // 2 * LANES, LANES)] = out
        low_ref[:, pl.ds(h // 2 * LANES, LANES)] = out.astype(half)
    lse_ref[...] = lse

def attention_forward(qkv, seg_bounds, starts, size):
    seq = qkv.shape[0]
    hh = qkv.shape[1] // 3
    heads = hh // HEAD_DIM
    return pl.pallas_call(
        functools.partial(fwd_kernel, heads),
        grid_spec=pltpu.PrefetchScalarGridSpec(
            num_scalar_prefetch=1,
            grid=(seq // size,),
            in_specs=[
                pl.BlockSpec((size, hh), lambda i, b: (i, 0)),
                pl.BlockSpec((seq, hh), lambda i, b: (0, 1)),
                pl.BlockSpec((seq, hh), lambda i, b: (0, 2)),
                pl.BlockSpec((size, 1), lambda i, b: (i, 0)),
            ],
            out_specs=[
                pl.BlockSpec((size, hh), lambda i, b: (i, 0)),
                pl.BlockSpec((size, hh), lambda i, b: (i, 0)),
                pl.BlockSpec((size, LANES), lambda i, b: (i, 0)),
            ],
            scratch_shapes=[
                pltpu.VMEM((heads, seq // size, size, size), single),
                pltpu.VMEM((heads, size, LANES), single),
                pltpu.VMEM((heads, size, LANES), single),
                pltpu.VMEM((heads, size, LANES), single),
                pltpu.VMEM((heads, size, LANES), half),
            ],
        ),
        out_shape=[
            jax.ShapeDtypeStruct((seq, hh), single),
            jax.ShapeDtypeStruct((seq, hh), half),
            jax.ShapeDtypeStruct((seq, LANES), single),
        ],
        compiler_params=pltpu.CompilerParams(vmem_limit_bytes=48 << 20),
        cost_estimate=pl.CostEstimate(flops=4 * seq * seq * LANES * heads, bytes_accessed=16 * seq * hh, transcendentals=0),
    )(seg_bounds, qkv, qkv, qkv, starts[:, None])

def bwd_kernel(
    heads, bounds, q_ref, k_ref, v_ref, do_ref, o_ref, lse_ref, start_ref, out_ref, dq_ref, dk_ref, dv_ref, stat_ref
):
    size = k_ref.shape[0]
    j = pl.program_id(0)
    high, clear = bounds[2, j], bounds[3, j]
    factor = LOG2E * HEAD_DIM ** -0.5
    hh = k_ref.shape[1]

    @pl.when(j == 0)
    def _():
        dq_ref[...] = jnp.zeros(dq_ref.shape, single)
        feature = lax.broadcasted_iota(jnp.int32, (hh, LANES), 0)
        lane = lax.broadcasted_iota(jnp.int32, (hh, LANES), 1)
        pick = (feature // HEAD_DIM + 8 == lane).astype(half)

        @pl.loop(0, q_ref.shape[0] // size)
        def _(i):
            rows = pl.ds(pl.multiple_of(i * size, size), size)
            product = o_ref[rows, :] * do_ref[rows, :].astype(single)
            top = product.astype(half)
            low = (product - top.astype(single)).astype(half)
            both = mm(top, pick) + mm(low, pick) + lse_ref[rows, :]
            stat_ref[:, rows] = both.T[:16, :]

    dk_ref[...] = jnp.zeros(dk_ref.shape, single)
    dv_ref[...] = jnp.zeros(dv_ref.shape, single)

    def step(i, masked):
        rows = pl.ds(pl.multiple_of(i * size, size), size)
        if masked:
            key = j * size + lax.broadcasted_iota(jnp.int32, (size, size), 0)
            query = i * size + lax.broadcasted_iota(jnp.int32, (size, size), 1)
            allowed = (key <= query) & (key >= start_ref[:, rows])
        for pair in range(heads // 2):
            lanes = pl.ds(pair * LANES, LANES)
            k, v = k_ref[:, lanes], v_ref[:, lanes]
            q, do = q_ref[rows, lanes], do_ref[rows, lanes]
            ps, dss, qs, dos, ks = [], [], [], [], []
            for h in (2 * pair, 2 * pair + 1):
                mine = head_lanes(h, size)
                qm = jnp.where(mine, q, 0).astype(half)
                dom = jnp.where(mine, do, 0).astype(half)
                s = mm_nt(k, qm) * factor - stat_ref[pl.ds(h, 1), rows]
                if masked:
                    s = jnp.where(allowed, s, NEG)
                p = jnp.exp2(s)
                ds = p * (mm_nt(v, dom) - stat_ref[pl.ds(8 + h, 1), rows])
                ps.append(p.astype(half))
                dss.append(ds.astype(half))
                qs.append(qm)
                dos.append(dom)
                ks.append(jnp.where(mine, k, 0).astype(half))
            dv_ref[:, lanes] += jnp.dot(jnp.concatenate(ps, 1), jnp.concatenate(dos, 0), preferred_element_type=single)
            dk_ref[:, lanes] += jnp.dot(jnp.concatenate(dss, 1), jnp.concatenate(qs, 0), preferred_element_type=single)
            dq_ref[rows, lanes] += mm_tn(jnp.concatenate(dss, 0), jnp.concatenate(ks, 0))

    step(j, True)
    pl.loop(j + 1, clear)(lambda i: step(i, False))
    pl.loop(clear, high + 1)(lambda i: step(i, True))
    mine = pl.ds(pl.multiple_of(j * size, size), size)
    out_ref[mine, pl.ds(hh, hh)] = (dk_ref[...] * HEAD_DIM ** -0.5).astype(half)
    out_ref[mine, pl.ds(2 * hh, hh)] = dv_ref[...].astype(half)
    out_ref[mine, pl.ds(0, hh)] = (dq_ref[mine, :] * HEAD_DIM ** -0.5).astype(half)

def attention_backward(qkv, do, heads_out, lse, seg_bounds, starts, size):
    seq = qkv.shape[0]
    hh = qkv.shape[1] // 3
    heads = hh // HEAD_DIM
    return pl.pallas_call(
        functools.partial(bwd_kernel, heads),
        grid_spec=pltpu.PrefetchScalarGridSpec(
            num_scalar_prefetch=1,
            grid=(seq // size,),
            in_specs=[
                pl.BlockSpec((seq, hh), lambda j, b: (0, 0)),
                pl.BlockSpec((size, hh), lambda j, b: (j, 1)),
                pl.BlockSpec((size, hh), lambda j, b: (j, 2)),
                pl.BlockSpec((seq, hh), lambda j, b: (0, 0)),
                pl.BlockSpec((seq, hh), lambda j, b: (0, 0)),
                pl.BlockSpec((seq, LANES), lambda j, b: (0, 0)),
                pl.BlockSpec((1, seq), lambda j, b: (0, 0)),
            ],
            out_specs=pl.BlockSpec((seq, 3 * hh), lambda j, b: (0, 0)),
            scratch_shapes=[
                pltpu.VMEM((seq, hh), single),
                pltpu.VMEM((size, hh), single),
                pltpu.VMEM((size, hh), single),
                pltpu.VMEM((16, seq), single),
            ],
        ),
        out_shape=jax.ShapeDtypeStruct((seq, 3 * hh), half),
        compiler_params=pltpu.CompilerParams(vmem_limit_bytes=48 << 20),
        cost_estimate=pl.CostEstimate(flops=10 * seq * seq * LANES * heads, bytes_accessed=20 * seq * hh, transcendentals=0),
    )(seg_bounds, qkv, qkv, qkv, do, heads_out, lse, starts[None, :])


def flip(number, k):
    out = 0
    for bit in (1, 2, 4):
        digit = lax.rem(number // bit, 2)
        out = out + bit * ((1 - digit) if k & bit else digit)
    return out


BESIDE = (3, 1, 2)
NEAR = (3, 4, 5, 2, 6, 1, 7)
PAIRS = ((0, 3), (4, 5), (2, 6), (1, 7))


def start_kernel(
    members,
    low,
    per_core,
    padded,
    pack_ref,
    tok_ref,
    dy_ref,
    ids_ref,
    w_ref,
    full_ref,
    all_ref,
    rows_ref,
    hot_ref,
    info_ref,
    down_ref,
    ids_all_ref,
    dy_all_ref,
    place_ref,
    send_sem,
    recv_sem,
    own_sem,
    swap_send,
    swap_recv,
    down_send,
    down_recv,
):
    size = EXPERTS_FF
    me = lax.axis_index("dp")
    core = lax.axis_index("tensor")
    high = members // low
    inside, row = lax.rem(me, low), me // low
    mine = lax.rem(me, size)
    base = me - mine
    local = tok_ref.shape[0]
    seq = 2 * local
    partner = {"tensor": 1 - core}

    def beside(k):
        return row * low + flip(inside, k)

    def across(k):
        return lax.rem(row + k, high) * low + inside

    peers = [beside(k) for k in BESIDE] + [across(k) for k in range(1, high)]
    groups = members // size

    def device_at(g, k):
        return lax.rem(base + g * size, members) + lax.rem(mine + k, size)

    distant = [(g, k) for k in range(size) for g in range(groups) if g or k]
    peers += [device_at(g, k) for g, k in distant]
    barrier = pltpu.get_barrier_semaphore()
    for peer in peers:
        pl.semaphore_signal(barrier, inc=1, device_id={"dp": peer}, device_id_type=MESH)
    pl.semaphore_signal(barrier, inc=1, device_id=partner, device_id_type=MESH)
    pl.semaphore_wait(barrier, len(peers) + 1)

    def remote(src, dst, send, recv, device):
        return pltpu.make_async_remote_copy(
            src_ref=src,
            dst_ref=dst,
            send_sem=send,
            recv_sem=recv,
            device_id=device,
            device_id_type=MESH,
        )

    def push(source, block, target, slot):
        copy = remote(
            source, full_ref.at[block], send_sem.at[slot], recv_sem.at[block], {"dp": target}
        )
        copy.start()
        return copy

    def arrived(block):
        remote(
            pack_ref, full_ref.at[block], send_sem.at[0], recv_sem.at[block], {"dp": peers[0]}
        ).wait_recv()

    sent = [push(pack_ref, me, across(k), k) for k in range(1, high)]
    sent += [push(pack_ref, me, beside(k), high + k) for k in BESIDE]
    own_rows = pl.ds(pl.multiple_of(core * local, local), local)
    swaps = [
        remote(ids_ref, ids_all_ref.at[core], swap_send.at[0], swap_recv.at[0], partner),
        remote(dy_ref, dy_all_ref.at[own_rows], swap_send.at[1], swap_recv.at[1], partner),
        remote(tok_ref, all_ref.at[own_rows], swap_send.at[2], swap_recv.at[2], partner),
    ]
    owns = [
        pltpu.make_async_copy(ids_ref, ids_all_ref.at[core], own_sem.at[0]),
        pltpu.make_async_copy(dy_ref, dy_all_ref.at[own_rows], own_sem.at[1]),
        pltpu.make_async_copy(tok_ref, all_ref.at[own_rows], own_sem.at[2]),
        pltpu.make_async_copy(pack_ref, full_ref.at[me], own_sem.at[3]),
        pltpu.make_async_copy(w_ref.at[mine, 2], down_ref.at[me], own_sem.at[4]),
    ]
    for copy in swaps + owns:
        copy.start()

    swaps[0].wait()
    owns[0].wait()
    ids = jnp.concatenate([ids_all_ref[0], ids_all_ref[1]], 1)
    seg = ids[:1]
    number = lax.broadcasted_iota(jnp.int32, (8, seq), 0)
    starts = jnp.zeros((1, seq), jnp.int32)
    ends = jnp.zeros((1, seq), jnp.int32)
    total = jnp.zeros((1, 1), jnp.int32)
    for d in range(DOCS):
        here = seg == d
        starts = jnp.where(here, total, starts)
        total = total + jnp.sum(here.astype(jnp.int32), axis=1, keepdims=True)
        ends = jnp.where(here, total - 1, ends)
    row16 = lax.broadcasted_iota(jnp.int32, (16, LANES), 0)
    first = lax.broadcasted_iota(jnp.int32, (LANES, LANES), 0)
    second = lax.broadcasted_iota(jnp.int32, (LANES, LANES), 1)
    upper = (first < second).astype(half)
    before = jnp.zeros((16, 1), single)
    for c in range(seq // LANES):
        lanes = slice(c * LANES, (c + 1) * LANES)
        member = (ids[1:2, lanes] == row16) | (ids[2:3, lanes] == row16)
        member = jnp.where(member & (row16 < size), 1.0, 0.0)
        position = mm(member.astype(half), upper) + before
        before = before + jnp.sum(member, axis=1, keepdims=True)
        place = position - (core * per_core).astype(single)
        kept = (member > 0.5) & (position < CAPACITY) & (place >= 0) & (place < per_core)
        place_ref[:, lanes] = jnp.where(kept, place, -1.0).astype(jnp.int32)
    slot = lax.broadcasted_iota(jnp.int32, (padded, seq), 0)
    for e in range(size):
        hot_ref[e * padded : (e + 1) * padded, :] = jnp.where(
            place_ref[e : e + 1, :] == slot, 1.0, 0.0
        ).astype(half)

    info = jnp.where(number == 0, starts, jnp.where(number == 1, ends, -1))
    for k in range(2):
        chosen = jnp.full((1, seq), -1, jnp.int32)
        for e in range(size):
            place = place_ref[e : e + 1, :]
            chosen = jnp.where(
                (ids[k + 1 : k + 2] == e) & (place >= 0), place + e * padded, chosen
            )
        info = jnp.where(number == k + 2, chosen, info)
    info_ref[...] = info

    for k in range(1, high):
        block = across(high - k)
        arrived(block)
        for step in BESIDE:
            sent.append(push(full_ref.at[block], block, beside(step), high + k * low + step))

    for g, k in distant:
        copy = remote(
            w_ref.at[lax.rem(mine + k, size), 2],
            down_ref.at[me],
            down_send.at[g * size + k],
            down_recv.at[me],
            {"dp": device_at(g, k)},
        )
        copy.start()
        sent.append(copy)

    swaps[1].wait()
    owns[1].wait()
    for e in range(0, size, 2):
        slots = slice(e * padded, (e + 2) * padded)
        rows = mm(hot_ref[slots, :], dy_all_ref[...])
        rows_ref[e : e + 2] = rows.astype(half).reshape(2, padded, rows.shape[1])
    for k in BESIDE:
        block = beside(k)
        arrived(block)
        for step in range(1, high):
            arrived(lax.rem(block + step * low, members))
    for g, k in distant:
        block = device_at((groups - g) % groups, (size - k) % size)
        remote(
            w_ref.at[0, 2], down_ref.at[block], down_send.at[0], down_recv.at[block], partner
        ).wait_recv()
    for copy in sent:
        copy.wait_send()
    for copy in owns[2:]:
        copy.wait()
    swaps[2].wait()


def start(pack, tokens, dy, ids, w, members, per_core, padded):
    low = 4
    high = members // low
    local, width = tokens.shape
    count = EXPERTS_FF * padded
    any_spec = pl.BlockSpec(memory_space=pl.ANY)
    vmem = pl.BlockSpec(memory_space=pltpu.VMEM)
    dma = pltpu.SemaphoreType.DMA
    return pl.pallas_call(
        functools.partial(start_kernel, members, low, per_core, padded),
        out_shape=[
            jax.ShapeDtypeStruct((members,) + pack.shape, half),
            jax.ShapeDtypeStruct((2 * local, width), half),
            jax.ShapeDtypeStruct((EXPERTS_FF, padded, width), half),
            jax.ShapeDtypeStruct((count, 2 * local), half),
            jax.ShapeDtypeStruct((8, 2 * local), jnp.int32),
            jax.ShapeDtypeStruct((members,) + w.shape[2:], half),
        ],
        in_specs=[pl.BlockSpec(memory_space=pltpu.HBM)] * 5,
        out_specs=[any_spec] * 2 + [vmem] * 3 + [any_spec],
        scratch_shapes=[
            pltpu.VMEM((2, 8, local), jnp.int32),
            pltpu.VMEM((2 * local, width), half),
            pltpu.VMEM((16, 2 * local), jnp.int32),
            dma((high * (low + 1),)),
            dma((members,)),
            dma((5,)),
            dma((3,)),
            dma((3,)),
            dma((members,)),
            dma((members,)),
        ],
        compiler_params=pltpu.CompilerParams(
            collective_id=0, has_side_effects=True, vmem_limit_bytes=40 << 20
        ),
        name="start",
    )(pack, tokens, dy, ids, w)


def experts_kernel(
    members,
    padded,
    down_hbm_ref,
    in_ref,
    dy_hbm_ref,
    ho_ref,
    tok_ref,
    own_w_ref,
    other_w_ref,
    gain_ref,
    router_ref,
    prev_ref,
    routes_ref,
    hot_ref,
    back_ref,
    out_ref,
    x_ref,
    og_ref,
    hid_ref,
    pg_ref,
    pu_ref,
    resid_ref,
    normed_ref,
    misc_ref,
    ho_in_ref,
    both_ref,
    acc_ref,
    stage_ref,
    row_ref,
    win_ref,
    down_ref,
    dy_ref,
    ig_ref,
    spill_ref,
    gate_ref,
    dot_ref,
    x_send,
    x_recv,
    dy_send,
    dy_recv,
    own_sem,
    swap_send,
    swap_recv,
    ig_send,
    ig_recv,
    spill_sem,
):
    size = EXPERTS_FF
    groups = members // size
    me = lax.axis_index("dp")
    core = lax.axis_index("tensor")
    mine = lax.rem(me, size)
    base = me - mine
    local, width = tok_ref.shape
    partner = {"tensor": 1 - core}
    near = [base + lax.rem(mine + k, size) for k in range(1, size)]
    barrier = pltpu.get_barrier_semaphore()
    for peer in near:
        pl.semaphore_signal(barrier, inc=1, device_id={"dp": peer}, device_id_type=MESH)
    pl.semaphore_signal(barrier, inc=1, device_id=partner, device_id_type=MESH)
    pl.semaphore_wait(barrier, size)

    def remote(src, dst, send, recv, device):
        return pltpu.make_async_remote_copy(
            src_ref=src,
            dst_ref=dst,
            send_sem=send,
            recv_sem=recv,
            device_id=device,
            device_id_type=MESH,
        )

    own_rows = pl.ds(pl.multiple_of(core * local, local), local)
    other_rows = pl.ds(pl.multiple_of((1 - core) * local, local), local)
    heads = remote(ho_ref.at[other_rows], ho_in_ref, swap_send.at[0], swap_recv.at[0], partner)
    heads.start()
    waits = []
    for k in NEAR:
        to = flip(mine, k)
        copy = remote(
            dy_hbm_ref.at[to], dy_ref.at[mine], dy_send.at[k], dy_recv.at[k], {"dp": base + to}
        )
        copy.start()
        waits.append(copy)
    pair_in = remote(in_ref, win_ref.at[1], swap_send.at[2], swap_recv.at[2], partner)
    pair_in.start()
    pair_down = remote(down_hbm_ref, down_ref.at[1], swap_send.at[3], swap_recv.at[3], partner)
    pair_down.start()
    owns = [
        pltpu.make_async_copy(in_ref, win_ref.at[0], own_sem.at[1]),
        pltpu.make_async_copy(dy_hbm_ref.at[mine], dy_ref.at[mine], own_sem.at[2]),
        pltpu.make_async_copy(down_hbm_ref, down_ref.at[0], own_sem.at[3]),
    ]
    for copy in owns:
        copy.start()

    step = fit(local, 256)
    heads.wait()

    @pl.loop(0, local // step)
    def _(r):
        rows = pl.ds(pl.multiple_of(r * step, step), step)
        mine_rows = pl.ds(pl.multiple_of(core * local + r * step, step), step)
        resid = tok_ref[rows, :].astype(single)
        resid += mm_nt(ho_ref[mine_rows, :], own_w_ref[...])
        resid += mm_nt(ho_in_ref[rows, :], other_w_ref[...])
        resid_ref[rows, :] = resid
        normed = (resid * rms_scale(resid) * gain_ref[1:2, :]).astype(half)
        normed_ref[rows, :] = normed
        router = mm(normed, router_ref[...])
        lane = lax.broadcasted_iota(jnp.int32, (step, LANES), 1)
        logits = jnp.where(lane < EXPERTS, router + prev_ref[rows, :], 0.0)
        hits = [lane == routes_ref[rows, k : k + 1] for k in range(2)]
        picked = [jnp.sum(jnp.where(hit, logits, 0.0), axis=1, keepdims=True) for hit in hits]
        peak = jnp.maximum(picked[0], picked[1])
        expo = [jnp.exp(p - peak) for p in picked]
        total = expo[0] + expo[1]
        gates = [e / total for e in expo]
        misc_ref[rows, :] = jnp.where(lane == 0, gates[0], jnp.where(lane == 1, gates[1], router))
        spread = sum(
            jnp.where(hit & (lane < size), gate.astype(half).astype(single), 0.0)
            for hit, gate in zip(hits, gates)
        )
        both_ref[mine_rows, pl.ds(0, width)] = normed
        both_ref[mine_rows, pl.ds(width, LANES)] = spread.astype(half)

    swap_rows = remote(
        both_ref.at[own_rows], both_ref.at[own_rows], swap_send.at[1], swap_recv.at[1], partner
    )
    swap_rows.start()

    for number, pair in enumerate(PAIRS):
        slots = [
            pl.ds(pl.multiple_of(flip(mine, k) * padded, 16), padded) for k in pair
        ]
        hot = jnp.concatenate([hot_ref[s, own_rows] for s in slots], 0)
        acc_ref[number] = mm(hot, both_ref[own_rows, :])
    swap_rows.wait_recv()
    row_ref[...] = jnp.zeros(row_ref.shape, single)
    for number, pair in enumerate(PAIRS):
        slots = [
            pl.ds(pl.multiple_of(flip(mine, k) * padded, 16), padded) for k in pair
        ]
        hot = jnp.concatenate([hot_ref[s, other_rows] for s in slots], 0)
        acc_ref[number] += mm(hot, both_ref[other_rows, :])
        for place, k in enumerate(pair):
            to = flip(mine, k)
            first = place * padded
            tail = acc_ref[number, first : first + padded, width:].astype(half)
            lane = lax.broadcasted_iota(jnp.int32, (16, LANES), 1)
            row_ref[:, :padded] = mm_nt((lane == to).astype(half), tail)
            stage_ref[to] = acc_ref[number, first : first + padded, :width].astype(half)
            last = acc_ref[number, first + padded - 16 : first + padded, : 2 * LANES]
            row = lax.broadcasted_iota(jnp.int32, (16, 2 * LANES), 0)
            last = jnp.where(row == 15, row_ref[...], last)
            stage_ref[to, padded - 16 :, : 2 * LANES] = last.astype(half)
            if k:
                copy = remote(
                    stage_ref.at[to], x_ref.at[mine], x_send.at[k], x_recv.at[k], {"dp": base + to}
                )
                waits.append(copy)
            else:
                copy = pltpu.make_async_copy(stage_ref.at[to], x_ref.at[mine], own_sem.at[0])
            copy.start()

    for copy in owns:
        copy.wait()
    pair_in.wait_recv()
    pair_down.wait_recv()

    ff = in_ref.shape[3]
    block = fit(ff, 256)
    steps = ff // block
    rows2 = 2 * padded
    dot_ref[...] = jnp.zeros(dot_ref.shape, single)

    def spill(slot, array, place, source, part, f):
        out = (hid_ref, pg_ref, pu_ref)[array]
        rows = pl.ds(pl.multiple_of(source * padded, 16), padded)
        return pltpu.make_async_copy(
            spill_ref.at[slot, array, pl.ds(place * padded, padded)],
            out.at[part, rows, pl.ds(f * block, block)],
            spill_sem.at[slot, array, place],
        )

    def arrived(k):
        remote(dy_hbm_ref.at[0], dy_ref.at[0], dy_send.at[0], dy_recv.at[k], partner).wait_recv()
        remote(stage_ref.at[0], x_ref.at[0], x_send.at[0], x_recv.at[k], partner).wait_recv()

    def give_back(k, source):
        return remote(
            ig_ref.at[source], back_ref.at[mine], ig_send.at[k], ig_recv.at[k], {"dp": base + source}
        )

    @pl.loop(0, size // 2)
    def _(q):
        ks, sources = [], []
        for place in range(2):
            k, source = PAIRS[0][place], flip(mine, PAIRS[0][place])
            for number in range(1, size // 2):
                k = jnp.where(q == number, PAIRS[number][place], k)
                source = jnp.where(q == number, flip(mine, PAIRS[number][place]), source)
            ks.append(k)
            sources.append(source)

        @pl.when(q == 0)
        def _():
            pltpu.make_async_copy(stage_ref.at[0], x_ref.at[0], own_sem.at[0]).wait()

        @pl.when(q > 0)
        def _():
            arrived(ks[0])

        arrived(ks[1])
        for place, source in enumerate(sources):
            rows = pl.ds(place * padded, padded)
            gates = x_ref[source, padded - 16 :, : 2 * LANES].astype(single).T
            gate = jnp.broadcast_to(gates[:padded, 15:16], (padded, LANES))
            gate_ref[rows, :] = gate
            og_ref[source] = (dy_ref[source].astype(single) * gate[:, :1]).astype(half)
        for number in range(2):
            acc_ref[number, :, :width] = jnp.zeros((rows2, width), single)

        @pl.loop(0, 2)
        def _(part):
            for f in range(steps):
                lanes = pl.ds(f * block, block)
                slot = f % 2
                if f >= 2:
                    for array in range(3):
                        for place, source in enumerate(sources):
                            spill(slot, array, place, source, part, f - 2).wait()
                gate_w = win_ref[part, :, 0, :, lanes].reshape(width, block)
                up_w = win_ref[part, :, 1, :, lanes].reshape(width, block)
                down_w = down_ref[part, :, :, lanes].reshape(width, block)
                x = jnp.concatenate([x_ref[source] for source in sources], 0)
                og = jnp.concatenate([og_ref[source] for source in sources], 0)
                pre = mm(x, gate_w)
                up = mm(x, up_w)
                hg = mm(og, down_w)
                sigma = jax.nn.sigmoid(pre)
                active = pre * sigma
                hidden = (active * up).astype(half)
                pg = (hg * up * (sigma * (1.0 + pre * (1.0 - sigma)))).astype(half)
                pu = (hg * active).astype(half)
                spill_ref[slot, 0] = hidden
                spill_ref[slot, 1] = pg
                spill_ref[slot, 2] = pu
                acc_ref[0, :, :width] += mm_nt(hidden, down_w)
                acc_ref[1, :, :width] += mm_nt(pg, gate_w) + mm_nt(pu, up_w)
                for array in range(3):
                    for place, source in enumerate(sources):
                        spill(slot, array, place, source, part, f).start()
            for f in range(max(0, steps - 2), steps):
                for array in range(3):
                    for place, source in enumerate(sources):
                        spill(f % 2, array, place, source, part, f).wait()

        ones = jnp.ones((16, width), half)
        for place, source in enumerate(sources):
            rows = pl.ds(place * padded, padded)
            eo = acc_ref[0, rows, :width]
            out_ref[source] = (eo * gate_ref[rows, :1]).astype(half)
            ig_ref[source] = acc_ref[1, rows, :width].astype(half)
            product = eo * dy_ref[source].astype(single)
            top = product.astype(half)
            low = (product - top.astype(single)).astype(half)
            dot_ref[:, :padded] = mm_nt(ones, top) + mm_nt(ones, low)
            dots = dot_ref[...]
            high = dots.astype(half).astype(single)
            row = lax.broadcasted_iota(jnp.int32, dots.shape, 0)
            last = acc_ref[1, pl.ds((place + 1) * padded - 16, 16), : 2 * LANES]
            last = jnp.where(row == 14, high, jnp.where(row == 15, dots - high, last))
            ig_ref[source, padded - 16 :, : 2 * LANES] = last.astype(half)

        @pl.when(q == 0)
        def _():
            pltpu.make_async_copy(ig_ref.at[mine], back_ref.at[mine], own_sem.at[0]).start()

        @pl.when(q > 0)
        def _():
            give_back(ks[0], sources[0]).start()

        give_back(ks[1], sources[1]).start()

    pltpu.make_async_copy(ig_ref.at[mine], back_ref.at[mine], own_sem.at[0]).wait()
    for k in range(1, size):
        give_back(k, flip(mine, k)).wait()
    for copy in waits + [swap_rows, pair_in, pair_down]:
        copy.wait_send()


def experts(
    down, inward, dy, heads, tokens, own_w, other_w, gains, router, prev, routes, hot, padded
):
    members, _, d_rows, ff = inward.shape
    local, width = tokens.shape
    seq = heads.shape[0]
    size = EXPERTS_FF
    block = fit(ff, 256)
    any_spec = pl.BlockSpec(memory_space=pl.ANY)
    vmem = pl.BlockSpec(memory_space=pltpu.VMEM)
    dma = pltpu.SemaphoreType.DMA
    rows = jax.ShapeDtypeStruct((size, padded, width), half)
    wide = jax.ShapeDtypeStruct((2, size * padded, ff), half)
    return pl.pallas_call(
        functools.partial(experts_kernel, members, padded),
        out_shape=[
            rows,
            rows,
            rows,
            rows,
            wide,
            wide,
            wide,
            jax.ShapeDtypeStruct((local, width), single),
            jax.ShapeDtypeStruct((local, width), half),
            jax.ShapeDtypeStruct((local, LANES), single),
        ],
        in_specs=[any_spec] * 3 + [vmem] * 9,
        out_specs=[any_spec] + [vmem] * 3 + [any_spec] * 3 + [vmem] * 3,
        scratch_shapes=[
            pltpu.VMEM((local, heads.shape[1]), half),
            pltpu.VMEM((seq, width + LANES), half),
            pltpu.VMEM((size // 2, 2 * padded, width + LANES), single),
            pltpu.VMEM((size, padded, width), half),
            pltpu.VMEM((16, 2 * LANES), single),
            pltpu.VMEM((2,) + inward.shape, half),
            pltpu.VMEM((2, members, d_rows, ff), half),
            pltpu.VMEM((size, padded, width), half),
            pltpu.VMEM((size, padded, width), half),
            pltpu.VMEM((2, 3, 2 * padded, block), half),
            pltpu.VMEM((2 * padded, LANES), single),
            pltpu.VMEM((16, 2 * LANES), single),
            dma((size,)),
            dma((size,)),
            dma((size,)),
            dma((size,)),
            dma((4,)),
            dma((4,)),
            dma((4,)),
            dma((size,)),
            dma((size,)),
            dma((2, 3, 2)),
        ],
        compiler_params=pltpu.CompilerParams(
            collective_id=1, has_side_effects=True, vmem_limit_bytes=62 << 20
        ),
        name="experts",
    )(down, inward, dy, heads, tokens, own_w, other_w, gains, router, prev, routes, hot)


def split(x):
    high = x.astype(half)
    return high, (x - high.astype(single)).astype(half)


def slot_rows(columns, count):
    slot = lax.broadcasted_iota(jnp.int32, (columns.shape[0], count), 1)
    hit = (columns[:, 2:3] == slot) | (columns[:, 3:4] == slot)
    return jnp.where(hit, 1.0, 0.0).astype(half)


def lane_sum(x):
    return jnp.sum(x, axis=1, keepdims=True)


def back_kernel(
    padded,
    back_ref,
    info_ref,
    resid_ref,
    normed_ref,
    misc_ref,
    dy_ref,
    routes_ref,
    gain_ref,
    const_ref,
    router_ref,
    own_w_ref,
    other_w_ref,
    prev_ref,
    mix_ref,
    rgrad_ref,
    attn_ref,
    heads_ref,
    base_ref,
    pgrad_ref,
    small_ref,
    mgrad_ref,
    ext_ref,
    out_ref,
    in_ref,
    hg_ref,
    send_sem,
    recv_sem,
):
    core = lax.axis_index("tensor")
    partner = {"tensor": 1 - core}
    sources, _, width = back_ref.shape
    count = sources * padded
    local = dy_ref.shape[0]
    step = fit(local, 256)
    barrier = pltpu.get_barrier_semaphore()
    pl.semaphore_signal(barrier, inc=1, device_id=partner, device_id_type=MESH)
    pl.semaphore_wait(barrier, 1)

    def remote(src, dst, number):
        return pltpu.make_async_remote_copy(
            src_ref=src,
            dst_ref=dst,
            send_sem=send_sem.at[number],
            recv_sem=recv_sem.at[number],
            device_id=partner,
            device_id_type=MESH,
        )

    own_rows = pl.ds(pl.multiple_of(core * local, local), local)
    lane = lax.broadcasted_iota(jnp.int32, (step, LANES), 1)
    for s in range(sources):
        dots = back_ref[s, padded - 16 :, : 2 * LANES].astype(single).T
        number = lax.broadcasted_iota(jnp.int32, (padded, LANES), 1)
        ext = jnp.where(
            number == s,
            dots[:padded, 14:15],
            jnp.where(number == s + EXPERTS_FF, dots[:padded, 15:16], 0.0),
        )
        ext_ref[pl.ds(s * padded, padded), :] = ext.astype(half)
    back_all = back_ref.reshape(count, width)

    @pl.loop(0, local // step)
    def _(r):
        rows = pl.ds(pl.multiple_of(r * step, step), step)
        there = pl.ds(pl.multiple_of((1 - core) * local + r * step, step), step)
        hot = slot_rows(info_ref[there, :], count)
        out_ref[rows, pl.ds(0, width)] = mm(hot, back_all[...]).astype(half)
        out_ref[rows, pl.ds(width, LANES)] = mm(hot, ext_ref[...]).astype(half)

    sums = remote(out_ref, in_ref, 0)
    sums.start()
    small_ref[...] = jnp.zeros(small_ref.shape, single)
    mgrad_ref[...] = jnp.zeros(mgrad_ref.shape, single)

    @pl.loop(0, local // step)
    def _(r):
        rows = pl.ds(pl.multiple_of(r * step, step), step)
        here = pl.ds(pl.multiple_of(core * local + r * step, step), step)
        hot = slot_rows(info_ref[here, :], count)
        rgrad_ref[rows, :] = mm(hot, back_all[...])
        pgrad_ref[rows, :] = mm(hot, ext_ref[...])

    sums.wait()

    @pl.loop(0, local // step)
    def _(r):
        rows = pl.ds(pl.multiple_of(r * step, step), step)
        here = pl.ds(pl.multiple_of(core * local + r * step, step), step)
        dy = dy_ref[rows, :].astype(single)
        normed = normed_ref[rows, :].astype(single)
        resid = resid_ref[rows, :]
        misc = misc_ref[rows, :]
        expert_dot = pgrad_ref[rows, :] + in_ref[rows, pl.ds(width, LANES)].astype(single)
        own_dot = lane_sum(dy * normed)
        vec_dot = [lane_sum(dy * const_ref[j : j + 1, :]) for j in range(2)]
        gates = [misc[:, k : k + 1] for k in range(2)]
        routes = [routes_ref[rows, k : k + 1] for k in range(2)]
        alphas = []
        for j in range(2):
            columns = [misc[:, EXPERTS + 2 * j + m : EXPERTS + 2 * j + m + 1] for m in range(2)]
            peak = jnp.maximum(columns[0], columns[1])
            expo = [jnp.exp(c - peak) for c in columns]
            total = expo[0] + expo[1]
            alphas.append([e / total for e in expo])
        gate_grads = []
        for k in range(2):
            hit = (lane == routes[k]) | (lane == routes[k] + EXPERTS_FF)
            dot = lane_sum(jnp.where(hit & (routes[k] < EXPERTS_FF), expert_dot, 0.0))
            dot += jnp.where(routes[k] == EXPERTS_FF + 1, own_dot, 0.0)
            for j in range(2):
                value = alphas[j][0] * own_dot + alphas[j][1] * vec_dot[j]
                dot += jnp.where(routes[k] == EXPERTS_FF + 2 + j, value, 0.0)
            gate_grads.append(dot)
        centre = gates[0] * gate_grads[0] + gates[1] * gate_grads[1]
        chosen = [gates[k] * (gate_grads[k] - centre) for k in range(2)]
        router_grad = jnp.zeros((step, LANES), single)
        own_weight = jnp.zeros((step, 1), single)
        for k in range(2):
            router_grad = jnp.where(lane == routes[k], chosen[k], router_grad)
            own_weight += jnp.where(routes[k] == EXPERTS_FF + 1, gates[k], 0.0)
        logit_grad = router_grad
        vec_lanes = jnp.zeros((step, LANES), single)
        other = jnp.zeros((step, width), single)
        for j in range(2):
            weight = sum(jnp.where(routes[k] == EXPERTS_FF + 2 + j, gates[k], 0.0) for k in range(2))
            grads = [weight * own_dot, weight * vec_dot[j]]
            mean = alphas[j][0] * grads[0] + alphas[j][1] * grads[1]
            for m in range(2):
                router_grad = jnp.where(
                    lane == EXPERTS + 2 * j + m, alphas[j][m] * (grads[m] - mean), router_grad
                )
            own_weight += weight * alphas[j][0]
            vec_weight = weight * alphas[j][1]
            vec_lanes = jnp.where(lane == 16 + j, vec_weight, vec_lanes)
            other += vec_weight * const_ref[j : j + 1, :]
        base_ref[rows, :] = resid + own_weight * normed + other
        rg_high, rg_low = split(router_grad)
        two_grad = rgrad_ref[rows, :] + in_ref[rows, pl.ds(0, width)].astype(single)
        two_grad += own_weight * dy
        two_grad += mm_nt(rg_high, router_ref[...]) + mm_nt(rg_low, router_ref[...])
        normed_low = normed_ref[rows, :]
        vec_high, vec_low = split(vec_lanes)
        small_ref[...] += (
            mm_tn(rg_high, normed_low)
            + mm_tn(rg_low, normed_low)
            + mm_tn(vec_high, dy_ref[rows, :])
            + mm_tn(vec_low, dy_ref[rows, :])
        )[:24]
        scale = rms_scale(resid)
        gain_part = jnp.sum(two_grad * resid * scale, axis=0, keepdims=True)
        small_ref[19:20, :] += gain_part
        weighted = two_grad * gain_ref[1:2, :]
        mean = jnp.mean(weighted * resid, axis=-1, keepdims=True)
        grad = dy + scale * (weighted - resid * scale * scale * mean)
        rgrad_ref[rows, :] = grad
        low = grad.astype(half)
        attn_ref[here, :] = low
        heads_ref[here, :] = mm(low, own_w_ref[...]).astype(half)
        hg_ref[rows, :] = mm(low, other_w_ref[...]).astype(half)
        lg_high, lg_low = split(logit_grad)
        mix_high, mix_low = split(mix_ref[...])
        pgrad_ref[rows, :] = (
            mm_nt(lg_high, mix_high) + mm_nt(lg_high, mix_low) + mm_nt(lg_low, mix_high)
        )
        prev_high, prev_low = split(prev_ref[rows, :])
        mgrad_ref[...] += (
            mm_tn(prev_high, lg_high) + mm_tn(prev_high, lg_low) + mm_tn(prev_low, lg_high)
        )

    for i in range(EXPERTS):
        place = pl.ds(i % 6 * LANES, LANES)
        small_ref[20 + i // 6 : 21 + i // 6, place] = mgrad_ref[i : i + 1, :]

    heads = remote(hg_ref, heads_ref.at[own_rows], 1)
    heads.start()
    attn = remote(attn_ref.at[own_rows], attn_ref.at[own_rows], 2)
    attn.start()
    heads.wait()
    attn.wait()


def backward_middle(
    back, info, resid, normed, misc, dy, routes, gains, const, router, own_w, other_w, prev, mix, padded
):
    local, width = dy.shape
    seq = info.shape[0]
    hh = own_w.shape[1]
    count = EXPERTS_FF * padded
    vmem = pl.BlockSpec(memory_space=pltpu.VMEM)
    return pl.pallas_call(
        functools.partial(back_kernel, padded),
        out_shape=[
            jax.ShapeDtypeStruct((local, width), single),
            jax.ShapeDtypeStruct((seq, width), half),
            jax.ShapeDtypeStruct((seq, hh), half),
            jax.ShapeDtypeStruct((local, width), single),
            jax.ShapeDtypeStruct((local, LANES), single),
            jax.ShapeDtypeStruct((24, width), single),
            jax.ShapeDtypeStruct((LANES, LANES), single),
        ],
        in_specs=[vmem] * 14,
        out_specs=[vmem] * 7,
        scratch_shapes=[
            pltpu.VMEM((count, LANES), half),
            pltpu.VMEM((local, width + LANES), half),
            pltpu.VMEM((local, width + LANES), half),
            pltpu.VMEM((local, hh), half),
            pltpu.SemaphoreType.DMA((3,)),
            pltpu.SemaphoreType.DMA((3,)),
        ],
        compiler_params=pltpu.CompilerParams(
            collective_id=2, has_side_effects=True, vmem_limit_bytes=56 << 20
        ),
        name="backward_middle",
    )(back, info, resid, normed, misc, dy, routes, gains, const, router, own_w, other_w, prev, mix)


def weight_kernel(
    x_ref,
    og_ref,
    hid_ref,
    pg_ref,
    pu_ref,
    out_ref,
    xt_ref,
    ogt_ref,
    send_ref,
    got_ref,
    own_ref,
    send_sem,
    recv_sem,
):
    f = pl.program_id(0)
    partner = {"tensor": 1 - lax.axis_index("tensor")}
    shape = out_ref.shape[0], out_ref.shape[2], out_ref.shape[3]

    @pl.when(f == 0)
    def _():
        barrier = pltpu.get_barrier_semaphore()
        pl.semaphore_signal(barrier, inc=1, device_id=partner, device_id_type=MESH)
        pl.semaphore_wait(barrier, 1)
        xt_ref[...] = x_ref[...].T
        ogt_ref[...] = og_ref[...].T

    def remote(number):
        return pltpu.make_async_remote_copy(
            src_ref=send_ref.at[number],
            dst_ref=got_ref.at[number],
            send_sem=send_sem.at[number],
            recv_sem=recv_sem.at[number],
            device_id=partner,
            device_id_type=MESH,
        )

    factors = (xt_ref, pg_ref), (xt_ref, pu_ref), (ogt_ref, hid_ref)
    for k, (left, right) in enumerate(factors):
        send_ref[f, k] = mm(left[...], right[1]).astype(half)
    remote(f).start()
    for k, (left, right) in enumerate(factors):
        own_ref[k] = mm(left[...], right[0])
    remote(f).wait_recv()
    for k in range(3):
        total = own_ref[k] + got_ref[f, k].astype(single)
        out_ref[:, k] = total.astype(half).reshape(shape)

    @pl.when(f == pl.num_programs(0) - 1)
    def _():
        for number in range(send_ref.shape[0]):
            remote(number).wait_send()


def weight_step(x, og, hidden, pg, pu, m):
    count, width = og.shape
    ff = hidden.shape[2]
    block = fit(ff, 256)
    steps = ff // block
    whole = pl.BlockSpec((count, width), lambda f: (0, 0))
    wide = pl.BlockSpec((2, count, block), lambda f: (0, 0, f))
    part = pl.BlockSpec((m, 3, width // m, block), lambda f: (0, 0, 0, f))
    return pl.pallas_call(
        weight_kernel,
        grid=(steps,),
        in_specs=[whole, whole, wide, wide, wide],
        out_specs=part,
        out_shape=jax.ShapeDtypeStruct((m, 3, width // m, ff), half),
        scratch_shapes=[
            pltpu.VMEM((width, count), half),
            pltpu.VMEM((width, count), half),
            pltpu.VMEM((steps, 3, width, block), half),
            pltpu.VMEM((steps, 3, width, block), half),
            pltpu.VMEM((3, width, block), single),
            pltpu.SemaphoreType.DMA((steps,)),
            pltpu.SemaphoreType.DMA((steps,)),
        ],
        compiler_params=pltpu.CompilerParams(
            collective_id=3, has_side_effects=True, vmem_limit_bytes=56 << 20
        ),
        cost_estimate=pl.CostEstimate(
            flops=12 * count * width * ff,
            bytes_accessed=12 * width * ff + 12 * count * ff,
            transcendentals=0,
        ),
        name="weight_step",
    )(x, og, hidden, pg, pu)


def tail_kernel(
    members,
    low,
    padded,
    eo_ref,
    qkv_ref,
    one_ref,
    proj_ref,
    outg_ref,
    x_ref,
    base_ref,
    resid_ref,
    info_ref,
    gain_ref,
    small_ref,
    grads_ref,
    proj_out_ref,
    outw_ref,
    tokens_ref,
    mixed_ref,
    small_out_ref,
    expert_ref,
    dense_ref,
    first_ref,
    stage_ref,
    second_ref,
    one_out_ref,
    one_in_ref,
    ffn_out_ref,
    ffn_in_ref,
    ffn_ref,
    mine_ref,
    pair_ref,
    near_ref,
    far_ref,
    dense_out_ref,
    send1,
    recv1,
    send2,
    recv2,
    pair_send,
    pair_recv,
    near_send,
    near_recv,
    far_send,
    far_recv,
    part_ref,
    sum_ref,
    part_sem,
    sum_sem,
):
    size = EXPERTS_FF
    me = lax.axis_index("dp")
    core = lax.axis_index("tensor")
    high = members // low
    inside, row = lax.rem(me, low), me // low
    local, width = base_ref.shape
    count = size * padded
    d_rows = outw_ref.shape[0]
    hh3 = qkv_ref.shape[1]
    step = fit(local, 256)
    partner = {"tensor": 1 - core}

    def beside(k):
        return row * low + flip(inside, k)

    def across(k):
        return lax.rem(row + k, high) * low + inside

    peers = [beside(k) for k in range(1, low)] + [across(k) for k in range(1, high)]
    barrier = pltpu.get_barrier_semaphore()
    for peer in peers:
        pl.semaphore_signal(barrier, inc=1, device_id={"dp": peer}, device_id_type=MESH)
    pl.semaphore_signal(barrier, inc=1, device_id=partner, device_id_type=MESH)
    pl.semaphore_wait(barrier, len(peers) + 1)

    def remote(src, dst, send, recv, device):
        return pltpu.make_async_remote_copy(
            src_ref=src,
            dst_ref=dst,
            send_sem=send,
            recv_sem=recv,
            device_id=device,
            device_id_type=MESH,
        )

    sent = []
    chunks = 2
    rows_each = width // chunks
    for c in range(chunks):
        lanes = pl.ds(c * rows_each, rows_each)
        grad = mm_tn(one_ref[:, lanes], qkv_ref[...])
        for j in range(members // chunks):
            owner = c * (members // chunks) + j
            dense_ref[owner, :, :hh3] = grad[j * d_rows : (j + 1) * d_rows].astype(half)
            dense_ref[owner, :, hh3:] = outg_ref[owner * d_rows : (owner + 1) * d_rows, :]
        for h in range(c * high // chunks, (c + 1) * high // chunks):
            for k in BESIDE:
                copy = remote(
                    dense_ref.at[h * low + flip(inside, k)],
                    first_ref.at[k - 1, h],
                    send1.at[k - 1, h],
                    recv1.at[k - 1, h],
                    {"dp": beside(k)},
                )
                copy.start()
                sent.append(copy)

    def one_part(rows):
        part = mm_nt(qkv_ref[rows, :], proj_ref[...])
        x = x_ref[rows, :].astype(single)
        mine_ref[18:19, :] += jnp.sum(part * x * rms_scale(x), axis=0, keepdims=True)
        return part

    mine_ref[...] = small_ref[...]

    @pl.loop(0, local // step)
    def _(r):
        rows = pl.ds(pl.multiple_of(r * step, step), step)
        there = pl.ds(pl.multiple_of((1 - core) * local + r * step, step), step)
        one_out_ref[rows, :] = one_part(there).astype(half)

    one_sent = remote(one_out_ref, one_in_ref, pair_send.at[0], pair_recv.at[0], partner)
    one_sent.start()

    @pl.loop(0, local // step)
    def _(r):
        rows = pl.ds(pl.multiple_of(r * step, step), step)
        here = pl.ds(pl.multiple_of(core * local + r * step, step), step)
        tokens_ref[rows, :] = one_part(here)

    eo_all = eo_ref.reshape(count, width)

    @pl.loop(0, local // step)
    def _(r):
        rows = pl.ds(pl.multiple_of(r * step, step), step)
        there = pl.ds(pl.multiple_of((1 - core) * local + r * step, step), step)
        ffn_out_ref[rows, :] = mm(slot_rows(info_ref[there, :], count), eo_all[...]).astype(half)

    ffn_sent = remote(ffn_out_ref, ffn_in_ref, pair_send.at[2], pair_recv.at[2], partner)
    ffn_sent.start()

    @pl.loop(0, local // step)
    def _(r):
        rows = pl.ds(pl.multiple_of(r * step, step), step)
        here = pl.ds(pl.multiple_of(core * local + r * step, step), step)
        ffn_ref[rows, :] = mm(slot_rows(info_ref[here, :], count), eo_all[...])

    def second(h):
        return remote(
            stage_ref.at[h],
            second_ref.at[row],
            send2.at[h],
            recv2.at[row],
            {"dp": h * low + inside},
        )

    pair = remote(mine_ref, pair_ref, pair_send.at[1], pair_recv.at[1], partner)
    pair.start()
    pair.wait()
    near_ref[inside] = mine_ref[...] + pair_ref[...]
    near = []
    for k in range(1, low):
        near.append(
            remote(
                near_ref.at[inside],
                near_ref.at[inside],
                near_send.at[k],
                near_recv.at[inside],
                {"dp": beside(k)},
            )
        )
        near[-1].start()

    groups = members // size

    def load(e):
        return [
            pltpu.make_async_copy(
                grads_ref.at[g * size + e], part_ref.at[e % 2, g], part_sem.at[e % 2, g]
            )
            for g in range(groups)
        ]

    def store(e):
        return pltpu.make_async_copy(sum_ref.at[e % 2], expert_ref.at[e], sum_sem.at[e % 2])

    for copy in load(0):
        copy.start()
    for e in range(size):
        if e + 1 < size:
            for copy in load(e + 1):
                copy.start()
        for copy in load(e):
            copy.wait()
        if e >= 2:
            store(e - 2).wait()
        total = part_ref[e % 2, 0].astype(single)
        for g in range(1, groups):
            total += part_ref[e % 2, g].astype(single)
        sum_ref[e % 2] = total
        store(e).start()
    for e in range(size - 2, size):
        store(e).wait()

    for h in range(high):
        for k in range(low - 1):
            remote(
                dense_ref.at[0], first_ref.at[k, h], send1.at[k, h], recv1.at[k, h], partner
            ).wait_recv()
        total = dense_ref[h * low + inside].astype(single)
        for k in range(low - 1):
            total += first_ref[k, h].astype(single)

        @pl.when(h == row)
        def _():
            dense_out_ref[...] = total

        @pl.when(h != row)
        def _():
            stage_ref[h] = total.astype(half)
            second(h).start()

    for k in range(1, low):
        block = lax.rem(inside + k, low)
        remote(
            mine_ref, near_ref.at[block], near_send.at[0], near_recv.at[block], partner
        ).wait_recv()
    total = near_ref[0]
    for k in range(1, low):
        total = total + near_ref[k]
    far_ref[row] = total
    far = []
    for k in range(1, high):
        far.append(
            remote(
                far_ref.at[row], far_ref.at[row], far_send.at[k], far_recv.at[row], {"dp": across(k)}
            )
        )
        far[-1].start()

    one_sent.wait()

    @pl.loop(0, local // step)
    def _(r):
        rows = pl.ds(pl.multiple_of(r * step, step), step)
        here = pl.ds(pl.multiple_of(core * local + r * step, step), step)
        x = x_ref[here, :].astype(single)
        scale = rms_scale(x)
        weighted = (tokens_ref[rows, :] + one_in_ref[rows, :].astype(single)) * gain_ref[0:1, :]
        mean = jnp.mean(weighted * x, axis=-1, keepdims=True)
        tokens_ref[rows, :] = resid_ref[rows, :] + scale * (weighted - x * scale * scale * mean)

    ffn_sent.wait()

    @pl.loop(0, local // step)
    def _(r):
        rows = pl.ds(pl.multiple_of(r * step, step), step)
        total = base_ref[rows, :] + ffn_ref[rows, :] + ffn_in_ref[rows, :].astype(single)
        mixed_ref[rows, :] = total.astype(half)

    for h in range(high):

        @pl.when(h != row)
        def _():
            remote(
                stage_ref.at[0], second_ref.at[h], send2.at[0], recv2.at[h], partner
            ).wait_recv()
            dense_out_ref[...] += second_ref[h].astype(single)
            second(h).wait_send()

    hh = outw_ref.shape[1]
    for c in range(3):
        proj_out_ref[c] = dense_out_ref[:, c * hh : (c + 1) * hh]
    outw_ref[...] = dense_out_ref[:, 3 * hh :]
    for k in range(1, high):
        block = lax.rem(row + k, high)
        remote(
            mine_ref, far_ref.at[block], far_send.at[0], far_recv.at[block], partner
        ).wait_recv()
    total = far_ref[0]
    for k in range(1, high):
        total = total + far_ref[k]
    small_out_ref[...] = total
    for copy in sent + near + far:
        copy.wait_send()


def tail(members, eo, qkv, one, proj, outg, x, base, resid, info, gains, small, grads, padded):
    low = 4
    high = members // low
    local, width = base.shape
    d_rows = width // members
    hh = outg.shape[1]
    wide = qkv.shape[1] + hh
    groups = members // EXPERTS_FF
    vmem = pl.BlockSpec(memory_space=pltpu.VMEM)
    hbm = pl.BlockSpec(memory_space=pltpu.HBM)
    dma = pltpu.SemaphoreType.DMA
    rows_half = pltpu.VMEM((local, width), half)
    small_one = pltpu.VMEM(small.shape, single)
    return pl.pallas_call(
        functools.partial(tail_kernel, members, low, padded),
        out_shape=[
            jax.ShapeDtypeStruct((3, d_rows, hh), single),
            jax.ShapeDtypeStruct((d_rows, hh), single),
            jax.ShapeDtypeStruct((local, width), single),
            jax.ShapeDtypeStruct((local, width), half),
            jax.ShapeDtypeStruct(small.shape, single),
            jax.ShapeDtypeStruct((EXPERTS_FF,) + grads.shape[1:], single),
        ],
        in_specs=[vmem] * 11 + [hbm],
        out_specs=[vmem] * 5 + [hbm],
        scratch_shapes=[
            pltpu.VMEM((members, d_rows, wide), half),
            pltpu.VMEM((low - 1, high, d_rows, wide), half),
            pltpu.VMEM((high, d_rows, wide), half),
            pltpu.VMEM((high, d_rows, wide), half),
            rows_half,
            rows_half,
            rows_half,
            rows_half,
            pltpu.VMEM((local, width), single),
            small_one,
            small_one,
            pltpu.VMEM((low,) + small.shape, single),
            pltpu.VMEM((high,) + small.shape, single),
            pltpu.VMEM((d_rows, wide), single),
            dma((low - 1, high)),
            dma((low - 1, high)),
            dma((high,)),
            dma((high,)),
            dma((3,)),
            dma((3,)),
            dma((low,)),
            dma((low,)),
            dma((high,)),
            dma((high,)),
            pltpu.VMEM((2, groups) + grads.shape[1:], half),
            pltpu.VMEM((2,) + grads.shape[1:], single),
            dma((2, groups)),
            dma((2,)),
        ],
        compiler_params=pltpu.CompilerParams(
            collective_id=4, has_side_effects=True, vmem_limit_bytes=60 << 20
        ),
        name="tail",
    )(eo, qkv, one, proj, outg, x, base, resid, info, gains, small, grads)


def per_device(
    tokens,
    segment_ids,
    routes,
    prev_logits,
    cotangent,
    proj_weight,
    out_weight,
    norm_gain,
    expert_weight,
    router,
    constant_vectors,
    gate_mixing,
):
    members = lax.axis_size("dp")
    groups = members // EXPERTS_FF
    cubes = [[g * EXPERTS_FF + i for i in range(EXPERTS_FF)] for g in range(groups)]
    core = lax.axis_index("tensor")
    d_rows, hh = out_weight.shape
    per_core = -(-CAPACITY // 2)
    padded = -(-(per_core + 3) // 16) * 16

    def in_group(blocks):
        return lax.all_to_all(blocks, "dp", 0, 0, axis_index_groups=cubes, tiled=True)

    def plain_tail(eo, qkv, one, proj, outg, x, base, resid, gains, small, grads):
        ffn = pair_sum(mm_tn(onehot, eo.reshape(-1, width)))
        part = mm_nt(qkv, proj)
        scale = rms_scale(x)
        small = small.at[18].set(jnp.sum(part * x * scale, axis=0))
        weighted = pair_sum(part) * gains[0]
        x, scale = half_of(x, core), half_of(scale, core)
        mean = jnp.mean(weighted * x, axis=-1, keepdims=True)
        tokens_grad = resid + scale * (weighted - x * scale * scale * mean)
        dense = jnp.concatenate([mm_tn(one, qkv).astype(half), outg], 1)
        dense = lax.all_to_all(dense.reshape(members, d_rows, -1), "dp", 0, 0, tiled=True)
        dense = jnp.sum(dense.astype(single), axis=0)
        grads = grads.reshape((groups, EXPERTS_FF) + grads.shape[1:]).astype(single)
        return (
            dense[:, : 3 * hh].reshape(d_rows, 3, hh).transpose(1, 0, 2),
            dense[:, 3 * hh :],
            tokens_grad,
            (base + ffn).astype(half),
            lax.psum(small, ("dp", "tensor")),
            jnp.sum(grads, axis=0),
        )

    pack = jnp.concatenate(
        [
            proj_weight.transpose(1, 0, 2).reshape(d_rows, 3 * hh),
            out_weight,
            norm_gain.T,
            constant_vectors.T,
            router,
        ],
        1,
    )
    columns = pack.shape[1]
    pack = jnp.pad(pack, ((0, 0), (0, -columns % LANES)))
    ids = jnp.concatenate([segment_ids, routes[0].T], 0)
    ids = jnp.pad(ids, ((0, 5), (0, 0)))
    full_pack, tokens_all, dy_rows, onehot, info, my_down = start(
        pack, tokens[0], cotangent[0], ids, expert_weight, members, per_core, padded
    )
    full_pack, expert_weight = lax.optimization_barrier((full_pack, expert_weight))
    full_pack = full_pack.reshape(members * d_rows, -1)[:, :columns]
    width = members * d_rows
    proj_full = full_pack[:, : 3 * hh]
    outw_own = full_pack[:, 3 * hh : 4 * hh]
    outw_other = swap(outw_own)
    rest = full_pack[:, 4 * hh :]
    gains = rest[:, :2].T.astype(single)
    const_f = rest[:, 2:4].T.astype(single)
    router_full = rest[:, 4:]
    in_weight = jnp.broadcast_to(
        expert_weight[None, :, :2], (groups, EXPERTS_FF, 2) + expert_weight.shape[2:]
    ).reshape((members, 2) + expert_weight.shape[2:])
    my_in = lax.all_to_all(in_weight, "dp", 0, 0, tiled=True)

    x_rows = tokens[0].astype(single)
    local_rows = x_rows.shape[0]
    x_all = tokens_all.astype(single)
    scale_all = rms_scale(x_all)
    full_one = (x_all * scale_all * gains[0]).astype(half)
    scale_one = half_of(scale_all, core)
    seq = full_one.shape[0]
    qkv = mm(full_one, proj_full).astype(half)
    size = fit(seq, 256)
    starts = info[0]
    bounds = block_bounds(starts, info[1], size)
    columns = info.T
    heads_full, heads_out, lse = attention_forward(qkv, bounds, starts, size)
    prev_rows = prev_logits[0]
    mixed_prev = jnp.dot(prev_rows, gate_mixing, precision=HIGH)
    mixed_prev = jnp.pad(mixed_prev, ((0, 0), (0, LANES - EXPERTS)))
    router_wide = jnp.pad(router_full, ((0, 0), (0, LANES - router_full.shape[1])))
    back_grad, gated_out, got_rows, out_grad, hidden, pg, pu, resid, normed_two, misc = experts(
        my_down,
        my_in,
        dy_rows,
        heads_out,
        tokens[0],
        outw_own,
        outw_other,
        gains,
        router_wide,
        mixed_prev,
        routes[0],
        onehot,
        padded,
    )
    count = EXPERTS_FF * padded
    grads_sent = weight_step(
        got_rows.reshape(count, width),
        out_grad.reshape(count, width),
        hidden,
        pg,
        pu,
        1 if d_rows % 16 else members,
    )
    back_out = in_group(gated_out)
    back_grad, grads_sent, back_out = lax.optimization_barrier((back_grad, grads_sent, back_out))
    if d_rows % 16:
        grads_sent = grads_sent.reshape(3, members, d_rows, -1).transpose(1, 0, 2, 3)
    grads_got = lax.all_to_all(grads_sent, "dp", 0, 0, tiled=True)

    mix_wide = jnp.pad(gate_mixing, ((0, LANES - EXPERTS), (0, LANES - EXPERTS)))
    prev_wide = jnp.pad(prev_rows, ((0, 0), (0, LANES - EXPERTS)))
    resid_grad, attn_all, heads_grad, base, prev_grad, small, mixing_grad = backward_middle(
        back_grad,
        columns,
        resid,
        normed_two,
        misc,
        cotangent[0],
        routes[0],
        gains,
        const_f,
        router_wide,
        outw_own,
        outw_other,
        prev_wide,
        mix_wide,
        padded,
    )
    out_w_grad = mm_tn(attn_all, heads_out)
    qkv_grad = attention_backward(qkv, heads_grad, heads_full, lse, bounds, starts, size)
    qkv_grad, grads_got = lax.optimization_barrier((qkv_grad, grads_got))
    out_w_grad = out_w_grad.astype(half)
    if d_rows % 16 or members != 16:
        outs = plain_tail(
            back_out, qkv_grad, full_one, proj_full, out_w_grad, x_all, base, resid_grad, gains, small, grads_got
        )
    else:
        outs = tail(
            members,
            back_out,
            qkv_grad,
            full_one,
            proj_full,
            out_w_grad,
            tokens_all,
            base,
            resid_grad,
            columns,
            gains,
            small,
            grads_got,
            padded,
        )
    proj_shard, outw_shard, tokens_grad, mixed, small, expert_shard = outs
    mixing_total = small[20:22].reshape(EXPERTS, LANES)[:, :EXPERTS]
    features = lax.dynamic_slice_in_dim(small, lax.axis_index("dp") * d_rows, d_rows, 1)
    return (
        mixed[None],
        tokens_grad[None],
        prev_grad[None, :, :EXPERTS],
        proj_shard,
        outw_shard,
        features[18:20],
        expert_shard,
        features[:16].T,
        features[16:18],
        mixing_total,
    )


def solution(mesh):
    return jax.shard_map(
        per_device,
        mesh=mesh,
        in_specs=(
            P("dp", "tensor", None),
            P("dp", "tensor"),
            P("dp", "tensor", None),
            P("dp", "tensor", None),
            P("dp", "tensor", None),
            P(None, "dp", "tensor"),
            P("dp", "tensor"),
            P(None, "dp"),
            P(None, None, "dp", "tensor"),
            P("dp", None),
            P(None, "dp"),
            P(),
        ),
        out_specs=(
            P("dp", "tensor", None),
            P("dp", "tensor", None),
            P("dp", "tensor", None),
            P(None, "dp", "tensor"),
            P("dp", "tensor"),
            P(None, "dp"),
            P(None, None, "dp", "tensor"),
            P("dp", None),
            P(None, "dp"),
            P(),
        ),
        check_vma=False,
    )
```

```python
import functools

import jax
import jax.numpy as jnp
from jax import lax
from jax.experimental import pallas as pl
from jax.experimental.pallas import tpu as pltpu
from jax.sharding import PartitionSpec as P

HEAD_DIM = 64
EXPERTS_FF = 8
EXPERTS = 12
CAPACITY = 341


EPS = 1e-05
HIGH = lax.Precision.HIGHEST
NEG = -1e30
LANES = 128
DOCS = 8
LOG2E = 1.4426950408889634
MESH = pl.DeviceIdType.MESH
single = jnp.float32
half = jnp.bfloat16


def rms_scale(rows):
    return lax.rsqrt(jnp.mean(rows * rows, axis=-1, keepdims=True) + EPS)


def softmax_last(values):
    peak = jnp.max(values, axis=-1, keepdims=True)
    expo = jnp.exp(values - peak)
    return expo / jnp.sum(expo, axis=-1, keepdims=True)


def mm(a, b):
    return jnp.dot(a, b, preferred_element_type=single)


def mm_nt(a, b):
    return lax.dot_general(a, b, (((1,), (1,)), ((), ())), preferred_element_type=single)


def mm_tn(a, b):
    return lax.dot_general(a, b, (((0,), (0,)), ((), ())), preferred_element_type=single)


def swap(x):
    return lax.ppermute(x, "tensor", [(0, 1), (1, 0)])


def in_order(own, other):
    first = lax.axis_index("tensor") == 0
    return jnp.concatenate([jnp.where(first, own, other), jnp.where(first, other, own)], 0)


def half_of(full, which):
    count = full.shape[0] // 2
    return lax.dynamic_slice_in_dim(full, which * count, count, 0)


def pair_sum(full):
    core = lax.axis_index("tensor")
    other = swap(half_of(full, 1 - core).astype(half))
    return half_of(full, core) + other.astype(single)


def fit(seq, want):
    return want if seq % want == 0 else seq

def block_bounds(start, end, size):
    edges = start.reshape(-1, size)
    number = jnp.arange(edges.shape[0], dtype=jnp.int32)
    low = edges[:, 0] // size
    plain = jnp.clip((edges[:, -1] + size - 1) // size, low, number)
    high = end.reshape(-1, size)[:, -1] // size
    clear = jnp.sum((edges[None, :, -1] <= number[:, None] * size).astype(jnp.int32), axis=1)
    clear = jnp.clip(clear, number + 1, high + 1)
    return jnp.stack([low, plain, high, clear])


def head_lanes(h, rows):
    lane = lax.broadcasted_iota(jnp.int32, (rows, LANES), 1)
    return (lane < HEAD_DIM) if h % 2 == 0 else (lane >= HEAD_DIM)

def fwd_kernel(heads, bounds, q_ref, k_ref, v_ref, start_ref, o_ref, low_ref, lse_ref, s_ref, m_ref, l_ref, acc_ref, qm_ref):
    size = q_ref.shape[0]
    i = pl.program_id(0)
    low, plain = bounds[0, i], bounds[1, i]
    factor = LOG2E * HEAD_DIM ** -0.5
    for h in range(heads):
        pair = pl.ds(h // 2 * LANES, LANES)
        qm_ref[h] = jnp.where(head_lanes(h, size), q_ref[:, pair], 0).astype(half)
    m_ref[...] = jnp.full(m_ref.shape, NEG, single)
    l_ref[...] = jnp.zeros(l_ref.shape, single)
    acc_ref[...] = jnp.zeros(acc_ref.shape, single)

    def score(j, masked):
        rows = pl.ds(pl.multiple_of(j * size, size), size)
        if masked:
            row = i * size + lax.broadcasted_iota(jnp.int32, (size, size), 0)
            col = j * size + lax.broadcasted_iota(jnp.int32, (size, size), 1)
            allowed = (col <= row) & (col >= start_ref[...])
        for h in range(heads):
            s = mm_nt(qm_ref[h], k_ref[rows, pl.ds(h // 2 * LANES, LANES)])
            if masked:
                s = jnp.where(allowed, s, NEG)
            s_ref[h, j] = s
            m = m_ref[h]
            for c in range(size // LANES):
                m = jnp.maximum(m, s[:, c * LANES : (c + 1) * LANES])
            m_ref[h] = m

    pl.loop(low, plain)(lambda j: score(j, True))
    pl.loop(plain, i)(lambda j: score(j, False))
    score(i, True)
    for h in range(heads):
        m_ref[h] = jnp.broadcast_to(jnp.max(m_ref[h], axis=1, keepdims=True) * factor, (size, LANES))

    def gather(j):
        rows = pl.ds(pl.multiple_of(j * size, size), size)
        for h in range(heads):
            s = s_ref[h, j]
            m = m_ref[h]
            l = l_ref[h]
            parts = []
            for c in range(size // LANES):
                p = jnp.exp2(s[:, c * LANES : (c + 1) * LANES] * factor - m)
                l = l + p
                parts.append(p.astype(half))
            l_ref[h] = l
            acc_ref[h] += jnp.dot(jnp.concatenate(parts, 1), v_ref[rows, pl.ds(h // 2 * LANES, LANES)], preferred_element_type=single)

    pl.loop(low, i + 1)(gather)
    lane = lax.broadcasted_iota(jnp.int32, (size, LANES), 1)
    lse = jnp.zeros((size, LANES), single)
    for h in range(0, heads, 2):
        outs = []
        for k in (h, h + 1):
            l = jnp.sum(l_ref[k], axis=1, keepdims=True)
            outs.append(acc_ref[k] / l)
            lse = jnp.where(lane == k, m_ref[k] + jnp.log2(l), lse)
        out = jnp.where(lane < HEAD_DIM, outs[0], outs[1])
        o_ref[:, pl.ds(h // 2 * LANES, LANES)] = out
        low_ref[:, pl.ds(h // 2 * LANES, LANES)] = out.astype(half)
    lse_ref[...] = lse

def attention_forward(qkv, seg_bounds, starts, size):
    seq = qkv.shape[0]
    hh = qkv.shape[1] // 3
    heads = hh // HEAD_DIM
    return pl.pallas_call(
        functools.partial(fwd_kernel, heads),
        grid_spec=pltpu.PrefetchScalarGridSpec(
            num_scalar_prefetch=1,
            grid=(seq // size,),
            in_specs=[
                pl.BlockSpec((size, hh), lambda i, b: (i, 0)),
                pl.BlockSpec((seq, hh), lambda i, b: (0, 1)),
                pl.BlockSpec((seq, hh), lambda i, b: (0, 2)),
                pl.BlockSpec((size, 1), lambda i, b: (i, 0)),
            ],
            out_specs=[
                pl.BlockSpec((size, hh), lambda i, b: (i, 0)),
                pl.BlockSpec((size, hh), lambda i, b: (i, 0)),
                pl.BlockSpec((size, LANES), lambda i, b: (i, 0)),
            ],
            scratch_shapes=[
                pltpu.VMEM((heads, seq // size, size, size), single),
                pltpu.VMEM((heads, size, LANES), single),
                pltpu.VMEM((heads, size, LANES), single),
                pltpu.VMEM((heads, size, LANES), single),
                pltpu.VMEM((heads, size, LANES), half),
            ],
        ),
        out_shape=[
            jax.ShapeDtypeStruct((seq, hh), single),
            jax.ShapeDtypeStruct((seq, hh), half),
            jax.ShapeDtypeStruct((seq, LANES), single),
        ],
        compiler_params=pltpu.CompilerParams(vmem_limit_bytes=48 << 20),
        cost_estimate=pl.CostEstimate(flops=4 * seq * seq * LANES * heads, bytes_accessed=16 * seq * hh, transcendentals=0),
    )(seg_bounds, qkv, qkv, qkv, starts[:, None])

def bwd_kernel(
    heads, bounds, q_ref, k_ref, v_ref, do_ref, o_ref, lse_ref, start_ref, out_ref, dq_ref, dk_ref, dv_ref, stat_ref
):
    size = k_ref.shape[0]
    j = pl.program_id(0)
    high, clear = bounds[2, j], bounds[3, j]
    factor = LOG2E * HEAD_DIM ** -0.5
    hh = k_ref.shape[1]

    @pl.when(j == 0)
    def _():
        dq_ref[...] = jnp.zeros(dq_ref.shape, single)
        feature = lax.broadcasted_iota(jnp.int32, (hh, LANES), 0)
        lane = lax.broadcasted_iota(jnp.int32, (hh, LANES), 1)
        pick = (feature // HEAD_DIM + 8 == lane).astype(half)

        @pl.loop(0, q_ref.shape[0] // size)
        def _(i):
            rows = pl.ds(pl.multiple_of(i * size, size), size)
            product = o_ref[rows, :] * do_ref[rows, :].astype(single)
            top = product.astype(half)
            low = (product - top.astype(single)).astype(half)
            both = mm(top, pick) + mm(low, pick) + lse_ref[rows, :]
            stat_ref[:, rows] = both.T[:16, :]

    dk_ref[...] = jnp.zeros(dk_ref.shape, single)
    dv_ref[...] = jnp.zeros(dv_ref.shape, single)

    def step(i, masked):
        rows = pl.ds(pl.multiple_of(i * size, size), size)
        if masked:
            key = j * size + lax.broadcasted_iota(jnp.int32, (size, size), 0)
            query = i * size + lax.broadcasted_iota(jnp.int32, (size, size), 1)
            allowed = (key <= query) & (key >= start_ref[:, rows])
        for pair in range(heads // 2):
            lanes = pl.ds(pair * LANES, LANES)
            k, v = k_ref[:, lanes], v_ref[:, lanes]
            q, do = q_ref[rows, lanes], do_ref[rows, lanes]
            ps, dss, qs, dos, ks = [], [], [], [], []
            for h in (2 * pair, 2 * pair + 1):
                mine = head_lanes(h, size)
                qm = jnp.where(mine, q, 0).astype(half)
                dom = jnp.where(mine, do, 0).astype(half)
                s = mm_nt(k, qm) * factor - stat_ref[pl.ds(h, 1), rows]
                if masked:
                    s = jnp.where(allowed, s, NEG)
                p = jnp.exp2(s)
                ds = p * (mm_nt(v, dom) - stat_ref[pl.ds(8 + h, 1), rows])
                ps.append(p.astype(half))
                dss.append(ds.astype(half))
                qs.append(qm)
                dos.append(dom)
                ks.append(jnp.where(mine, k, 0).astype(half))
            dv_ref[:, lanes] += jnp.dot(jnp.concatenate(ps, 1), jnp.concatenate(dos, 0), preferred_element_type=single)
            dk_ref[:, lanes] += jnp.dot(jnp.concatenate(dss, 1), jnp.concatenate(qs, 0), preferred_element_type=single)
            dq_ref[rows, lanes] += mm_tn(jnp.concatenate(dss, 0), jnp.concatenate(ks, 0))

    step(j, True)
    pl.loop(j + 1, clear)(lambda i: step(i, False))
    pl.loop(clear, high + 1)(lambda i: step(i, True))
    mine = pl.ds(pl.multiple_of(j * size, size), size)
    out_ref[mine, pl.ds(hh, hh)] = (dk_ref[...] * HEAD_DIM ** -0.5).astype(half)
    out_ref[mine, pl.ds(2 * hh, hh)] = dv_ref[...].astype(half)
    out_ref[mine, pl.ds(0, hh)] = (dq_ref[mine, :] * HEAD_DIM ** -0.5).astype(half)

def attention_backward(qkv, do, heads_out, lse, seg_bounds, starts, size):
    seq = qkv.shape[0]
    hh = qkv.shape[1] // 3
    heads = hh // HEAD_DIM
    return pl.pallas_call(
        functools.partial(bwd_kernel, heads),
        grid_spec=pltpu.PrefetchScalarGridSpec(
            num_scalar_prefetch=1,
            grid=(seq // size,),
            in_specs=[
                pl.BlockSpec((seq, hh), lambda j, b: (0, 0)),
                pl.BlockSpec((size, hh), lambda j, b: (j, 1)),
                pl.BlockSpec((size, hh), lambda j, b: (j, 2)),
                pl.BlockSpec((seq, hh), lambda j, b: (0, 0)),
                pl.BlockSpec((seq, hh), lambda j, b: (0, 0)),
                pl.BlockSpec((seq, LANES), lambda j, b: (0, 0)),
                pl.BlockSpec((1, seq), lambda j, b: (0, 0)),
            ],
            out_specs=pl.BlockSpec((seq, 3 * hh), lambda j, b: (0, 0)),
            scratch_shapes=[
                pltpu.VMEM((seq, hh), single),
                pltpu.VMEM((size, hh), single),
                pltpu.VMEM((size, hh), single),
                pltpu.VMEM((16, seq), single),
            ],
        ),
        out_shape=jax.ShapeDtypeStruct((seq, 3 * hh), half),
        compiler_params=pltpu.CompilerParams(vmem_limit_bytes=48 << 20),
        cost_estimate=pl.CostEstimate(flops=10 * seq * seq * LANES * heads, bytes_accessed=20 * seq * hh, transcendentals=0),
    )(seg_bounds, qkv, qkv, qkv, do, heads_out, lse, starts[None, :])


def flip(number, k):
    out = 0
    for bit in (1, 2, 4):
        digit = lax.rem(number // bit, 2)
        out = out + bit * ((1 - digit) if k & bit else digit)
    return out


BESIDE = (3, 1, 2)
NEAR = (3, 4, 5, 2, 6, 1, 7)
PAIRS = ((0, 3), (4, 5), (2, 6), (1, 7))


def start_kernel(
    members,
    low,
    per_core,
    padded,
    pack_ref,
    tok_ref,
    dy_ref,
    ids_ref,
    w_ref,
    full_ref,
    all_ref,
    rows_ref,
    hot_ref,
    info_ref,
    down_ref,
    in_ref,
    ids_all_ref,
    dy_all_ref,
    place_ref,
    send_sem,
    recv_sem,
    own_sem,
    swap_send,
    swap_recv,
    down_send,
    down_recv,
):
    size = EXPERTS_FF
    me = lax.axis_index("dp")
    core = lax.axis_index("tensor")
    high = members // low
    inside, row = lax.rem(me, low), me // low
    mine = lax.rem(me, size)
    base = me - mine
    local = tok_ref.shape[0]
    seq = 2 * local
    partner = {"tensor": 1 - core}

    def beside(k):
        return row * low + flip(inside, k)

    def across(k):
        return lax.rem(row + k, high) * low + inside

    peers = [beside(k) for k in BESIDE] + [across(k) for k in range(1, high)]
    groups = members // size

    def device_at(g, k):
        return lax.rem(base + g * size, members) + flip(mine, k)

    distant = [(g, k) for k in (0,) + NEAR for g in range(groups) if g or k]
    peers += [device_at(g, k) for g, k in distant]
    barrier = pltpu.get_barrier_semaphore()
    for peer in peers:
        pl.semaphore_signal(barrier, inc=1, device_id={"dp": peer}, device_id_type=MESH)
    pl.semaphore_signal(barrier, inc=1, device_id=partner, device_id_type=MESH)
    pl.semaphore_wait(barrier, len(peers) + 1)

    def remote(src, dst, send, recv, device):
        return pltpu.make_async_remote_copy(
            src_ref=src,
            dst_ref=dst,
            send_sem=send,
            recv_sem=recv,
            device_id=device,
            device_id_type=MESH,
        )

    def push(source, block, target, slot):
        copy = remote(
            source, full_ref.at[block], send_sem.at[slot], recv_sem.at[block], {"dp": target}
        )
        copy.start()
        return copy

    def arrived(block):
        remote(
            pack_ref, full_ref.at[block], send_sem.at[0], recv_sem.at[block], {"dp": peers[0]}
        ).wait_recv()

    sent = [push(pack_ref, me, across(k), k) for k in range(1, high)]
    sent += [push(pack_ref, me, beside(k), high + k) for k in BESIDE]
    own_rows = pl.ds(pl.multiple_of(core * local, local), local)
    swaps = [
        remote(ids_ref, ids_all_ref.at[core], swap_send.at[0], swap_recv.at[0], partner),
        remote(dy_ref, dy_all_ref.at[own_rows], swap_send.at[1], swap_recv.at[1], partner),
        remote(tok_ref, all_ref.at[own_rows], swap_send.at[2], swap_recv.at[2], partner),
    ]
    owns = [
        pltpu.make_async_copy(ids_ref, ids_all_ref.at[core], own_sem.at[0]),
        pltpu.make_async_copy(dy_ref, dy_all_ref.at[own_rows], own_sem.at[1]),
        pltpu.make_async_copy(tok_ref, all_ref.at[own_rows], own_sem.at[2]),
        pltpu.make_async_copy(pack_ref, full_ref.at[me], own_sem.at[3]),
        pltpu.make_async_copy(w_ref.at[mine, 2], down_ref.at[me], own_sem.at[4]),
    ]
    owns += [
        pltpu.make_async_copy(
            w_ref.at[:, pl.ds(0, 2)], in_ref.at[pl.ds(g * size, size)], own_sem.at[5 + g]
        )
        for g in range(groups)
    ]
    for copy in swaps + owns:
        copy.start()

    swaps[0].wait()
    owns[0].wait()
    ids = jnp.concatenate([ids_all_ref[0], ids_all_ref[1]], 1)
    seg = ids[:1]
    number = lax.broadcasted_iota(jnp.int32, (8, seq), 0)
    starts = jnp.zeros((1, seq), jnp.int32)
    ends = jnp.zeros((1, seq), jnp.int32)
    total = jnp.zeros((1, 1), jnp.int32)
    for d in range(DOCS):
        here = seg == d
        starts = jnp.where(here, total, starts)
        total = total + jnp.sum(here.astype(jnp.int32), axis=1, keepdims=True)
        ends = jnp.where(here, total - 1, ends)
    row16 = lax.broadcasted_iota(jnp.int32, (16, LANES), 0)
    first = lax.broadcasted_iota(jnp.int32, (LANES, LANES), 0)
    second = lax.broadcasted_iota(jnp.int32, (LANES, LANES), 1)
    upper = (first < second).astype(half)
    before = jnp.zeros((16, 1), single)
    for c in range(seq // LANES):
        lanes = slice(c * LANES, (c + 1) * LANES)
        member = (ids[1:2, lanes] == row16) | (ids[2:3, lanes] == row16)
        member = jnp.where(member & (row16 < size), 1.0, 0.0)
        position = mm(member.astype(half), upper) + before
        before = before + jnp.sum(member, axis=1, keepdims=True)
        place = position - (core * per_core).astype(single)
        kept = (member > 0.5) & (position < CAPACITY) & (place >= 0) & (place < per_core)
        place_ref[:, lanes] = jnp.where(kept, place, -1.0).astype(jnp.int32)
    slot = lax.broadcasted_iota(jnp.int32, (padded, seq), 0)
    for e in range(size):
        hot_ref[e * padded : (e + 1) * padded, :] = jnp.where(
            place_ref[e : e + 1, :] == slot, 1.0, 0.0
        ).astype(half)

    info = jnp.where(number == 0, starts, jnp.where(number == 1, ends, -1))
    for k in range(2):
        chosen = jnp.full((1, seq), -1, jnp.int32)
        for e in range(size):
            place = place_ref[e : e + 1, :]
            chosen = jnp.where(
                (ids[k + 1 : k + 2] == e) & (place >= 0), place + e * padded, chosen
            )
        info = jnp.where(number == k + 2, chosen, info)
    info_ref[...] = info

    for k in range(1, high):
        block = across(high - k)
        arrived(block)
        for step in BESIDE:
            sent.append(push(full_ref.at[block], block, beside(step), high + k * low + step))

    for g, k in distant:
        copy = remote(
            w_ref.at[flip(mine, k), 2],
            down_ref.at[me],
            down_send.at[g * size + k],
            down_recv.at[me],
            {"dp": device_at(g, k)},
        )
        copy.start()
        sent.append(copy)

    swaps[1].wait()
    owns[1].wait()
    for e in range(0, size, 2):
        slots = slice(e * padded, (e + 2) * padded)
        rows = mm(hot_ref[slots, :], dy_all_ref[...])
        rows_ref[e : e + 2] = rows.astype(half).reshape(2, padded, rows.shape[1])
    for k in BESIDE:
        block = beside(k)
        arrived(block)
        for step in range(1, high):
            arrived(lax.rem(block + step * low, members))
    for g, k in distant:
        block = device_at((groups - g) % groups, k)
        remote(
            w_ref.at[0, 2], down_ref.at[block], down_send.at[0], down_recv.at[block], partner
        ).wait_recv()
    for copy in sent:
        copy.wait_send()
    for copy in owns[2:]:
        copy.wait()
    swaps[2].wait()


def start(pack, tokens, dy, ids, w, members, per_core, padded):
    low = 4
    high = members // low
    local, width = tokens.shape
    count = EXPERTS_FF * padded
    any_spec = pl.BlockSpec(memory_space=pl.ANY)
    vmem = pl.BlockSpec(memory_space=pltpu.VMEM)
    hbm = pl.BlockSpec(memory_space=pltpu.HBM)
    dma = pltpu.SemaphoreType.DMA
    return pl.pallas_call(
        functools.partial(start_kernel, members, low, per_core, padded),
        out_shape=[
            jax.ShapeDtypeStruct((members,) + pack.shape, half),
            jax.ShapeDtypeStruct((2 * local, width), half),
            jax.ShapeDtypeStruct((EXPERTS_FF, padded, width), half),
            jax.ShapeDtypeStruct((count, 2 * local), half),
            jax.ShapeDtypeStruct((8, 2 * local), jnp.int32),
            jax.ShapeDtypeStruct((members,) + w.shape[2:], half),
            jax.ShapeDtypeStruct((members, 2) + w.shape[2:], half),
        ],
        in_specs=[any_spec, hbm, hbm, any_spec, hbm],
        out_specs=[any_spec] * 2 + [vmem] * 3 + [any_spec, hbm],
        scratch_shapes=[
            pltpu.VMEM((2, 8, local), jnp.int32),
            pltpu.VMEM((2 * local, width), half),
            pltpu.VMEM((16, 2 * local), jnp.int32),
            dma((high * (low + 1),)),
            dma((members,)),
            dma((5 + members // EXPERTS_FF,)),
            dma((3,)),
            dma((3,)),
            dma((members,)),
            dma((members,)),
        ],
        compiler_params=pltpu.CompilerParams(
            collective_id=0, has_side_effects=True, vmem_limit_bytes=40 << 20
        ),
        name="start",
    )(pack, tokens, dy, ids, w)


def experts_kernel(
    members,
    padded,
    down_hbm_ref,
    in_ref,
    dy_hbm_ref,
    ho_ref,
    tok_ref,
    own_w_ref,
    other_w_ref,
    gain_ref,
    router_ref,
    prev_ref,
    routes_ref,
    hot_hbm_ref,
    back_ref,
    out_ref,
    x_ref,
    og_ref,
    hid_ref,
    pg_ref,
    pu_ref,
    resid_ref,
    normed_ref,
    misc_ref,
    ho_in_ref,
    both_ref,
    acc_ref,
    stage_ref,
    row_ref,
    win_ref,
    down_ref,
    dy_ref,
    ig_ref,
    spill_ref,
    gate_ref,
    dot_ref,
    hot_ref,
    x_send,
    x_recv,
    dy_send,
    dy_recv,
    own_sem,
    swap_send,
    swap_recv,
    ig_send,
    ig_recv,
    spill_sem,
):
    size = EXPERTS_FF
    groups = members // size
    me = lax.axis_index("dp")
    core = lax.axis_index("tensor")
    mine = lax.rem(me, size)
    base = me - mine
    local, width = tok_ref.shape
    partner = {"tensor": 1 - core}
    near = [base + lax.rem(mine + k, size) for k in range(1, size)]
    barrier = pltpu.get_barrier_semaphore()
    for peer in near:
        pl.semaphore_signal(barrier, inc=1, device_id={"dp": peer}, device_id_type=MESH)
    pl.semaphore_signal(barrier, inc=1, device_id=partner, device_id_type=MESH)
    pl.semaphore_wait(barrier, size)

    def remote(src, dst, send, recv, device):
        return pltpu.make_async_remote_copy(
            src_ref=src,
            dst_ref=dst,
            send_sem=send,
            recv_sem=recv,
            device_id=device,
            device_id_type=MESH,
        )

    own_rows = pl.ds(pl.multiple_of(core * local, local), local)
    other_rows = pl.ds(pl.multiple_of((1 - core) * local, local), local)
    heads = remote(ho_ref.at[other_rows], ho_in_ref, swap_send.at[0], swap_recv.at[0], partner)
    heads.start()
    load_hot = pltpu.make_async_copy(hot_hbm_ref, hot_ref, own_sem.at[4])
    load_hot.start()
    waits = []
    for k in NEAR:
        to = flip(mine, k)
        copy = remote(
            dy_hbm_ref.at[to], dy_ref.at[mine], dy_send.at[k], dy_recv.at[k], {"dp": base + to}
        )
        copy.start()
        waits.append(copy)
    pair_in = remote(in_ref, win_ref.at[1], swap_send.at[2], swap_recv.at[2], partner)
    pair_in.start()
    pair_down = remote(down_hbm_ref, down_ref.at[1], swap_send.at[3], swap_recv.at[3], partner)
    pair_down.start()
    owns = [
        pltpu.make_async_copy(in_ref, win_ref.at[0], own_sem.at[1]),
        pltpu.make_async_copy(dy_hbm_ref.at[mine], dy_ref.at[mine], own_sem.at[2]),
        pltpu.make_async_copy(down_hbm_ref, down_ref.at[0], own_sem.at[3]),
    ]
    for copy in owns:
        copy.start()

    step = fit(local, 256)
    heads.wait()

    @pl.loop(0, local // step)
    def _(r):
        rows = pl.ds(pl.multiple_of(r * step, step), step)
        mine_rows = pl.ds(pl.multiple_of(core * local + r * step, step), step)
        resid = tok_ref[rows, :].astype(single)
        resid += mm_nt(ho_ref[mine_rows, :], own_w_ref[...])
        resid += mm_nt(ho_in_ref[rows, :], other_w_ref[...])
        resid_ref[rows, :] = resid
        normed = (resid * rms_scale(resid) * gain_ref[1:2, :]).astype(half)
        normed_ref[rows, :] = normed
        router = mm(normed, router_ref[...])
        lane = lax.broadcasted_iota(jnp.int32, (step, LANES), 1)
        logits = jnp.where(lane < EXPERTS, router + prev_ref[rows, :], 0.0)
        hits = [lane == routes_ref[rows, k : k + 1] for k in range(2)]
        picked = [jnp.sum(jnp.where(hit, logits, 0.0), axis=1, keepdims=True) for hit in hits]
        peak = jnp.maximum(picked[0], picked[1])
        expo = [jnp.exp(p - peak) for p in picked]
        total = expo[0] + expo[1]
        gates = [e / total for e in expo]
        misc_ref[rows, :] = jnp.where(lane == 0, gates[0], jnp.where(lane == 1, gates[1], router))
        spread = sum(
            jnp.where(hit & (lane < size), gate.astype(half).astype(single), 0.0)
            for hit, gate in zip(hits, gates)
        )
        both_ref[mine_rows, pl.ds(0, width)] = normed
        both_ref[mine_rows, pl.ds(width, LANES)] = spread.astype(half)

    swap_rows = remote(
        both_ref.at[own_rows], both_ref.at[own_rows], swap_send.at[1], swap_recv.at[1], partner
    )
    swap_rows.start()

    load_hot.wait()
    for number, pair in enumerate(PAIRS):
        slots = [
            pl.ds(pl.multiple_of(flip(mine, k) * padded, 16), padded) for k in pair
        ]
        hot = jnp.concatenate([hot_ref[s, own_rows] for s in slots], 0)
        acc_ref[number] = mm(hot, both_ref[own_rows, :])
    swap_rows.wait_recv()
    row_ref[...] = jnp.zeros(row_ref.shape, single)
    for number, pair in enumerate(PAIRS):
        slots = [
            pl.ds(pl.multiple_of(flip(mine, k) * padded, 16), padded) for k in pair
        ]
        hot = jnp.concatenate([hot_ref[s, other_rows] for s in slots], 0)
        acc_ref[number] += mm(hot, both_ref[other_rows, :])
        for place, k in enumerate(pair):
            to = flip(mine, k)
            first = place * padded
            tail = acc_ref[number, first : first + padded, width:].astype(half)
            lane = lax.broadcasted_iota(jnp.int32, (16, LANES), 1)
            row_ref[:, :padded] = mm_nt((lane == to).astype(half), tail)
            stage_ref[to] = acc_ref[number, first : first + padded, :width].astype(half)
            last = acc_ref[number, first + padded - 16 : first + padded, : 2 * LANES]
            row = lax.broadcasted_iota(jnp.int32, (16, 2 * LANES), 0)
            last = jnp.where(row == 15, row_ref[...], last)
            stage_ref[to, padded - 16 :, : 2 * LANES] = last.astype(half)
            if k:
                copy = remote(
                    stage_ref.at[to], x_ref.at[mine], x_send.at[k], x_recv.at[k], {"dp": base + to}
                )
                waits.append(copy)
            else:
                copy = pltpu.make_async_copy(stage_ref.at[to], x_ref.at[mine], own_sem.at[0])
            copy.start()

    for copy in owns:
        copy.wait()
    pair_in.wait_recv()
    pair_down.wait_recv()

    ff = in_ref.shape[3]
    block = fit(ff, 256)
    steps = ff // block
    rows2 = 2 * padded
    dot_ref[...] = jnp.zeros(dot_ref.shape, single)

    def spill(slot, array, place, source, part, f):
        out = (hid_ref, pg_ref, pu_ref)[array]
        rows = pl.ds(pl.multiple_of(source * padded, 16), padded)
        return pltpu.make_async_copy(
            spill_ref.at[slot, array, pl.ds(place * padded, padded)],
            out.at[part, rows, pl.ds(f * block, block)],
            spill_sem.at[slot, array, place],
        )

    def arrived(k):
        remote(dy_hbm_ref.at[0], dy_ref.at[0], dy_send.at[0], dy_recv.at[k], partner).wait_recv()
        remote(stage_ref.at[0], x_ref.at[0], x_send.at[0], x_recv.at[k], partner).wait_recv()

    def give_back(k, source):
        return remote(
            ig_ref.at[source], back_ref.at[mine], ig_send.at[k], ig_recv.at[k], {"dp": base + source}
        )

    @pl.loop(0, size // 2)
    def _(q):
        ks, sources = [], []
        for place in range(2):
            k, source = PAIRS[0][place], flip(mine, PAIRS[0][place])
            for number in range(1, size // 2):
                k = jnp.where(q == number, PAIRS[number][place], k)
                source = jnp.where(q == number, flip(mine, PAIRS[number][place]), source)
            ks.append(k)
            sources.append(source)

        @pl.when(q == 0)
        def _():
            pltpu.make_async_copy(stage_ref.at[0], x_ref.at[0], own_sem.at[0]).wait()

        @pl.when(q > 0)
        def _():
            arrived(ks[0])

        arrived(ks[1])
        for place, source in enumerate(sources):
            rows = pl.ds(place * padded, padded)
            gates = x_ref[source, padded - 16 :, : 2 * LANES].astype(single).T
            gate = jnp.broadcast_to(gates[:padded, 15:16], (padded, LANES))
            gate_ref[rows, :] = gate
            og_ref[source] = (dy_ref[source].astype(single) * gate[:, :1]).astype(half)
        for number in range(2):
            acc_ref[number, :, :width] = jnp.zeros((rows2, width), single)

        @pl.loop(0, 2)
        def _(part):
            for f in range(steps):
                lanes = pl.ds(f * block, block)
                slot = f % 2
                if f >= 2:
                    for array in range(3):
                        for place, source in enumerate(sources):
                            spill(slot, array, place, source, part, f - 2).wait()
                gate_w = win_ref[part, :, 0, :, lanes].reshape(width, block)
                up_w = win_ref[part, :, 1, :, lanes].reshape(width, block)
                down_w = down_ref[part, :, :, lanes].reshape(width, block)
                x = jnp.concatenate([x_ref[source] for source in sources], 0)
                og = jnp.concatenate([og_ref[source] for source in sources], 0)
                pre = mm(x, gate_w)
                up = mm(x, up_w)
                hg = mm(og, down_w)
                sigma = jax.nn.sigmoid(pre)
                active = pre * sigma
                hidden = (active * up).astype(half)
                pg = (hg * up * (sigma * (1.0 + pre * (1.0 - sigma)))).astype(half)
                pu = (hg * active).astype(half)
                spill_ref[slot, 0] = hidden
                spill_ref[slot, 1] = pg
                spill_ref[slot, 2] = pu
                acc_ref[0, :, :width] += mm_nt(hidden, down_w)
                acc_ref[1, :, :width] += mm_nt(pg, gate_w) + mm_nt(pu, up_w)
                for array in range(3):
                    for place, source in enumerate(sources):
                        spill(slot, array, place, source, part, f).start()
            for f in range(max(0, steps - 2), steps):
                for array in range(3):
                    for place, source in enumerate(sources):
                        spill(f % 2, array, place, source, part, f).wait()

        ones = jnp.ones((16, width), half)
        for place, source in enumerate(sources):
            rows = pl.ds(place * padded, padded)
            eo = acc_ref[0, rows, :width]
            out_ref[source] = (eo * gate_ref[rows, :1]).astype(half)
            ig_ref[source] = acc_ref[1, rows, :width].astype(half)
            product = eo * dy_ref[source].astype(single)
            top = product.astype(half)
            low = (product - top.astype(single)).astype(half)
            dot_ref[:, :padded] = mm_nt(ones, top) + mm_nt(ones, low)
            dots = dot_ref[...]
            high = dots.astype(half).astype(single)
            row = lax.broadcasted_iota(jnp.int32, dots.shape, 0)
            last = acc_ref[1, pl.ds((place + 1) * padded - 16, 16), : 2 * LANES]
            last = jnp.where(row == 14, high, jnp.where(row == 15, dots - high, last))
            ig_ref[source, padded - 16 :, : 2 * LANES] = last.astype(half)

        @pl.when(q == 0)
        def _():
            pltpu.make_async_copy(ig_ref.at[mine], back_ref.at[mine], own_sem.at[0]).start()

        @pl.when(q > 0)
        def _():
            give_back(ks[0], sources[0]).start()

        give_back(ks[1], sources[1]).start()

    pltpu.make_async_copy(ig_ref.at[mine], back_ref.at[mine], own_sem.at[0]).wait()
    for k in range(1, size):
        give_back(k, flip(mine, k)).wait()
    for copy in waits + [swap_rows, pair_in, pair_down]:
        copy.wait_send()


def experts(
    down, inward, dy, heads, tokens, own_w, other_w, gains, router, prev, routes, hot, padded
):
    members, _, d_rows, ff = inward.shape
    local, width = tokens.shape
    seq = heads.shape[0]
    size = EXPERTS_FF
    block = fit(ff, 256)
    any_spec = pl.BlockSpec(memory_space=pl.ANY)
    vmem = pl.BlockSpec(memory_space=pltpu.VMEM)
    dma = pltpu.SemaphoreType.DMA
    rows = jax.ShapeDtypeStruct((size, padded, width), half)
    wide = jax.ShapeDtypeStruct((2, size * padded, ff), half)
    return pl.pallas_call(
        functools.partial(experts_kernel, members, padded),
        out_shape=[
            rows,
            rows,
            rows,
            rows,
            wide,
            wide,
            wide,
            jax.ShapeDtypeStruct((local, width), single),
            jax.ShapeDtypeStruct((local, width), half),
            jax.ShapeDtypeStruct((local, LANES), single),
        ],
        in_specs=[any_spec] * 3 + [vmem] * 8 + [any_spec],
        out_specs=[any_spec] + [vmem] * 3 + [any_spec] * 3 + [vmem] * 3,
        scratch_shapes=[
            pltpu.VMEM((local, heads.shape[1]), half),
            pltpu.VMEM((seq, width + LANES), half),
            pltpu.VMEM((size // 2, 2 * padded, width + LANES), single),
            pltpu.VMEM((size, padded, width), half),
            pltpu.VMEM((16, 2 * LANES), single),
            pltpu.VMEM((2,) + inward.shape, half),
            pltpu.VMEM((2, members, d_rows, ff), half),
            pltpu.VMEM((size, padded, width), half),
            pltpu.VMEM((size, padded, width), half),
            pltpu.VMEM((2, 3, 2 * padded, block), half),
            pltpu.VMEM((2 * padded, LANES), single),
            pltpu.VMEM((16, 2 * LANES), single),
            pltpu.VMEM(hot.shape, half),
            dma((size,)),
            dma((size,)),
            dma((size,)),
            dma((size,)),
            dma((5,)),
            dma((4,)),
            dma((4,)),
            dma((size,)),
            dma((size,)),
            dma((2, 3, 2)),
        ],
        compiler_params=pltpu.CompilerParams(
            collective_id=1, has_side_effects=True, vmem_limit_bytes=62 << 20
        ),
        name="experts",
    )(down, inward, dy, heads, tokens, own_w, other_w, gains, router, prev, routes, hot)


def split(x):
    high = x.astype(half)
    return high, (x - high.astype(single)).astype(half)


def slot_rows(columns, count):
    slot = lax.broadcasted_iota(jnp.int32, (columns.shape[0], count), 1)
    hit = (columns[:, 2:3] == slot) | (columns[:, 3:4] == slot)
    return jnp.where(hit, 1.0, 0.0).astype(half)


def lane_sum(x):
    return jnp.sum(x, axis=1, keepdims=True)


def back_kernel(
    padded,
    back_ref,
    info_ref,
    resid_hbm_ref,
    normed_hbm_ref,
    misc_ref,
    dy_hbm_ref,
    routes_ref,
    gain_ref,
    const_ref,
    router_ref,
    own_w_ref,
    other_w_ref,
    prev_ref,
    mix_ref,
    rgrad_ref,
    attn_ref,
    heads_ref,
    base_ref,
    pgrad_ref,
    small_ref,
    mgrad_ref,
    ext_ref,
    out_ref,
    in_ref,
    hg_ref,
    send_sem,
    recv_sem,
    resid_ref,
    normed_ref,
    dy_ref,
    load_sem,
):
    core = lax.axis_index("tensor")
    partner = {"tensor": 1 - core}
    sources, _, width = back_ref.shape
    count = sources * padded
    local = dy_ref.shape[0]
    step = fit(local, 256)
    pairs = (resid_hbm_ref, resid_ref), (normed_hbm_ref, normed_ref), (dy_hbm_ref, dy_ref)
    loads = [
        pltpu.make_async_copy(source, target, load_sem.at[i])
        for i, (source, target) in enumerate(pairs)
    ]
    for copy in loads:
        copy.start()
    barrier = pltpu.get_barrier_semaphore()
    pl.semaphore_signal(barrier, inc=1, device_id=partner, device_id_type=MESH)
    pl.semaphore_wait(barrier, 1)

    def remote(src, dst, number):
        return pltpu.make_async_remote_copy(
            src_ref=src,
            dst_ref=dst,
            send_sem=send_sem.at[number],
            recv_sem=recv_sem.at[number],
            device_id=partner,
            device_id_type=MESH,
        )

    own_rows = pl.ds(pl.multiple_of(core * local, local), local)
    lane = lax.broadcasted_iota(jnp.int32, (step, LANES), 1)
    for s in range(sources):
        dots = back_ref[s, padded - 16 :, : 2 * LANES].astype(single).T
        number = lax.broadcasted_iota(jnp.int32, (padded, LANES), 1)
        ext = jnp.where(
            number == s,
            dots[:padded, 14:15],
            jnp.where(number == s + EXPERTS_FF, dots[:padded, 15:16], 0.0),
        )
        ext_ref[pl.ds(s * padded, padded), :] = ext.astype(half)
    back_all = back_ref.reshape(count, width)

    @pl.loop(0, local // step)
    def _(r):
        rows = pl.ds(pl.multiple_of(r * step, step), step)
        there = pl.ds(pl.multiple_of((1 - core) * local + r * step, step), step)
        hot = slot_rows(info_ref[there, :], count)
        out_ref[rows, pl.ds(0, width)] = mm(hot, back_all[...]).astype(half)
        out_ref[rows, pl.ds(width, LANES)] = mm(hot, ext_ref[...]).astype(half)

    sums = remote(out_ref, in_ref, 0)
    sums.start()
    small_ref[...] = jnp.zeros(small_ref.shape, single)
    mgrad_ref[...] = jnp.zeros(mgrad_ref.shape, single)

    @pl.loop(0, local // step)
    def _(r):
        rows = pl.ds(pl.multiple_of(r * step, step), step)
        here = pl.ds(pl.multiple_of(core * local + r * step, step), step)
        hot = slot_rows(info_ref[here, :], count)
        rgrad_ref[rows, :] = mm(hot, back_all[...])
        pgrad_ref[rows, :] = mm(hot, ext_ref[...])

    for copy in loads:
        copy.wait()
    sums.wait()

    @pl.loop(0, local // step)
    def _(r):
        rows = pl.ds(pl.multiple_of(r * step, step), step)
        here = pl.ds(pl.multiple_of(core * local + r * step, step), step)
        dy = dy_ref[rows, :].astype(single)
        normed = normed_ref[rows, :].astype(single)
        resid = resid_ref[rows, :]
        misc = misc_ref[rows, :]
        expert_dot = pgrad_ref[rows, :] + in_ref[rows, pl.ds(width, LANES)].astype(single)
        own_dot = lane_sum(dy * normed)
        vec_dot = [lane_sum(dy * const_ref[j : j + 1, :]) for j in range(2)]
        gates = [misc[:, k : k + 1] for k in range(2)]
        routes = [routes_ref[rows, k : k + 1] for k in range(2)]
        alphas = []
        for j in range(2):
            columns = [misc[:, EXPERTS + 2 * j + m : EXPERTS + 2 * j + m + 1] for m in range(2)]
            peak = jnp.maximum(columns[0], columns[1])
            expo = [jnp.exp(c - peak) for c in columns]
            total = expo[0] + expo[1]
            alphas.append([e / total for e in expo])
        gate_grads = []
        for k in range(2):
            hit = (lane == routes[k]) | (lane == routes[k] + EXPERTS_FF)
            dot = lane_sum(jnp.where(hit & (routes[k] < EXPERTS_FF), expert_dot, 0.0))
            dot += jnp.where(routes[k] == EXPERTS_FF + 1, own_dot, 0.0)
            for j in range(2):
                value = alphas[j][0] * own_dot + alphas[j][1] * vec_dot[j]
                dot += jnp.where(routes[k] == EXPERTS_FF + 2 + j, value, 0.0)
            gate_grads.append(dot)
        centre = gates[0] * gate_grads[0] + gates[1] * gate_grads[1]
        chosen = [gates[k] * (gate_grads[k] - centre) for k in range(2)]
        router_grad = jnp.zeros((step, LANES), single)
        own_weight = jnp.zeros((step, 1), single)
        for k in range(2):
            router_grad = jnp.where(lane == routes[k], chosen[k], router_grad)
            own_weight += jnp.where(routes[k] == EXPERTS_FF + 1, gates[k], 0.0)
        logit_grad = router_grad
        vec_lanes = jnp.zeros((step, LANES), single)
        other = jnp.zeros((step, width), single)
        for j in range(2):
            weight = sum(jnp.where(routes[k] == EXPERTS_FF + 2 + j, gates[k], 0.0) for k in range(2))
            grads = [weight * own_dot, weight * vec_dot[j]]
            mean = alphas[j][0] * grads[0] + alphas[j][1] * grads[1]
            for m in range(2):
                router_grad = jnp.where(
                    lane == EXPERTS + 2 * j + m, alphas[j][m] * (grads[m] - mean), router_grad
                )
            own_weight += weight * alphas[j][0]
            vec_weight = weight * alphas[j][1]
            vec_lanes = jnp.where(lane == 16 + j, vec_weight, vec_lanes)
            other += vec_weight * const_ref[j : j + 1, :]
        base_ref[rows, :] = resid + own_weight * normed + other
        rg_high, rg_low = split(router_grad)
        two_grad = rgrad_ref[rows, :] + in_ref[rows, pl.ds(0, width)].astype(single)
        two_grad += own_weight * dy
        two_grad += mm_nt(rg_high, router_ref[...]) + mm_nt(rg_low, router_ref[...])
        normed_low = normed_ref[rows, :]
        vec_high, vec_low = split(vec_lanes)
        small_ref[...] += (
            mm_tn(rg_high, normed_low)
            + mm_tn(rg_low, normed_low)
            + mm_tn(vec_high, dy_ref[rows, :])
            + mm_tn(vec_low, dy_ref[rows, :])
        )[:24]
        scale = rms_scale(resid)
        gain_part = jnp.sum(two_grad * resid * scale, axis=0, keepdims=True)
        small_ref[19:20, :] += gain_part
        weighted = two_grad * gain_ref[1:2, :]
        mean = jnp.mean(weighted * resid, axis=-1, keepdims=True)
        grad = dy + scale * (weighted - resid * scale * scale * mean)
        rgrad_ref[rows, :] = grad
        low = grad.astype(half)
        attn_ref[here, :] = low
        heads_ref[here, :] = mm(low, own_w_ref[...]).astype(half)
        hg_ref[rows, :] = mm(low, other_w_ref[...]).astype(half)
        lg_high, lg_low = split(logit_grad)
        mix_high, mix_low = split(mix_ref[...])
        pgrad_ref[rows, :] = (
            mm_nt(lg_high, mix_high) + mm_nt(lg_high, mix_low) + mm_nt(lg_low, mix_high)
        )
        prev_high, prev_low = split(prev_ref[rows, :])
        mgrad_ref[...] += (
            mm_tn(prev_high, lg_high) + mm_tn(prev_high, lg_low) + mm_tn(prev_low, lg_high)
        )

    for i in range(EXPERTS):
        place = pl.ds(i % 6 * LANES, LANES)
        small_ref[20 + i // 6 : 21 + i // 6, place] = mgrad_ref[i : i + 1, :]

    heads = remote(hg_ref, heads_ref.at[own_rows], 1)
    heads.start()
    attn = remote(attn_ref.at[own_rows], attn_ref.at[own_rows], 2)
    attn.start()
    heads.wait()
    attn.wait()


def backward_middle(
    back, info, resid, normed, misc, dy, routes, gains, const, router, own_w, other_w, prev, mix, padded
):
    local, width = dy.shape
    seq = info.shape[0]
    hh = own_w.shape[1]
    count = EXPERTS_FF * padded
    vmem = pl.BlockSpec(memory_space=pltpu.VMEM)
    hbm = pl.BlockSpec(memory_space=pltpu.HBM)
    return pl.pallas_call(
        functools.partial(back_kernel, padded),
        out_shape=[
            jax.ShapeDtypeStruct((local, width), single),
            jax.ShapeDtypeStruct((seq, width), half),
            jax.ShapeDtypeStruct((seq, hh), half),
            jax.ShapeDtypeStruct((local, width), single),
            jax.ShapeDtypeStruct((local, LANES), single),
            jax.ShapeDtypeStruct((24, width), single),
            jax.ShapeDtypeStruct((LANES, LANES), single),
        ],
        in_specs=[vmem] * 2 + [hbm] * 2 + [vmem, hbm] + [vmem] * 8,
        out_specs=[vmem] * 7,
        scratch_shapes=[
            pltpu.VMEM((count, LANES), half),
            pltpu.VMEM((local, width + LANES), half),
            pltpu.VMEM((local, width + LANES), half),
            pltpu.VMEM((local, hh), half),
            pltpu.SemaphoreType.DMA((3,)),
            pltpu.SemaphoreType.DMA((3,)),
            pltpu.VMEM((local, width), single),
            pltpu.VMEM((local, width), half),
            pltpu.VMEM((local, width), half),
            pltpu.SemaphoreType.DMA((3,)),
        ],
        compiler_params=pltpu.CompilerParams(
            collective_id=2, has_side_effects=True, vmem_limit_bytes=56 << 20
        ),
        name="backward_middle",
    )(back, info, resid, normed, misc, dy, routes, gains, const, router, own_w, other_w, prev, mix)


def weight_kernel(
    x_ref,
    og_ref,
    hid_ref,
    pg_ref,
    pu_ref,
    out_ref,
    xt_ref,
    ogt_ref,
    send_ref,
    got_ref,
    own_ref,
    send_sem,
    recv_sem,
):
    f = pl.program_id(0)
    partner = {"tensor": 1 - lax.axis_index("tensor")}
    shape = out_ref.shape[0], out_ref.shape[2], out_ref.shape[3]

    @pl.when(f == 0)
    def _():
        barrier = pltpu.get_barrier_semaphore()
        pl.semaphore_signal(barrier, inc=1, device_id=partner, device_id_type=MESH)
        pl.semaphore_wait(barrier, 1)
        xt_ref[...] = x_ref[...].T
        ogt_ref[...] = og_ref[...].T

    def remote(number):
        return pltpu.make_async_remote_copy(
            src_ref=send_ref.at[number],
            dst_ref=got_ref.at[number],
            send_sem=send_sem.at[number],
            recv_sem=recv_sem.at[number],
            device_id=partner,
            device_id_type=MESH,
        )

    factors = (xt_ref, pg_ref), (xt_ref, pu_ref), (ogt_ref, hid_ref)
    for k, (left, right) in enumerate(factors):
        send_ref[f, k] = mm(left[...], right[1]).astype(half)
    remote(f).start()
    for k, (left, right) in enumerate(factors):
        own_ref[k] = mm(left[...], right[0])
    remote(f).wait_recv()
    for k in range(3):
        total = own_ref[k] + got_ref[f, k].astype(single)
        out_ref[:, k] = total.astype(half).reshape(shape)

    @pl.when(f == pl.num_programs(0) - 1)
    def _():
        for number in range(send_ref.shape[0]):
            remote(number).wait_send()


def weight_step(x, og, hidden, pg, pu, m):
    count, width = og.shape
    ff = hidden.shape[2]
    block = fit(ff, 256)
    steps = ff // block
    whole = pl.BlockSpec((count, width), lambda f: (0, 0))
    wide = pl.BlockSpec((2, count, block), lambda f: (0, 0, f))
    part = pl.BlockSpec((m, 3, width // m, block), lambda f: (0, 0, 0, f))
    return pl.pallas_call(
        weight_kernel,
        grid=(steps,),
        in_specs=[whole, whole, wide, wide, wide],
        out_specs=part,
        out_shape=jax.ShapeDtypeStruct((m, 3, width // m, ff), half),
        scratch_shapes=[
            pltpu.VMEM((width, count), half),
            pltpu.VMEM((width, count), half),
            pltpu.VMEM((steps, 3, width, block), half),
            pltpu.VMEM((steps, 3, width, block), half),
            pltpu.VMEM((3, width, block), single),
            pltpu.SemaphoreType.DMA((steps,)),
            pltpu.SemaphoreType.DMA((steps,)),
        ],
        compiler_params=pltpu.CompilerParams(
            collective_id=3, has_side_effects=True, vmem_limit_bytes=56 << 20
        ),
        cost_estimate=pl.CostEstimate(
            flops=12 * count * width * ff,
            bytes_accessed=12 * width * ff + 12 * count * ff,
            transcendentals=0,
        ),
        name="weight_step",
    )(x, og, hidden, pg, pu)


def tail_kernel(
    members,
    low,
    padded,
    eo_hbm_ref,
    qkv_ref,
    one_ref,
    proj_ref,
    outg_ref,
    x_hbm_ref,
    base_hbm_ref,
    resid_hbm_ref,
    info_ref,
    gain_ref,
    small_ref,
    grads_ref,
    proj_out_ref,
    outw_ref,
    tokens_ref,
    mixed_ref,
    small_out_ref,
    expert_ref,
    dense_ref,
    first_ref,
    stage_ref,
    second_ref,
    one_out_ref,
    one_in_ref,
    ffn_out_ref,
    ffn_in_ref,
    ffn_ref,
    mine_ref,
    pair_ref,
    near_ref,
    far_ref,
    dense_out_ref,
    send1,
    recv1,
    send2,
    recv2,
    pair_send,
    pair_recv,
    near_send,
    near_recv,
    far_send,
    far_recv,
    part_ref,
    sum_ref,
    part_sem,
    sum_sem,
    eo_ref,
    x_ref,
    base_ref,
    resid_ref,
    load_sem,
):
    size = EXPERTS_FF
    me = lax.axis_index("dp")
    core = lax.axis_index("tensor")
    high = members // low
    inside, row = lax.rem(me, low), me // low
    local, width = base_ref.shape
    count = size * padded
    d_rows = outw_ref.shape[0]
    hh3 = qkv_ref.shape[1]
    step = fit(local, 256)
    partner = {"tensor": 1 - core}

    def beside(k):
        return row * low + flip(inside, k)

    def across(k):
        return lax.rem(row + k, high) * low + inside

    peers = [beside(k) for k in range(1, low)] + [across(k) for k in range(1, high)]
    barrier = pltpu.get_barrier_semaphore()
    for peer in peers:
        pl.semaphore_signal(barrier, inc=1, device_id={"dp": peer}, device_id_type=MESH)
    pl.semaphore_signal(barrier, inc=1, device_id=partner, device_id_type=MESH)
    pl.semaphore_wait(barrier, len(peers) + 1)

    def remote(src, dst, send, recv, device):
        return pltpu.make_async_remote_copy(
            src_ref=src,
            dst_ref=dst,
            send_sem=send,
            recv_sem=recv,
            device_id=device,
            device_id_type=MESH,
        )

    pairs = (x_hbm_ref, x_ref), (eo_hbm_ref, eo_ref), (base_hbm_ref, base_ref), (resid_hbm_ref, resid_ref)
    loads = [
        pltpu.make_async_copy(source, target, load_sem.at[i])
        for i, (source, target) in enumerate(pairs)
    ]
    for copy in loads:
        copy.start()

    sent = []
    chunks = 2
    rows_each = width // chunks
    for c in range(chunks):
        lanes = pl.ds(c * rows_each, rows_each)
        grad = mm_tn(one_ref[:, lanes], qkv_ref[...])
        for j in range(members // chunks):
            owner = c * (members // chunks) + j
            dense_ref[owner, :, :hh3] = grad[j * d_rows : (j + 1) * d_rows].astype(half)
            dense_ref[owner, :, hh3:] = outg_ref[owner * d_rows : (owner + 1) * d_rows, :]
        for h in range(c * high // chunks, (c + 1) * high // chunks):
            for k in BESIDE:
                copy = remote(
                    dense_ref.at[h * low + flip(inside, k)],
                    first_ref.at[k - 1, h],
                    send1.at[k - 1, h],
                    recv1.at[k - 1, h],
                    {"dp": beside(k)},
                )
                copy.start()
                sent.append(copy)

    def one_part(rows):
        part = mm_nt(qkv_ref[rows, :], proj_ref[...])
        x = x_ref[rows, :].astype(single)
        mine_ref[18:19, :] += jnp.sum(part * x * rms_scale(x), axis=0, keepdims=True)
        return part

    mine_ref[...] = small_ref[...]
    for copy in loads:
        copy.wait()

    @pl.loop(0, local // step)
    def _(r):
        rows = pl.ds(pl.multiple_of(r * step, step), step)
        there = pl.ds(pl.multiple_of((1 - core) * local + r * step, step), step)
        one_out_ref[rows, :] = one_part(there).astype(half)

    one_sent = remote(one_out_ref, one_in_ref, pair_send.at[0], pair_recv.at[0], partner)
    one_sent.start()

    @pl.loop(0, local // step)
    def _(r):
        rows = pl.ds(pl.multiple_of(r * step, step), step)
        here = pl.ds(pl.multiple_of(core * local + r * step, step), step)
        tokens_ref[rows, :] = one_part(here)

    pair = remote(mine_ref, pair_ref, pair_send.at[1], pair_recv.at[1], partner)
    pair.start()

    eo_all = eo_ref.reshape(count, width)

    @pl.loop(0, local // step)
    def _(r):
        rows = pl.ds(pl.multiple_of(r * step, step), step)
        there = pl.ds(pl.multiple_of((1 - core) * local + r * step, step), step)
        ffn_out_ref[rows, :] = mm(slot_rows(info_ref[there, :], count), eo_all[...]).astype(half)

    ffn_sent = remote(ffn_out_ref, ffn_in_ref, pair_send.at[2], pair_recv.at[2], partner)
    ffn_sent.start()

    @pl.loop(0, local // step)
    def _(r):
        rows = pl.ds(pl.multiple_of(r * step, step), step)
        here = pl.ds(pl.multiple_of(core * local + r * step, step), step)
        ffn_ref[rows, :] = mm(slot_rows(info_ref[here, :], count), eo_all[...])

    def second(h):
        return remote(
            stage_ref.at[h],
            second_ref.at[row],
            send2.at[h],
            recv2.at[row],
            {"dp": h * low + inside},
        )

    pair.wait()
    near_ref[inside] = mine_ref[...] + pair_ref[...]
    near = []
    for k in range(1, low):
        near.append(
            remote(
                near_ref.at[inside],
                near_ref.at[inside],
                near_send.at[k],
                near_recv.at[inside],
                {"dp": beside(k)},
            )
        )
        near[-1].start()

    for h in range(high):
        for k in range(low - 1):
            remote(
                dense_ref.at[0], first_ref.at[k, h], send1.at[k, h], recv1.at[k, h], partner
            ).wait_recv()
        total = dense_ref[h * low + inside].astype(single)
        for k in range(low - 1):
            total += first_ref[k, h].astype(single)

        @pl.when(h == row)
        def _():
            dense_out_ref[...] = total

        @pl.when(h != row)
        def _():
            stage_ref[h] = total.astype(half)
            second(h).start()

    for k in range(1, low):
        block = lax.rem(inside + k, low)
        remote(
            mine_ref, near_ref.at[block], near_send.at[0], near_recv.at[block], partner
        ).wait_recv()
    total = near_ref[0]
    for k in range(1, low):
        total = total + near_ref[k]
    far_ref[row] = total
    far = []
    for k in range(1, high):
        far.append(
            remote(
                far_ref.at[row], far_ref.at[row], far_send.at[k], far_recv.at[row], {"dp": across(k)}
            )
        )
        far[-1].start()

    groups = members // size

    def load(e):
        return [
            pltpu.make_async_copy(
                grads_ref.at[g * size + e], part_ref.at[e % 2, g], part_sem.at[e % 2, g]
            )
            for g in range(groups)
        ]

    def store(e):
        return pltpu.make_async_copy(sum_ref.at[e % 2], expert_ref.at[e], sum_sem.at[e % 2])

    for copy in load(0):
        copy.start()
    for e in range(size):
        if e + 1 < size:
            for copy in load(e + 1):
                copy.start()
        for copy in load(e):
            copy.wait()
        if e >= 2:
            store(e - 2).wait()
        total = part_ref[e % 2, 0].astype(single)
        for g in range(1, groups):
            total += part_ref[e % 2, g].astype(single)
        sum_ref[e % 2] = total
        store(e).start()
    for e in range(size - 2, size):
        store(e).wait()

    one_sent.wait()

    @pl.loop(0, local // step)
    def _(r):
        rows = pl.ds(pl.multiple_of(r * step, step), step)
        here = pl.ds(pl.multiple_of(core * local + r * step, step), step)
        x = x_ref[here, :].astype(single)
        scale = rms_scale(x)
        weighted = (tokens_ref[rows, :] + one_in_ref[rows, :].astype(single)) * gain_ref[0:1, :]
        mean = jnp.mean(weighted * x, axis=-1, keepdims=True)
        tokens_ref[rows, :] = resid_ref[rows, :] + scale * (weighted - x * scale * scale * mean)

    ffn_sent.wait()

    @pl.loop(0, local // step)
    def _(r):
        rows = pl.ds(pl.multiple_of(r * step, step), step)
        total = base_ref[rows, :] + ffn_ref[rows, :] + ffn_in_ref[rows, :].astype(single)
        mixed_ref[rows, :] = total.astype(half)

    for h in range(high):

        @pl.when(h != row)
        def _():
            remote(
                stage_ref.at[0], second_ref.at[h], send2.at[0], recv2.at[h], partner
            ).wait_recv()
            dense_out_ref[...] += second_ref[h].astype(single)
            second(h).wait_send()

    hh = outw_ref.shape[1]
    for c in range(3):
        proj_out_ref[c] = dense_out_ref[:, c * hh : (c + 1) * hh]
    outw_ref[...] = dense_out_ref[:, 3 * hh :]
    for k in range(1, high):
        block = lax.rem(row + k, high)
        remote(
            mine_ref, far_ref.at[block], far_send.at[0], far_recv.at[block], partner
        ).wait_recv()
    total = far_ref[0]
    for k in range(1, high):
        total = total + far_ref[k]
    small_out_ref[...] = total
    for copy in sent + near + far:
        copy.wait_send()


def tail(members, eo, qkv, one, proj, outg, x, base, resid, info, gains, small, grads, padded):
    low = 4
    high = members // low
    local, width = base.shape
    d_rows = width // members
    hh = outg.shape[1]
    wide = qkv.shape[1] + hh
    groups = members // EXPERTS_FF
    vmem = pl.BlockSpec(memory_space=pltpu.VMEM)
    hbm = pl.BlockSpec(memory_space=pltpu.HBM)
    dma = pltpu.SemaphoreType.DMA
    rows_half = pltpu.VMEM((local, width), half)
    small_one = pltpu.VMEM(small.shape, single)
    return pl.pallas_call(
        functools.partial(tail_kernel, members, low, padded),
        out_shape=[
            jax.ShapeDtypeStruct((3, d_rows, hh), single),
            jax.ShapeDtypeStruct((d_rows, hh), single),
            jax.ShapeDtypeStruct((local, width), single),
            jax.ShapeDtypeStruct((local, width), half),
            jax.ShapeDtypeStruct(small.shape, single),
            jax.ShapeDtypeStruct((EXPERTS_FF,) + grads.shape[1:], single),
        ],
        in_specs=[hbm] + [vmem] * 4 + [hbm] * 3 + [vmem] * 3 + [hbm],
        out_specs=[vmem] * 5 + [hbm],
        scratch_shapes=[
            pltpu.VMEM((members, d_rows, wide), half),
            pltpu.VMEM((low - 1, high, d_rows, wide), half),
            pltpu.VMEM((high, d_rows, wide), half),
            pltpu.VMEM((high, d_rows, wide), half),
            rows_half,
            rows_half,
            rows_half,
            rows_half,
            pltpu.VMEM((local, width), single),
            small_one,
            small_one,
            pltpu.VMEM((low,) + small.shape, single),
            pltpu.VMEM((high,) + small.shape, single),
            pltpu.VMEM((d_rows, wide), single),
            dma((low - 1, high)),
            dma((low - 1, high)),
            dma((high,)),
            dma((high,)),
            dma((3,)),
            dma((3,)),
            dma((low,)),
            dma((low,)),
            dma((high,)),
            dma((high,)),
            pltpu.VMEM((2, groups) + grads.shape[1:], half),
            pltpu.VMEM((2,) + grads.shape[1:], single),
            dma((2, groups)),
            dma((2,)),
            pltpu.VMEM(eo.shape, half),
            pltpu.VMEM(x.shape, half),
            pltpu.VMEM(base.shape, single),
            pltpu.VMEM(resid.shape, single),
            dma((4,)),
        ],
        compiler_params=pltpu.CompilerParams(
            collective_id=4, has_side_effects=True, vmem_limit_bytes=60 << 20
        ),
        name="tail",
    )(eo, qkv, one, proj, outg, x, base, resid, info, gains, small, grads)


def per_device(
    tokens,
    segment_ids,
    routes,
    prev_logits,
    cotangent,
    proj_weight,
    out_weight,
    norm_gain,
    expert_weight,
    router,
    constant_vectors,
    gate_mixing,
):
    members = lax.axis_size("dp")
    groups = members // EXPERTS_FF
    cubes = [[g * EXPERTS_FF + i for i in range(EXPERTS_FF)] for g in range(groups)]
    core = lax.axis_index("tensor")
    d_rows, hh = out_weight.shape
    per_core = -(-CAPACITY // 2)
    padded = -(-(per_core + 3) // 16) * 16

    def in_group(blocks):
        return lax.all_to_all(blocks, "dp", 0, 0, axis_index_groups=cubes, tiled=True)

    def plain_tail(eo, qkv, one, proj, outg, x, base, resid, gains, small, grads):
        ffn = pair_sum(mm_tn(onehot, eo.reshape(-1, width)))
        part = mm_nt(qkv, proj)
        scale = rms_scale(x)
        small = small.at[18].set(jnp.sum(part * x * scale, axis=0))
        weighted = pair_sum(part) * gains[0]
        x, scale = half_of(x, core), half_of(scale, core)
        mean = jnp.mean(weighted * x, axis=-1, keepdims=True)
        tokens_grad = resid + scale * (weighted - x * scale * scale * mean)
        dense = jnp.concatenate([mm_tn(one, qkv).astype(half), outg], 1)
        dense = lax.all_to_all(dense.reshape(members, d_rows, -1), "dp", 0, 0, tiled=True)
        dense = jnp.sum(dense.astype(single), axis=0)
        grads = grads.reshape((groups, EXPERTS_FF) + grads.shape[1:]).astype(single)
        return (
            dense[:, : 3 * hh].reshape(d_rows, 3, hh).transpose(1, 0, 2),
            dense[:, 3 * hh :],
            tokens_grad,
            (base + ffn).astype(half),
            lax.psum(small, ("dp", "tensor")),
            jnp.sum(grads, axis=0),
        )

    pack = jnp.concatenate(
        [
            proj_weight.transpose(1, 0, 2).reshape(d_rows, 3 * hh),
            out_weight,
            norm_gain.T,
            constant_vectors.T,
            router,
        ],
        1,
    )
    columns = pack.shape[1]
    pack = jnp.pad(pack, ((0, 0), (0, -columns % LANES)))
    ids = jnp.concatenate([segment_ids, routes[0].T], 0)
    ids = jnp.pad(ids, ((0, 5), (0, 0)))
    full_pack, tokens_all, dy_rows, onehot, info, my_down, in_weight = start(
        pack, tokens[0], cotangent[0], ids, expert_weight, members, per_core, padded
    )
    full_pack = full_pack.reshape(members * d_rows, -1)[:, :columns]
    width = members * d_rows
    proj_full = full_pack[:, : 3 * hh]
    outw_own = full_pack[:, 3 * hh : 4 * hh]
    outw_other = swap(outw_own)
    rest = full_pack[:, 4 * hh :]
    gains = rest[:, :2].T.astype(single)
    const_f = rest[:, 2:4].T.astype(single)
    router_full = rest[:, 4:]
    my_in = lax.all_to_all(in_weight, "dp", 0, 0, tiled=True)

    x_rows = tokens[0].astype(single)
    local_rows = x_rows.shape[0]
    x_all = tokens_all.astype(single)
    scale_all = rms_scale(x_all)
    full_one = (x_all * scale_all * gains[0]).astype(half)
    scale_one = half_of(scale_all, core)
    seq = full_one.shape[0]
    qkv = mm(full_one, proj_full).astype(half)
    size = fit(seq, 256)
    starts = info[0]
    bounds = block_bounds(starts, info[1], size)
    columns = info.T
    heads_full, heads_out, lse = attention_forward(qkv, bounds, starts, size)
    prev_rows = prev_logits[0]
    mixed_prev = jnp.dot(prev_rows, gate_mixing, precision=HIGH)
    mixed_prev = jnp.pad(mixed_prev, ((0, 0), (0, LANES - EXPERTS)))
    router_wide = jnp.pad(router_full, ((0, 0), (0, LANES - router_full.shape[1])))
    mix_wide = jnp.pad(gate_mixing, ((0, LANES - EXPERTS), (0, LANES - EXPERTS)))
    prev_wide = jnp.pad(prev_rows, ((0, 0), (0, LANES - EXPERTS)))
    router_wide, mixed_prev, mix_wide, prev_wide, columns, proj_full = lax.optimization_barrier(
        (router_wide, mixed_prev, mix_wide, prev_wide, columns, proj_full)
    )
    back_grad, gated_out, got_rows, out_grad, hidden, pg, pu, resid, normed_two, misc = experts(
        my_down,
        my_in,
        dy_rows,
        heads_out,
        tokens[0],
        outw_own,
        outw_other,
        gains,
        router_wide,
        mixed_prev,
        routes[0],
        onehot,
        padded,
    )
    count = EXPERTS_FF * padded
    grads_sent = weight_step(
        got_rows.reshape(count, width),
        out_grad.reshape(count, width),
        hidden,
        pg,
        pu,
        1 if d_rows % 16 else members,
    )
    back_out = in_group(gated_out)
    back_grad, grads_sent, back_out = lax.optimization_barrier((back_grad, grads_sent, back_out))
    if d_rows % 16:
        grads_sent = grads_sent.reshape(3, members, d_rows, -1).transpose(1, 0, 2, 3)
    grads_got = lax.all_to_all(grads_sent, "dp", 0, 0, tiled=True)

    resid_grad, attn_all, heads_grad, base, prev_grad, small, mixing_grad = backward_middle(
        back_grad,
        columns,
        resid,
        normed_two,
        misc,
        cotangent[0],
        routes[0],
        gains,
        const_f,
        router_wide,
        outw_own,
        outw_other,
        prev_wide,
        mix_wide,
        padded,
    )
    out_w_grad = mm_tn(attn_all, heads_out)
    qkv_grad = attention_backward(qkv, heads_grad, heads_full, lse, bounds, starts, size)
    qkv_grad, grads_got = lax.optimization_barrier((qkv_grad, grads_got))
    out_w_grad = out_w_grad.astype(half)
    if d_rows % 16 or members != 16:
        outs = plain_tail(
            back_out, qkv_grad, full_one, proj_full, out_w_grad, x_all, base, resid_grad, gains, small, grads_got
        )
    else:
        outs = tail(
            members,
            back_out,
            qkv_grad,
            full_one,
            proj_full,
            out_w_grad,
            tokens_all,
            base,
            resid_grad,
            columns,
            gains,
            small,
            grads_got,
            padded,
        )
    proj_shard, outw_shard, tokens_grad, mixed, small, expert_shard = outs
    mixing_total = small[20:22].reshape(EXPERTS, LANES)[:, :EXPERTS]
    features = lax.dynamic_slice_in_dim(small, lax.axis_index("dp") * d_rows, d_rows, 1)
    return (
        mixed[None],
        tokens_grad[None],
        prev_grad[None, :, :EXPERTS],
        proj_shard,
        outw_shard,
        features[18:20],
        expert_shard,
        features[:16].T,
        features[16:18],
        mixing_total,
    )


def solution(mesh):
    return jax.shard_map(
        per_device,
        mesh=mesh,
        in_specs=(
            P("dp", "tensor", None),
            P("dp", "tensor"),
            P("dp", "tensor", None),
            P("dp", "tensor", None),
            P("dp", "tensor", None),
            P(None, "dp", "tensor"),
            P("dp", "tensor"),
            P(None, "dp"),
            P(None, None, "dp", "tensor"),
            P("dp", None),
            P(None, "dp"),
            P(),
        ),
        out_specs=(
            P("dp", "tensor", None),
            P("dp", "tensor", None),
            P("dp", "tensor", None),
            P(None, "dp", "tensor"),
            P("dp", "tensor"),
            P(None, "dp"),
            P(None, None, "dp", "tensor"),
            P("dp", None),
            P(None, "dp"),
            P(),
        ),
        check_vma=False,
    )
```

```python
import functools

import jax
import jax.numpy as jnp
from jax import lax
from jax.experimental import pallas as pl
from jax.experimental.pallas import tpu as pltpu
from jax.sharding import PartitionSpec as P

HEAD_DIM = 64
EXPERTS_FF = 8
EXPERTS = 12
CAPACITY = 341


EPS = 1e-05
HIGH = lax.Precision.HIGHEST
NEG = -1e30
LANES = 128
DOCS = 8
LOG2E = 1.4426950408889634
MESH = pl.DeviceIdType.MESH
single = jnp.float32
half = jnp.bfloat16


def rms_scale(rows):
    return lax.rsqrt(jnp.mean(rows * rows, axis=-1, keepdims=True) + EPS)


def softmax_last(values):
    peak = jnp.max(values, axis=-1, keepdims=True)
    expo = jnp.exp(values - peak)
    return expo / jnp.sum(expo, axis=-1, keepdims=True)


def mm(a, b):
    return jnp.dot(a, b, preferred_element_type=single)


def mm_nt(a, b):
    return lax.dot_general(a, b, (((1,), (1,)), ((), ())), preferred_element_type=single)


def mm_tn(a, b):
    return lax.dot_general(a, b, (((0,), (0,)), ((), ())), preferred_element_type=single)


def swap(x):
    return lax.ppermute(x, "tensor", [(0, 1), (1, 0)])


def in_order(own, other):
    first = lax.axis_index("tensor") == 0
    return jnp.concatenate([jnp.where(first, own, other), jnp.where(first, other, own)], 0)


def half_of(full, which):
    count = full.shape[0] // 2
    return lax.dynamic_slice_in_dim(full, which * count, count, 0)


def pair_sum(full):
    core = lax.axis_index("tensor")
    other = swap(half_of(full, 1 - core).astype(half))
    return half_of(full, core) + other.astype(single)


def fit(seq, want):
    return want if seq % want == 0 else seq

def block_bounds(start, end, size):
    edges = start.reshape(-1, size)
    number = jnp.arange(edges.shape[0], dtype=jnp.int32)
    low = edges[:, 0] // size
    plain = jnp.clip((edges[:, -1] + size - 1) // size, low, number)
    high = end.reshape(-1, size)[:, -1] // size
    clear = jnp.sum((edges[None, :, -1] <= number[:, None] * size).astype(jnp.int32), axis=1)
    clear = jnp.clip(clear, number + 1, high + 1)
    return jnp.stack([low, plain, high, clear])


def head_lanes(h, rows):
    lane = lax.broadcasted_iota(jnp.int32, (rows, LANES), 1)
    return (lane < HEAD_DIM) if h % 2 == 0 else (lane >= HEAD_DIM)

def fwd_kernel(heads, bounds, q_ref, k_ref, v_ref, start_ref, o_ref, low_ref, lse_ref, s_ref, m_ref, l_ref, acc_ref, qm_ref):
    size = q_ref.shape[0]
    i = pl.program_id(0)
    low, plain = bounds[0, i], bounds[1, i]
    factor = LOG2E * HEAD_DIM ** -0.5
    for h in range(heads):
        pair = pl.ds(h // 2 * LANES, LANES)
        qm_ref[h] = jnp.where(head_lanes(h, size), q_ref[:, pair], 0).astype(half)
    m_ref[...] = jnp.full(m_ref.shape, NEG, single)
    l_ref[...] = jnp.zeros(l_ref.shape, single)
    acc_ref[...] = jnp.zeros(acc_ref.shape, single)

    def score(j, masked):
        rows = pl.ds(pl.multiple_of(j * size, size), size)
        if masked:
            row = i * size + lax.broadcasted_iota(jnp.int32, (size, size), 0)
            col = j * size + lax.broadcasted_iota(jnp.int32, (size, size), 1)
            allowed = (col <= row) & (col >= start_ref[...])
        for h in range(heads):
            s = mm_nt(qm_ref[h], k_ref[rows, pl.ds(h // 2 * LANES, LANES)])
            if masked:
                s = jnp.where(allowed, s, NEG)
            s_ref[h, j] = s
            m = m_ref[h]
            for c in range(size // LANES):
                m = jnp.maximum(m, s[:, c * LANES : (c + 1) * LANES])
            m_ref[h] = m

    pl.loop(low, plain)(lambda j: score(j, True))
    pl.loop(plain, i)(lambda j: score(j, False))
    score(i, True)
    for h in range(heads):
        m_ref[h] = jnp.broadcast_to(jnp.max(m_ref[h], axis=1, keepdims=True) * factor, (size, LANES))

    def gather(j):
        rows = pl.ds(pl.multiple_of(j * size, size), size)
        for h in range(heads):
            s = s_ref[h, j]
            m = m_ref[h]
            l = l_ref[h]
            parts = []
            for c in range(size // LANES):
                p = jnp.exp2(s[:, c * LANES : (c + 1) * LANES] * factor - m)
                l = l + p
                parts.append(p.astype(half))
            l_ref[h] = l
            acc_ref[h] += jnp.dot(jnp.concatenate(parts, 1), v_ref[rows, pl.ds(h // 2 * LANES, LANES)], preferred_element_type=single)

    pl.loop(low, i + 1)(gather)
    lane = lax.broadcasted_iota(jnp.int32, (size, LANES), 1)
    lse = jnp.zeros((size, LANES), single)
    for h in range(0, heads, 2):
        outs = []
        for k in (h, h + 1):
            l = jnp.sum(l_ref[k], axis=1, keepdims=True)
            outs.append(acc_ref[k] / l)
            lse = jnp.where(lane == k, m_ref[k] + jnp.log2(l), lse)
        out = jnp.where(lane < HEAD_DIM, outs[0], outs[1])
        o_ref[:, pl.ds(h // 2 * LANES, LANES)] = out
        low_ref[:, pl.ds(h // 2 * LANES, LANES)] = out.astype(half)
    lse_ref[...] = lse

def attention_forward(qkv, seg_bounds, starts, size):
    seq = qkv.shape[0]
    hh = qkv.shape[1] // 3
    heads = hh // HEAD_DIM
    return pl.pallas_call(
        functools.partial(fwd_kernel, heads),
        grid_spec=pltpu.PrefetchScalarGridSpec(
            num_scalar_prefetch=1,
            grid=(seq // size,),
            in_specs=[
                pl.BlockSpec((size, hh), lambda i, b: (i, 0)),
                pl.BlockSpec((seq, hh), lambda i, b: (0, 1)),
                pl.BlockSpec((seq, hh), lambda i, b: (0, 2)),
                pl.BlockSpec((size, 1), lambda i, b: (i, 0)),
            ],
            out_specs=[
                pl.BlockSpec((size, hh), lambda i, b: (i, 0)),
                pl.BlockSpec((size, hh), lambda i, b: (i, 0)),
                pl.BlockSpec((size, LANES), lambda i, b: (i, 0)),
            ],
            scratch_shapes=[
                pltpu.VMEM((heads, seq // size, size, size), single),
                pltpu.VMEM((heads, size, LANES), single),
                pltpu.VMEM((heads, size, LANES), single),
                pltpu.VMEM((heads, size, LANES), single),
                pltpu.VMEM((heads, size, LANES), half),
            ],
        ),
        out_shape=[
            jax.ShapeDtypeStruct((seq, hh), single),
            jax.ShapeDtypeStruct((seq, hh), half),
            jax.ShapeDtypeStruct((seq, LANES), single),
        ],
        compiler_params=pltpu.CompilerParams(vmem_limit_bytes=48 << 20),
        cost_estimate=pl.CostEstimate(flops=4 * seq * seq * LANES * heads, bytes_accessed=16 * seq * hh, transcendentals=0),
    )(seg_bounds, qkv, qkv, qkv, starts[:, None])

def bwd_kernel(
    heads, bounds, q_ref, k_ref, v_ref, do_ref, o_ref, lse_ref, start_ref, out_ref, dq_ref, dk_ref, dv_ref, stat_ref
):
    size = k_ref.shape[0]
    j = pl.program_id(0)
    high, clear = bounds[2, j], bounds[3, j]
    factor = LOG2E * HEAD_DIM ** -0.5
    hh = k_ref.shape[1]

    @pl.when(j == 0)
    def _():
        dq_ref[...] = jnp.zeros(dq_ref.shape, single)
        feature = lax.broadcasted_iota(jnp.int32, (hh, LANES), 0)
        lane = lax.broadcasted_iota(jnp.int32, (hh, LANES), 1)
        pick = (feature // HEAD_DIM + 8 == lane).astype(half)

        @pl.loop(0, q_ref.shape[0] // size)
        def _(i):
            rows = pl.ds(pl.multiple_of(i * size, size), size)
            product = o_ref[rows, :] * do_ref[rows, :].astype(single)
            top = product.astype(half)
            low = (product - top.astype(single)).astype(half)
            both = mm(top, pick) + mm(low, pick) + lse_ref[rows, :]
            stat_ref[:, rows] = both.T[:16, :]

    dk_ref[...] = jnp.zeros(dk_ref.shape, single)
    dv_ref[...] = jnp.zeros(dv_ref.shape, single)

    def step(i, masked):
        rows = pl.ds(pl.multiple_of(i * size, size), size)
        if masked:
            key = j * size + lax.broadcasted_iota(jnp.int32, (size, size), 0)
            query = i * size + lax.broadcasted_iota(jnp.int32, (size, size), 1)
            allowed = (key <= query) & (key >= start_ref[:, rows])
        for pair in range(heads // 2):
            lanes = pl.ds(pair * LANES, LANES)
            k, v = k_ref[:, lanes], v_ref[:, lanes]
            q, do = q_ref[rows, lanes], do_ref[rows, lanes]
            ps, dss, qs, dos, ks = [], [], [], [], []
            for h in (2 * pair, 2 * pair + 1):
                mine = head_lanes(h, size)
                qm = jnp.where(mine, q, 0).astype(half)
                dom = jnp.where(mine, do, 0).astype(half)
                s = mm_nt(k, qm) * factor - stat_ref[pl.ds(h, 1), rows]
                if masked:
                    s = jnp.where(allowed, s, NEG)
                p = jnp.exp2(s)
                ds = p * (mm_nt(v, dom) - stat_ref[pl.ds(8 + h, 1), rows])
                ps.append(p.astype(half))
                dss.append(ds.astype(half))
                qs.append(qm)
                dos.append(dom)
                ks.append(jnp.where(mine, k, 0).astype(half))
            dv_ref[:, lanes] += jnp.dot(jnp.concatenate(ps, 1), jnp.concatenate(dos, 0), preferred_element_type=single)
            dk_ref[:, lanes] += jnp.dot(jnp.concatenate(dss, 1), jnp.concatenate(qs, 0), preferred_element_type=single)
            dq_ref[rows, lanes] += mm_tn(jnp.concatenate(dss, 0), jnp.concatenate(ks, 0))

    step(j, True)
    pl.loop(j + 1, clear)(lambda i: step(i, False))
    pl.loop(clear, high + 1)(lambda i: step(i, True))
    mine = pl.ds(pl.multiple_of(j * size, size), size)
    out_ref[mine, pl.ds(hh, hh)] = (dk_ref[...] * HEAD_DIM ** -0.5).astype(half)
    out_ref[mine, pl.ds(2 * hh, hh)] = dv_ref[...].astype(half)
    out_ref[mine, pl.ds(0, hh)] = (dq_ref[mine, :] * HEAD_DIM ** -0.5).astype(half)

def attention_backward(qkv, do, heads_out, lse, seg_bounds, starts, size):
    seq = qkv.shape[0]
    hh = qkv.shape[1] // 3
    heads = hh // HEAD_DIM
    return pl.pallas_call(
        functools.partial(bwd_kernel, heads),
        grid_spec=pltpu.PrefetchScalarGridSpec(
            num_scalar_prefetch=1,
            grid=(seq // size,),
            in_specs=[
                pl.BlockSpec((seq, hh), lambda j, b: (0, 0)),
                pl.BlockSpec((size, hh), lambda j, b: (j, 1)),
                pl.BlockSpec((size, hh), lambda j, b: (j, 2)),
                pl.BlockSpec((seq, hh), lambda j, b: (0, 0)),
                pl.BlockSpec((seq, hh), lambda j, b: (0, 0)),
                pl.BlockSpec((seq, LANES), lambda j, b: (0, 0)),
                pl.BlockSpec((1, seq), lambda j, b: (0, 0)),
            ],
            out_specs=pl.BlockSpec((seq, 3 * hh), lambda j, b: (0, 0)),
            scratch_shapes=[
                pltpu.VMEM((seq, hh), single),
                pltpu.VMEM((size, hh), single),
                pltpu.VMEM((size, hh), single),
                pltpu.VMEM((16, seq), single),
            ],
        ),
        out_shape=jax.ShapeDtypeStruct((seq, 3 * hh), half),
        compiler_params=pltpu.CompilerParams(vmem_limit_bytes=48 << 20),
        cost_estimate=pl.CostEstimate(flops=10 * seq * seq * LANES * heads, bytes_accessed=20 * seq * hh, transcendentals=0),
    )(seg_bounds, qkv, qkv, qkv, do, heads_out, lse, starts[None, :])


def flip(number, k):
    out = 0
    for bit in (1, 2, 4):
        digit = lax.rem(number // bit, 2)
        out = out + bit * ((1 - digit) if k & bit else digit)
    return out


BESIDE = (3, 1, 2)
NEAR = (3, 4, 5, 2, 6, 1, 7)
PAIRS = ((0, 3), (4, 5), (2, 6), (1, 7))


def start_kernel(
    members,
    low,
    per_core,
    padded,
    pack_ref,
    tok_ref,
    dy_ref,
    ids_ref,
    w_ref,
    full_ref,
    all_ref,
    rows_ref,
    hot_ref,
    info_ref,
    down_ref,
    in_ref,
    ids_all_ref,
    dy_all_ref,
    place_ref,
    send_sem,
    recv_sem,
    own_sem,
    swap_send,
    swap_recv,
    down_send,
    down_recv,
):
    size = EXPERTS_FF
    me = lax.axis_index("dp")
    core = lax.axis_index("tensor")
    high = members // low
    inside, row = lax.rem(me, low), me // low
    mine = lax.rem(me, size)
    base = me - mine
    local = tok_ref.shape[0]
    seq = 2 * local
    partner = {"tensor": 1 - core}

    def beside(k):
        return row * low + flip(inside, k)

    def across(k):
        return lax.rem(row + k, high) * low + inside

    peers = [beside(k) for k in BESIDE] + [across(k) for k in range(1, high)]
    groups = members // size

    def device_at(g, k):
        return lax.rem(base + g * size, members) + flip(mine, k)

    distant = [(g, k) for k in (0,) + NEAR for g in range(groups) if g or k]
    peers += [device_at(g, k) for g, k in distant]
    barrier = pltpu.get_barrier_semaphore()
    for peer in peers:
        pl.semaphore_signal(barrier, inc=1, device_id={"dp": peer}, device_id_type=MESH)
    pl.semaphore_signal(barrier, inc=1, device_id=partner, device_id_type=MESH)
    pl.semaphore_wait(barrier, len(peers) + 1)

    def remote(src, dst, send, recv, device):
        return pltpu.make_async_remote_copy(
            src_ref=src,
            dst_ref=dst,
            send_sem=send,
            recv_sem=recv,
            device_id=device,
            device_id_type=MESH,
        )

    def push(source, block, target, slot):
        copy = remote(
            source, full_ref.at[block], send_sem.at[slot], recv_sem.at[block], {"dp": target}
        )
        copy.start()
        return copy

    def arrived(block):
        remote(
            pack_ref, full_ref.at[block], send_sem.at[0], recv_sem.at[block], {"dp": peers[0]}
        ).wait_recv()

    sent = [push(pack_ref, me, across(k), k) for k in range(1, high)]
    sent += [push(pack_ref, me, beside(k), high + k) for k in BESIDE]
    own_rows = pl.ds(pl.multiple_of(core * local, local), local)
    swaps = [
        remote(ids_ref, ids_all_ref.at[core], swap_send.at[0], swap_recv.at[0], partner),
        remote(dy_ref, dy_all_ref.at[own_rows], swap_send.at[1], swap_recv.at[1], partner),
        remote(tok_ref, all_ref.at[own_rows], swap_send.at[2], swap_recv.at[2], partner),
    ]
    owns = [
        pltpu.make_async_copy(ids_ref, ids_all_ref.at[core], own_sem.at[0]),
        pltpu.make_async_copy(dy_ref, dy_all_ref.at[own_rows], own_sem.at[1]),
        pltpu.make_async_copy(tok_ref, all_ref.at[own_rows], own_sem.at[2]),
        pltpu.make_async_copy(pack_ref, full_ref.at[me], own_sem.at[3]),
        pltpu.make_async_copy(w_ref.at[mine, 2], down_ref.at[me], own_sem.at[4]),
    ]
    owns += [
        pltpu.make_async_copy(
            w_ref.at[:, pl.ds(0, 2)], in_ref.at[pl.ds(g * size, size)], own_sem.at[5 + g]
        )
        for g in range(groups)
    ]
    for copy in swaps + owns:
        copy.start()

    swaps[0].wait()
    owns[0].wait()
    ids = jnp.concatenate([ids_all_ref[0], ids_all_ref[1]], 1)
    seg = ids[:1]
    number = lax.broadcasted_iota(jnp.int32, (8, seq), 0)
    starts = jnp.zeros((1, seq), jnp.int32)
    ends = jnp.zeros((1, seq), jnp.int32)
    total = jnp.zeros((1, 1), jnp.int32)
    for d in range(DOCS):
        here = seg == d
        starts = jnp.where(here, total, starts)
        total = total + jnp.sum(here.astype(jnp.int32), axis=1, keepdims=True)
        ends = jnp.where(here, total - 1, ends)
    row16 = lax.broadcasted_iota(jnp.int32, (16, LANES), 0)
    first = lax.broadcasted_iota(jnp.int32, (LANES, LANES), 0)
    second = lax.broadcasted_iota(jnp.int32, (LANES, LANES), 1)
    upper = (first < second).astype(half)
    before = jnp.zeros((16, 1), single)
    for c in range(seq // LANES):
        lanes = slice(c * LANES, (c + 1) * LANES)
        member = (ids[1:2, lanes] == row16) | (ids[2:3, lanes] == row16)
        member = jnp.where(member & (row16 < size), 1.0, 0.0)
        position = mm(member.astype(half), upper) + before
        before = before + jnp.sum(member, axis=1, keepdims=True)
        place = position - (core * per_core).astype(single)
        kept = (member > 0.5) & (position < CAPACITY) & (place >= 0) & (place < per_core)
        place_ref[:, lanes] = jnp.where(kept, place, -1.0).astype(jnp.int32)
    slot = lax.broadcasted_iota(jnp.int32, (padded, seq), 0)
    for e in range(size):
        hot_ref[e * padded : (e + 1) * padded, :] = jnp.where(
            place_ref[e : e + 1, :] == slot, 1.0, 0.0
        ).astype(half)

    info = jnp.where(number == 0, starts, jnp.where(number == 1, ends, -1))
    for k in range(2):
        chosen = jnp.full((1, seq), -1, jnp.int32)
        for e in range(size):
            place = place_ref[e : e + 1, :]
            chosen = jnp.where(
                (ids[k + 1 : k + 2] == e) & (place >= 0), place + e * padded, chosen
            )
        info = jnp.where(number == k + 2, chosen, info)
    info_ref[...] = info

    for k in range(1, high):
        block = across(high - k)
        arrived(block)
        for step in BESIDE:
            sent.append(push(full_ref.at[block], block, beside(step), high + k * low + step))

    for g, k in distant:
        copy = remote(
            w_ref.at[flip(mine, k), 2],
            down_ref.at[me],
            down_send.at[g * size + k],
            down_recv.at[me],
            {"dp": device_at(g, k)},
        )
        copy.start()
        sent.append(copy)

    swaps[1].wait()
    owns[1].wait()
    for e in range(0, size, 2):
        slots = slice(e * padded, (e + 2) * padded)
        rows = mm(hot_ref[slots, :], dy_all_ref[...])
        rows_ref[e : e + 2] = rows.astype(half).reshape(2, padded, rows.shape[1])
    for k in BESIDE:
        block = beside(k)
        arrived(block)
        for step in range(1, high):
            arrived(lax.rem(block + step * low, members))
    for g, k in distant:
        block = device_at((groups - g) % groups, k)
        remote(
            w_ref.at[0, 2], down_ref.at[block], down_send.at[0], down_recv.at[block], partner
        ).wait_recv()
    for copy in sent:
        copy.wait_send()
    for copy in owns[2:]:
        copy.wait()
    swaps[2].wait()


def start(pack, tokens, dy, ids, w, members, per_core, padded):
    low = 4
    high = members // low
    local, width = tokens.shape
    count = EXPERTS_FF * padded
    any_spec = pl.BlockSpec(memory_space=pl.ANY)
    vmem = pl.BlockSpec(memory_space=pltpu.VMEM)
    hbm = pl.BlockSpec(memory_space=pltpu.HBM)
    dma = pltpu.SemaphoreType.DMA
    return pl.pallas_call(
        functools.partial(start_kernel, members, low, per_core, padded),
        out_shape=[
            jax.ShapeDtypeStruct((members,) + pack.shape, half),
            jax.ShapeDtypeStruct((2 * local, width), half),
            jax.ShapeDtypeStruct((EXPERTS_FF, padded, width), half),
            jax.ShapeDtypeStruct((count, 2 * local), half),
            jax.ShapeDtypeStruct((8, 2 * local), jnp.int32),
            jax.ShapeDtypeStruct((members,) + w.shape[2:], half),
            jax.ShapeDtypeStruct((members, 2) + w.shape[2:], half),
        ],
        in_specs=[any_spec, hbm, hbm, any_spec, hbm],
        out_specs=[any_spec] * 2 + [vmem] * 3 + [any_spec, hbm],
        scratch_shapes=[
            pltpu.VMEM((2, 8, local), jnp.int32),
            pltpu.VMEM((2 * local, width), half),
            pltpu.VMEM((16, 2 * local), jnp.int32),
            dma((high * (low + 1),)),
            dma((members,)),
            dma((5 + members // EXPERTS_FF,)),
            dma((3,)),
            dma((3,)),
            dma((members,)),
            dma((members,)),
        ],
        compiler_params=pltpu.CompilerParams(
            collective_id=0, has_side_effects=True, vmem_limit_bytes=40 << 20
        ),
        name="start",
    )(pack, tokens, dy, ids, w)


def experts_kernel(
    members,
    padded,
    down_hbm_ref,
    in_ref,
    dy_hbm_ref,
    ho_ref,
    tok_ref,
    own_w_ref,
    other_w_ref,
    gain_ref,
    router_ref,
    prev_ref,
    routes_ref,
    hot_hbm_ref,
    back_ref,
    out_ref,
    x_ref,
    og_ref,
    hid_ref,
    pg_ref,
    pu_ref,
    resid_ref,
    normed_ref,
    misc_ref,
    ho_in_ref,
    both_ref,
    acc_ref,
    stage_ref,
    row_ref,
    win_ref,
    down_ref,
    dy_ref,
    ig_ref,
    spill_ref,
    gate_ref,
    dot_ref,
    hot_ref,
    x_send,
    x_recv,
    dy_send,
    dy_recv,
    own_sem,
    swap_send,
    swap_recv,
    ig_send,
    ig_recv,
    spill_sem,
):
    size = EXPERTS_FF
    groups = members // size
    me = lax.axis_index("dp")
    core = lax.axis_index("tensor")
    mine = lax.rem(me, size)
    base = me - mine
    local, width = tok_ref.shape
    partner = {"tensor": 1 - core}
    near = [base + lax.rem(mine + k, size) for k in range(1, size)]
    barrier = pltpu.get_barrier_semaphore()
    for peer in near:
        pl.semaphore_signal(barrier, inc=1, device_id={"dp": peer}, device_id_type=MESH)
    pl.semaphore_signal(barrier, inc=1, device_id=partner, device_id_type=MESH)
    pl.semaphore_wait(barrier, size)

    def remote(src, dst, send, recv, device):
        return pltpu.make_async_remote_copy(
            src_ref=src,
            dst_ref=dst,
            send_sem=send,
            recv_sem=recv,
            device_id=device,
            device_id_type=MESH,
        )

    own_rows = pl.ds(pl.multiple_of(core * local, local), local)
    other_rows = pl.ds(pl.multiple_of((1 - core) * local, local), local)
    heads = remote(ho_ref.at[other_rows], ho_in_ref, swap_send.at[0], swap_recv.at[0], partner)
    heads.start()
    load_hot = pltpu.make_async_copy(hot_hbm_ref, hot_ref, own_sem.at[4])
    load_hot.start()
    waits = []
    for k in NEAR:
        to = flip(mine, k)
        copy = remote(
            dy_hbm_ref.at[to], dy_ref.at[mine], dy_send.at[k], dy_recv.at[k], {"dp": base + to}
        )
        copy.start()
        waits.append(copy)
    pair_in = remote(in_ref, win_ref.at[1], swap_send.at[2], swap_recv.at[2], partner)
    pair_in.start()
    pair_down = remote(down_hbm_ref, down_ref.at[1], swap_send.at[3], swap_recv.at[3], partner)
    pair_down.start()
    owns = [
        pltpu.make_async_copy(in_ref, win_ref.at[0], own_sem.at[1]),
        pltpu.make_async_copy(dy_hbm_ref.at[mine], dy_ref.at[mine], own_sem.at[2]),
        pltpu.make_async_copy(down_hbm_ref, down_ref.at[0], own_sem.at[3]),
    ]
    for copy in owns:
        copy.start()

    step = fit(local, 256)
    heads.wait()

    @pl.loop(0, local // step)
    def _(r):
        rows = pl.ds(pl.multiple_of(r * step, step), step)
        mine_rows = pl.ds(pl.multiple_of(core * local + r * step, step), step)
        resid = tok_ref[rows, :].astype(single)
        resid += mm_nt(ho_ref[mine_rows, :], own_w_ref[...])
        resid += mm_nt(ho_in_ref[rows, :], other_w_ref[...])
        resid_ref[rows, :] = resid
        normed = (resid * rms_scale(resid) * gain_ref[1:2, :]).astype(half)
        normed_ref[rows, :] = normed
        router = mm(normed, router_ref[...])
        lane = lax.broadcasted_iota(jnp.int32, (step, LANES), 1)
        logits = jnp.where(lane < EXPERTS, router + prev_ref[rows, :], 0.0)
        hits = [lane == routes_ref[rows, k : k + 1] for k in range(2)]
        picked = [jnp.sum(jnp.where(hit, logits, 0.0), axis=1, keepdims=True) for hit in hits]
        peak = jnp.maximum(picked[0], picked[1])
        expo = [jnp.exp(p - peak) for p in picked]
        total = expo[0] + expo[1]
        gates = [e / total for e in expo]
        misc_ref[rows, :] = jnp.where(lane == 0, gates[0], jnp.where(lane == 1, gates[1], router))
        spread = sum(
            jnp.where(hit & (lane < size), gate.astype(half).astype(single), 0.0)
            for hit, gate in zip(hits, gates)
        )
        both_ref[mine_rows, pl.ds(0, width)] = normed
        both_ref[mine_rows, pl.ds(width, LANES)] = spread.astype(half)

    swap_rows = remote(
        both_ref.at[own_rows], both_ref.at[own_rows], swap_send.at[1], swap_recv.at[1], partner
    )
    swap_rows.start()

    load_hot.wait()
    for number, pair in enumerate(PAIRS):
        slots = [
            pl.ds(pl.multiple_of(flip(mine, k) * padded, 16), padded) for k in pair
        ]
        hot = jnp.concatenate([hot_ref[s, own_rows] for s in slots], 0)
        acc_ref[number] = mm(hot, both_ref[own_rows, :])
    swap_rows.wait_recv()
    row_ref[...] = jnp.zeros(row_ref.shape, single)
    for number, pair in enumerate(PAIRS):
        slots = [
            pl.ds(pl.multiple_of(flip(mine, k) * padded, 16), padded) for k in pair
        ]
        hot = jnp.concatenate([hot_ref[s, other_rows] for s in slots], 0)
        acc_ref[number] += mm(hot, both_ref[other_rows, :])
        for place, k in enumerate(pair):
            to = flip(mine, k)
            first = place * padded
            tail = acc_ref[number, first : first + padded, width:].astype(half)
            lane = lax.broadcasted_iota(jnp.int32, (16, LANES), 1)
            row_ref[:, :padded] = mm_nt((lane == to).astype(half), tail)
            stage_ref[to] = acc_ref[number, first : first + padded, :width].astype(half)
            last = acc_ref[number, first + padded - 16 : first + padded, : 2 * LANES]
            row = lax.broadcasted_iota(jnp.int32, (16, 2 * LANES), 0)
            last = jnp.where(row == 15, row_ref[...], last)
            stage_ref[to, padded - 16 :, : 2 * LANES] = last.astype(half)
            if k:
                copy = remote(
                    stage_ref.at[to], x_ref.at[mine], x_send.at[k], x_recv.at[k], {"dp": base + to}
                )
                waits.append(copy)
            else:
                copy = pltpu.make_async_copy(stage_ref.at[to], x_ref.at[mine], own_sem.at[0])
            copy.start()

    for copy in owns:
        copy.wait()
    pair_in.wait_recv()
    pair_down.wait_recv()

    ff = in_ref.shape[3]
    block = fit(ff, 512)
    steps = ff // block
    rows2 = 2 * padded
    dot_ref[...] = jnp.zeros(dot_ref.shape, single)

    def spill(slot, array, place, source, part, f):
        out = (hid_ref, pg_ref, pu_ref)[array]
        rows = pl.ds(pl.multiple_of(source * padded, 16), padded)
        return pltpu.make_async_copy(
            spill_ref.at[slot, array, pl.ds(place * padded, padded)],
            out.at[part, rows, pl.ds(f * block, block)],
            spill_sem.at[slot, array, place],
        )

    def arrived(k):
        remote(dy_hbm_ref.at[0], dy_ref.at[0], dy_send.at[0], dy_recv.at[k], partner).wait_recv()
        remote(stage_ref.at[0], x_ref.at[0], x_send.at[0], x_recv.at[k], partner).wait_recv()

    def give_back(k, source):
        return remote(
            ig_ref.at[source], back_ref.at[mine], ig_send.at[k], ig_recv.at[k], {"dp": base + source}
        )

    @pl.loop(0, size // 2)
    def _(q):
        ks, sources = [], []
        for place in range(2):
            k, source = PAIRS[0][place], flip(mine, PAIRS[0][place])
            for number in range(1, size // 2):
                k = jnp.where(q == number, PAIRS[number][place], k)
                source = jnp.where(q == number, flip(mine, PAIRS[number][place]), source)
            ks.append(k)
            sources.append(source)

        @pl.when(q == 0)
        def _():
            pltpu.make_async_copy(stage_ref.at[0], x_ref.at[0], own_sem.at[0]).wait()

        @pl.when(q > 0)
        def _():
            arrived(ks[0])

        arrived(ks[1])
        for place, source in enumerate(sources):
            rows = pl.ds(place * padded, padded)
            gates = x_ref[source, padded - 16 :, : 2 * LANES].astype(single).T
            gate = jnp.broadcast_to(gates[:padded, 15:16], (padded, LANES))
            gate_ref[rows, :] = gate
            og_ref[source] = (dy_ref[source].astype(single) * gate[:, :1]).astype(half)
        for number in range(2):
            acc_ref[number, :, :width] = jnp.zeros((rows2, width), single)

        @pl.loop(0, 2)
        def _(part):
            for f in range(steps):
                lanes = pl.ds(f * block, block)
                slot = f % 2
                if f >= 2:
                    for array in range(3):
                        for place, source in enumerate(sources):
                            spill(slot, array, place, source, part, f - 2).wait()
                gate_w = win_ref[part, :, 0, :, lanes].reshape(width, block)
                up_w = win_ref[part, :, 1, :, lanes].reshape(width, block)
                down_w = down_ref[part, :, :, lanes].reshape(width, block)
                x = jnp.concatenate([x_ref[source] for source in sources], 0)
                og = jnp.concatenate([og_ref[source] for source in sources], 0)
                pre = mm(x, gate_w)
                up = mm(x, up_w)
                hg = mm(og, down_w)
                sigma = jax.nn.sigmoid(pre)
                active = pre * sigma
                hidden = (active * up).astype(half)
                pg = (hg * up * (sigma * (1.0 + pre * (1.0 - sigma)))).astype(half)
                pu = (hg * active).astype(half)
                spill_ref[slot, 0] = hidden
                spill_ref[slot, 1] = pg
                spill_ref[slot, 2] = pu
                acc_ref[0, :, :width] += mm_nt(hidden, down_w)
                acc_ref[1, :, :width] += mm_nt(pg, gate_w) + mm_nt(pu, up_w)
                for array in range(3):
                    for place, source in enumerate(sources):
                        spill(slot, array, place, source, part, f).start()
            for f in range(max(0, steps - 2), steps):
                for array in range(3):
                    for place, source in enumerate(sources):
                        spill(f % 2, array, place, source, part, f).wait()

        ones = jnp.ones((16, width), half)
        for place, source in enumerate(sources):
            rows = pl.ds(place * padded, padded)
            eo = acc_ref[0, rows, :width]
            out_ref[source] = (eo * gate_ref[rows, :1]).astype(half)
            ig_ref[source] = acc_ref[1, rows, :width].astype(half)
            product = eo * dy_ref[source].astype(single)
            top = product.astype(half)
            low = (product - top.astype(single)).astype(half)
            dot_ref[:, :padded] = mm_nt(ones, top) + mm_nt(ones, low)
            dots = dot_ref[...]
            high = dots.astype(half).astype(single)
            row = lax.broadcasted_iota(jnp.int32, dots.shape, 0)
            last = acc_ref[1, pl.ds((place + 1) * padded - 16, 16), : 2 * LANES]
            last = jnp.where(row == 14, high, jnp.where(row == 15, dots - high, last))
            ig_ref[source, padded - 16 :, : 2 * LANES] = last.astype(half)

        @pl.when(q == 0)
        def _():
            pltpu.make_async_copy(ig_ref.at[mine], back_ref.at[mine], own_sem.at[0]).start()

        @pl.when(q > 0)
        def _():
            give_back(ks[0], sources[0]).start()

        give_back(ks[1], sources[1]).start()

    pltpu.make_async_copy(ig_ref.at[mine], back_ref.at[mine], own_sem.at[0]).wait()
    for k in range(1, size):
        give_back(k, flip(mine, k)).wait()
    for copy in waits + [swap_rows, pair_in, pair_down]:
        copy.wait_send()


def experts(
    down, inward, dy, heads, tokens, own_w, other_w, gains, router, prev, routes, hot, padded
):
    members, _, d_rows, ff = inward.shape
    local, width = tokens.shape
    seq = heads.shape[0]
    size = EXPERTS_FF
    block = fit(ff, 512)
    any_spec = pl.BlockSpec(memory_space=pl.ANY)
    vmem = pl.BlockSpec(memory_space=pltpu.VMEM)
    dma = pltpu.SemaphoreType.DMA
    rows = jax.ShapeDtypeStruct((size, padded, width), half)
    wide = jax.ShapeDtypeStruct((2, size * padded, ff), half)
    return pl.pallas_call(
        functools.partial(experts_kernel, members, padded),
        out_shape=[
            rows,
            rows,
            rows,
            rows,
            wide,
            wide,
            wide,
            jax.ShapeDtypeStruct((local, width), single),
            jax.ShapeDtypeStruct((local, width), half),
            jax.ShapeDtypeStruct((local, LANES), single),
        ],
        in_specs=[any_spec] * 3 + [vmem] * 8 + [any_spec],
        out_specs=[any_spec] + [vmem] * 3 + [any_spec] * 3 + [vmem] * 3,
        scratch_shapes=[
            pltpu.VMEM((local, heads.shape[1]), half),
            pltpu.VMEM((seq, width + LANES), half),
            pltpu.VMEM((size // 2, 2 * padded, width + LANES), single),
            pltpu.VMEM((size, padded, width), half),
            pltpu.VMEM((16, 2 * LANES), single),
            pltpu.VMEM((2,) + inward.shape, half),
            pltpu.VMEM((2, members, d_rows, ff), half),
            pltpu.VMEM((size, padded, width), half),
            pltpu.VMEM((size, padded, width), half),
            pltpu.VMEM((2, 3, 2 * padded, block), half),
            pltpu.VMEM((2 * padded, LANES), single),
            pltpu.VMEM((16, 2 * LANES), single),
            pltpu.VMEM(hot.shape, half),
            dma((size,)),
            dma((size,)),
            dma((size,)),
            dma((size,)),
            dma((5,)),
            dma((4,)),
            dma((4,)),
            dma((size,)),
            dma((size,)),
            dma((2, 3, 2)),
        ],
        compiler_params=pltpu.CompilerParams(
            collective_id=1, has_side_effects=True, vmem_limit_bytes=62 << 20
        ),
        name="experts",
    )(down, inward, dy, heads, tokens, own_w, other_w, gains, router, prev, routes, hot)


def split(x):
    high = x.astype(half)
    return high, (x - high.astype(single)).astype(half)


def slot_rows(columns, count):
    slot = lax.broadcasted_iota(jnp.int32, (columns.shape[0], count), 1)
    hit = (columns[:, 2:3] == slot) | (columns[:, 3:4] == slot)
    return jnp.where(hit, 1.0, 0.0).astype(half)


def lane_sum(x):
    return jnp.sum(x, axis=1, keepdims=True)


def back_kernel(
    padded,
    back_ref,
    info_ref,
    resid_hbm_ref,
    normed_hbm_ref,
    misc_ref,
    dy_hbm_ref,
    routes_ref,
    gain_ref,
    const_ref,
    router_ref,
    own_w_ref,
    other_w_ref,
    prev_ref,
    mix_ref,
    rgrad_ref,
    attn_ref,
    heads_ref,
    base_ref,
    pgrad_ref,
    small_ref,
    mgrad_ref,
    ext_ref,
    out_ref,
    in_ref,
    hg_ref,
    send_sem,
    recv_sem,
    resid_ref,
    normed_ref,
    dy_ref,
    load_sem,
):
    core = lax.axis_index("tensor")
    partner = {"tensor": 1 - core}
    sources, _, width = back_ref.shape
    count = sources * padded
    local = dy_ref.shape[0]
    step = fit(local, 256)
    pairs = (resid_hbm_ref, resid_ref), (normed_hbm_ref, normed_ref), (dy_hbm_ref, dy_ref)
    loads = [
        pltpu.make_async_copy(source, target, load_sem.at[i])
        for i, (source, target) in enumerate(pairs)
    ]
    for copy in loads:
        copy.start()
    barrier = pltpu.get_barrier_semaphore()
    pl.semaphore_signal(barrier, inc=1, device_id=partner, device_id_type=MESH)
    pl.semaphore_wait(barrier, 1)

    def remote(src, dst, number):
        return pltpu.make_async_remote_copy(
            src_ref=src,
            dst_ref=dst,
            send_sem=send_sem.at[number],
            recv_sem=recv_sem.at[number],
            device_id=partner,
            device_id_type=MESH,
        )

    own_rows = pl.ds(pl.multiple_of(core * local, local), local)
    lane = lax.broadcasted_iota(jnp.int32, (step, LANES), 1)
    for s in range(sources):
        dots = back_ref[s, padded - 16 :, : 2 * LANES].astype(single).T
        number = lax.broadcasted_iota(jnp.int32, (padded, LANES), 1)
        ext = jnp.where(
            number == s,
            dots[:padded, 14:15],
            jnp.where(number == s + EXPERTS_FF, dots[:padded, 15:16], 0.0),
        )
        ext_ref[pl.ds(s * padded, padded), :] = ext.astype(half)
    back_all = back_ref.reshape(count, width)

    @pl.loop(0, local // step)
    def _(r):
        rows = pl.ds(pl.multiple_of(r * step, step), step)
        there = pl.ds(pl.multiple_of((1 - core) * local + r * step, step), step)
        hot = slot_rows(info_ref[there, :], count)
        out_ref[rows, pl.ds(0, width)] = mm(hot, back_all[...]).astype(half)
        out_ref[rows, pl.ds(width, LANES)] = mm(hot, ext_ref[...]).astype(half)

    sums = remote(out_ref, in_ref, 0)
    sums.start()
    small_ref[...] = jnp.zeros(small_ref.shape, single)
    mgrad_ref[...] = jnp.zeros(mgrad_ref.shape, single)

    @pl.loop(0, local // step)
    def _(r):
        rows = pl.ds(pl.multiple_of(r * step, step), step)
        here = pl.ds(pl.multiple_of(core * local + r * step, step), step)
        hot = slot_rows(info_ref[here, :], count)
        rgrad_ref[rows, :] = mm(hot, back_all[...])
        pgrad_ref[rows, :] = mm(hot, ext_ref[...])

    for copy in loads:
        copy.wait()
    sums.wait()

    @pl.loop(0, local // step)
    def _(r):
        rows = pl.ds(pl.multiple_of(r * step, step), step)
        here = pl.ds(pl.multiple_of(core * local + r * step, step), step)
        dy = dy_ref[rows, :].astype(single)
        normed = normed_ref[rows, :].astype(single)
        resid = resid_ref[rows, :]
        misc = misc_ref[rows, :]
        expert_dot = pgrad_ref[rows, :] + in_ref[rows, pl.ds(width, LANES)].astype(single)
        own_dot = lane_sum(dy * normed)
        vec_dot = [lane_sum(dy * const_ref[j : j + 1, :]) for j in range(2)]
        gates = [misc[:, k : k + 1] for k in range(2)]
        routes = [routes_ref[rows, k : k + 1] for k in range(2)]
        alphas = []
        for j in range(2):
            columns = [misc[:, EXPERTS + 2 * j + m : EXPERTS + 2 * j + m + 1] for m in range(2)]
            peak = jnp.maximum(columns[0], columns[1])
            expo = [jnp.exp(c - peak) for c in columns]
            total = expo[0] + expo[1]
            alphas.append([e / total for e in expo])
        gate_grads = []
        for k in range(2):
            hit = (lane == routes[k]) | (lane == routes[k] + EXPERTS_FF)
            dot = lane_sum(jnp.where(hit & (routes[k] < EXPERTS_FF), expert_dot, 0.0))
            dot += jnp.where(routes[k] == EXPERTS_FF + 1, own_dot, 0.0)
            for j in range(2):
                value = alphas[j][0] * own_dot + alphas[j][1] * vec_dot[j]
                dot += jnp.where(routes[k] == EXPERTS_FF + 2 + j, value, 0.0)
            gate_grads.append(dot)
        centre = gates[0] * gate_grads[0] + gates[1] * gate_grads[1]
        chosen = [gates[k] * (gate_grads[k] - centre) for k in range(2)]
        router_grad = jnp.zeros((step, LANES), single)
        own_weight = jnp.zeros((step, 1), single)
        for k in range(2):
            router_grad = jnp.where(lane == routes[k], chosen[k], router_grad)
            own_weight += jnp.where(routes[k] == EXPERTS_FF + 1, gates[k], 0.0)
        logit_grad = router_grad
        vec_lanes = jnp.zeros((step, LANES), single)
        other = jnp.zeros((step, width), single)
        for j in range(2):
            weight = sum(jnp.where(routes[k] == EXPERTS_FF + 2 + j, gates[k], 0.0) for k in range(2))
            grads = [weight * own_dot, weight * vec_dot[j]]
            mean = alphas[j][0] * grads[0] + alphas[j][1] * grads[1]
            for m in range(2):
                router_grad = jnp.where(
                    lane == EXPERTS + 2 * j + m, alphas[j][m] * (grads[m] - mean), router_grad
                )
            own_weight += weight * alphas[j][0]
            vec_weight = weight * alphas[j][1]
            vec_lanes = jnp.where(lane == 16 + j, vec_weight, vec_lanes)
            other += vec_weight * const_ref[j : j + 1, :]
        base_ref[rows, :] = resid + own_weight * normed + other
        rg_high, rg_low = split(router_grad)
        two_grad = rgrad_ref[rows, :] + in_ref[rows, pl.ds(0, width)].astype(single)
        two_grad += own_weight * dy
        two_grad += mm_nt(rg_high, router_ref[...]) + mm_nt(rg_low, router_ref[...])
        normed_low = normed_ref[rows, :]
        vec_high, vec_low = split(vec_lanes)
        small_ref[...] += (
            mm_tn(rg_high, normed_low)
            + mm_tn(rg_low, normed_low)
            + mm_tn(vec_high, dy_ref[rows, :])
            + mm_tn(vec_low, dy_ref[rows, :])
        )[:24]
        scale = rms_scale(resid)
        gain_part = jnp.sum(two_grad * resid * scale, axis=0, keepdims=True)
        small_ref[19:20, :] += gain_part
        weighted = two_grad * gain_ref[1:2, :]
        mean = jnp.mean(weighted * resid, axis=-1, keepdims=True)
        grad = dy + scale * (weighted - resid * scale * scale * mean)
        rgrad_ref[rows, :] = grad
        low = grad.astype(half)
        attn_ref[here, :] = low
        heads_ref[here, :] = mm(low, own_w_ref[...]).astype(half)
        hg_ref[rows, :] = mm(low, other_w_ref[...]).astype(half)
        lg_high, lg_low = split(logit_grad)
        mix_high, mix_low = split(mix_ref[...])
        pgrad_ref[rows, :] = (
            mm_nt(lg_high, mix_high) + mm_nt(lg_high, mix_low) + mm_nt(lg_low, mix_high)
        )
        prev_high, prev_low = split(prev_ref[rows, :])
        mgrad_ref[...] += (
            mm_tn(prev_high, lg_high) + mm_tn(prev_high, lg_low) + mm_tn(prev_low, lg_high)
        )

    for i in range(EXPERTS):
        place = pl.ds(i % 6 * LANES, LANES)
        small_ref[20 + i // 6 : 21 + i // 6, place] = mgrad_ref[i : i + 1, :]

    heads = remote(hg_ref, heads_ref.at[own_rows], 1)
    heads.start()
    attn = remote(attn_ref.at[own_rows], attn_ref.at[own_rows], 2)
    attn.start()
    heads.wait()
    attn.wait()


def backward_middle(
    back, info, resid, normed, misc, dy, routes, gains, const, router, own_w, other_w, prev, mix, padded
):
    local, width = dy.shape
    seq = info.shape[0]
    hh = own_w.shape[1]
    count = EXPERTS_FF * padded
    vmem = pl.BlockSpec(memory_space=pltpu.VMEM)
    hbm = pl.BlockSpec(memory_space=pltpu.HBM)
    return pl.pallas_call(
        functools.partial(back_kernel, padded),
        out_shape=[
            jax.ShapeDtypeStruct((local, width), single),
            jax.ShapeDtypeStruct((seq, width), half),
            jax.ShapeDtypeStruct((seq, hh), half),
            jax.ShapeDtypeStruct((local, width), single),
            jax.ShapeDtypeStruct((local, LANES), single),
            jax.ShapeDtypeStruct((24, width), single),
            jax.ShapeDtypeStruct((LANES, LANES), single),
        ],
        in_specs=[vmem] * 2 + [hbm] * 2 + [vmem, hbm] + [vmem] * 8,
        out_specs=[vmem] * 7,
        scratch_shapes=[
            pltpu.VMEM((count, LANES), half),
            pltpu.VMEM((local, width + LANES), half),
            pltpu.VMEM((local, width + LANES), half),
            pltpu.VMEM((local, hh), half),
            pltpu.SemaphoreType.DMA((3,)),
            pltpu.SemaphoreType.DMA((3,)),
            pltpu.VMEM((local, width), single),
            pltpu.VMEM((local, width), half),
            pltpu.VMEM((local, width), half),
            pltpu.SemaphoreType.DMA((3,)),
        ],
        compiler_params=pltpu.CompilerParams(
            collective_id=2, has_side_effects=True, vmem_limit_bytes=56 << 20
        ),
        name="backward_middle",
    )(back, info, resid, normed, misc, dy, routes, gains, const, router, own_w, other_w, prev, mix)


def weight_kernel(
    x_ref,
    og_ref,
    hid_ref,
    pg_ref,
    pu_ref,
    out_ref,
    xt_ref,
    ogt_ref,
    send_ref,
    got_ref,
    own_ref,
    send_sem,
    recv_sem,
):
    f = pl.program_id(0)
    partner = {"tensor": 1 - lax.axis_index("tensor")}
    shape = out_ref.shape[0], out_ref.shape[2], out_ref.shape[3]

    @pl.when(f == 0)
    def _():
        barrier = pltpu.get_barrier_semaphore()
        pl.semaphore_signal(barrier, inc=1, device_id=partner, device_id_type=MESH)
        pl.semaphore_wait(barrier, 1)
        xt_ref[...] = x_ref[...].T
        ogt_ref[...] = og_ref[...].T

    def remote(number):
        return pltpu.make_async_remote_copy(
            src_ref=send_ref.at[number],
            dst_ref=got_ref.at[number],
            send_sem=send_sem.at[number],
            recv_sem=recv_sem.at[number],
            device_id=partner,
            device_id_type=MESH,
        )

    factors = (xt_ref, pg_ref), (xt_ref, pu_ref), (ogt_ref, hid_ref)
    for k, (left, right) in enumerate(factors):
        send_ref[f, k] = mm(left[...], right[1]).astype(half)
    remote(f).start()
    for k, (left, right) in enumerate(factors):
        own_ref[k] = mm(left[...], right[0])
    remote(f).wait_recv()
    for k in range(3):
        total = own_ref[k] + got_ref[f, k].astype(single)
        out_ref[:, k] = total.astype(half).reshape(shape)

    @pl.when(f == pl.num_programs(0) - 1)
    def _():
        for number in range(send_ref.shape[0]):
            remote(number).wait_send()


def weight_step(x, og, hidden, pg, pu, m):
    count, width = og.shape
    ff = hidden.shape[2]
    block = fit(ff, 256)
    steps = ff // block
    whole = pl.BlockSpec((count, width), lambda f: (0, 0))
    wide = pl.BlockSpec((2, count, block), lambda f: (0, 0, f))
    part = pl.BlockSpec((m, 3, width // m, block), lambda f: (0, 0, 0, f))
    return pl.pallas_call(
        weight_kernel,
        grid=(steps,),
        in_specs=[whole, whole, wide, wide, wide],
        out_specs=part,
        out_shape=jax.ShapeDtypeStruct((m, 3, width // m, ff), half),
        scratch_shapes=[
            pltpu.VMEM((width, count), half),
            pltpu.VMEM((width, count), half),
            pltpu.VMEM((steps, 3, width, block), half),
            pltpu.VMEM((steps, 3, width, block), half),
            pltpu.VMEM((3, width, block), single),
            pltpu.SemaphoreType.DMA((steps,)),
            pltpu.SemaphoreType.DMA((steps,)),
        ],
        compiler_params=pltpu.CompilerParams(
            collective_id=3, has_side_effects=True, vmem_limit_bytes=56 << 20
        ),
        cost_estimate=pl.CostEstimate(
            flops=12 * count * width * ff,
            bytes_accessed=12 * width * ff + 12 * count * ff,
            transcendentals=0,
        ),
        name="weight_step",
    )(x, og, hidden, pg, pu)


def tail_kernel(
    members,
    low,
    padded,
    eo_hbm_ref,
    qkv_ref,
    one_ref,
    proj_ref,
    outg_ref,
    x_hbm_ref,
    base_hbm_ref,
    resid_hbm_ref,
    info_ref,
    gain_ref,
    small_ref,
    grads_ref,
    proj_out_ref,
    outw_ref,
    tokens_ref,
    mixed_ref,
    small_out_ref,
    expert_ref,
    dense_ref,
    first_ref,
    stage_ref,
    second_ref,
    one_out_ref,
    one_in_ref,
    ffn_out_ref,
    ffn_in_ref,
    ffn_ref,
    mine_ref,
    pair_ref,
    near_ref,
    far_ref,
    dense_out_ref,
    send1,
    recv1,
    send2,
    recv2,
    pair_send,
    pair_recv,
    near_send,
    near_recv,
    far_send,
    far_recv,
    part_ref,
    sum_ref,
    part_sem,
    sum_sem,
    eo_ref,
    x_ref,
    base_ref,
    resid_ref,
    load_sem,
):
    size = EXPERTS_FF
    me = lax.axis_index("dp")
    core = lax.axis_index("tensor")
    high = members // low
    inside, row = lax.rem(me, low), me // low
    local, width = base_ref.shape
    count = size * padded
    d_rows = outw_ref.shape[0]
    hh3 = qkv_ref.shape[1]
    step = fit(local, 256)
    partner = {"tensor": 1 - core}

    def beside(k):
        return row * low + flip(inside, k)

    def across(k):
        return lax.rem(row + k, high) * low + inside

    peers = [beside(k) for k in range(1, low)] + [across(k) for k in range(1, high)]
    barrier = pltpu.get_barrier_semaphore()
    for peer in peers:
        pl.semaphore_signal(barrier, inc=1, device_id={"dp": peer}, device_id_type=MESH)
    pl.semaphore_signal(barrier, inc=1, device_id=partner, device_id_type=MESH)
    pl.semaphore_wait(barrier, len(peers) + 1)

    def remote(src, dst, send, recv, device):
        return pltpu.make_async_remote_copy(
            src_ref=src,
            dst_ref=dst,
            send_sem=send,
            recv_sem=recv,
            device_id=device,
            device_id_type=MESH,
        )

    pairs = (x_hbm_ref, x_ref), (eo_hbm_ref, eo_ref), (base_hbm_ref, base_ref), (resid_hbm_ref, resid_ref)
    loads = [
        pltpu.make_async_copy(source, target, load_sem.at[i])
        for i, (source, target) in enumerate(pairs)
    ]
    for copy in loads:
        copy.start()

    sent = []
    chunks = 2
    rows_each = width // chunks
    for c in range(chunks):
        lanes = pl.ds(c * rows_each, rows_each)
        grad = mm_tn(one_ref[:, lanes], qkv_ref[...])
        for j in range(members // chunks):
            owner = c * (members // chunks) + j
            dense_ref[owner, :, :hh3] = grad[j * d_rows : (j + 1) * d_rows].astype(half)
            dense_ref[owner, :, hh3:] = outg_ref[owner * d_rows : (owner + 1) * d_rows, :]
        for h in range(c * high // chunks, (c + 1) * high // chunks):
            for k in BESIDE:
                copy = remote(
                    dense_ref.at[h * low + flip(inside, k)],
                    first_ref.at[k - 1, h],
                    send1.at[k - 1, h],
                    recv1.at[k - 1, h],
                    {"dp": beside(k)},
                )
                copy.start()
                sent.append(copy)

    def one_part(rows):
        part = mm_nt(qkv_ref[rows, :], proj_ref[...])
        x = x_ref[rows, :].astype(single)
        mine_ref[18:19, :] += jnp.sum(part * x * rms_scale(x), axis=0, keepdims=True)
        return part

    mine_ref[...] = small_ref[...]
    for copy in loads:
        copy.wait()

    @pl.loop(0, local // step)
    def _(r):
        rows = pl.ds(pl.multiple_of(r * step, step), step)
        there = pl.ds(pl.multiple_of((1 - core) * local + r * step, step), step)
        one_out_ref[rows, :] = one_part(there).astype(half)

    one_sent = remote(one_out_ref, one_in_ref, pair_send.at[0], pair_recv.at[0], partner)
    one_sent.start()

    @pl.loop(0, local // step)
    def _(r):
        rows = pl.ds(pl.multiple_of(r * step, step), step)
        here = pl.ds(pl.multiple_of(core * local + r * step, step), step)
        tokens_ref[rows, :] = one_part(here)

    pair = remote(mine_ref, pair_ref, pair_send.at[1], pair_recv.at[1], partner)
    pair.start()

    eo_all = eo_ref.reshape(count, width)

    @pl.loop(0, local // step)
    def _(r):
        rows = pl.ds(pl.multiple_of(r * step, step), step)
        there = pl.ds(pl.multiple_of((1 - core) * local + r * step, step), step)
        ffn_out_ref[rows, :] = mm(slot_rows(info_ref[there, :], count), eo_all[...]).astype(half)

    ffn_sent = remote(ffn_out_ref, ffn_in_ref, pair_send.at[2], pair_recv.at[2], partner)
    ffn_sent.start()

    @pl.loop(0, local // step)
    def _(r):
        rows = pl.ds(pl.multiple_of(r * step, step), step)
        here = pl.ds(pl.multiple_of(core * local + r * step, step), step)
        ffn_ref[rows, :] = mm(slot_rows(info_ref[here, :], count), eo_all[...])

    def second(h):
        return remote(
            stage_ref.at[h],
            second_ref.at[row],
            send2.at[h],
            recv2.at[row],
            {"dp": h * low + inside},
        )

    pair.wait()
    near_ref[inside] = mine_ref[...] + pair_ref[...]
    near = []
    for k in range(1, low):
        near.append(
            remote(
                near_ref.at[inside],
                near_ref.at[inside],
                near_send.at[k],
                near_recv.at[inside],
                {"dp": beside(k)},
            )
        )
        near[-1].start()

    for h in range(high):
        for k in range(low - 1):
            remote(
                dense_ref.at[0], first_ref.at[k, h], send1.at[k, h], recv1.at[k, h], partner
            ).wait_recv()
        total = dense_ref[h * low + inside].astype(single)
        for k in range(low - 1):
            total += first_ref[k, h].astype(single)

        @pl.when(h == row)
        def _():
            dense_out_ref[...] = total

        @pl.when(h != row)
        def _():
            stage_ref[h] = total.astype(half)
            second(h).start()

    for k in range(1, low):
        block = lax.rem(inside + k, low)
        remote(
            mine_ref, near_ref.at[block], near_send.at[0], near_recv.at[block], partner
        ).wait_recv()
    total = near_ref[0]
    for k in range(1, low):
        total = total + near_ref[k]
    far_ref[row] = total
    far = []
    for k in range(1, high):
        far.append(
            remote(
                far_ref.at[row], far_ref.at[row], far_send.at[k], far_recv.at[row], {"dp": across(k)}
            )
        )
        far[-1].start()

    groups = members // size

    def load(e):
        return [
            pltpu.make_async_copy(
                grads_ref.at[g * size + e], part_ref.at[e % 2, g], part_sem.at[e % 2, g]
            )
            for g in range(groups)
        ]

    def store(e):
        return pltpu.make_async_copy(sum_ref.at[e % 2], expert_ref.at[e], sum_sem.at[e % 2])

    for copy in load(0):
        copy.start()
    for e in range(size):
        if e + 1 < size:
            for copy in load(e + 1):
                copy.start()
        for copy in load(e):
            copy.wait()
        if e >= 2:
            store(e - 2).wait()
        total = part_ref[e % 2, 0].astype(single)
        for g in range(1, groups):
            total += part_ref[e % 2, g].astype(single)
        sum_ref[e % 2] = total
        store(e).start()
    for e in range(size - 2, size):
        store(e).wait()

    one_sent.wait()

    @pl.loop(0, local // step)
    def _(r):
        rows = pl.ds(pl.multiple_of(r * step, step), step)
        here = pl.ds(pl.multiple_of(core * local + r * step, step), step)
        x = x_ref[here, :].astype(single)
        scale = rms_scale(x)
        weighted = (tokens_ref[rows, :] + one_in_ref[rows, :].astype(single)) * gain_ref[0:1, :]
        mean = jnp.mean(weighted * x, axis=-1, keepdims=True)
        tokens_ref[rows, :] = resid_ref[rows, :] + scale * (weighted - x * scale * scale * mean)

    ffn_sent.wait()

    @pl.loop(0, local // step)
    def _(r):
        rows = pl.ds(pl.multiple_of(r * step, step), step)
        total = base_ref[rows, :] + ffn_ref[rows, :] + ffn_in_ref[rows, :].astype(single)
        mixed_ref[rows, :] = total.astype(half)

    for h in range(high):

        @pl.when(h != row)
        def _():
            remote(
                stage_ref.at[0], second_ref.at[h], send2.at[0], recv2.at[h], partner
            ).wait_recv()
            dense_out_ref[...] += second_ref[h].astype(single)
            second(h).wait_send()

    hh = outw_ref.shape[1]
    for c in range(3):
        proj_out_ref[c] = dense_out_ref[:, c * hh : (c + 1) * hh]
    outw_ref[...] = dense_out_ref[:, 3 * hh :]
    for k in range(1, high):
        block = lax.rem(row + k, high)
        remote(
            mine_ref, far_ref.at[block], far_send.at[0], far_recv.at[block], partner
        ).wait_recv()
    total = far_ref[0]
    for k in range(1, high):
        total = total + far_ref[k]
    small_out_ref[...] = total
    for copy in sent + near + far:
        copy.wait_send()


def tail(members, eo, qkv, one, proj, outg, x, base, resid, info, gains, small, grads, padded):
    low = 4
    high = members // low
    local, width = base.shape
    d_rows = width // members
    hh = outg.shape[1]
    wide = qkv.shape[1] + hh
    groups = members // EXPERTS_FF
    vmem = pl.BlockSpec(memory_space=pltpu.VMEM)
    hbm = pl.BlockSpec(memory_space=pltpu.HBM)
    dma = pltpu.SemaphoreType.DMA
    rows_half = pltpu.VMEM((local, width), half)
    small_one = pltpu.VMEM(small.shape, single)
    return pl.pallas_call(
        functools.partial(tail_kernel, members, low, padded),
        out_shape=[
            jax.ShapeDtypeStruct((3, d_rows, hh), single),
            jax.ShapeDtypeStruct((d_rows, hh), single),
            jax.ShapeDtypeStruct((local, width), single),
            jax.ShapeDtypeStruct((local, width), half),
            jax.ShapeDtypeStruct(small.shape, single),
            jax.ShapeDtypeStruct((EXPERTS_FF,) + grads.shape[1:], single),
        ],
        in_specs=[hbm] + [vmem] * 4 + [hbm] * 3 + [vmem] * 3 + [hbm],
        out_specs=[vmem] * 5 + [hbm],
        scratch_shapes=[
            pltpu.VMEM((members, d_rows, wide), half),
            pltpu.VMEM((low - 1, high, d_rows, wide), half),
            pltpu.VMEM((high, d_rows, wide), half),
            pltpu.VMEM((high, d_rows, wide), half),
            rows_half,
            rows_half,
            rows_half,
            rows_half,
            pltpu.VMEM((local, width), single),
            small_one,
            small_one,
            pltpu.VMEM((low,) + small.shape, single),
            pltpu.VMEM((high,) + small.shape, single),
            pltpu.VMEM((d_rows, wide), single),
            dma((low - 1, high)),
            dma((low - 1, high)),
            dma((high,)),
            dma((high,)),
            dma((3,)),
            dma((3,)),
            dma((low,)),
            dma((low,)),
            dma((high,)),
            dma((high,)),
            pltpu.VMEM((2, groups) + grads.shape[1:], half),
            pltpu.VMEM((2,) + grads.shape[1:], single),
            dma((2, groups)),
            dma((2,)),
            pltpu.VMEM(eo.shape, half),
            pltpu.VMEM(x.shape, half),
            pltpu.VMEM(base.shape, single),
            pltpu.VMEM(resid.shape, single),
            dma((4,)),
        ],
        compiler_params=pltpu.CompilerParams(
            collective_id=4, has_side_effects=True, vmem_limit_bytes=60 << 20
        ),
        name="tail",
    )(eo, qkv, one, proj, outg, x, base, resid, info, gains, small, grads)


def per_device(
    tokens,
    segment_ids,
    routes,
    prev_logits,
    cotangent,
    proj_weight,
    out_weight,
    norm_gain,
    expert_weight,
    router,
    constant_vectors,
    gate_mixing,
):
    members = lax.axis_size("dp")
    groups = members // EXPERTS_FF
    cubes = [[g * EXPERTS_FF + i for i in range(EXPERTS_FF)] for g in range(groups)]
    core = lax.axis_index("tensor")
    d_rows, hh = out_weight.shape
    per_core = -(-CAPACITY // 2)
    padded = -(-(per_core + 3) // 16) * 16

    def in_group(blocks):
        return lax.all_to_all(blocks, "dp", 0, 0, axis_index_groups=cubes, tiled=True)

    def plain_tail(eo, qkv, one, proj, outg, x, base, resid, gains, small, grads):
        ffn = pair_sum(mm_tn(onehot, eo.reshape(-1, width)))
        part = mm_nt(qkv, proj)
        scale = rms_scale(x)
        small = small.at[18].set(jnp.sum(part * x * scale, axis=0))
        weighted = pair_sum(part) * gains[0]
        x, scale = half_of(x, core), half_of(scale, core)
        mean = jnp.mean(weighted * x, axis=-1, keepdims=True)
        tokens_grad = resid + scale * (weighted - x * scale * scale * mean)
        dense = jnp.concatenate([mm_tn(one, qkv).astype(half), outg], 1)
        dense = lax.all_to_all(dense.reshape(members, d_rows, -1), "dp", 0, 0, tiled=True)
        dense = jnp.sum(dense.astype(single), axis=0)
        grads = grads.reshape((groups, EXPERTS_FF) + grads.shape[1:]).astype(single)
        return (
            dense[:, : 3 * hh].reshape(d_rows, 3, hh).transpose(1, 0, 2),
            dense[:, 3 * hh :],
            tokens_grad,
            (base + ffn).astype(half),
            lax.psum(small, ("dp", "tensor")),
            jnp.sum(grads, axis=0),
        )

    pack = jnp.concatenate(
        [
            proj_weight.transpose(1, 0, 2).reshape(d_rows, 3 * hh),
            out_weight,
            norm_gain.T,
            constant_vectors.T,
            router,
        ],
        1,
    )
    columns = pack.shape[1]
    pack = jnp.pad(pack, ((0, 0), (0, -columns % LANES)))
    ids = jnp.concatenate([segment_ids, routes[0].T], 0)
    ids = jnp.pad(ids, ((0, 5), (0, 0)))
    full_pack, tokens_all, dy_rows, onehot, info, my_down, in_weight = start(
        pack, tokens[0], cotangent[0], ids, expert_weight, members, per_core, padded
    )
    full_pack = full_pack.reshape(members * d_rows, -1)[:, :columns]
    width = members * d_rows
    proj_full = full_pack[:, : 3 * hh]
    outw_own = full_pack[:, 3 * hh : 4 * hh]
    outw_other = swap(outw_own)
    rest = full_pack[:, 4 * hh :]
    gains = rest[:, :2].T.astype(single)
    const_f = rest[:, 2:4].T.astype(single)
    router_full = rest[:, 4:]
    my_in = lax.all_to_all(in_weight, "dp", 0, 0, tiled=True)

    x_rows = tokens[0].astype(single)
    local_rows = x_rows.shape[0]
    x_all = tokens_all.astype(single)
    scale_all = rms_scale(x_all)
    full_one = (x_all * scale_all * gains[0]).astype(half)
    scale_one = half_of(scale_all, core)
    seq = full_one.shape[0]
    qkv = mm(full_one, proj_full).astype(half)
    size = fit(seq, 256)
    starts = info[0]
    bounds = block_bounds(starts, info[1], size)
    columns = info.T
    heads_full, heads_out, lse = attention_forward(qkv, bounds, starts, size)
    prev_rows = prev_logits[0]
    mixed_prev = jnp.dot(prev_rows, gate_mixing, precision=HIGH)
    mixed_prev = jnp.pad(mixed_prev, ((0, 0), (0, LANES - EXPERTS)))
    router_wide = jnp.pad(router_full, ((0, 0), (0, LANES - router_full.shape[1])))
    mix_wide = jnp.pad(gate_mixing, ((0, LANES - EXPERTS), (0, LANES - EXPERTS)))
    prev_wide = jnp.pad(prev_rows, ((0, 0), (0, LANES - EXPERTS)))
    router_wide, mixed_prev, mix_wide, prev_wide, columns, proj_full = lax.optimization_barrier(
        (router_wide, mixed_prev, mix_wide, prev_wide, columns, proj_full)
    )
    back_grad, gated_out, got_rows, out_grad, hidden, pg, pu, resid, normed_two, misc = experts(
        my_down,
        my_in,
        dy_rows,
        heads_out,
        tokens[0],
        outw_own,
        outw_other,
        gains,
        router_wide,
        mixed_prev,
        routes[0],
        onehot,
        padded,
    )
    count = EXPERTS_FF * padded
    grads_sent = weight_step(
        got_rows.reshape(count, width),
        out_grad.reshape(count, width),
        hidden,
        pg,
        pu,
        1 if d_rows % 16 else members,
    )
    back_out = in_group(gated_out)
    back_grad, grads_sent, back_out = lax.optimization_barrier((back_grad, grads_sent, back_out))
    if d_rows % 16:
        grads_sent = grads_sent.reshape(3, members, d_rows, -1).transpose(1, 0, 2, 3)
    grads_got = lax.all_to_all(grads_sent, "dp", 0, 0, tiled=True)

    resid_grad, attn_all, heads_grad, base, prev_grad, small, mixing_grad = backward_middle(
        back_grad,
        columns,
        resid,
        normed_two,
        misc,
        cotangent[0],
        routes[0],
        gains,
        const_f,
        router_wide,
        outw_own,
        outw_other,
        prev_wide,
        mix_wide,
        padded,
    )
    out_w_grad = mm_tn(attn_all, heads_out)
    qkv_grad = attention_backward(qkv, heads_grad, heads_full, lse, bounds, starts, size)
    qkv_grad, grads_got = lax.optimization_barrier((qkv_grad, grads_got))
    out_w_grad = out_w_grad.astype(half)
    if d_rows % 16 or members != 16:
        outs = plain_tail(
            back_out, qkv_grad, full_one, proj_full, out_w_grad, x_all, base, resid_grad, gains, small, grads_got
        )
    else:
        outs = tail(
            members,
            back_out,
            qkv_grad,
            full_one,
            proj_full,
            out_w_grad,
            tokens_all,
            base,
            resid_grad,
            columns,
            gains,
            small,
            grads_got,
            padded,
        )
    proj_shard, outw_shard, tokens_grad, mixed, small, expert_shard = outs
    mixing_total = small[20:22].reshape(EXPERTS, LANES)[:, :EXPERTS]
    features = lax.dynamic_slice_in_dim(small, lax.axis_index("dp") * d_rows, d_rows, 1)
    return (
        mixed[None],
        tokens_grad[None],
        prev_grad[None, :, :EXPERTS],
        proj_shard,
        outw_shard,
        features[18:20],
        expert_shard,
        features[:16].T,
        features[16:18],
        mixing_total,
    )


def solution(mesh):
    return jax.shard_map(
        per_device,
        mesh=mesh,
        in_specs=(
            P("dp", "tensor", None),
            P("dp", "tensor"),
            P("dp", "tensor", None),
            P("dp", "tensor", None),
            P("dp", "tensor", None),
            P(None, "dp", "tensor"),
            P("dp", "tensor"),
            P(None, "dp"),
            P(None, None, "dp", "tensor"),
            P("dp", None),
            P(None, "dp"),
            P(),
        ),
        out_specs=(
            P("dp", "tensor", None),
            P("dp", "tensor", None),
            P("dp", "tensor", None),
            P(None, "dp", "tensor"),
            P("dp", "tensor"),
            P(None, "dp"),
            P(None, None, "dp", "tensor"),
            P("dp", None),
            P(None, "dp"),
            P(),
        ),
        check_vma=False,
    )
```
